32 devices in a mesh: ep: 16 (over z, y, x), et: 2 (over core).
Axes of the slice: x: 2, y: 2, z: 4, core: 2. Of those that a mesh axis runs over, the one named last changes fastest.
Arguments:
- tokens: bfloat16 [2048, 3584], P('ep', 'et'), may hold values from -6 to 6
- slot_ids: int32 [2048, 8], P('ep'), may hold values from 0 to 15, all different within a row; in each aligned block of 128 rows (0 to 127, 128 to 255, ...) at most 80 rows name the same one
- gate_weights: float32 [2048, 8], P('ep'), may hold values from 0.1 to 1
- old_expert: int32 [16], replicated, may hold values from 0 to 13, as said below
- new_expert: int32 [16], replicated, may hold values from 0 to 13, as said below
- gate_proj: bfloat16 [16, 3584, 1024], P(None, 'ep', 'et'), may hold values from -0.09375 to 0.09375
- up_proj: bfloat16 [16, 3584, 1024], P(None, 'ep', 'et'), may hold values from -0.09375 to 0.09375
- down_proj: bfloat16 [16, 3584, 1024], P(None, 'ep', 'et'), may hold values from -0.1875 to 0.1875
Outputs:
- layer_out: bfloat16 [2048, 3584], P('ep', 'et')
The draws below stay inside these ranges and needn't reach their ends.
Inputs may be any that keep to these rules, and one draw needn't show every extreme that they name: `slot_ids`: each row names 8 different slots. The rows of one index of ep name no slot more than 80 times, and in every draw some slot exactly 80 times on some index. `old_expert`: names every expert 0 to 13 once or twice; 2 of them twice. `new_expert`: names every expert 0 to 13 once or twice; 2 of them twice.
All inputs are finite; a program needn't handle non-finite values.
Results may differ from the reference program's by a relative error of at most 0.015.
Values may be sent and summed in bfloat16 or wider, within the bound.
No kernel may reach another device: no remote copies, remote signals or barrier semaphores. Data moves between devices by JAX's collectives and lax.ppermute only.
A program may use at most 128 MiB of HBM per device.

```python
import math
import jax
import jax.numpy as jnp
import numpy as np
from jax import lax

D = 3584
FF = 1024
TOP = 8
TOK_DEV = 128
SLOTS = 16
EXPERTS = 14
CAP = 80
TOKENS = 2048
N_EP = 16
N_ET = 2


def draw_old_expert(key, part):
    key = jax.random.fold_in(key, 11)
    ordering = jax.random.permutation(key, SLOTS)
    return (ordering % EXPERTS).astype(jnp.int32)


def draw_new_expert(key, part):
    key = jax.random.fold_in(key, 23)
    key_order, key_shift = jax.random.split(key)
    ordering = jax.random.permutation(key_order, SLOTS)
    offset = jax.random.randint(key_shift, (), 0, EXPERTS)
    return ((ordering % EXPERTS + offset) % EXPERTS).astype(jnp.int32)


def shard_levels(stream_key, shape, cuts, least, largest):
    gain = 1.0
    for dim, blocks in cuts:
        draws = jax.random.uniform(jax.random.fold_in(jax.random.fold_in(stream_key, 6), dim), (blocks,), jnp.float32, least / len(cuts), largest / len(cuts))
        gain = gain * jnp.repeat(jnp.exp(draws), shape[dim] // blocks).reshape((-1,) + (1,) * (len(shape) - 1 - dim))
    return gain


def assign_block(own_key, own, number, rows, amount, top, bound, slope):
    order = jax.random.permutation(own_key, amount)
    crowded, usual = load_shares(amount, rows * top, bound, slope, True), load_shares(amount, rows * top, bound, slope, False)
    places = jnp.arange(amount)

    def named(tallies, rotation):
        used = int((tallies > 0).sum())
        fixed = max(1, used // 4)
        moved = fixed + (places - fixed + rotation * (used - fixed)) % max(1, amount - fixed)
        return jnp.zeros((amount,), jnp.int32).at[order[jnp.where(places < fixed, places, moved)]].set(jnp.asarray(tallies, jnp.int32))

    tallies = jnp.where(number % 4 == 0, named(crowded, number // 4), named(usual, number - number // 4 - 1))
    mixed = jax.random.permutation(jax.random.fold_in(own, 3), amount)
    source_of, sink = mixed[0:amount // 2 * 2:2], mixed[1:amount // 2 * 2:2]
    margin = jnp.minimum(tallies[source_of] - 1, bound - tallies[sink]) // 2
    margin = jnp.where((source_of == order[0]) | (sink == order[0]) | (tallies[sink] == 0), 0, jnp.maximum(margin, 0))
    moved = jax.random.randint(jax.random.fold_in(own, 4), (amount // 2,), 0, 1 << 20) % (margin + 1)
    tallies = tallies.at[source_of].add(-moved).at[sink].add(moved)
    labels = jnp.searchsorted(jnp.cumsum(tallies), jnp.arange(rows * top), side="right").astype(jnp.int32)
    listing = labels.reshape(top, rows).T
    listing = listing[jax.random.permutation(jax.random.fold_in(own, 1), rows)]
    rotation = jax.random.randint(jax.random.fold_in(own, 2), (rows, 1), 0, top)
    return jnp.take_along_axis(listing, (jnp.arange(top)[None, :] + rotation) % top, axis=1)


def load_shares(number_of, total, most, skew, full):
    weights = [(1 << 20) // math.isqrt(standing ** skew) + 1 for standing in range(1, number_of + 1)]
    largest = most if full else min(most, max(-(-total // number_of), total * weights[0] // sum(weights)))
    least = 1 if total - largest >= number_of - 1 else 0
    counts, spare = [largest] + [least] * (number_of - 1), total - largest - least * (number_of - 1)
    while spare > 0:
        free = [i for i in range(1, number_of) if counts[i] < largest] or [i for i in range(1, number_of) if counts[i] < most]
        whole, remaining = sum([weights[i] for i in free]), spare
        for i in free:
            extra = min(most - counts[i], max(1, remaining * weights[i] // whole), spare)
            counts[i] = counts[i] + extra
            spare = spare - extra
    return np.array(counts)


def gaussian(key, extent, width, most, shards=(), kind=jnp.bfloat16):
    factor_of = shard_levels(key, extent, shards, -0.22, 0.18) if shards else 1.0
    array = jax.random.normal(key, extent, jnp.float32) * width * factor_of
    return jnp.minimum(jnp.maximum(array, -most), most).astype(kind)


def setup_inputs(seed: int = 0) -> dict:
    streams_of = jax.random.split(jax.random.key(seed), 9)
    tokens = gaussian(streams_of[0], (TOKENS, D), 1.0, 6.0, ((0, 16), (1, 2)))
    slot_ids_keys = jax.random.split(jax.random.fold_in(streams_of[1], 1), TOKENS // TOK_DEV)
    slot_ids_turns = jax.random.permutation(jax.random.fold_in(streams_of[1], 3), TOKENS // TOK_DEV)
    slot_ids = jax.vmap(lambda own, number: assign_block(jax.random.fold_in(streams_of[1], 2), own, number, TOK_DEV, SLOTS, TOP, CAP, 2))(slot_ids_keys, slot_ids_turns).reshape((TOKENS, TOP))
    gate_weights = jnp.clip(jnp.exp(math.log(1.0) - 2.3025851 * jax.random.uniform(streams_of[2], (TOKENS, TOP), jnp.float32) ** shard_levels(streams_of[2], (TOKENS, TOP), ((0, 16),), -0.2, 0.2)), 0.1, 1.0)
    old_expert = draw_old_expert(jax.random.fold_in(streams_of[8], 71), 0)
    new_expert = draw_new_expert(jax.random.fold_in(streams_of[8], 71), 0)
    gate_proj = gaussian(streams_of[5], (SLOTS, D, FF), D ** -0.5, 0.09375, ((1, 16), (2, 2)))
    up_proj = gaussian(streams_of[6], (SLOTS, D, FF), D ** -0.5, 0.09375, ((1, 16), (2, 2)))
    down_proj = gaussian(streams_of[7], (SLOTS, D, FF), FF ** -0.5, 0.1875, ((1, 16), (2, 2)))
    return dict(tokens=tokens, slot_ids=slot_ids, gate_weights=gate_weights, old_expert=old_expert, new_expert=new_expert, gate_proj=gate_proj, up_proj=up_proj, down_proj=down_proj)


def expert_rows(slot_rows, gate_slab, up_slab, down_slab):
    share_width = gate_slab.shape[1] // N_ET
    running = jnp.zeros((slot_rows.shape[0], down_slab.shape[0]), jnp.float32)
    for share in range(N_ET):
        offset = share * share_width
        gate_part = jnp.dot(slot_rows, gate_slab[:, offset:offset + share_width], preferred_element_type=jnp.float32)
        up_part = jnp.dot(slot_rows, up_slab[:, offset:offset + share_width], preferred_element_type=jnp.float32)
        hidden = (jax.nn.silu(gate_part) * up_part).astype(jnp.bfloat16)
        partial_value = jnp.dot(hidden, down_slab[:, offset:offset + share_width].T, preferred_element_type=jnp.float32)
        running = running + partial_value.astype(jnp.bfloat16).astype(jnp.float32)
    return running


def reference(tokens, slot_ids, gate_weights, old_expert, new_expert, gate_proj, up_proj, down_proj):
    slot_index = jnp.arange(SLOTS, dtype=jnp.int32)
    holders = new_expert[:, None] == old_expert[None, :]
    source = jnp.min(jnp.where(holders, slot_index[None, :], SLOTS), axis=1).astype(jnp.int32)
    flat_slot = slot_ids.reshape(-1)
    gate_pad = jnp.concatenate([gate_weights.reshape(-1), jnp.zeros((1,), jnp.float32)])
    padded = jnp.concatenate([tokens, jnp.zeros((1, D), tokens.dtype)], axis=0)
    row_limit = N_EP * CAP

    def one_slot(accumulated, slot_number):
        chosen = jnp.nonzero(flat_slot == slot_number, size=row_limit, fill_value=TOKENS * TOP)[0].astype(jnp.int32)
        token_row = (chosen // TOP).astype(jnp.int32)
        slot_rows = padded[token_row]
        anchor = source[slot_number]
        result = expert_rows(slot_rows, gate_proj[anchor], up_proj[anchor], down_proj[anchor])
        scaled = result * gate_pad[chosen][:, None]
        return accumulated.at[token_row].add(scaled), None

    start_sum = jnp.zeros((TOKENS + 1, D), jnp.float32)
    accumulated, unused = lax.scan(one_slot, start_sum, slot_index)
    return accumulated[:TOKENS].astype(jnp.bfloat16)
```

```python
import functools

import jax
import jax.numpy as jnp
from jax import lax
from jax.experimental import pallas as pl
from jax.experimental.layout import Layout, with_layout_constraint
from jax.experimental.pallas import tpu as pltpu
from jax.sharding import PartitionSpec as P

LANES = 128
HALF = 64
MIB = 1 << 20


def distinct_sources(old_expert, new_expert):
    slots = old_expert.shape[0]
    index = jnp.arange(slots, dtype=jnp.int32)
    holders = new_expert[:, None] == old_expert[None, :]
    source = jnp.min(jnp.where(holders, index[None, :], slots), axis=1)
    used = jnp.any(source[:, None] == index[None, :], axis=0)
    earlier = (index[None, :] < index[:, None]) & used[None, :]
    place = jnp.sum(earlier.astype(jnp.int32), axis=1)
    count = slots - slots // 8
    wanted = jnp.arange(count, dtype=jnp.int32)
    listing = jnp.sum(
        jnp.where(used[None, :] & (place[None, :] == wanted[:, None]), index[None, :], 0), axis=1
    )
    slot_place = jnp.sum(jnp.where(source[:, None] == index[None, :], place[None, :], 0), axis=1)
    return source, listing, slot_place


def units_of(dest):
    if dest % 2 == 0:
        start = 7 * dest // 2
        return start, start + 3, 0
    start = (7 * dest + 1) // 2
    return start, start - 1, 1


def pack_rows(slab_of, out_ref, base, dest, lo, rows, per_slab):
    first, half, side = units_of(dest)
    for number in range(3):
        unit = first + number
        ref, slab = slab_of(unit // per_slab)
        lane = (unit % per_slab) * LANES
        out_ref[dest, base + number * rows : base + (number + 1) * rows, :] = ref[
            slab, lo : lo + rows, lane : lane + LANES
        ]
    ref, slab = slab_of(half // per_slab)
    lane = (half % per_slab) * LANES
    mid = rows // 2
    top = ref[slab, lo : lo + mid, lane : lane + LANES].astype(jnp.float32)
    low = ref[slab, lo + mid : lo + rows, lane : lane + LANES].astype(jnp.float32)
    left = lax.broadcasted_iota(jnp.int32, (mid, LANES), 1) < HALF
    if side == 0:
        both = jnp.where(left, top, pltpu.roll(low, HALF, 1))
    else:
        both = jnp.where(left, pltpu.roll(top, HALF, 1), low)
    out_ref[dest, base + 3 * rows : base + 3 * rows + mid, :] = both.astype(out_ref.dtype)


def pack_pair_kernel(list_ref, gate_ref, up_ref, out_ref):
    slots, depth, width = gate_ref.shape
    size = depth * 7 // 2
    for dest in range(out_ref.shape[0]):
        for number, ref in enumerate((gate_ref, up_ref)):
            pack_rows(
                lambda place, ref=ref: (ref, list_ref[place]),
                out_ref, number * size, dest, 0, depth, width // LANES,
            )


def pack_down_kernel(parts, list_ref, down_ref, *out_refs):
    slots, depth, width = down_ref.shape
    for dest in range(out_refs[0].shape[0]):
        lo = 0
        for rows, out_ref in zip(parts, out_refs):
            pack_rows(
                lambda place: (down_ref, list_ref[place]),
                out_ref, 0, dest, lo, rows, width // LANES,
            )
            lo += rows


def whole(*shape):
    return pl.BlockSpec(shape, lambda *_: (0,) * len(shape))


def pack_pair(listing, gate_proj, up_proj, dests):
    slots, depth, width = gate_proj.shape
    shape = (dests, depth * 7, LANES)
    return pl.pallas_call(
        pack_pair_kernel,
        out_shape=jax.ShapeDtypeStruct(shape, gate_proj.dtype),
        in_specs=[pl.BlockSpec(memory_space=pltpu.SMEM)]
        + [pl.BlockSpec(memory_space=pltpu.VMEM)] * 2,
        out_specs=pl.BlockSpec(memory_space=pltpu.VMEM),
        compiler_params=pltpu.CompilerParams(vmem_limit_bytes=32 * MIB),
        name="pack_gate_up",
    )(listing, gate_proj, up_proj)


def pack_down(listing, down_proj, dests, parts):
    return pl.pallas_call(
        functools.partial(pack_down_kernel, parts),
        out_shape=[
            jax.ShapeDtypeStruct((dests, rows * 7 // 2, LANES), down_proj.dtype) for rows in parts
        ],
        in_specs=[
            pl.BlockSpec(memory_space=pltpu.SMEM),
            pl.BlockSpec(memory_space=pltpu.VMEM),
        ],
        out_specs=[pl.BlockSpec(memory_space=pltpu.VMEM)] * len(parts),
        compiler_params=pltpu.CompilerParams(vmem_limit_bytes=32 * MIB),
        name="pack_down",
    )(listing, down_proj)


def unpack_rows(in_ref, at, base, rows, out_ref, out_row, out_lane):
    for number in range(3):
        out_ref[out_row : out_row + rows, out_lane + number * LANES : out_lane + (number + 1) * LANES] = (
            in_ref[at, base + number * rows : base + (number + 1) * rows, :]
        )
    mid = rows // 2
    both = in_ref[at, base + 3 * rows : base + 3 * rows + mid, :]
    lanes = slice(out_lane + 3 * LANES, out_lane + 4 * LANES)
    out_ref[out_row : out_row + mid, lanes] = both
    out_ref[out_row + mid : out_row + rows, lanes] = pltpu.roll(
        both.astype(jnp.float32), HALF, 1
    ).astype(out_ref.dtype)


def hidden_kernel(core_ref, own_ref, other_ref, share_ref, packed_ref, out_ref, gate_w, up_w):
    sources, packed_rows, _ = packed_ref.shape
    depth = packed_rows // 7
    size = packed_rows // 2
    group = sources // 2

    @pl.when(pl.program_id(0) == 0)
    def _():
        for at in range(sources):
            place = (core_ref[0] + at // group) % 2 * group + at % group
            unpack_rows(packed_ref, place, 0, depth, gate_w, at * depth, 0)
            unpack_rows(packed_ref, place, size, depth, up_w, at * depth, 0)

    own, other = own_ref[...], other_ref[...]
    mid = own.shape[1]

    def product(w_ref):
        return jnp.dot(own, w_ref[:mid, :], preferred_element_type=jnp.float32) + jnp.dot(
            other, w_ref[mid:, :], preferred_element_type=jnp.float32
        )

    gate = product(gate_w)
    value = gate / (1.0 + jnp.exp(-gate)) * product(up_w)
    left = lax.broadcasted_iota(jnp.int32, (own.shape[0], LANES), 1) < HALF
    for number in range(4):
        lanes = slice(number * LANES, (number + 1) * LANES)
        part = value[:, lanes] * share_ref[:, number : number + 1]
        if number == 3:
            part = jnp.where(left, part, 0.0)
        out_ref[:, lanes] = part.astype(out_ref.dtype)


def hidden_units(core, own, other, share, packed):
    total, model = own.shape
    tile = 256
    wide = 4 * LANES
    return pl.pallas_call(
        hidden_kernel,
        grid=(total // tile,),
        out_shape=jax.ShapeDtypeStruct((total, wide), own.dtype),
        in_specs=[
            pl.BlockSpec(memory_space=pltpu.SMEM),
            pl.BlockSpec((tile, model), lambda i: (i, 0)),
            pl.BlockSpec((tile, model), lambda i: (i, 0)),
            pl.BlockSpec((tile, 4), lambda i: (i, 0)),
            whole(*packed.shape),
        ],
        out_specs=pl.BlockSpec((tile, wide), lambda i: (i, 0)),
        scratch_shapes=[pltpu.VMEM((2 * model, wide), own.dtype)] * 2,
        compiler_params=pltpu.CompilerParams(vmem_limit_bytes=40 * MIB),
        cost_estimate=pl.CostEstimate(
            flops=8 * total * model * wide, bytes_accessed=24 * MIB, transcendentals=total * wide
        ),
        name="hidden",
    )(core.reshape(1), own, other, share, packed)


def down_kernel(rows, side, own_h, other_h, own_ref, other_ref, out_a, out_b, own_w, other_w):
    for in_ref, w_ref in ((own_ref, own_w), (other_ref, other_w)):
        for at in range(in_ref.shape[0]):
            unpack_rows(in_ref, at, 0, rows, w_ref, at * rows, 0)
    half = own_w.shape[0] // 2
    quarter = own_h.shape[0] // 4

    def product(at, size, span):
        tokens = slice(at * quarter, (at + size) * quarter)
        dims = (((1,), (1,)), ((), ()))
        return lax.dot_general(
            own_h[tokens, :], own_w[span, :], dims, preferred_element_type=jnp.float32
        ) + lax.dot_general(
            other_h[tokens, :], other_w[span, :], dims, preferred_element_type=jnp.float32
        )

    out_a[...] = product(2 * side, 2, slice(0, half)).astype(out_a.dtype)
    for first in range(2):
        out_b[first * quarter : (first + 1) * quarter, :] = product(
            2 * first + side, 1, slice(half, 2 * half)
        ).astype(out_b.dtype)


def down_product(own_h, other_h, own, other, rows, side, dtype, name):
    sources = own.shape[0]
    total, wide = own_h.shape
    tokens = total // 2
    features = sources * rows // 2
    vmem = pl.BlockSpec(memory_space=pltpu.VMEM)
    return pl.pallas_call(
        functools.partial(down_kernel, rows, side),
        out_shape=[jax.ShapeDtypeStruct((tokens, features), dtype)] * 2,
        in_specs=[vmem] * 4,
        out_specs=[vmem] * 2,
        scratch_shapes=[pltpu.VMEM((sources * rows, wide), own.dtype)] * 2,
        compiler_params=pltpu.CompilerParams(vmem_limit_bytes=40 * MIB),
        cost_estimate=pl.CostEstimate(
            flops=8 * tokens * wide * features, bytes_accessed=8 * MIB, transcendentals=0
        ),
        name=name,
    )(own_h, other_h, own, other)


def swap(value, bit):
    size = lax.axis_size("ep")
    return lax.ppermute(value, "ep", [(i, i ^ (1 << bit)) for i in range(size)])


def gather_bits(value, bits, order, have=()):
    have = list(have)
    for bit in order:
        axis = sum(1 for b in have if b < bit)
        value = jnp.stack([value, swap(value, bit)], axis=axis)
        have.append(bit)
    return value


def take_half(value, axis, number):
    return lax.index_in_dim(value, number, axis, keepdims=False)


def sum_stages(keep, arrived, order, left):
    left = list(left)
    for bit in order:
        axis = left.index(bit)
        total = keep + arrived.astype(jnp.float32)
        arrived = swap(take_half(total, axis, 1).astype(jnp.bfloat16), bit)
        keep = take_half(total, axis, 0)
        left.remove(bit)
    return keep, arrived


def share_of_slots(slot_ids, gate_weights, slots):
    index = jnp.arange(slots, dtype=jnp.int32)
    picked = slot_ids.T[None, :, :] == index[:, None, None]
    return jnp.sum(jnp.where(picked, gate_weights.T[None, :, :], 0.0), axis=1)


def packed_layer(
    tokens, slot_ids, gate_weights, old_expert, new_expert, gate_proj, up_proj, down_proj
):
    devices = lax.axis_size("ep")
    bits = devices.bit_length() - 1
    slots, depth, width = gate_proj.shape
    me = lax.axis_index("ep")
    core = lax.axis_index("et")
    other_core = [(0, 1), (1, 0)]
    _, listing, slot_place = distinct_sources(old_expert, new_expert)

    places = []
    for dest in range(devices):
        first, half, _ = units_of(dest)
        places.append([unit // (width // LANES) for unit in (first, first + 1, first + 2, half)])
    places = jnp.asarray(places, jnp.int32)
    share = share_of_slots(slot_ids, gate_weights, slots)
    belongs = slot_place[None, None, :, None] == places[:, :, None, None]
    unit_share = jnp.sum(jnp.where(belongs, share[None, None], 0.0), axis=2)
    unit_share = lax.all_to_all(unit_share, "ep", 0, 0, tiled=True)
    unit_share = jnp.take(unit_share, me ^ jnp.arange(devices), axis=0, mode="clip")
    unit_share = unit_share.reshape((2,) * bits + unit_share.shape[1:])
    unit_share = unit_share.transpose(tuple(range(bits - 1, -1, -1)) + (bits + 1, bits))
    unit_share = unit_share.reshape(-1, 4)

    parts = (96, 64, 64)
    down_packed = pack_down(listing, down_proj, devices, parts)

    packed, tokens_in = lax.optimization_barrier(
        (pack_pair(listing, gate_proj, up_proj, devices), tokens)
    )
    moved = lax.all_to_all(packed, "ep", 0, 0, tiled=True)
    late = list(range(bits - 1, 1, -1))
    rows = gather_bits(tokens_in, bits, late)
    mid = tokens.shape[1] // 2
    rows = jnp.concatenate(
        [
            gather_bits(rows[..., :mid], bits, (1, 0), late),
            gather_bits(rows[..., mid:], bits, (0, 1), late),
        ],
        axis=-1,
    ).reshape(-1, tokens.shape[1])
    rows_other = lax.ppermute(rows, "et", other_core)

    def hidden_of(moved):
        hidden = hidden_units(core, rows, rows_other, unit_share, moved)
        return hidden, lax.ppermute(hidden, "et", other_core)

    group = devices // 2
    tie = lax.optimization_barrier
    row_major = Layout(major_to_minor=(0, 1))

    def move_down(packed, after):
        packed, after = tie((packed, after))
        return lax.all_to_all(packed, "ep", 0, 0, tiled=True), after

    def products(down, rows_in):
        own = lax.dynamic_slice_in_dim(down, core * group, group, 0)
        other = lax.dynamic_slice_in_dim(down, (1 - core) * group, group, 0)
        other = lax.ppermute(other, "et", other_core)
        args = (hidden, hidden_other, own, other)
        sent = down_product(*args, rows_in, 1, jnp.bfloat16, "down_send")
        sent, args = tie((sent, args))
        arrived = [swap(value, bit) for bit, value in enumerate(sent)]
        return down_product(*args, rows_in, 0, jnp.float32, "down_keep"), arrived

    def stages(kept, arrived, rows_in, count, done=0):
        out = [], []
        for bit in (0, 1):
            left = [b for b in range(bits) if b != bit]
            order = ([1 - bit] + left[1:])[done : done + count]
            left = [b for b in left if b not in ([1 - bit] + left[1:])[:done]]
            shape = (2,) * len(left) + tokens.shape[:1] + (group // 2 * rows_in,)
            keep, come = sum_stages(
                kept[bit].reshape(shape), arrived[bit].reshape(shape), order, left
            )
            out[0].append(keep)
            out[1].append(come)
        return out

    def finish(kept, arrived, rows_in):
        sums = []
        for keep, come in zip(kept, arrived):
            total = (keep + come.astype(jnp.float32)).astype(jnp.bfloat16)
            total = with_layout_constraint(total, row_major)
            sums.append(total.reshape(total.shape[0], group // 2, rows_in))
        return jnp.concatenate(sums, axis=1)

    down0, moved = move_down(down_packed[0], moved)
    hidden, hidden_other = hidden_of(moved)
    down1, (down0, hidden, hidden_other) = move_down(
        down_packed[1], (down0, hidden, hidden_other)
    )
    kept0, arrived0 = products(down0, parts[0])
    down2, (down1, kept0) = move_down(down_packed[2], (down1, kept0))
    kept0, arrived0 = stages(kept0, arrived0, parts[0], 1)
    kept1, arrived1 = products(down1, parts[1])
    down2, kept0, kept1 = tie((down2, kept0, kept1))
    kept2, arrived2 = products(down2, parts[2])
    kept0, arrived0 = stages(kept0, arrived0, parts[0], bits - 2, 1)
    kept1, arrived1 = stages(kept1, arrived1, parts[1], bits - 1)
    kept2, arrived2 = stages(kept2, arrived2, parts[2], bits - 1)
    done = [
        finish(kept0, arrived0, parts[0]),
        finish(kept1, arrived1, parts[1]),
        finish(kept2, arrived2, parts[2]),
    ]
    return jnp.concatenate(done, axis=2).reshape(tokens.shape)


def plain_layer(
    tokens, slot_ids, gate_weights, old_expert, new_expert, gate_proj, up_proj, down_proj
):
    devices = lax.axis_size("ep")
    bits = devices.bit_length() - 1
    slots = gate_proj.shape[0]
    me = lax.axis_index("ep")
    source, _, _ = distinct_sources(old_expert, new_expert)

    def move(weights):
        chosen = jnp.take(weights, source, axis=0, mode="clip")
        return lax.all_to_all(chosen, "ep", 0, 0, tiled=True)

    gate_slab = move(gate_proj).reshape(-1, gate_proj.shape[-1])
    up_slab = move(up_proj).reshape(-1, up_proj.shape[-1])
    down = move(down_proj)
    order = range(bits - 1, -1, -1)
    rows = gather_bits(tokens, bits, order).reshape(-1, tokens.shape[1])
    rows = lax.all_gather(rows, "et", axis=1, tiled=True)
    share = gather_bits(share_of_slots(slot_ids, gate_weights, slots), bits, order)
    share = lax.dynamic_index_in_dim(share, me, bits, keepdims=False).reshape(-1, 1)
    gate_part = jnp.dot(rows, gate_slab, preferred_element_type=jnp.float32)
    up_part = jnp.dot(rows, up_slab, preferred_element_type=jnp.float32)
    hidden = (jax.nn.silu(gate_part) * up_part * share).astype(jnp.bfloat16)
    hidden = lax.all_gather(hidden, "et", axis=1, tiled=True)
    down = lax.all_to_all(down, "et", 0, 2, tiled=True)
    value = lax.dot_general(
        hidden,
        down.reshape(-1, down.shape[-1]),
        (((1,), (1,)), ((), ())),
        preferred_element_type=jnp.float32,
    )
    value = value.reshape((2,) * bits + (-1,) + value.shape[1:])
    arrived = swap(take_half(value, 0, 1).astype(jnp.bfloat16), 0)
    left = list(range(1, bits))
    keep, arrived = sum_stages(take_half(value, 0, 0), arrived, left, left)
    return (keep + arrived.astype(jnp.float32)).astype(jnp.bfloat16)


def per_device(tokens, slot_ids, gate_weights, old_expert, new_expert, gate_proj, up_proj, down_proj):
    slots, depth, width = gate_proj.shape
    count = slots - slots // 8
    devices = lax.axis_size("ep")
    fits = (
        lax.axis_size("et") == 2
        and depth == 224
        and width % LANES == 0
        and count * width == devices * 7 * HALF
        and devices % 8 == 0
    )
    layer = packed_layer if fits else plain_layer
    return layer(
        tokens, slot_ids, gate_weights, old_expert, new_expert, gate_proj, up_proj, down_proj
    )


def solution(mesh):
    placed = (
        P("ep", "et"),
        P("ep", None),
        P("ep", None),
        P(),
        P(),
        P(None, "ep", "et"),
        P(None, "ep", "et"),
        P(None, "ep", "et"),
    )
    return jax.shard_map(
        per_device, mesh=mesh, in_specs=placed, out_specs=P("ep", "et"), check_vma=False
    )
```

```python
import functools

import jax
import jax.numpy as jnp
from jax import lax
from jax.experimental import pallas as pl
from jax.experimental.pallas import tpu as pltpu
from jax.sharding import PartitionSpec as P

LANES = 128
HALF = 64
MIB = 1 << 20


def distinct_sources(old_expert, new_expert):
    slots = old_expert.shape[0]
    index = jnp.arange(slots, dtype=jnp.int32)
    holders = new_expert[:, None] == old_expert[None, :]
    source = jnp.min(jnp.where(holders, index[None, :], slots), axis=1)
    used = jnp.any(source[:, None] == index[None, :], axis=0)
    earlier = (index[None, :] < index[:, None]) & used[None, :]
    place = jnp.sum(earlier.astype(jnp.int32), axis=1)
    count = slots - slots // 8
    wanted = jnp.arange(count, dtype=jnp.int32)
    listing = jnp.sum(
        jnp.where(used[None, :] & (place[None, :] == wanted[:, None]), index[None, :], 0), axis=1
    )
    slot_place = jnp.sum(jnp.where(source[:, None] == index[None, :], place[None, :], 0), axis=1)
    return source, listing, slot_place


def units_of(dest):
    if dest % 2 == 0:
        start = 7 * dest // 2
        return start, start + 3, 0
    start = (7 * dest + 1) // 2
    return start, start - 1, 1


def pack_rows(slab_of, out_ref, base, dest, lo, rows, per_slab):
    first, half, side = units_of(dest)
    for number in range(3):
        unit = first + number
        ref, slab = slab_of(unit // per_slab)
        lane = (unit % per_slab) * LANES
        out_ref[dest, base + number * rows : base + (number + 1) * rows, :] = ref[
            slab, lo : lo + rows, lane : lane + LANES
        ]
    ref, slab = slab_of(half // per_slab)
    lane = (half % per_slab) * LANES
    mid = rows // 2
    top = ref[slab, lo : lo + mid, lane : lane + LANES].astype(jnp.float32)
    low = ref[slab, lo + mid : lo + rows, lane : lane + LANES].astype(jnp.float32)
    left = lax.broadcasted_iota(jnp.int32, (mid, LANES), 1) < HALF
    if side == 0:
        both = jnp.where(left, top, pltpu.roll(low, HALF, 1))
    else:
        both = jnp.where(left, pltpu.roll(top, HALF, 1), low)
    out_ref[dest, base + 3 * rows : base + 3 * rows + mid, :] = both.astype(out_ref.dtype)


def pack_gate_kernel(list_ref, gate_ref, share_ref, out_ref):
    slots, depth, width = gate_ref.shape
    size = depth * 7 // 2
    row = lax.broadcasted_iota(jnp.int32, share_ref.shape[1:], 0) // 4
    for dest in range(out_ref.shape[0]):
        pack_rows(
            lambda place: (gate_ref, list_ref[place]),
            out_ref, 0, dest, 0, depth, width // LANES,
        )
        value = share_ref[dest]
        high = value.astype(out_ref.dtype)
        rest = value - high.astype(jnp.float32)
        middle = rest.astype(out_ref.dtype)
        low = (rest - middle.astype(jnp.float32)).astype(out_ref.dtype)
        terms = jnp.where(
            row == 0,
            high.astype(jnp.float32),
            jnp.where(
                row == 1,
                middle.astype(jnp.float32),
                jnp.where(row == 2, low.astype(jnp.float32), 0.0),
            ),
        )
        out_ref[dest, size:, :] = terms.astype(out_ref.dtype)


def pack_kernel(parts, list_ref, in_ref, *out_refs):
    slots, depth, width = in_ref.shape
    for dest in range(out_refs[0].shape[0]):
        lo = 0
        for rows, out_ref in zip(parts, out_refs):
            pack_rows(
                lambda place: (in_ref, list_ref[place]),
                out_ref, 0, dest, lo, rows, width // LANES,
            )
            lo += rows


def vmem():
    return pl.BlockSpec(memory_space=pltpu.VMEM)


def smem():
    return pl.BlockSpec(memory_space=pltpu.SMEM)


def pack_gate(listing, gate_proj, share, dests):
    slots, depth, width = gate_proj.shape
    shape = (dests, depth * 7 // 2 + share.shape[1], LANES)
    return pl.pallas_call(
        pack_gate_kernel,
        out_shape=jax.ShapeDtypeStruct(shape, gate_proj.dtype),
        in_specs=[smem(), vmem(), vmem()],
        out_specs=vmem(),
        compiler_params=pltpu.CompilerParams(vmem_limit_bytes=32 * MIB),
        name="pack_gate",
    )(listing, gate_proj, share)


def pack(listing, weights, dests, parts, name):
    return pl.pallas_call(
        functools.partial(pack_kernel, parts),
        out_shape=[
            jax.ShapeDtypeStruct((dests, rows * 7 // 2, LANES), weights.dtype) for rows in parts
        ],
        in_specs=[smem(), vmem()],
        out_specs=[vmem()] * len(parts),
        compiler_params=pltpu.CompilerParams(vmem_limit_bytes=32 * MIB),
        name=name,
    )(listing, weights)


def unpack_rows(in_ref, at, base, rows, out_ref, out_row, out_lane):
    for number in range(3):
        out_ref[out_row : out_row + rows, out_lane + number * LANES : out_lane + (number + 1) * LANES] = (
            in_ref[at, base + number * rows : base + (number + 1) * rows, :]
        )
    mid = rows // 2
    both = in_ref[at, base + 3 * rows : base + 3 * rows + mid, :]
    lanes = slice(out_lane + 3 * LANES, out_lane + 4 * LANES)
    out_ref[out_row : out_row + mid, lanes] = both
    out_ref[out_row + mid : out_row + rows, lanes] = pltpu.roll(
        both.astype(jnp.float32), HALF, 1
    ).astype(out_ref.dtype)


def hidden_kernel(at_ref, *refs):
    pieces, (gate_ref, up_ref, out_ref, gate_w, up_w, rows) = refs[:8], refs[8:]
    sources, packed_rows, _ = up_ref.shape
    depth = packed_rows * 2 // 7
    group = sources // 2
    tile = pl.program_id(0)
    x, y, zl = tile // 4, tile // 2 % 2, tile % 2
    me, core = at_ref[0], at_ref[1]

    @pl.when(tile == 0)
    def _():
        for at in range(sources):
            place = (core + at // group) % 2 * group + at % group
            unpack_rows(gate_ref, place, 0, depth, gate_w, at * depth, 0)
            unpack_rows(up_ref, place, 0, depth, up_w, at * depth, 0)

    mid = pieces[0].shape[1]
    for number in range(4):
        lanes = slice(number * mid, (number + 1) * mid)
        coordinate = (x, y)[number % 2]
        for value in range(2):

            @pl.when(coordinate == value)
            def _():
                rows[:, lanes] = pieces[2 * number + value][...]

    gate = jnp.dot(rows[...], gate_w[...], preferred_element_type=jnp.float32)
    up = jnp.dot(rows[...], up_w[...], preferred_element_type=jnp.float32)
    value = gate / (1.0 + jnp.exp(-gate)) * up

    wide = gate.shape[1]
    term = lax.broadcasted_iota(jnp.int32, (16, wide), 0)
    lane = lax.broadcasted_iota(jnp.int32, (16, wide), 1)
    chosen = (term % 4 == lane // LANES) & (term < 12) & (lane < wide - HALF)
    chosen = jnp.where(chosen, 1.0, 0.0).astype(jnp.bfloat16)
    block = rows.shape[0] // 2
    for zh in range(2):
        source = me ^ (x + 2 * y + 4 * zl + 8 * zh)
        weight = lax.dot_general(
            gate_ref[source, packed_rows:, :],
            chosen,
            (((0,), (0,)), ((), ())),
            preferred_element_type=jnp.float32,
        )
        span = slice(zh * block, (zh + 1) * block)
        out_ref[span, :] = (value[span, :] * weight).astype(out_ref.dtype)


def hidden_units(at, pieces, gate, up):
    total = 2 * pieces[0].shape[0]
    mid = pieces[0].shape[1]
    tile = total // 8
    wide = 4 * LANES
    model = 4 * mid
    by_x = [lambda i: (jnp.minimum(i, 3), 0), lambda i: (jnp.maximum(i - 4, 0), 0)]
    by_y = [
        lambda i: (i // 4 * 2 + jnp.where(i // 2 % 2 == 0, i % 2, 1), 0),
        lambda i: (i // 4 * 2 + jnp.where(i // 2 % 2 == 1, i % 2, 0), 0),
    ]
    maps = (by_x + by_y) * 2
    return pl.pallas_call(
        hidden_kernel,
        grid=(8,),
        out_shape=jax.ShapeDtypeStruct((total, wide), up.dtype),
        in_specs=[smem()]
        + [pl.BlockSpec((tile, mid), where) for where in maps]
        + [vmem(), vmem()],
        out_specs=pl.BlockSpec((tile, wide), lambda i: (i, 0)),
        scratch_shapes=[pltpu.VMEM((model, wide), up.dtype)] * 2
        + [pltpu.VMEM((tile, model), up.dtype)],
        compiler_params=pltpu.CompilerParams(vmem_limit_bytes=40 * MIB),
        cost_estimate=pl.CostEstimate(
            flops=4 * total * model * wide, bytes_accessed=24 * MIB, transcendentals=total * wide
        ),
        name="hidden",
    )(at, *pieces, gate, up)


def down_kernel(rows, side, own_h, other_h, own_ref, other_ref, out_a, out_b, own_w, other_w):
    for in_ref, w_ref in ((own_ref, own_w), (other_ref, other_w)):
        for at in range(in_ref.shape[0]):
            unpack_rows(in_ref, at, 0, rows, w_ref, at * rows, 0)
    half = own_w.shape[0] // 2
    quarter = own_h.shape[0] // 4

    def product(at, size, span):
        tokens = slice(at * quarter, (at + size) * quarter)
        dims = (((1,), (1,)), ((), ()))
        return lax.dot_general(
            own_h[tokens, :], own_w[span, :], dims, preferred_element_type=jnp.float32
        ) + lax.dot_general(
            other_h[tokens, :], other_w[span, :], dims, preferred_element_type=jnp.float32
        )

    out_a[...] = product(2 * side, 2, slice(0, half)).astype(out_a.dtype)
    for first in range(2):
        out_b[first * quarter : (first + 1) * quarter, :] = product(
            2 * first + side, 1, slice(half, 2 * half)
        ).astype(out_b.dtype)


def down_product(own_h, other_h, own, other, rows, side, dtype, name):
    sources = own.shape[0]
    total, wide = own_h.shape
    tokens = total // 2
    features = sources * rows // 2
    return pl.pallas_call(
        functools.partial(down_kernel, rows, side),
        out_shape=[jax.ShapeDtypeStruct((tokens, features), dtype)] * 2,
        in_specs=[vmem()] * 4,
        out_specs=[vmem()] * 2,
        scratch_shapes=[pltpu.VMEM((sources * rows, wide), own.dtype)] * 2,
        compiler_params=pltpu.CompilerParams(vmem_limit_bytes=40 * MIB),
        cost_estimate=pl.CostEstimate(
            flops=8 * tokens * wide * features, bytes_accessed=8 * MIB, transcendentals=0
        ),
        name=name,
    )(own_h, other_h, own, other)


def halve_kernel(joined, *refs):
    count = (len(refs) - 2 * (1 if joined else 0)) // 2 if joined else len(refs) // 4
    out_refs = refs[2 * count :]
    lane = 0
    for number in range(count):
        keep_ref, come_ref = refs[2 * number : 2 * number + 2]
        half = keep_ref.shape[0] // 2
        total = keep_ref[...] + come_ref[...].astype(jnp.float32)
        if joined:
            send_ref, left_ref = out_refs
            lanes = slice(lane, lane + keep_ref.shape[1])
            lane += keep_ref.shape[1]
        else:
            send_ref, left_ref = out_refs[2 * number : 2 * number + 2]
            lanes = slice(0, keep_ref.shape[1])
        send_ref[:, lanes] = total[half:, :].astype(send_ref.dtype)
        left_ref[:, lanes] = total[:half, :]


def halve(pairs, joined):
    sizes = [(keep.shape[0] // 2, keep.shape[1]) for keep, _ in pairs]
    if joined:
        sizes = [(sizes[0][0], sum(width for _, width in sizes))]
    shapes = []
    for size in sizes:
        shapes += [jax.ShapeDtypeStruct(size, jnp.bfloat16), jax.ShapeDtypeStruct(size, jnp.float32)]
    out = pl.pallas_call(
        functools.partial(halve_kernel, joined),
        out_shape=shapes,
        in_specs=[vmem()] * (2 * len(pairs)),
        out_specs=[vmem()] * len(shapes),
        compiler_params=pltpu.CompilerParams(vmem_limit_bytes=40 * MIB),
        cost_estimate=pl.CostEstimate(
            flops=sum(keep.size for keep, _ in pairs), bytes_accessed=4 * MIB, transcendentals=0
        ),
        name="sum_stage",
    )(*[value for pair in pairs for value in pair])
    return [(out[2 * n], out[2 * n + 1]) for n in range(len(out) // 2)]


def swap(value, bit):
    size = lax.axis_size("ep")
    return lax.ppermute(value, "ep", [(i, i ^ (1 << bit)) for i in range(size)])


def gather_bits(value, bits, order, have=()):
    have = list(have)
    for bit in order:
        axis = sum(1 for b in have if b < bit)
        value = jnp.stack([value, swap(value, bit)], axis=axis)
        have.append(bit)
    return value


def take_half(value, axis, number):
    return lax.index_in_dim(value, number, axis, keepdims=False)


def sum_stages(keep, arrived, order, left):
    left = list(left)
    for bit in order:
        axis = left.index(bit)
        total = keep + arrived.astype(jnp.float32)
        arrived = swap(take_half(total, axis, 1).astype(jnp.bfloat16), bit)
        keep = take_half(total, axis, 0)
        left.remove(bit)
    return keep, arrived


def share_of_slots(slot_ids, gate_weights, slots):
    index = jnp.arange(slots, dtype=jnp.int32)
    picked = slot_ids.T[None, :, :] == index[:, None, None]
    return jnp.sum(jnp.where(picked, gate_weights.T[None, :, :], 0.0), axis=1)


def packed_layer(
    tokens, slot_ids, gate_weights, old_expert, new_expert, gate_proj, up_proj, down_proj
):
    devices = lax.axis_size("ep")
    slots, depth, width = gate_proj.shape
    block = tokens.shape[0]
    me = lax.axis_index("ep")
    core = lax.axis_index("et")
    group = devices // 2
    tie = lax.optimization_barrier
    _, listing, slot_place = distinct_sources(old_expert, new_expert)

    def exchange(value):
        return lax.ppermute(value, "et", [(0, 1), (1, 0)])

    def move(packed):
        return lax.all_to_all(packed, "ep", 0, 0, tiled=True)

    places = []
    for dest in range(devices):
        first, half, _ = units_of(dest)
        places.append([unit // (width // LANES) for unit in (first, first + 1, first + 2, half)] * 4)
    places = jnp.asarray(places, jnp.int32)
    share = share_of_slots(slot_ids, gate_weights, slots)
    belongs = slot_place[None, None, :, None] == places[:, :, None, None]
    share = jnp.sum(jnp.where(belongs, share[None, None], 0.0), axis=2)

    gate = move(pack_gate(listing, gate_proj, share, devices))
    mid = tokens.shape[1] // 2
    rows = jnp.concatenate([tokens, swap(tokens, 3)], axis=0)
    rows = jnp.concatenate([rows, swap(rows, 2)], axis=0)
    first, second = rows[:, :mid], rows[:, mid:]
    first = jnp.concatenate([first, swap(first, 1)], axis=0)
    second = jnp.concatenate([second, swap(second, 0)], axis=0)
    (up_packed,) = pack(listing, up_proj, devices, (depth,), "pack_up")
    gate, first, second, up_packed = tie((gate, first, second, up_packed))

    up = move(up_packed)
    pieces = [first, swap(first, 0), second, swap(second, 1)]
    others = [exchange(first), None, exchange(second), None]
    parts = (128, 64, 32)
    down_packed = pack(listing, down_proj, devices, parts, "pack_down")
    up, pieces, others[0], others[2], down_packed = tie(
        (up, pieces, others[0], others[2], down_packed)
    )

    down0 = move(down_packed[0])
    others[1], others[3] = exchange(pieces[1]), exchange(pieces[3])
    at = jnp.stack([me, core]).astype(jnp.int32)
    hidden = hidden_units(at, pieces + others, gate, up)
    hidden_other = exchange(hidden)
    down0, hidden, hidden_other, packed = tie((down0, hidden, hidden_other, down_packed[1]))

    def products(down, rows_in):
        own = lax.dynamic_slice_in_dim(down, core * group, group, 0)
        other = exchange(lax.dynamic_slice_in_dim(down, (1 - core) * group, group, 0))
        args = (hidden, hidden_other, own, other)
        sent = down_product(*args, rows_in, 1, jnp.bfloat16, "down_send")
        sent, args = tie((sent, args))
        come = [swap(value, bit) for bit, value in enumerate(sent)]
        return list(zip(down_product(*args, rows_in, 0, jnp.float32, "down_keep"), come))

    def cross(pairs):
        (send_a, keep_a), (send_b, keep_b) = halve(pairs, False)
        return [(keep_a, swap(send_a, 1)), (keep_b, swap(send_b, 0))]

    def along(pairs, bit):
        ((send, keep),) = halve(pairs, True)
        return [(keep, swap(send, bit))]

    def finish(pairs):
        ((keep, come),) = pairs
        return (keep + come.astype(jnp.float32)).astype(jnp.bfloat16)

    down1 = move(packed)
    sums0 = products(down0, parts[0])
    down1, sums0, packed = tie((down1, sums0, down_packed[2]))
    down2 = move(packed)
    sums0 = cross(sums0)
    sums1 = products(down1, parts[1])
    down2, sums0, sums1 = tie((down2, sums0, sums1))
    sums2 = products(down2, parts[2])
    sums1 = cross(sums1)
    sums01 = along(sums0 + sums1, 2)
    sums2 = cross(sums2)
    sums01 = along(sums01, 3)
    sums2 = along(along(sums2, 2), 3)

    out01, out2 = finish(sums01), finish(sums2)
    out = []
    lane = 0
    for rows_in in parts[:2]:
        wide = group * rows_in
        out.append(out01[:, lane : lane + wide].reshape(block, group, rows_in))
        lane += wide
    out.append(out2.reshape(block, group, parts[2]))
    return jnp.concatenate(out, axis=2).reshape(tokens.shape)


def plain_layer(
    tokens, slot_ids, gate_weights, old_expert, new_expert, gate_proj, up_proj, down_proj
):
    devices = lax.axis_size("ep")
    bits = devices.bit_length() - 1
    slots = gate_proj.shape[0]
    me = lax.axis_index("ep")
    source, _, _ = distinct_sources(old_expert, new_expert)

    def move(weights):
        chosen = jnp.take(weights, source, axis=0, mode="clip")
        return lax.all_to_all(chosen, "ep", 0, 0, tiled=True)

    gate_slab = move(gate_proj).reshape(-1, gate_proj.shape[-1])
    up_slab = move(up_proj).reshape(-1, up_proj.shape[-1])
    down = move(down_proj)
    order = range(bits - 1, -1, -1)
    rows = gather_bits(tokens, bits, order).reshape(-1, tokens.shape[1])
    rows = lax.all_gather(rows, "et", axis=1, tiled=True)
    share = gather_bits(share_of_slots(slot_ids, gate_weights, slots), bits, order)
    share = lax.dynamic_index_in_dim(share, me, bits, keepdims=False).reshape(-1, 1)
    gate_part = jnp.dot(rows, gate_slab, preferred_element_type=jnp.float32)
    up_part = jnp.dot(rows, up_slab, preferred_element_type=jnp.float32)
    hidden = (jax.nn.silu(gate_part) * up_part * share).astype(jnp.bfloat16)
    hidden = lax.all_gather(hidden, "et", axis=1, tiled=True)
    down = lax.all_to_all(down, "et", 0, 2, tiled=True)
    value = lax.dot_general(
        hidden,
        down.reshape(-1, down.shape[-1]),
        (((1,), (1,)), ((), ())),
        preferred_element_type=jnp.float32,
    )
    value = value.reshape((2,) * bits + (-1,) + value.shape[1:])
    arrived = swap(take_half(value, 0, 1).astype(jnp.bfloat16), 0)
    left = list(range(1, bits))
    keep, arrived = sum_stages(take_half(value, 0, 0), arrived, left, left)
    return (keep + arrived.astype(jnp.float32)).astype(jnp.bfloat16)


def per_device(tokens, slot_ids, gate_weights, old_expert, new_expert, gate_proj, up_proj, down_proj):
    slots, depth, width = gate_proj.shape
    count = slots - slots // 8
    devices = lax.axis_size("ep")
    fits = (
        lax.axis_size("et") == 2
        and depth == 224
        and width % LANES == 0
        and count * width == devices * 7 * HALF
        and devices == 16
        and tokens.shape[0] == LANES
    )
    layer = packed_layer if fits else plain_layer
    return layer(
        tokens, slot_ids, gate_weights, old_expert, new_expert, gate_proj, up_proj, down_proj
    )


def solution(mesh):
    placed = (
        P("ep", "et"),
        P("ep", None),
        P("ep", None),
        P(),
        P(),
        P(None, "ep", "et"),
        P(None, "ep", "et"),
        P(None, "ep", "et"),
    )
    return jax.shard_map(
        per_device, mesh=mesh, in_specs=placed, out_specs=P("ep", "et"), check_vma=False
    )
```

```python
import functools

import jax
import jax.numpy as jnp
from jax import lax
from jax.experimental import pallas as pl
from jax.experimental.pallas import tpu as pltpu
from jax.sharding import PartitionSpec as P

LANES = 128
HALF = 64
MIB = 1 << 20


def distinct_sources(old_expert, new_expert):
    slots = old_expert.shape[0]
    index = jnp.arange(slots, dtype=jnp.int32)
    holders = new_expert[:, None] == old_expert[None, :]
    source = jnp.min(jnp.where(holders, index[None, :], slots), axis=1)
    used = jnp.any(source[:, None] == index[None, :], axis=0)
    earlier = (index[None, :] < index[:, None]) & used[None, :]
    place = jnp.sum(earlier.astype(jnp.int32), axis=1)
    count = slots - slots // 8
    wanted = jnp.arange(count, dtype=jnp.int32)
    listing = jnp.sum(
        jnp.where(used[None, :] & (place[None, :] == wanted[:, None]), index[None, :], 0), axis=1
    )
    slot_place = jnp.sum(jnp.where(source[:, None] == index[None, :], place[None, :], 0), axis=1)
    return source, listing, slot_place


def units_of(dest):
    if dest % 2 == 0:
        start = 7 * dest // 2
        return start, start + 3, 0
    start = (7 * dest + 1) // 2
    return start, start - 1, 1


def pack_rows(slab_of, out_ref, base, dest, lo, rows, per_slab):
    first, half, side = units_of(dest)
    for number in range(3):
        unit = first + number
        ref, slab = slab_of(unit // per_slab)
        lane = (unit % per_slab) * LANES
        out_ref[dest, base + number * rows : base + (number + 1) * rows, :] = ref[
            slab, lo : lo + rows, lane : lane + LANES
        ]
    ref, slab = slab_of(half // per_slab)
    lane = (half % per_slab) * LANES
    mid = rows // 2
    top = ref[slab, lo : lo + mid, lane : lane + LANES].astype(jnp.float32)
    low = ref[slab, lo + mid : lo + rows, lane : lane + LANES].astype(jnp.float32)
    left = lax.broadcasted_iota(jnp.int32, (mid, LANES), 1) < HALF
    if side == 0:
        both = jnp.where(left, top, pltpu.roll(low, HALF, 1))
    else:
        both = jnp.where(left, pltpu.roll(top, HALF, 1), low)
    out_ref[dest, base + 3 * rows : base + 3 * rows + mid, :] = both.astype(out_ref.dtype)


def pack_gate_kernel(list_ref, gate_ref, share_ref, out_ref):
    slots, depth, width = gate_ref.shape
    size = depth * 7 // 2
    row = lax.broadcasted_iota(jnp.int32, share_ref.shape[1:], 0) // 4
    for dest in range(out_ref.shape[0]):
        pack_rows(
            lambda place: (gate_ref, list_ref[place]),
            out_ref, 0, dest, 0, depth, width // LANES,
        )
        value = share_ref[dest]
        high = value.astype(out_ref.dtype)
        rest = value - high.astype(jnp.float32)
        middle = rest.astype(out_ref.dtype)
        low = (rest - middle.astype(jnp.float32)).astype(out_ref.dtype)
        terms = jnp.where(
            row == 0,
            high.astype(jnp.float32),
            jnp.where(
                row == 1,
                middle.astype(jnp.float32),
                jnp.where(row == 2, low.astype(jnp.float32), 0.0),
            ),
        )
        out_ref[dest, size:, :] = terms.astype(out_ref.dtype)


def pack_kernel(parts, list_ref, in_ref, *out_refs):
    slots, depth, width = in_ref.shape
    for dest in range(out_refs[0].shape[0]):
        lo = 0
        for rows, out_ref in zip(parts, out_refs):
            pack_rows(
                lambda place: (in_ref, list_ref[place]),
                out_ref, 0, dest, lo, rows, width // LANES,
            )
            lo += rows


def vmem():
    return pl.BlockSpec(memory_space=pltpu.VMEM)


def smem():
    return pl.BlockSpec(memory_space=pltpu.SMEM)


def pack_gate(listing, gate_proj, share, dests):
    slots, depth, width = gate_proj.shape
    shape = (dests, depth * 7 // 2 + share.shape[1], LANES)
    return pl.pallas_call(
        pack_gate_kernel,
        out_shape=jax.ShapeDtypeStruct(shape, gate_proj.dtype),
        in_specs=[smem(), vmem(), vmem()],
        out_specs=vmem(),
        compiler_params=pltpu.CompilerParams(vmem_limit_bytes=32 * MIB),
        name="pack_gate",
    )(listing, gate_proj, share)


def pack(listing, weights, dests, parts, name):
    return pl.pallas_call(
        functools.partial(pack_kernel, parts),
        out_shape=[
            jax.ShapeDtypeStruct((dests, rows * 7 // 2, LANES), weights.dtype) for rows in parts
        ],
        in_specs=[smem(), vmem()],
        out_specs=[vmem()] * len(parts),
        compiler_params=pltpu.CompilerParams(vmem_limit_bytes=32 * MIB),
        name=name,
    )(listing, weights)


def unpack_rows(in_ref, at, base, rows, out_ref, out_row, out_lane):
    for number in range(3):
        out_ref[out_row : out_row + rows, out_lane + number * LANES : out_lane + (number + 1) * LANES] = (
            in_ref[at, base + number * rows : base + (number + 1) * rows, :]
        )
    mid = rows // 2
    both = in_ref[at, base + 3 * rows : base + 3 * rows + mid, :]
    lanes = slice(out_lane + 3 * LANES, out_lane + 4 * LANES)
    out_ref[out_row : out_row + mid, lanes] = both
    out_ref[out_row + mid : out_row + rows, lanes] = pltpu.roll(
        both.astype(jnp.float32), HALF, 1
    ).astype(out_ref.dtype)


def hidden_kernel(at_ref, *refs):
    pieces, (gate_ref, up_ref, out_ref, gate_w, up_w, rows) = refs[:8], refs[8:]
    sources, packed_rows, _ = up_ref.shape
    depth = packed_rows * 2 // 7
    group = sources // 2
    tile = pl.program_id(0)
    x, y, zl = tile // 4, tile // 2 % 2, tile % 2
    me, core = at_ref[0], at_ref[1]

    @pl.when(tile == 0)
    def _():
        for at in range(sources):
            place = (core + at // group) % 2 * group + at % group
            unpack_rows(gate_ref, place, 0, depth, gate_w, at * depth, 0)
            unpack_rows(up_ref, place, 0, depth, up_w, at * depth, 0)

    mid = pieces[0].shape[1]
    for number in range(4):
        lanes = slice(number * mid, (number + 1) * mid)
        coordinate = (x, y)[number % 2]
        for value in range(2):

            @pl.when(coordinate == value)
            def _():
                rows[:, lanes] = pieces[2 * number + value][...]

    gate = jnp.dot(rows[...], gate_w[...], preferred_element_type=jnp.float32)
    up = jnp.dot(rows[...], up_w[...], preferred_element_type=jnp.float32)
    value = gate / (1.0 + jnp.exp(-gate)) * up

    wide = gate.shape[1]
    term = lax.broadcasted_iota(jnp.int32, (16, wide), 0)
    lane = lax.broadcasted_iota(jnp.int32, (16, wide), 1)
    chosen = (term % 4 == lane // LANES) & (term < 12) & (lane < wide - HALF)
    chosen = jnp.where(chosen, 1.0, 0.0).astype(jnp.bfloat16)
    block = rows.shape[0] // 2
    for zh in range(2):
        source = me ^ (x + 2 * y + 4 * zl + 8 * zh)
        weight = lax.dot_general(
            gate_ref[source, packed_rows:, :],
            chosen,
            (((0,), (0,)), ((), ())),
            preferred_element_type=jnp.float32,
        )
        span = slice(zh * block, (zh + 1) * block)
        out_ref[span, :] = (value[span, :] * weight).astype(out_ref.dtype)


def hidden_units(at, pieces, gate, up):
    total = 2 * pieces[0].shape[0]
    mid = pieces[0].shape[1]
    tile = total // 8
    wide = 4 * LANES
    model = 4 * mid
    by_x = [lambda i: (jnp.minimum(i, 3), 0), lambda i: (jnp.maximum(i - 4, 0), 0)]
    by_y = [
        lambda i: (i // 4 * 2 + jnp.where(i // 2 % 2 == 0, i % 2, 1), 0),
        lambda i: (i // 4 * 2 + jnp.where(i // 2 % 2 == 1, i % 2, 0), 0),
    ]
    maps = (by_x + by_y) * 2
    return pl.pallas_call(
        hidden_kernel,
        grid=(8,),
        out_shape=jax.ShapeDtypeStruct((total, wide), up.dtype),
        in_specs=[smem()]
        + [pl.BlockSpec((tile, mid), where) for where in maps]
        + [vmem(), vmem()],
        out_specs=pl.BlockSpec((tile, wide), lambda i: (i, 0)),
        scratch_shapes=[pltpu.VMEM((model, wide), up.dtype)] * 2
        + [pltpu.VMEM((tile, model), up.dtype)],
        compiler_params=pltpu.CompilerParams(vmem_limit_bytes=56 * MIB),
        cost_estimate=pl.CostEstimate(
            flops=4 * total * model * wide, bytes_accessed=24 * MIB, transcendentals=total * wide
        ),
        name="hidden",
    )(at, *pieces, gate, up)


ORDERS = ((0, 1, 2), (1, 2, 0), (2, 0, 1))


def group_spans(features):
    tiles = features // LANES
    cuts = [0, -(-tiles // 3), -(-tiles // 3) + -(-(tiles - -(-tiles // 3)) // 2), tiles]
    return [slice(lo * LANES, hi * LANES) for lo, hi in zip(cuts, cuts[1:])]


def stage_axis(number, stage):
    order = ORDERS[number]
    return sum(1 for bit in order[stage:] if bit < order[stage])


def half_spans(rows, axis, side):
    size = rows >> (axis + 1)
    return [slice((2 * at + side) * size, (2 * at + side + 1) * size) for at in range(1 << axis)]


def down_kernel(rows, side, own_h, other_h, own_ref, other_ref, *refs):
    out_refs, (own_w, other_w) = refs[:-2], refs[-2:]
    for in_ref, w_ref in ((own_ref, own_w), (other_ref, other_w)):
        for at in range(in_ref.shape[0]):
            unpack_rows(in_ref, at, 0, rows, w_ref, at * rows, 0)
    dims = (((1,), (1,)), ((), ()))
    for number, span in enumerate(group_spans(own_w.shape[0])):
        done = 0
        for tokens in half_spans(own_h.shape[0], stage_axis(number, 0), side):
            value = lax.dot_general(
                own_h[tokens, :], own_w[span, :], dims, preferred_element_type=jnp.float32
            ) + lax.dot_general(
                other_h[tokens, :], other_w[span, :], dims, preferred_element_type=jnp.float32
            )
            size = tokens.stop - tokens.start
            out_refs[number][done : done + size, :] = value.astype(out_refs[number].dtype)
            done += size


def down_product(own_h, other_h, own, other, rows, side, dtype, name):
    sources = own.shape[0]
    total, wide = own_h.shape
    tokens = total // 2
    features = sources * rows
    shapes = [
        jax.ShapeDtypeStruct((tokens, span.stop - span.start), dtype)
        for span in group_spans(features)
    ]
    return pl.pallas_call(
        functools.partial(down_kernel, rows, side),
        out_shape=shapes,
        in_specs=[vmem()] * 4,
        out_specs=[vmem()] * len(shapes),
        scratch_shapes=[pltpu.VMEM((features, wide), own.dtype)] * 2,
        compiler_params=pltpu.CompilerParams(vmem_limit_bytes=40 * MIB),
        cost_estimate=pl.CostEstimate(
            flops=4 * tokens * wide * features, bytes_accessed=8 * MIB, transcendentals=0
        ),
        name=name,
    )(own_h, other_h, own, other)


def halve_kernel(axes, *refs):
    count = len(refs) // 4 if axes else 3
    out_refs = refs[2 * count :]
    lane = 0
    for number in range(count):
        keep_ref, come_ref = refs[2 * number : 2 * number + 2]
        if axes:
            send_ref, left_ref = out_refs[2 * number : 2 * number + 2]
            lanes = slice(0, keep_ref.shape[1])
        else:
            send_ref, left_ref = out_refs
            lanes = slice(lane, lane + keep_ref.shape[1])
            lane = lanes.stop
        axis = axes[number] if axes else 0
        for side, out_ref in enumerate((left_ref, send_ref)):
            done = 0
            for rows in half_spans(keep_ref.shape[0], axis, side):
                size = rows.stop - rows.start
                total = keep_ref[rows, :] + come_ref[rows, :].astype(jnp.float32)
                out_ref[done : done + size, lanes] = total.astype(out_ref.dtype)
                done += size


def halve(pairs, axes):
    sizes = [(keep.shape[0] // 2, keep.shape[1]) for keep, _ in pairs]
    if not axes:
        sizes = [(sizes[0][0], sum(width for _, width in sizes))]
    shapes = []
    for size in sizes:
        shapes += [jax.ShapeDtypeStruct(size, jnp.bfloat16), jax.ShapeDtypeStruct(size, jnp.float32)]
    out = pl.pallas_call(
        functools.partial(halve_kernel, axes),
        out_shape=shapes,
        in_specs=[vmem()] * (2 * len(pairs)),
        out_specs=[vmem()] * len(shapes),
        compiler_params=pltpu.CompilerParams(vmem_limit_bytes=40 * MIB),
        cost_estimate=pl.CostEstimate(
            flops=sum(keep.size for keep, _ in pairs), bytes_accessed=4 * MIB, transcendentals=0
        ),
        name="sum_stage",
    )(*[value for pair in pairs for value in pair])
    return [(out[2 * n], out[2 * n + 1]) for n in range(len(out) // 2)]


def swap(value, bit):
    size = lax.axis_size("ep")
    return lax.ppermute(value, "ep", [(i, i ^ (1 << bit)) for i in range(size)])


def gather_bits(value, bits, order, have=()):
    have = list(have)
    for bit in order:
        axis = sum(1 for b in have if b < bit)
        value = jnp.stack([value, swap(value, bit)], axis=axis)
        have.append(bit)
    return value


def take_half(value, axis, number):
    return lax.index_in_dim(value, number, axis, keepdims=False)


def sum_stages(keep, arrived, order, left):
    left = list(left)
    for bit in order:
        axis = left.index(bit)
        total = keep + arrived.astype(jnp.float32)
        arrived = swap(take_half(total, axis, 1).astype(jnp.bfloat16), bit)
        keep = take_half(total, axis, 0)
        left.remove(bit)
    return keep, arrived


def share_of_slots(slot_ids, gate_weights, slots):
    index = jnp.arange(slots, dtype=jnp.int32)
    picked = slot_ids.T[None, :, :] == index[:, None, None]
    return jnp.sum(jnp.where(picked, gate_weights.T[None, :, :], 0.0), axis=1)


def packed_layer(
    tokens, slot_ids, gate_weights, old_expert, new_expert, gate_proj, up_proj, down_proj
):
    devices = lax.axis_size("ep")
    slots, depth, width = gate_proj.shape
    block = tokens.shape[0]
    me = lax.axis_index("ep")
    core = lax.axis_index("et")
    group = devices // 2
    tie = lax.optimization_barrier
    _, listing, slot_place = distinct_sources(old_expert, new_expert)

    def exchange(value):
        return lax.ppermute(value, "et", [(0, 1), (1, 0)])

    def move(packed):
        return lax.all_to_all(packed, "ep", 0, 0, tiled=True)

    places = []
    for dest in range(devices):
        first, half, _ = units_of(dest)
        places.append([unit // (width // LANES) for unit in (first, first + 1, first + 2, half)] * 4)
    places = jnp.asarray(places, jnp.int32)
    share = share_of_slots(slot_ids, gate_weights, slots)
    belongs = slot_place[None, None, :, None] == places[:, :, None, None]
    share = jnp.sum(jnp.where(belongs, share[None, None], 0.0), axis=2)

    far = swap(tokens, 3)
    gate_packed, far = tie((pack_gate(listing, gate_proj, share, devices), far))
    (up_packed,) = pack(listing, up_proj, devices, (depth,), "pack_up")

    gate = move(gate_packed)
    mid = tokens.shape[1] // 2
    rows = jnp.concatenate([tokens, far], axis=0)
    rows = jnp.concatenate([rows, swap(rows, 2)], axis=0)
    first, second = rows[:, :mid], rows[:, mid:]
    first = jnp.concatenate([first, swap(first, 1)], axis=0)
    second = jnp.concatenate([second, swap(second, 0)], axis=0)
    gate, first, second, up_packed = tie((gate, first, second, up_packed))

    up = move(up_packed)
    pieces = [first, swap(first, 0), second, swap(second, 1)]
    others = [exchange(first), None, exchange(second), None]
    parts = (128, 96)
    down_packed = pack(listing, down_proj, devices, parts, "pack_down")
    up, pieces, others[0], others[2], down_packed = tie(
        (up, pieces, others[0], others[2], down_packed)
    )

    down0 = move(down_packed[0])
    others[1], others[3] = exchange(pieces[1]), exchange(pieces[3])
    at = jnp.stack([me, core]).astype(jnp.int32)
    hidden = hidden_units(at, pieces + others, gate, up)
    hidden_other = exchange(hidden)
    down0, hidden, hidden_other, packed = tie((down0, hidden, hidden_other, down_packed[1]))

    def products(down, rows_in):
        own = lax.dynamic_slice_in_dim(down, core * group, group, 0)
        other = exchange(lax.dynamic_slice_in_dim(down, (1 - core) * group, group, 0))
        args = (hidden, hidden_other, own, other)
        sent = down_product(*args, rows_in, 1, jnp.bfloat16, "down_send")
        sent, args = tie((sent, args))
        come = [swap(value, order[0]) for value, order in zip(sent, ORDERS)]
        return down_product(*args, rows_in, 0, jnp.float32, "down_keep"), come

    def stage(kept, come, number):
        axes = tuple(stage_axis(at, number) for at in range(3))
        out = halve(list(zip(kept, come)), axes)
        come = [swap(send, order[number]) for (send, _), order in zip(out, ORDERS)]
        return [keep for _, keep in out], come

    def last_stage(kept, come):
        ((send, keep),) = halve(list(zip(kept, come)), None)
        come = swap(send, 3)
        return (keep + come.astype(jnp.float32)).astype(jnp.bfloat16)

    down1 = move(packed)
    kept0, come0 = products(down0, parts[0])
    down1, kept0 = tie((down1, kept0))
    kept1, come1 = products(down1, parts[1])
    kept0, come0 = stage(kept0, come0, 1)
    kept1, come1 = stage(kept1, come1, 1)
    kept0, come0 = stage(kept0, come0, 2)
    kept1, come1 = stage(kept1, come1, 2)
    out = []
    for rows_in, total in zip(parts, (last_stage(kept0, come0), last_stage(kept1, come1))):
        out.append(total.reshape(block, group, rows_in))
    return jnp.concatenate(out, axis=2).reshape(tokens.shape)


def plain_layer(
    tokens, slot_ids, gate_weights, old_expert, new_expert, gate_proj, up_proj, down_proj
):
    devices = lax.axis_size("ep")
    bits = devices.bit_length() - 1
    slots = gate_proj.shape[0]
    me = lax.axis_index("ep")
    source, _, _ = distinct_sources(old_expert, new_expert)

    def move(weights):
        chosen = jnp.take(weights, source, axis=0, mode="clip")
        return lax.all_to_all(chosen, "ep", 0, 0, tiled=True)

    gate_slab = move(gate_proj).reshape(-1, gate_proj.shape[-1])
    up_slab = move(up_proj).reshape(-1, up_proj.shape[-1])
    down = move(down_proj)
    order = range(bits - 1, -1, -1)
    rows = gather_bits(tokens, bits, order).reshape(-1, tokens.shape[1])
    rows = lax.all_gather(rows, "et", axis=1, tiled=True)
    share = gather_bits(share_of_slots(slot_ids, gate_weights, slots), bits, order)
    share = lax.dynamic_index_in_dim(share, me, bits, keepdims=False).reshape(-1, 1)
    gate_part = jnp.dot(rows, gate_slab, preferred_element_type=jnp.float32)
    up_part = jnp.dot(rows, up_slab, preferred_element_type=jnp.float32)
    hidden = (jax.nn.silu(gate_part) * up_part * share).astype(jnp.bfloat16)
    hidden = lax.all_gather(hidden, "et", axis=1, tiled=True)
    down = lax.all_to_all(down, "et", 0, 2, tiled=True)
    value = lax.dot_general(
        hidden,
        down.reshape(-1, down.shape[-1]),
        (((1,), (1,)), ((), ())),
        preferred_element_type=jnp.float32,
    )
    value = value.reshape((2,) * bits + (-1,) + value.shape[1:])
    arrived = swap(take_half(value, 0, 1).astype(jnp.bfloat16), 0)
    left = list(range(1, bits))
    keep, arrived = sum_stages(take_half(value, 0, 0), arrived, left, left)
    return (keep + arrived.astype(jnp.float32)).astype(jnp.bfloat16)


def per_device(tokens, slot_ids, gate_weights, old_expert, new_expert, gate_proj, up_proj, down_proj):
    slots, depth, width = gate_proj.shape
    count = slots - slots // 8
    devices = lax.axis_size("ep")
    fits = (
        lax.axis_size("et") == 2
        and depth == 224
        and width % LANES == 0
        and count * width == devices * 7 * HALF
        and devices == 16
        and tokens.shape[0] == LANES
    )
    layer = packed_layer if fits else plain_layer
    return layer(
        tokens, slot_ids, gate_weights, old_expert, new_expert, gate_proj, up_proj, down_proj
    )


def solution(mesh):
    placed = (
        P("ep", "et"),
        P("ep", None),
        P("ep", None),
        P(),
        P(),
        P(None, "ep", "et"),
        P(None, "ep", "et"),
        P(None, "ep", "et"),
    )
    return jax.shard_map(
        per_device, mesh=mesh, in_specs=placed, out_specs=P("ep", "et"), check_vma=False
    )
```

```python
import functools

import jax
import jax.numpy as jnp
from jax import lax
from jax.experimental import pallas as pl
from jax.experimental.pallas import tpu as pltpu
from jax.sharding import PartitionSpec as P

LANES = 128
HALF = 64
MIB = 1 << 20


def distinct_sources(old_expert, new_expert):
    slots = old_expert.shape[0]
    index = jnp.arange(slots, dtype=jnp.int32)
    holders = new_expert[:, None] == old_expert[None, :]
    source = jnp.min(jnp.where(holders, index[None, :], slots), axis=1)
    used = jnp.any(source[:, None] == index[None, :], axis=0)
    earlier = (index[None, :] < index[:, None]) & used[None, :]
    place = jnp.sum(earlier.astype(jnp.int32), axis=1)
    count = slots - slots // 8
    wanted = jnp.arange(count, dtype=jnp.int32)
    listing = jnp.sum(
        jnp.where(used[None, :] & (place[None, :] == wanted[:, None]), index[None, :], 0), axis=1
    )
    slot_place = jnp.sum(jnp.where(source[:, None] == index[None, :], place[None, :], 0), axis=1)
    return source, listing, slot_place


def units_of(dest):
    if dest % 2 == 0:
        start = 7 * dest // 2
        return start, start + 3, 0
    start = (7 * dest + 1) // 2
    return start, start - 1, 1


def pack_rows(slab_of, out_ref, base, dest, lo, rows, per_slab):
    first, half, side = units_of(dest)
    for number in range(3):
        unit = first + number
        ref, slab = slab_of(unit // per_slab)
        lane = (unit % per_slab) * LANES
        out_ref[dest, base + number * rows : base + (number + 1) * rows, :] = ref[
            slab, lo : lo + rows, lane : lane + LANES
        ]
    ref, slab = slab_of(half // per_slab)
    lane = (half % per_slab) * LANES
    mid = rows // 2
    top = ref[slab, lo : lo + mid, lane : lane + LANES].astype(jnp.float32)
    low = ref[slab, lo + mid : lo + rows, lane : lane + LANES].astype(jnp.float32)
    left = lax.broadcasted_iota(jnp.int32, (mid, LANES), 1) < HALF
    if side == 0:
        both = jnp.where(left, top, pltpu.roll(low, HALF, 1))
    else:
        both = jnp.where(left, pltpu.roll(top, HALF, 1), low)
    out_ref[dest, base + 3 * rows : base + 3 * rows + mid, :] = both.astype(out_ref.dtype)


def pack_pair_kernel(list_ref, gate_ref, up_ref, share_ref, out_ref):
    slots, depth, width = gate_ref.shape
    size = depth * 7 // 2
    row = lax.broadcasted_iota(jnp.int32, share_ref.shape[1:], 0) // 4
    for dest in range(out_ref.shape[0]):
        for number, in_ref in enumerate((gate_ref, up_ref)):
            pack_rows(
                lambda place, in_ref=in_ref: (in_ref, list_ref[place]),
                out_ref, number * size, dest, 0, depth, width // LANES,
            )
        value = share_ref[dest]
        high = value.astype(out_ref.dtype)
        rest = value - high.astype(jnp.float32)
        middle = rest.astype(out_ref.dtype)
        low = (rest - middle.astype(jnp.float32)).astype(out_ref.dtype)
        terms = jnp.where(
            row == 0,
            high.astype(jnp.float32),
            jnp.where(
                row == 1,
                middle.astype(jnp.float32),
                jnp.where(row == 2, low.astype(jnp.float32), 0.0),
            ),
        )
        out_ref[dest, 2 * size :, :] = terms.astype(out_ref.dtype)


def pack_kernel(parts, list_ref, in_ref, *out_refs):
    slots, depth, width = in_ref.shape
    for dest in range(out_refs[0].shape[0]):
        lo = 0
        for rows, out_ref in zip(parts, out_refs):
            pack_rows(
                lambda place: (in_ref, list_ref[place]),
                out_ref, 0, dest, lo, rows, width // LANES,
            )
            lo += rows


def vmem():
    return pl.BlockSpec(memory_space=pltpu.VMEM)


def smem():
    return pl.BlockSpec(memory_space=pltpu.SMEM)


def pack_pair(listing, gate_proj, up_proj, share, dests):
    slots, depth, width = gate_proj.shape
    shape = (dests, depth * 7 + share.shape[1], LANES)
    return pl.pallas_call(
        pack_pair_kernel,
        out_shape=jax.ShapeDtypeStruct(shape, gate_proj.dtype),
        in_specs=[smem(), vmem(), vmem(), vmem()],
        out_specs=vmem(),
        compiler_params=pltpu.CompilerParams(vmem_limit_bytes=40 * MIB),
        name="pack_gate_up",
    )(listing, gate_proj, up_proj, share)


def pack(listing, weights, dests, parts, name):
    return pl.pallas_call(
        functools.partial(pack_kernel, parts),
        out_shape=[
            jax.ShapeDtypeStruct((dests, rows * 7 // 2, LANES), weights.dtype) for rows in parts
        ],
        in_specs=[smem(), vmem()],
        out_specs=[vmem()] * len(parts),
        compiler_params=pltpu.CompilerParams(vmem_limit_bytes=32 * MIB),
        name=name,
    )(listing, weights)


def unpack_rows(in_ref, at, base, rows, out_ref, out_row, out_lane):
    for number in range(3):
        out_ref[out_row : out_row + rows, out_lane + number * LANES : out_lane + (number + 1) * LANES] = (
            in_ref[at, base + number * rows : base + (number + 1) * rows, :]
        )
    mid = rows // 2
    both = in_ref[at, base + 3 * rows : base + 3 * rows + mid, :]
    lanes = slice(out_lane + 3 * LANES, out_lane + 4 * LANES)
    out_ref[out_row : out_row + mid, lanes] = both
    out_ref[out_row + mid : out_row + rows, lanes] = pltpu.roll(
        both.astype(jnp.float32), HALF, 1
    ).astype(out_ref.dtype)


def hidden_kernel(at_ref, *refs):
    pieces, (packed_ref, out_ref, gate_w, up_w, rows) = refs[:8], refs[8:]
    sources = packed_ref.shape[0]
    depth = gate_w.shape[0] // sources
    size = depth * 7 // 2
    group = sources // 2
    tile = pl.program_id(0)
    x, y, zl = tile // 4, tile // 2 % 2, tile % 2
    me, core = at_ref[0], at_ref[1]

    @pl.when(tile == 0)
    def _():
        for at in range(sources):
            place = (core + at // group) % 2 * group + at % group
            unpack_rows(packed_ref, place, 0, depth, gate_w, at * depth, 0)
            unpack_rows(packed_ref, place, size, depth, up_w, at * depth, 0)

    mid = pieces[0].shape[1]
    for number in range(4):
        lanes = slice(number * mid, (number + 1) * mid)
        coordinate = (x, y)[number % 2]
        for value in range(2):

            @pl.when(coordinate == value)
            def _():
                rows[:, lanes] = pieces[2 * number + value][...]

    gate = jnp.dot(rows[...], gate_w[...], preferred_element_type=jnp.float32)
    up = jnp.dot(rows[...], up_w[...], preferred_element_type=jnp.float32)
    value = gate / (1.0 + jnp.exp(-gate)) * up

    wide = gate.shape[1]
    term = lax.broadcasted_iota(jnp.int32, (16, wide), 0)
    lane = lax.broadcasted_iota(jnp.int32, (16, wide), 1)
    chosen = (term % 4 == lane // LANES) & (term < 12) & (lane < wide - HALF)
    chosen = jnp.where(chosen, 1.0, 0.0).astype(jnp.bfloat16)
    block = rows.shape[0] // 2
    for zh in range(2):
        source = me ^ (x + 2 * y + 4 * zl + 8 * zh)
        weight = lax.dot_general(
            packed_ref[source, 2 * size :, :],
            chosen,
            (((0,), (0,)), ((), ())),
            preferred_element_type=jnp.float32,
        )
        span = slice(zh * block, (zh + 1) * block)
        out_ref[span, :] = (value[span, :] * weight).astype(out_ref.dtype)


def hidden_units(at, pieces, packed):
    total = 2 * pieces[0].shape[0]
    mid = pieces[0].shape[1]
    tile = total // 8
    wide = 4 * LANES
    model = 4 * mid
    by_x = [lambda i: (jnp.minimum(i, 3), 0), lambda i: (jnp.maximum(i - 4, 0), 0)]
    by_y = [
        lambda i: (i // 4 * 2 + jnp.where(i // 2 % 2 == 0, i % 2, 1), 0),
        lambda i: (i // 4 * 2 + jnp.where(i // 2 % 2 == 1, i % 2, 0), 0),
    ]
    maps = (by_x + by_y) * 2
    return pl.pallas_call(
        hidden_kernel,
        grid=(8,),
        out_shape=jax.ShapeDtypeStruct((total, wide), packed.dtype),
        in_specs=[smem()]
        + [pl.BlockSpec((tile, mid), where) for where in maps]
        + [vmem()],
        out_specs=pl.BlockSpec((tile, wide), lambda i: (i, 0)),
        scratch_shapes=[pltpu.VMEM((model, wide), packed.dtype)] * 2
        + [pltpu.VMEM((tile, model), packed.dtype)],
        compiler_params=pltpu.CompilerParams(vmem_limit_bytes=56 * MIB),
        cost_estimate=pl.CostEstimate(
            flops=4 * total * model * wide, bytes_accessed=24 * MIB, transcendentals=total * wide
        ),
        name="hidden",
    )(at, *pieces, packed)


HALVES = ((0, 1, 2), (1, 0, 2))
THIRDS = ((0, 1, 2), (1, 2, 0), (2, 0, 1))


def group_spans(features, count):
    tiles = features // LANES
    cuts = [-(-tiles * at // count) * LANES for at in range(count + 1)]
    return [slice(lo, hi) for lo, hi in zip(cuts, cuts[1:])]


def stage_axis(order, stage):
    return sum(1 for bit in order[stage:] if bit < order[stage])


def half_spans(rows, axis, side):
    size = rows >> (axis + 1)
    return [slice((2 * at + side) * size, (2 * at + side + 1) * size) for at in range(1 << axis)]


def down_kernel(rows, side, orders, own_h, other_h, own_ref, other_ref, *refs):
    out_refs, (own_w, other_w) = refs[:-2], refs[-2:]
    for in_ref, w_ref in ((own_ref, own_w), (other_ref, other_w)):
        for at in range(in_ref.shape[0]):
            unpack_rows(in_ref, at, 0, rows, w_ref, at * rows, 0)
    dims = (((1,), (1,)), ((), ()))
    for number, span in enumerate(group_spans(own_w.shape[0], len(orders))):
        done = 0
        for tokens in half_spans(own_h.shape[0], stage_axis(orders[number], 0), side):
            value = lax.dot_general(
                own_h[tokens, :], own_w[span, :], dims, preferred_element_type=jnp.float32
            ) + lax.dot_general(
                other_h[tokens, :], other_w[span, :], dims, preferred_element_type=jnp.float32
            )
            size = tokens.stop - tokens.start
            out_refs[number][done : done + size, :] = value.astype(out_refs[number].dtype)
            done += size


def down_product(own_h, other_h, own, other, rows, side, orders, dtype, name):
    sources = own.shape[0]
    total, wide = own_h.shape
    tokens = total // 2
    features = sources * rows
    shapes = [
        jax.ShapeDtypeStruct((tokens, span.stop - span.start), dtype)
        for span in group_spans(features, len(orders))
    ]
    return pl.pallas_call(
        functools.partial(down_kernel, rows, side, orders),
        out_shape=shapes,
        in_specs=[vmem()] * 4,
        out_specs=[vmem()] * len(shapes),
        scratch_shapes=[pltpu.VMEM((features, wide), own.dtype)] * 2,
        compiler_params=pltpu.CompilerParams(vmem_limit_bytes=40 * MIB),
        cost_estimate=pl.CostEstimate(
            flops=4 * tokens * wide * features, bytes_accessed=8 * MIB, transcendentals=0
        ),
        name=name,
    )(own_h, other_h, own, other)


def halve_kernel(axes, *refs):
    count = len(refs) // 4 if axes else len(refs) // 2 - 1
    out_refs = refs[2 * count :]
    lane = 0
    for number in range(count):
        keep_ref, come_ref = refs[2 * number : 2 * number + 2]
        if axes:
            send_ref, left_ref = out_refs[2 * number : 2 * number + 2]
            lanes = slice(0, keep_ref.shape[1])
        else:
            send_ref, left_ref = out_refs
            lanes = slice(lane, lane + keep_ref.shape[1])
            lane = lanes.stop
        axis = axes[number] if axes else 0
        for side, out_ref in enumerate((left_ref, send_ref)):
            done = 0
            for rows in half_spans(keep_ref.shape[0], axis, side):
                size = rows.stop - rows.start
                total = keep_ref[rows, :] + come_ref[rows, :].astype(jnp.float32)
                out_ref[done : done + size, lanes] = total.astype(out_ref.dtype)
                done += size


def halve(pairs, axes):
    sizes = [(keep.shape[0] // 2, keep.shape[1]) for keep, _ in pairs]
    if not axes:
        sizes = [(sizes[0][0], sum(width for _, width in sizes))]
    shapes = []
    for size in sizes:
        shapes += [jax.ShapeDtypeStruct(size, jnp.bfloat16), jax.ShapeDtypeStruct(size, jnp.float32)]
    out = pl.pallas_call(
        functools.partial(halve_kernel, axes),
        out_shape=shapes,
        in_specs=[vmem()] * (2 * len(pairs)),
        out_specs=[vmem()] * len(shapes),
        compiler_params=pltpu.CompilerParams(vmem_limit_bytes=40 * MIB),
        cost_estimate=pl.CostEstimate(
            flops=sum(keep.size for keep, _ in pairs), bytes_accessed=4 * MIB, transcendentals=0
        ),
        name="sum_stage",
    )(*[value for pair in pairs for value in pair])
    return [(out[2 * n], out[2 * n + 1]) for n in range(len(out) // 2)]


def swap(value, bit):
    size = lax.axis_size("ep")
    return lax.ppermute(value, "ep", [(i, i ^ (1 << bit)) for i in range(size)])


def gather_bits(value, bits, order, have=()):
    have = list(have)
    for bit in order:
        axis = sum(1 for b in have if b < bit)
        value = jnp.stack([value, swap(value, bit)], axis=axis)
        have.append(bit)
    return value


def take_half(value, axis, number):
    return lax.index_in_dim(value, number, axis, keepdims=False)


def sum_stages(keep, arrived, order, left):
    left = list(left)
    for bit in order:
        axis = left.index(bit)
        total = keep + arrived.astype(jnp.float32)
        arrived = swap(take_half(total, axis, 1).astype(jnp.bfloat16), bit)
        keep = take_half(total, axis, 0)
        left.remove(bit)
    return keep, arrived


def share_of_slots(slot_ids, gate_weights, slots):
    index = jnp.arange(slots, dtype=jnp.int32)
    picked = slot_ids.T[None, :, :] == index[:, None, None]
    return jnp.sum(jnp.where(picked, gate_weights.T[None, :, :], 0.0), axis=1)


def packed_layer(
    tokens, slot_ids, gate_weights, old_expert, new_expert, gate_proj, up_proj, down_proj
):
    devices = lax.axis_size("ep")
    slots, depth, width = gate_proj.shape
    block = tokens.shape[0]
    me = lax.axis_index("ep")
    core = lax.axis_index("et")
    group = devices // 2
    tie = lax.optimization_barrier
    _, listing, slot_place = distinct_sources(old_expert, new_expert)

    def exchange(value):
        return lax.ppermute(value, "et", [(0, 1), (1, 0)])

    def move(packed):
        return lax.all_to_all(packed, "ep", 0, 0, tiled=True)

    places = []
    for dest in range(devices):
        first, half, _ = units_of(dest)
        places.append([unit // (width // LANES) for unit in (first, first + 1, first + 2, half)] * 4)
    places = jnp.asarray(places, jnp.int32)
    share = share_of_slots(slot_ids, gate_weights, slots)
    belongs = slot_place[None, None, :, None] == places[:, :, None, None]
    share = jnp.sum(jnp.where(belongs, share[None, None], 0.0), axis=2)

    near, far = swap(tokens, 2), swap(tokens, 3)
    corner = swap(far, 2)
    packed = pack_pair(listing, gate_proj, up_proj, share, devices)
    packed, near, far, corner = tie((packed, near, far, corner))

    moved = move(packed)
    mid = tokens.shape[1] // 2
    rows = jnp.concatenate([tokens, far, near, corner], axis=0)
    first, second = rows[:, :mid], rows[:, mid:]
    first = jnp.concatenate([first, swap(first, 1)], axis=0)
    second = jnp.concatenate([second, swap(second, 0)], axis=0)
    pieces = [first, swap(first, 0), second, swap(second, 1)]
    others = [exchange(piece) for piece in pieces]
    parts = (128, 96)
    down_packed = pack(listing, down_proj, devices, parts, "pack_down")
    moved, down_packed = tie((moved, down_packed))

    down0 = move(down_packed[0])
    at = jnp.stack([me, core]).astype(jnp.int32)
    hidden = hidden_units(at, pieces + others, moved)
    hidden_other = exchange(hidden)
    down0, hidden, hidden_other, packed = tie((down0, hidden, hidden_other, down_packed[1]))

    def products(down, rows_in, orders):
        own = lax.dynamic_slice_in_dim(down, core * group, group, 0)
        other = exchange(lax.dynamic_slice_in_dim(down, (1 - core) * group, group, 0))
        args = (hidden, hidden_other, own, other)
        sent = down_product(*args, rows_in, 1, orders, jnp.bfloat16, "down_send")
        sent, args = tie((sent, args))
        come = [swap(value, order[0]) for value, order in zip(sent, orders)]
        return down_product(*args, rows_in, 0, orders, jnp.float32, "down_keep"), come

    def stage(kept, come, number, orders):
        axes = tuple(stage_axis(order, number) for order in orders)
        out = halve(list(zip(kept, come)), axes)
        come = [swap(send, order[number]) for (send, _), order in zip(out, orders)]
        return [keep for _, keep in out], come

    def last_stage(kept, come):
        ((send, keep),) = halve(list(zip(kept, come)), None)
        come = swap(send, 3)
        return (keep + come.astype(jnp.float32)).astype(jnp.bfloat16)

    down1 = move(packed)
    kept0, come0 = products(down0, parts[0], HALVES)
    down1, kept0 = tie((down1, kept0))
    kept1, come1 = products(down1, parts[1], THIRDS)
    kept0, come0 = stage(kept0, come0, 1, HALVES)
    kept1, come1 = stage(kept1, come1, 1, THIRDS)
    kept0, come0 = stage(kept0, come0, 2, HALVES)
    kept1, come1 = stage(kept1, come1, 2, THIRDS)
    out = []
    for rows_in, total in zip(parts, (last_stage(kept0, come0), last_stage(kept1, come1))):
        out.append(total.reshape(block, group, rows_in))
    return jnp.concatenate(out, axis=2).reshape(tokens.shape)


def plain_layer(
    tokens, slot_ids, gate_weights, old_expert, new_expert, gate_proj, up_proj, down_proj
):
    devices = lax.axis_size("ep")
    bits = devices.bit_length() - 1
    slots = gate_proj.shape[0]
    me = lax.axis_index("ep")
    source, _, _ = distinct_sources(old_expert, new_expert)

    def move(weights):
        chosen = jnp.take(weights, source, axis=0, mode="clip")
        return lax.all_to_all(chosen, "ep", 0, 0, tiled=True)

    gate_slab = move(gate_proj).reshape(-1, gate_proj.shape[-1])
    up_slab = move(up_proj).reshape(-1, up_proj.shape[-1])
    down = move(down_proj)
    order = range(bits - 1, -1, -1)
    rows = gather_bits(tokens, bits, order).reshape(-1, tokens.shape[1])
    rows = lax.all_gather(rows, "et", axis=1, tiled=True)
    share = gather_bits(share_of_slots(slot_ids, gate_weights, slots), bits, order)
    share = lax.dynamic_index_in_dim(share, me, bits, keepdims=False).reshape(-1, 1)
    gate_part = jnp.dot(rows, gate_slab, preferred_element_type=jnp.float32)
    up_part = jnp.dot(rows, up_slab, preferred_element_type=jnp.float32)
    hidden = (jax.nn.silu(gate_part) * up_part * share).astype(jnp.bfloat16)
    hidden = lax.all_gather(hidden, "et", axis=1, tiled=True)
    down = lax.all_to_all(down, "et", 0, 2, tiled=True)
    value = lax.dot_general(
        hidden,
        down.reshape(-1, down.shape[-1]),
        (((1,), (1,)), ((), ())),
        preferred_element_type=jnp.float32,
    )
    value = value.reshape((2,) * bits + (-1,) + value.shape[1:])
    arrived = swap(take_half(value, 0, 1).astype(jnp.bfloat16), 0)
    left = list(range(1, bits))
    keep, arrived = sum_stages(take_half(value, 0, 0), arrived, left, left)
    return (keep + arrived.astype(jnp.float32)).astype(jnp.bfloat16)


def per_device(tokens, slot_ids, gate_weights, old_expert, new_expert, gate_proj, up_proj, down_proj):
    slots, depth, width = gate_proj.shape
    count = slots - slots // 8
    devices = lax.axis_size("ep")
    fits = (
        lax.axis_size("et") == 2
        and depth == 224
        and width % LANES == 0
        and count * width == devices * 7 * HALF
        and devices == 16
        and tokens.shape[0] == LANES
    )
    layer = packed_layer if fits else plain_layer
    return layer(
        tokens, slot_ids, gate_weights, old_expert, new_expert, gate_proj, up_proj, down_proj
    )


def solution(mesh):
    placed = (
        P("ep", "et"),
        P("ep", None),
        P("ep", None),
        P(),
        P(),
        P(None, "ep", "et"),
        P(None, "ep", "et"),
        P(None, "ep", "et"),
    )
    return jax.shard_map(
        per_device, mesh=mesh, in_specs=placed, out_specs=P("ep", "et"), check_vma=False
    )
```

```python
import functools

import jax
import jax.numpy as jnp
from jax import lax
from jax.experimental import pallas as pl
from jax.experimental.pallas import tpu as pltpu
from jax.sharding import PartitionSpec as P

LANES = 128
HALF = 64
MIB = 1 << 20


def distinct_sources(old_expert, new_expert):
    slots = old_expert.shape[0]
    index = jnp.arange(slots, dtype=jnp.int32)
    holders = new_expert[:, None] == old_expert[None, :]
    source = jnp.min(jnp.where(holders, index[None, :], slots), axis=1)
    used = jnp.any(source[:, None] == index[None, :], axis=0)
    earlier = (index[None, :] < index[:, None]) & used[None, :]
    place = jnp.sum(earlier.astype(jnp.int32), axis=1)
    count = slots - slots // 8
    wanted = jnp.arange(count, dtype=jnp.int32)
    listing = jnp.sum(
        jnp.where(used[None, :] & (place[None, :] == wanted[:, None]), index[None, :], 0), axis=1
    )
    slot_place = jnp.sum(jnp.where(source[:, None] == index[None, :], place[None, :], 0), axis=1)
    return source, listing, slot_place


def units_of(dest):
    if dest % 2 == 0:
        start = 7 * dest // 2
        return start, start + 3, 0
    start = (7 * dest + 1) // 2
    return start, start - 1, 1


def pack_rows(slab_of, out_ref, base, dest, lo, rows, per_slab):
    first, half, side = units_of(dest)
    for number in range(3):
        unit = first + number
        ref, slab = slab_of(unit // per_slab)
        lane = (unit % per_slab) * LANES
        out_ref[dest, base + number * rows : base + (number + 1) * rows, :] = ref[
            slab, lo : lo + rows, lane : lane + LANES
        ]
    ref, slab = slab_of(half // per_slab)
    lane = (half % per_slab) * LANES
    mid = rows // 2
    top = ref[slab, lo : lo + mid, lane : lane + LANES].astype(jnp.float32)
    low = ref[slab, lo + mid : lo + rows, lane : lane + LANES].astype(jnp.float32)
    left = lax.broadcasted_iota(jnp.int32, (mid, LANES), 1) < HALF
    if side == 0:
        both = jnp.where(left, top, pltpu.roll(low, HALF, 1))
    else:
        both = jnp.where(left, pltpu.roll(top, HALF, 1), low)
    out_ref[dest, base + 3 * rows : base + 3 * rows + mid, :] = both.astype(out_ref.dtype)


def pack_first_kernel(rows, list_ref, gate_ref, up_ref, down_ref, share_ref, out_ref):
    slots, depth, width = gate_ref.shape
    size = depth * 7 // 2
    row = lax.broadcasted_iota(jnp.int32, share_ref.shape[1:], 0) // 4
    for dest in range(out_ref.shape[0]):
        for number, in_ref in enumerate((gate_ref, up_ref)):
            pack_rows(
                lambda place, in_ref=in_ref: (in_ref, list_ref[place]),
                out_ref, number * size, dest, 0, depth, width // LANES,
            )
        pack_rows(
            lambda place: (down_ref, list_ref[place]),
            out_ref, 2 * size, dest, 0, rows, width // LANES,
        )
        value = share_ref[dest]
        high = value.astype(out_ref.dtype)
        rest = value - high.astype(jnp.float32)
        middle = rest.astype(out_ref.dtype)
        low = (rest - middle.astype(jnp.float32)).astype(out_ref.dtype)
        terms = jnp.where(
            row == 0,
            high.astype(jnp.float32),
            jnp.where(
                row == 1,
                middle.astype(jnp.float32),
                jnp.where(row == 2, low.astype(jnp.float32), 0.0),
            ),
        )
        out_ref[dest, 2 * size + rows * 7 // 2 :, :] = terms.astype(out_ref.dtype)


def pack_rest_kernel(rows, list_ref, down_ref, out_ref):
    slots, depth, width = down_ref.shape
    for dest in range(out_ref.shape[0]):
        pack_rows(
            lambda place: (down_ref, list_ref[place]),
            out_ref, 0, dest, rows, depth - rows, width // LANES,
        )


def vmem():
    return pl.BlockSpec(memory_space=pltpu.VMEM)


def smem():
    return pl.BlockSpec(memory_space=pltpu.SMEM)


def pack_first(listing, gate_proj, up_proj, down_proj, rows, share, dests):
    slots, depth, width = gate_proj.shape
    shape = (dests, depth * 7 + rows * 7 // 2 + share.shape[1], LANES)
    return pl.pallas_call(
        functools.partial(pack_first_kernel, rows),
        out_shape=jax.ShapeDtypeStruct(shape, gate_proj.dtype),
        in_specs=[smem(), vmem(), vmem(), vmem(), vmem()],
        out_specs=vmem(),
        compiler_params=pltpu.CompilerParams(vmem_limit_bytes=40 * MIB),
        name="pack_first",
    )(listing, gate_proj, up_proj, down_proj, share)


def pack_rest(listing, down_proj, rows, dests):
    slots, depth, width = down_proj.shape
    shape = (dests, (depth - rows) * 7 // 2, LANES)
    return pl.pallas_call(
        functools.partial(pack_rest_kernel, rows),
        out_shape=jax.ShapeDtypeStruct(shape, down_proj.dtype),
        in_specs=[smem(), vmem()],
        out_specs=vmem(),
        compiler_params=pltpu.CompilerParams(vmem_limit_bytes=32 * MIB),
        name="pack_rest",
    )(listing, down_proj)


def unpack_rows(in_ref, at, base, rows, out_ref, out_row, out_lane):
    for number in range(3):
        out_ref[out_row : out_row + rows, out_lane + number * LANES : out_lane + (number + 1) * LANES] = (
            in_ref[at, base + number * rows : base + (number + 1) * rows, :]
        )
    mid = rows // 2
    both = in_ref[at, base + 3 * rows : base + 3 * rows + mid, :]
    lanes = slice(out_lane + 3 * LANES, out_lane + 4 * LANES)
    out_ref[out_row : out_row + mid, lanes] = both
    out_ref[out_row + mid : out_row + rows, lanes] = pltpu.roll(
        both.astype(jnp.float32), HALF, 1
    ).astype(out_ref.dtype)


def hidden_kernel(at_ref, *refs):
    pieces, (packed_ref, out_ref, gate_w, up_w, rows) = refs[:8], refs[8:]
    sources = packed_ref.shape[0]
    depth = gate_w.shape[0] // sources
    size = depth * 7 // 2
    group = sources // 2
    tile = pl.program_id(0)
    x, y, zl = tile // 4, tile // 2 % 2, tile % 2
    me, core = at_ref[0], at_ref[1]

    @pl.when(tile == 0)
    def _():
        for at in range(sources):
            place = (core + at // group) % 2 * group + at % group
            unpack_rows(packed_ref, place, 0, depth, gate_w, at * depth, 0)
            unpack_rows(packed_ref, place, size, depth, up_w, at * depth, 0)

    mid = pieces[0].shape[1]
    for number in range(4):
        lanes = slice(number * mid, (number + 1) * mid)
        coordinate = (x, y)[number % 2]
        for value in range(2):

            @pl.when(coordinate == value)
            def _():
                rows[:, lanes] = pieces[2 * number + value][...]

    gate = jnp.dot(rows[...], gate_w[...], preferred_element_type=jnp.float32)
    up = jnp.dot(rows[...], up_w[...], preferred_element_type=jnp.float32)
    value = gate / (1.0 + jnp.exp(-gate)) * up

    wide = gate.shape[1]
    term = lax.broadcasted_iota(jnp.int32, (16, wide), 0)
    lane = lax.broadcasted_iota(jnp.int32, (16, wide), 1)
    chosen = (term % 4 == lane // LANES) & (term < 12) & (lane < wide - HALF)
    chosen = jnp.where(chosen, 1.0, 0.0).astype(jnp.bfloat16)
    block = rows.shape[0] // 2
    for zh in range(2):
        source = me ^ (x + 2 * y + 4 * zl + 8 * zh)
        weight = lax.dot_general(
            packed_ref[source, packed_ref.shape[1] - 16 :, :],
            chosen,
            (((0,), (0,)), ((), ())),
            preferred_element_type=jnp.float32,
        )
        span = slice(zh * block, (zh + 1) * block)
        out_ref[span, :] = (value[span, :] * weight).astype(out_ref.dtype)


def hidden_units(at, pieces, packed):
    total = 2 * pieces[0].shape[0]
    mid = pieces[0].shape[1]
    tile = total // 8
    wide = 4 * LANES
    model = 4 * mid
    by_x = [lambda i: (jnp.minimum(i, 3), 0), lambda i: (jnp.maximum(i - 4, 0), 0)]
    by_y = [
        lambda i: (i // 4 * 2 + jnp.where(i // 2 % 2 == 0, i % 2, 1), 0),
        lambda i: (i // 4 * 2 + jnp.where(i // 2 % 2 == 1, i % 2, 0), 0),
    ]
    maps = (by_x + by_y) * 2
    return pl.pallas_call(
        hidden_kernel,
        grid=(8,),
        out_shape=jax.ShapeDtypeStruct((total, wide), packed.dtype),
        in_specs=[smem()]
        + [pl.BlockSpec((tile, mid), where) for where in maps]
        + [vmem()],
        out_specs=pl.BlockSpec((tile, wide), lambda i: (i, 0)),
        scratch_shapes=[pltpu.VMEM((model, wide), packed.dtype)] * 2
        + [pltpu.VMEM((tile, model), packed.dtype)],
        compiler_params=pltpu.CompilerParams(vmem_limit_bytes=56 * MIB),
        cost_estimate=pl.CostEstimate(
            flops=4 * total * model * wide, bytes_accessed=24 * MIB, transcendentals=total * wide
        ),
        name="hidden",
    )(at, *pieces, packed)


THIRDS = ((0, 1, 2), (1, 2, 0), (2, 0, 1))


def group_spans(features, count):
    tiles = features // LANES
    cuts = [-(-tiles * at // count) * LANES for at in range(count + 1)]
    return [slice(lo, hi) for lo, hi in zip(cuts, cuts[1:])]


def stage_axis(order, stage):
    return sum(1 for bit in order[stage:] if bit < order[stage])


def half_spans(rows, axis, side):
    size = rows >> (axis + 1)
    return [slice((2 * at + side) * size, (2 * at + side + 1) * size) for at in range(1 << axis)]


def down_kernel(rows, side, orders, own_h, other_h, own_ref, other_ref, *refs):
    out_refs, (own_w, other_w) = refs[:-2], refs[-2:]
    for in_ref, w_ref in ((own_ref, own_w), (other_ref, other_w)):
        for at in range(in_ref.shape[0]):
            unpack_rows(in_ref, at, 0, rows, w_ref, at * rows, 0)
    dims = (((1,), (1,)), ((), ()))
    for number, span in enumerate(group_spans(own_w.shape[0], len(orders))):
        done = 0
        for tokens in half_spans(own_h.shape[0], stage_axis(orders[number], 0), side):
            value = lax.dot_general(
                own_h[tokens, :], own_w[span, :], dims, preferred_element_type=jnp.float32
            ) + lax.dot_general(
                other_h[tokens, :], other_w[span, :], dims, preferred_element_type=jnp.float32
            )
            size = tokens.stop - tokens.start
            out_refs[number][done : done + size, :] = value.astype(out_refs[number].dtype)
            done += size


def down_product(own_h, other_h, own, other, rows, side, orders, dtype, name):
    sources = own.shape[0]
    total, wide = own_h.shape
    tokens = total // 2
    features = sources * rows
    shapes = [
        jax.ShapeDtypeStruct((tokens, span.stop - span.start), dtype)
        for span in group_spans(features, len(orders))
    ]
    return pl.pallas_call(
        functools.partial(down_kernel, rows, side, orders),
        out_shape=shapes,
        in_specs=[vmem()] * 4,
        out_specs=[vmem()] * len(shapes),
        scratch_shapes=[pltpu.VMEM((features, wide), own.dtype)] * 2,
        compiler_params=pltpu.CompilerParams(vmem_limit_bytes=40 * MIB),
        cost_estimate=pl.CostEstimate(
            flops=4 * tokens * wide * features, bytes_accessed=8 * MIB, transcendentals=0
        ),
        name=name,
    )(own_h, other_h, own, other)


def halve_kernel(axes, *refs):
    count = len(refs) // 4 if axes else len(refs) // 2 - 1
    out_refs = refs[2 * count :]
    lane = 0
    for number in range(count):
        keep_ref, come_ref = refs[2 * number : 2 * number + 2]
        if axes:
            send_ref, left_ref = out_refs[2 * number : 2 * number + 2]
            lanes = slice(0, keep_ref.shape[1])
        else:
            send_ref, left_ref = out_refs
            lanes = slice(lane, lane + keep_ref.shape[1])
            lane = lanes.stop
        axis = axes[number] if axes else 0
        for side, out_ref in enumerate((left_ref, send_ref)):
            done = 0
            for rows in half_spans(keep_ref.shape[0], axis, side):
                size = rows.stop - rows.start
                total = keep_ref[rows, :] + come_ref[rows, :].astype(jnp.float32)
                out_ref[done : done + size, lanes] = total.astype(out_ref.dtype)
                done += size


def halve(pairs, axes):
    sizes = [(keep.shape[0] // 2, keep.shape[1]) for keep, _ in pairs]
    if not axes:
        sizes = [(sizes[0][0], sum(width for _, width in sizes))]
    shapes = []
    for size in sizes:
        shapes += [jax.ShapeDtypeStruct(size, jnp.bfloat16), jax.ShapeDtypeStruct(size, jnp.float32)]
    out = pl.pallas_call(
        functools.partial(halve_kernel, axes),
        out_shape=shapes,
        in_specs=[vmem()] * (2 * len(pairs)),
        out_specs=[vmem()] * len(shapes),
        compiler_params=pltpu.CompilerParams(vmem_limit_bytes=40 * MIB),
        cost_estimate=pl.CostEstimate(
            flops=sum(keep.size for keep, _ in pairs), bytes_accessed=4 * MIB, transcendentals=0
        ),
        name="sum_stage",
    )(*[value for pair in pairs for value in pair])
    return [(out[2 * n], out[2 * n + 1]) for n in range(len(out) // 2)]


def swap(value, bit):
    size = lax.axis_size("ep")
    return lax.ppermute(value, "ep", [(i, i ^ (1 << bit)) for i in range(size)])


def gather_bits(value, bits, order, have=()):
    have = list(have)
    for bit in order:
        axis = sum(1 for b in have if b < bit)
        value = jnp.stack([value, swap(value, bit)], axis=axis)
        have.append(bit)
    return value


def take_half(value, axis, number):
    return lax.index_in_dim(value, number, axis, keepdims=False)


def sum_stages(keep, arrived, order, left):
    left = list(left)
    for bit in order:
        axis = left.index(bit)
        total = keep + arrived.astype(jnp.float32)
        arrived = swap(take_half(total, axis, 1).astype(jnp.bfloat16), bit)
        keep = take_half(total, axis, 0)
        left.remove(bit)
    return keep, arrived


def share_of_slots(slot_ids, gate_weights, slots):
    index = jnp.arange(slots, dtype=jnp.int32)
    picked = slot_ids.T[None, :, :] == index[:, None, None]
    return jnp.sum(jnp.where(picked, gate_weights.T[None, :, :], 0.0), axis=1)


def packed_layer(
    tokens, slot_ids, gate_weights, old_expert, new_expert, gate_proj, up_proj, down_proj
):
    devices = lax.axis_size("ep")
    slots, depth, width = gate_proj.shape
    block = tokens.shape[0]
    me = lax.axis_index("ep")
    core = lax.axis_index("et")
    group = devices // 2
    tie = lax.optimization_barrier
    _, listing, slot_place = distinct_sources(old_expert, new_expert)

    def exchange(value):
        return lax.ppermute(value, "et", [(0, 1), (1, 0)])

    def move(packed):
        return lax.all_to_all(packed, "ep", 0, 0, tiled=True)

    places = []
    for dest in range(devices):
        first, half, _ = units_of(dest)
        places.append([unit // (width // LANES) for unit in (first, first + 1, first + 2, half)] * 4)
    places = jnp.asarray(places, jnp.int32)
    share = share_of_slots(slot_ids, gate_weights, slots)
    belongs = slot_place[None, None, :, None] == places[:, :, None, None]
    share = jnp.sum(jnp.where(belongs, share[None, None], 0.0), axis=2)

    near, far = swap(tokens, 2), swap(tokens, 3)
    corner = swap(far, 2)
    parts = (128, 96)
    packed = pack_first(listing, gate_proj, up_proj, down_proj, parts[0], share, devices)
    packed, near, far, corner = tie((packed, near, far, corner))

    moved = move(packed)
    mid = tokens.shape[1] // 2
    rows = jnp.concatenate([tokens, far, near, corner], axis=0)
    first, second = rows[:, :mid], rows[:, mid:]
    first = jnp.concatenate([first, swap(first, 1)], axis=0)
    second = jnp.concatenate([second, swap(second, 0)], axis=0)
    pieces = [first, swap(first, 0), second, swap(second, 1)]
    others = [exchange(piece) for piece in pieces]
    rest = pack_rest(listing, down_proj, parts[0], devices)
    moved, rest = tie((moved, rest))

    down1 = move(rest)
    at = jnp.stack([me, core]).astype(jnp.int32)
    hidden = hidden_units(at, pieces + others, moved)
    hidden_other = exchange(hidden)
    down0 = moved[:, depth * 7 : depth * 7 + parts[0] * 7 // 2]

    def products(down, rows_in, orders):
        own = lax.dynamic_slice_in_dim(down, core * group, group, 0)
        other = exchange(lax.dynamic_slice_in_dim(down, (1 - core) * group, group, 0))
        args = (hidden, hidden_other, own, other)
        sent = down_product(*args, rows_in, 1, orders, jnp.bfloat16, "down_send")
        sent, args = tie((sent, args))
        come = [swap(value, order[0]) for value, order in zip(sent, orders)]
        kept = down_product(*args, rows_in, 0, orders, jnp.float32, "down_keep")
        return kept, come, sent

    def stage(kept, come, number, orders):
        axes = tuple(stage_axis(order, number) for order in orders)
        out = halve(list(zip(kept, come)), axes)
        come = [swap(send, order[number]) for (send, _), order in zip(out, orders)]
        return [keep for _, keep in out], come

    def last_stage(kept, come):
        ((send, keep),) = halve(list(zip(kept, come)), None)
        come = swap(send, 3)
        return (keep + come.astype(jnp.float32)).astype(jnp.bfloat16)

    kept0, come0, _ = products(down0, parts[0], THIRDS)
    down1, kept0 = tie((down1, kept0))
    kept1, come1, sent1 = products(down1, parts[1], THIRDS)
    kept0, _ = tie((kept0, sent1))
    kept0, come0 = stage(kept0, come0, 1, THIRDS)
    kept1, come1 = stage(kept1, come1, 1, THIRDS)
    kept0, come0 = stage(kept0, come0, 2, THIRDS)
    kept1, come1 = stage(kept1, come1, 2, THIRDS)
    out = []
    for rows_in, total in zip(parts, (last_stage(kept0, come0), last_stage(kept1, come1))):
        out.append(total.reshape(block, group, rows_in))
    return jnp.concatenate(out, axis=2).reshape(tokens.shape)


def plain_layer(
    tokens, slot_ids, gate_weights, old_expert, new_expert, gate_proj, up_proj, down_proj
):
    devices = lax.axis_size("ep")
    bits = devices.bit_length() - 1
    slots = gate_proj.shape[0]
    me = lax.axis_index("ep")
    source, _, _ = distinct_sources(old_expert, new_expert)

    def move(weights):
        chosen = jnp.take(weights, source, axis=0, mode="clip")
        return lax.all_to_all(chosen, "ep", 0, 0, tiled=True)

    gate_slab = move(gate_proj).reshape(-1, gate_proj.shape[-1])
    up_slab = move(up_proj).reshape(-1, up_proj.shape[-1])
    down = move(down_proj)
    order = range(bits - 1, -1, -1)
    rows = gather_bits(tokens, bits, order).reshape(-1, tokens.shape[1])
    rows = lax.all_gather(rows, "et", axis=1, tiled=True)
    share = gather_bits(share_of_slots(slot_ids, gate_weights, slots), bits, order)
    share = lax.dynamic_index_in_dim(share, me, bits, keepdims=False).reshape(-1, 1)
    gate_part = jnp.dot(rows, gate_slab, preferred_element_type=jnp.float32)
    up_part = jnp.dot(rows, up_slab, preferred_element_type=jnp.float32)
    hidden = (jax.nn.silu(gate_part) * up_part * share).astype(jnp.bfloat16)
    hidden = lax.all_gather(hidden, "et", axis=1, tiled=True)
    down = lax.all_to_all(down, "et", 0, 2, tiled=True)
    value = lax.dot_general(
        hidden,
        down.reshape(-1, down.shape[-1]),
        (((1,), (1,)), ((), ())),
        preferred_element_type=jnp.float32,
    )
    value = value.reshape((2,) * bits + (-1,) + value.shape[1:])
    arrived = swap(take_half(value, 0, 1).astype(jnp.bfloat16), 0)
    left = list(range(1, bits))
    keep, arrived = sum_stages(take_half(value, 0, 0), arrived, left, left)
    return (keep + arrived.astype(jnp.float32)).astype(jnp.bfloat16)


def per_device(tokens, slot_ids, gate_weights, old_expert, new_expert, gate_proj, up_proj, down_proj):
    slots, depth, width = gate_proj.shape
    count = slots - slots // 8
    devices = lax.axis_size("ep")
    fits = (
        lax.axis_size("et") == 2
        and depth == 224
        and width % LANES == 0
        and count * width == devices * 7 * HALF
        and devices == 16
        and tokens.shape[0] == LANES
    )
    layer = packed_layer if fits else plain_layer
    return layer(
        tokens, slot_ids, gate_weights, old_expert, new_expert, gate_proj, up_proj, down_proj
    )


def solution(mesh):
    placed = (
        P("ep", "et"),
        P("ep", None),
        P("ep", None),
        P(),
        P(),
        P(None, "ep", "et"),
        P(None, "ep", "et"),
        P(None, "ep", "et"),
    )
    return jax.shard_map(
        per_device, mesh=mesh, in_specs=placed, out_specs=P("ep", "et"), check_vma=False
    )
```

```python
import functools

import jax
import jax.numpy as jnp
from jax import lax
from jax.experimental import pallas as pl
from jax.experimental.pallas import tpu as pltpu
from jax.sharding import PartitionSpec as P

LANES = 128
HALF = 64
MIB = 1 << 20


def distinct_sources(old_expert, new_expert):
    slots = old_expert.shape[0]
    index = jnp.arange(slots, dtype=jnp.int32)
    holders = new_expert[:, None] == old_expert[None, :]
    source = jnp.min(jnp.where(holders, index[None, :], slots), axis=1)
    used = jnp.any(source[:, None] == index[None, :], axis=0)
    earlier = (index[None, :] < index[:, None]) & used[None, :]
    place = jnp.sum(earlier.astype(jnp.int32), axis=1)
    count = slots - slots // 8
    wanted = jnp.arange(count, dtype=jnp.int32)
    listing = jnp.sum(
        jnp.where(used[None, :] & (place[None, :] == wanted[:, None]), index[None, :], 0), axis=1
    )
    slot_place = jnp.sum(jnp.where(source[:, None] == index[None, :], place[None, :], 0), axis=1)
    return source, listing, slot_place


def units_of(dest):
    if dest % 2 == 0:
        start = 7 * dest // 2
        return start, start + 3, 0
    start = (7 * dest + 1) // 2
    return start, start - 1, 1


def pack_rows(slab_of, out_ref, base, dest, lo, rows, per_slab):
    first, half, side = units_of(dest)
    for number in range(3):
        unit = first + number
        ref, slab = slab_of(unit // per_slab)
        lane = (unit % per_slab) * LANES
        out_ref[dest, base + number * rows : base + (number + 1) * rows, :] = ref[
            slab, lo : lo + rows, lane : lane + LANES
        ]
    ref, slab = slab_of(half // per_slab)
    lane = (half % per_slab) * LANES
    mid = rows // 2
    top = ref[slab, lo : lo + mid, lane : lane + LANES].astype(jnp.float32)
    low = ref[slab, lo + mid : lo + rows, lane : lane + LANES].astype(jnp.float32)
    left = lax.broadcasted_iota(jnp.int32, (mid, LANES), 1) < HALF
    if side == 0:
        both = jnp.where(left, top, pltpu.roll(low, HALF, 1))
    else:
        both = jnp.where(left, pltpu.roll(top, HALF, 1), low)
    out_ref[dest, base + 3 * rows : base + 3 * rows + mid, :] = both.astype(out_ref.dtype)


def pack_gate_kernel(list_ref, gate_ref, share_ref, out_ref):
    slots, depth, width = gate_ref.shape
    size = depth * 7 // 2
    row = lax.broadcasted_iota(jnp.int32, share_ref.shape[1:], 0) // 4
    for dest in range(out_ref.shape[0]):
        pack_rows(
            lambda place: (gate_ref, list_ref[place]),
            out_ref, 0, dest, 0, depth, width // LANES,
        )
        value = share_ref[dest]
        high = value.astype(out_ref.dtype)
        rest = value - high.astype(jnp.float32)
        middle = rest.astype(out_ref.dtype)
        low = (rest - middle.astype(jnp.float32)).astype(out_ref.dtype)
        terms = jnp.where(
            row == 0,
            high.astype(jnp.float32),
            jnp.where(
                row == 1,
                middle.astype(jnp.float32),
                jnp.where(row == 2, low.astype(jnp.float32), 0.0),
            ),
        )
        out_ref[dest, size:, :] = terms.astype(out_ref.dtype)


def pack_up_kernel(rows, list_ref, up_ref, down_ref, out_ref):
    slots, depth, width = up_ref.shape
    for dest in range(out_ref.shape[0]):
        pack_rows(
            lambda place: (up_ref, list_ref[place]),
            out_ref, 0, dest, 0, depth, width // LANES,
        )
        pack_rows(
            lambda place: (down_ref, list_ref[place]),
            out_ref, depth * 7 // 2, dest, 0, rows, width // LANES,
        )


def pack_rest_kernel(rows, list_ref, down_ref, out_ref):
    slots, depth, width = down_ref.shape
    for dest in range(out_ref.shape[0]):
        pack_rows(
            lambda place: (down_ref, list_ref[place]),
            out_ref, 0, dest, rows, depth - rows, width // LANES,
        )


def vmem():
    return pl.BlockSpec(memory_space=pltpu.VMEM)


def smem():
    return pl.BlockSpec(memory_space=pltpu.SMEM)


def pack_gate(listing, gate_proj, share, dests):
    slots, depth, width = gate_proj.shape
    shape = (dests, depth * 7 // 2 + share.shape[1], LANES)
    return pl.pallas_call(
        pack_gate_kernel,
        out_shape=jax.ShapeDtypeStruct(shape, gate_proj.dtype),
        in_specs=[smem(), vmem(), vmem()],
        out_specs=vmem(),
        compiler_params=pltpu.CompilerParams(vmem_limit_bytes=32 * MIB),
        name="pack_gate",
    )(listing, gate_proj, share)


def pack_up(listing, up_proj, down_proj, rows, dests):
    slots, depth, width = up_proj.shape
    shape = (dests, (depth + rows) * 7 // 2, LANES)
    return pl.pallas_call(
        functools.partial(pack_up_kernel, rows),
        out_shape=jax.ShapeDtypeStruct(shape, up_proj.dtype),
        in_specs=[smem(), vmem(), vmem()],
        out_specs=vmem(),
        compiler_params=pltpu.CompilerParams(vmem_limit_bytes=40 * MIB),
        name="pack_up",
    )(listing, up_proj, down_proj)


def pack_rest(listing, down_proj, rows, dests):
    slots, depth, width = down_proj.shape
    shape = (dests, (depth - rows) * 7 // 2, LANES)
    return pl.pallas_call(
        functools.partial(pack_rest_kernel, rows),
        out_shape=jax.ShapeDtypeStruct(shape, down_proj.dtype),
        in_specs=[smem(), vmem()],
        out_specs=vmem(),
        compiler_params=pltpu.CompilerParams(vmem_limit_bytes=32 * MIB),
        name="pack_rest",
    )(listing, down_proj)


def unpack_rows(in_ref, at, base, rows, out_ref, out_row, out_lane):
    for number in range(3):
        out_ref[out_row : out_row + rows, out_lane + number * LANES : out_lane + (number + 1) * LANES] = (
            in_ref[at, base + number * rows : base + (number + 1) * rows, :]
        )
    mid = rows // 2
    both = in_ref[at, base + 3 * rows : base + 3 * rows + mid, :]
    lanes = slice(out_lane + 3 * LANES, out_lane + 4 * LANES)
    out_ref[out_row : out_row + mid, lanes] = both
    out_ref[out_row + mid : out_row + rows, lanes] = pltpu.roll(
        both.astype(jnp.float32), HALF, 1
    ).astype(out_ref.dtype)


def input_product(at_ref, pieces, packed_ref, weights, rows):
    sources = packed_ref.shape[0]
    depth = weights.shape[0] // sources
    group = sources // 2
    tile = pl.program_id(0)
    x, y = tile // 4, tile // 2 % 2

    @pl.when(tile == 0)
    def _():
        for at in range(sources):
            place = (at_ref[1] + at // group) % 2 * group + at % group
            unpack_rows(packed_ref, place, 0, depth, weights, at * depth, 0)

    mid = pieces[0].shape[1]
    for number in range(4):
        lanes = slice(number * mid, (number + 1) * mid)
        coordinate = (x, y)[number % 2]
        for value in range(2):

            @pl.when(coordinate == value)
            def _():
                rows[:, lanes] = pieces[2 * number + value][...]

    return jnp.dot(rows[...], weights[...], preferred_element_type=jnp.float32)


def gate_kernel(at_ref, *refs):
    pieces, (packed_ref, out_ref, weights, rows) = refs[:8], refs[8:]
    out_ref[...] = input_product(at_ref, pieces, packed_ref, weights, rows)


def hidden_kernel(at_ref, *refs):
    pieces, (packed_ref, gate_ref, terms_ref, out_ref, weights, rows) = refs[:8], refs[8:]
    up = input_product(at_ref, pieces, packed_ref, weights, rows)
    gate = gate_ref[...]
    value = gate / (1.0 + jnp.exp(-gate)) * up

    tile = pl.program_id(0)
    x, y, zl = tile // 4, tile // 2 % 2, tile % 2
    wide = gate.shape[1]
    term = lax.broadcasted_iota(jnp.int32, (16, wide), 0)
    lane = lax.broadcasted_iota(jnp.int32, (16, wide), 1)
    chosen = (term % 4 == lane // LANES) & (term < 12) & (lane < wide - HALF)
    chosen = jnp.where(chosen, 1.0, 0.0).astype(jnp.bfloat16)
    block = rows.shape[0] // 2
    for zh in range(2):
        source = at_ref[0] ^ (x + 2 * y + 4 * zl + 8 * zh)
        weight = lax.dot_general(
            terms_ref[source], chosen, (((0,), (0,)), ((), ())), preferred_element_type=jnp.float32
        )
        span = slice(zh * block, (zh + 1) * block)
        out_ref[span, :] = (value[span, :] * weight).astype(out_ref.dtype)


def input_call(kernel, at, pieces, packed, more, dtype, name):
    total = 2 * pieces[0].shape[0]
    mid = pieces[0].shape[1]
    tile = total // 8
    wide = 4 * LANES
    model = 4 * mid
    by_x = [lambda i: (jnp.minimum(i, 3), 0), lambda i: (jnp.maximum(i - 4, 0), 0)]
    by_y = [
        lambda i: (i // 4 * 2 + jnp.where(i // 2 % 2 == 0, i % 2, 1), 0),
        lambda i: (i // 4 * 2 + jnp.where(i // 2 % 2 == 1, i % 2, 0), 0),
    ]
    maps = (by_x + by_y) * 2
    tokens_spec = pl.BlockSpec((tile, wide), lambda i: (i, 0))
    return pl.pallas_call(
        kernel,
        grid=(8,),
        out_shape=jax.ShapeDtypeStruct((total, wide), dtype),
        in_specs=[smem()]
        + [pl.BlockSpec((tile, mid), where) for where in maps]
        + [vmem()]
        + [tokens_spec, vmem()][: len(more)],
        out_specs=tokens_spec,
        scratch_shapes=[
            pltpu.VMEM((model, wide), packed.dtype),
            pltpu.VMEM((tile, model), packed.dtype),
        ],
        compiler_params=pltpu.CompilerParams(vmem_limit_bytes=56 * MIB),
        cost_estimate=pl.CostEstimate(
            flops=2 * total * model * wide,
            bytes_accessed=20 * MIB,
            transcendentals=total * wide * len(more) // 2,
        ),
        name=name,
    )(at, *pieces, packed, *more)


THIRDS = ((0, 1, 2), (1, 2, 0), (2, 0, 1))


def group_spans(features, count):
    tiles = features // LANES
    cuts = [-(-tiles * at // count) * LANES for at in range(count + 1)]
    return [slice(lo, hi) for lo, hi in zip(cuts, cuts[1:])]


def stage_axis(order, stage):
    return sum(1 for bit in order[stage:] if bit < order[stage])


def half_spans(rows, axis, side):
    size = rows >> (axis + 1)
    return [slice((2 * at + side) * size, (2 * at + side + 1) * size) for at in range(1 << axis)]


def down_kernel(rows, side, orders, own_h, other_h, own_ref, other_ref, *refs):
    out_refs, (own_w, other_w) = refs[:-2], refs[-2:]
    for in_ref, w_ref in ((own_ref, own_w), (other_ref, other_w)):
        for at in range(in_ref.shape[0]):
            unpack_rows(in_ref, at, 0, rows, w_ref, at * rows, 0)
    dims = (((1,), (1,)), ((), ()))
    for number, span in enumerate(group_spans(own_w.shape[0], len(orders))):
        done = 0
        for tokens in half_spans(own_h.shape[0], stage_axis(orders[number], 0), side):
            value = lax.dot_general(
                own_h[tokens, :], own_w[span, :], dims, preferred_element_type=jnp.float32
            ) + lax.dot_general(
                other_h[tokens, :], other_w[span, :], dims, preferred_element_type=jnp.float32
            )
            size = tokens.stop - tokens.start
            out_refs[number][done : done + size, :] = value.astype(out_refs[number].dtype)
            done += size


def down_product(own_h, other_h, own, other, rows, side, orders, dtype, name):
    sources = own.shape[0]
    total, wide = own_h.shape
    tokens = total // 2
    features = sources * rows
    shapes = [
        jax.ShapeDtypeStruct((tokens, span.stop - span.start), dtype)
        for span in group_spans(features, len(orders))
    ]
    return pl.pallas_call(
        functools.partial(down_kernel, rows, side, orders),
        out_shape=shapes,
        in_specs=[vmem()] * 4,
        out_specs=[vmem()] * len(shapes),
        scratch_shapes=[pltpu.VMEM((features, wide), own.dtype)] * 2,
        compiler_params=pltpu.CompilerParams(vmem_limit_bytes=40 * MIB),
        cost_estimate=pl.CostEstimate(
            flops=4 * tokens * wide * features, bytes_accessed=8 * MIB, transcendentals=0
        ),
        name=name,
    )(own_h, other_h, own, other)


def halve_kernel(axes, *refs):
    count = len(refs) // 4 if axes else len(refs) // 2 - 1
    out_refs = refs[2 * count :]
    lane = 0
    for number in range(count):
        keep_ref, come_ref = refs[2 * number : 2 * number + 2]
        if axes:
            send_ref, left_ref = out_refs[2 * number : 2 * number + 2]
            lanes = slice(0, keep_ref.shape[1])
        else:
            send_ref, left_ref = out_refs
            lanes = slice(lane, lane + keep_ref.shape[1])
            lane = lanes.stop
        axis = axes[number] if axes else 0
        for side, out_ref in enumerate((left_ref, send_ref)):
            done = 0
            for rows in half_spans(keep_ref.shape[0], axis, side):
                size = rows.stop - rows.start
                total = keep_ref[rows, :] + come_ref[rows, :].astype(jnp.float32)
                out_ref[done : done + size, lanes] = total.astype(out_ref.dtype)
                done += size


def halve(pairs, axes):
    sizes = [(keep.shape[0] // 2, keep.shape[1]) for keep, _ in pairs]
    if not axes:
        sizes = [(sizes[0][0], sum(width for _, width in sizes))]
    shapes = []
    for size in sizes:
        shapes += [jax.ShapeDtypeStruct(size, jnp.bfloat16), jax.ShapeDtypeStruct(size, jnp.float32)]
    out = pl.pallas_call(
        functools.partial(halve_kernel, axes),
        out_shape=shapes,
        in_specs=[vmem()] * (2 * len(pairs)),
        out_specs=[vmem()] * len(shapes),
        compiler_params=pltpu.CompilerParams(vmem_limit_bytes=40 * MIB),
        cost_estimate=pl.CostEstimate(
            flops=sum(keep.size for keep, _ in pairs), bytes_accessed=4 * MIB, transcendentals=0
        ),
        name="sum_stage",
    )(*[value for pair in pairs for value in pair])
    return [(out[2 * n], out[2 * n + 1]) for n in range(len(out) // 2)]


def swap(value, bit):
    size = lax.axis_size("ep")
    return lax.ppermute(value, "ep", [(i, i ^ (1 << bit)) for i in range(size)])


def gather_bits(value, bits, order, have=()):
    have = list(have)
    for bit in order:
        axis = sum(1 for b in have if b < bit)
        value = jnp.stack([value, swap(value, bit)], axis=axis)
        have.append(bit)
    return value


def take_half(value, axis, number):
    return lax.index_in_dim(value, number, axis, keepdims=False)


def sum_stages(keep, arrived, order, left):
    left = list(left)
    for bit in order:
        axis = left.index(bit)
        total = keep + arrived.astype(jnp.float32)
        arrived = swap(take_half(total, axis, 1).astype(jnp.bfloat16), bit)
        keep = take_half(total, axis, 0)
        left.remove(bit)
    return keep, arrived


def share_of_slots(slot_ids, gate_weights, slots):
    index = jnp.arange(slots, dtype=jnp.int32)
    picked = slot_ids.T[None, :, :] == index[:, None, None]
    return jnp.sum(jnp.where(picked, gate_weights.T[None, :, :], 0.0), axis=1)


def packed_layer(
    tokens, slot_ids, gate_weights, old_expert, new_expert, gate_proj, up_proj, down_proj
):
    devices = lax.axis_size("ep")
    slots, depth, width = gate_proj.shape
    block = tokens.shape[0]
    me = lax.axis_index("ep")
    core = lax.axis_index("et")
    group = devices // 2
    tie = lax.optimization_barrier
    _, listing, slot_place = distinct_sources(old_expert, new_expert)

    def exchange(value):
        return lax.ppermute(value, "et", [(0, 1), (1, 0)])

    def move(packed):
        return lax.all_to_all(packed, "ep", 0, 0, tiled=True)

    places = []
    for dest in range(devices):
        first, half, _ = units_of(dest)
        places.append([unit // (width // LANES) for unit in (first, first + 1, first + 2, half)] * 4)
    places = jnp.asarray(places, jnp.int32)
    share = share_of_slots(slot_ids, gate_weights, slots)
    belongs = slot_place[None, None, :, None] == places[:, :, None, None]
    share = jnp.sum(jnp.where(belongs, share[None, None], 0.0), axis=2)

    parts = (128, 96)
    at = jnp.stack([me, core]).astype(jnp.int32)
    size = depth * 7 // 2

    near, far = swap(tokens, 2), swap(tokens, 3)
    gate_packed = pack_gate(listing, gate_proj, share, devices)
    moved = move(gate_packed)
    corner = swap(far, 2)
    mid = tokens.shape[1] // 2
    three = jnp.concatenate([tokens, far, near], axis=0)
    first, second = three[:, :mid], three[:, mid:]
    first_y, second_x = swap(first, 1), swap(second, 0)
    up_packed = pack_up(listing, up_proj, down_proj, parts[0], devices)
    moved, first, second, first_y, second_x, corner, up_packed = tie(
        (moved, first, second, first_y, second_x, corner, up_packed)
    )
    gate_moved, terms = moved[:, :size], moved[:, size:]

    moved = move(up_packed)
    first_c, second_c = corner[:, :mid], corner[:, mid:]
    first_most = jnp.concatenate([first, first_c, first_y], axis=0)
    second_most = jnp.concatenate([second, second_c, second_x], axis=0)
    cross = lax.ppermute(corner, "ep", [(i, i ^ 3) for i in range(devices)])
    pieces = [
        jnp.concatenate([first_most, swap(first_c, 1)], axis=0),
        jnp.concatenate([swap(first_most, 0), cross[:, :mid]], axis=0),
        jnp.concatenate([second_most, swap(second_c, 0)], axis=0),
        jnp.concatenate([swap(second_most, 1), cross[:, mid:]], axis=0),
    ]
    pieces += [exchange(piece) for piece in pieces]
    gate = input_call(gate_kernel, at, pieces, gate_moved, (), jnp.float32, "gate")
    rest = pack_rest(listing, down_proj, parts[0], devices)
    moved, gate, rest = tie((moved, gate, rest))
    up_moved, down0 = moved[:, :size], moved[:, size:]

    down1 = move(rest)
    hidden = input_call(
        hidden_kernel, at, pieces, up_moved, (gate, terms), jnp.bfloat16, "hidden"
    )
    hidden_other = exchange(hidden)

    def products(down, rows_in, orders):
        own = lax.dynamic_slice_in_dim(down, core * group, group, 0)
        other = exchange(lax.dynamic_slice_in_dim(down, (1 - core) * group, group, 0))
        args = (hidden, hidden_other, own, other)
        sent = down_product(*args, rows_in, 1, orders, jnp.bfloat16, "down_send")
        sent, args = tie((sent, args))
        come = [swap(value, order[0]) for value, order in zip(sent, orders)]
        return down_product(*args, rows_in, 0, orders, jnp.float32, "down_keep"), come

    def stage(kept, come, number, orders):
        axes = tuple(stage_axis(order, number) for order in orders)
        out = halve(list(zip(kept, come)), axes)
        come = [swap(send, order[number]) for (send, _), order in zip(out, orders)]
        return [keep for _, keep in out], come

    def last_stage(kept, come):
        ((send, keep),) = halve(list(zip(kept, come)), None)
        come = swap(send, 3)
        return (keep + come.astype(jnp.float32)).astype(jnp.bfloat16)

    kept0, come0 = products(down0, parts[0], THIRDS)
    down1, kept0, come0 = tie((down1, kept0, come0))
    kept1, come1 = products(down1, parts[1], THIRDS)
    kept0, come0 = stage(kept0, come0, 1, THIRDS)
    kept1, come1 = stage(kept1, come1, 1, THIRDS)
    kept0, come0 = stage(kept0, come0, 2, THIRDS)
    kept1, come1 = stage(kept1, come1, 2, THIRDS)
    out = []
    for rows_in, total in zip(parts, (last_stage(kept0, come0), last_stage(kept1, come1))):
        out.append(total.reshape(block, group, rows_in))
    return jnp.concatenate(out, axis=2).reshape(tokens.shape)


def plain_layer(
    tokens, slot_ids, gate_weights, old_expert, new_expert, gate_proj, up_proj, down_proj
):
    devices = lax.axis_size("ep")
    bits = devices.bit_length() - 1
    slots = gate_proj.shape[0]
    me = lax.axis_index("ep")
    source, _, _ = distinct_sources(old_expert, new_expert)

    def move(weights):
        chosen = jnp.take(weights, source, axis=0, mode="clip")
        return lax.all_to_all(chosen, "ep", 0, 0, tiled=True)

    gate_slab = move(gate_proj).reshape(-1, gate_proj.shape[-1])
    up_slab = move(up_proj).reshape(-1, up_proj.shape[-1])
    down = move(down_proj)
    order = range(bits - 1, -1, -1)
    rows = gather_bits(tokens, bits, order).reshape(-1, tokens.shape[1])
    rows = lax.all_gather(rows, "et", axis=1, tiled=True)
    share = gather_bits(share_of_slots(slot_ids, gate_weights, slots), bits, order)
    share = lax.dynamic_index_in_dim(share, me, bits, keepdims=False).reshape(-1, 1)
    gate_part = jnp.dot(rows, gate_slab, preferred_element_type=jnp.float32)
    up_part = jnp.dot(rows, up_slab, preferred_element_type=jnp.float32)
    hidden = (jax.nn.silu(gate_part) * up_part * share).astype(jnp.bfloat16)
    hidden = lax.all_gather(hidden, "et", axis=1, tiled=True)
    down = lax.all_to_all(down, "et", 0, 2, tiled=True)
    value = lax.dot_general(
        hidden,
        down.reshape(-1, down.shape[-1]),
        (((1,), (1,)), ((), ())),
        preferred_element_type=jnp.float32,
    )
    value = value.reshape((2,) * bits + (-1,) + value.shape[1:])
    arrived = swap(take_half(value, 0, 1).astype(jnp.bfloat16), 0)
    left = list(range(1, bits))
    keep, arrived = sum_stages(take_half(value, 0, 0), arrived, left, left)
    return (keep + arrived.astype(jnp.float32)).astype(jnp.bfloat16)


def per_device(tokens, slot_ids, gate_weights, old_expert, new_expert, gate_proj, up_proj, down_proj):
    slots, depth, width = gate_proj.shape
    count = slots - slots // 8
    devices = lax.axis_size("ep")
    fits = (
        lax.axis_size("et") == 2
        and depth == 224
        and width % LANES == 0
        and count * width == devices * 7 * HALF
        and devices == 16
        and tokens.shape[0] == LANES
    )
    layer = packed_layer if fits else plain_layer
    return layer(
        tokens, slot_ids, gate_weights, old_expert, new_expert, gate_proj, up_proj, down_proj
    )


def solution(mesh):
    placed = (
        P("ep", "et"),
        P("ep", None),
        P("ep", None),
        P(),
        P(),
        P(None, "ep", "et"),
        P(None, "ep", "et"),
        P(None, "ep", "et"),
    )
    return jax.shard_map(
        per_device, mesh=mesh, in_specs=placed, out_specs=P("ep", "et"), check_vma=False
    )
```

```python
import functools

import jax
import jax.numpy as jnp
from jax import lax
from jax.experimental import pallas as pl
from jax.experimental.pallas import tpu as pltpu
from jax.sharding import PartitionSpec as P

LANES = 128
HALF = 64
MIB = 1 << 20


def distinct_sources(old_expert, new_expert):
    slots = old_expert.shape[0]
    index = jnp.arange(slots, dtype=jnp.int32)
    holders = new_expert[:, None] == old_expert[None, :]
    source = jnp.min(jnp.where(holders, index[None, :], slots), axis=1)
    used = jnp.any(source[:, None] == index[None, :], axis=0)
    earlier = (index[None, :] < index[:, None]) & used[None, :]
    place = jnp.sum(earlier.astype(jnp.int32), axis=1)
    count = slots - slots // 8
    wanted = jnp.arange(count, dtype=jnp.int32)
    listing = jnp.sum(
        jnp.where(used[None, :] & (place[None, :] == wanted[:, None]), index[None, :], 0), axis=1
    )
    slot_place = jnp.sum(jnp.where(source[:, None] == index[None, :], place[None, :], 0), axis=1)
    return source, listing, slot_place


def units_of(dest):
    if dest % 2 == 0:
        start = 7 * dest // 2
        return start, start + 3, 0
    start = (7 * dest + 1) // 2
    return start, start - 1, 1


def pack_rows(slab_of, out_ref, base, dest, lo, rows, per_slab):
    first, half, side = units_of(dest)
    for number in range(3):
        unit = first + number
        ref, slab = slab_of(unit // per_slab)
        lane = (unit % per_slab) * LANES
        out_ref[dest, base + number * rows : base + (number + 1) * rows, :] = ref[
            slab, lo : lo + rows, lane : lane + LANES
        ]
    ref, slab = slab_of(half // per_slab)
    lane = (half % per_slab) * LANES
    mid = rows // 2
    top = ref[slab, lo : lo + mid, lane : lane + LANES].astype(jnp.float32)
    low = ref[slab, lo + mid : lo + rows, lane : lane + LANES].astype(jnp.float32)
    left = lax.broadcasted_iota(jnp.int32, (mid, LANES), 1) < HALF
    if side == 0:
        both = jnp.where(left, top, pltpu.roll(low, HALF, 1))
    else:
        both = jnp.where(left, pltpu.roll(top, HALF, 1), low)
    out_ref[dest, base + 3 * rows : base + 3 * rows + mid, :] = both.astype(out_ref.dtype)


def pack_first_kernel(rows, list_ref, gate_ref, up_ref, down_ref, share_ref, out_ref):
    slots, depth, width = gate_ref.shape
    size = depth * 7 // 2
    row = lax.broadcasted_iota(jnp.int32, share_ref.shape[1:], 0) // 4
    for dest in range(out_ref.shape[0]):
        for number, in_ref in enumerate((gate_ref, up_ref)):
            pack_rows(
                lambda place, in_ref=in_ref: (in_ref, list_ref[place]),
                out_ref, number * size, dest, 0, depth, width // LANES,
            )
        pack_rows(
            lambda place: (down_ref, list_ref[place]),
            out_ref, 2 * size, dest, 0, rows, width // LANES,
        )
        value = share_ref[dest]
        high = value.astype(out_ref.dtype)
        rest = value - high.astype(jnp.float32)
        middle = rest.astype(out_ref.dtype)
        low = (rest - middle.astype(jnp.float32)).astype(out_ref.dtype)
        terms = jnp.where(
            row == 0,
            high.astype(jnp.float32),
            jnp.where(
                row == 1,
                middle.astype(jnp.float32),
                jnp.where(row == 2, low.astype(jnp.float32), 0.0),
            ),
        )
        out_ref[dest, 2 * size + rows * 7 // 2 :, :] = terms.astype(out_ref.dtype)


def pack_rest_kernel(rows, list_ref, down_ref, out_ref):
    slots, depth, width = down_ref.shape
    for dest in range(out_ref.shape[0]):
        pack_rows(
            lambda place: (down_ref, list_ref[place]),
            out_ref, 0, dest, rows, depth - rows, width // LANES,
        )


def vmem():
    return pl.BlockSpec(memory_space=pltpu.VMEM)


def smem():
    return pl.BlockSpec(memory_space=pltpu.SMEM)


def pack_first(listing, gate_proj, up_proj, down_proj, rows, share, dests):
    slots, depth, width = gate_proj.shape
    shape = (dests, depth * 7 + rows * 7 // 2 + share.shape[1], LANES)
    return pl.pallas_call(
        functools.partial(pack_first_kernel, rows),
        out_shape=jax.ShapeDtypeStruct(shape, gate_proj.dtype),
        in_specs=[smem(), vmem(), vmem(), vmem(), vmem()],
        out_specs=vmem(),
        compiler_params=pltpu.CompilerParams(vmem_limit_bytes=40 * MIB),
        name="pack_first",
    )(listing, gate_proj, up_proj, down_proj, share)


def pack_rest(listing, down_proj, rows, dests):
    slots, depth, width = down_proj.shape
    shape = (dests, (depth - rows) * 7 // 2, LANES)
    return pl.pallas_call(
        functools.partial(pack_rest_kernel, rows),
        out_shape=jax.ShapeDtypeStruct(shape, down_proj.dtype),
        in_specs=[smem(), vmem()],
        out_specs=vmem(),
        compiler_params=pltpu.CompilerParams(vmem_limit_bytes=32 * MIB),
        name="pack_rest",
    )(listing, down_proj)


def unpack_rows(in_ref, at, base, rows, out_ref, out_row, out_lane):
    for number in range(3):
        out_ref[out_row : out_row + rows, out_lane + number * LANES : out_lane + (number + 1) * LANES] = (
            in_ref[at, base + number * rows : base + (number + 1) * rows, :]
        )
    mid = rows // 2
    both = in_ref[at, base + 3 * rows : base + 3 * rows + mid, :]
    lanes = slice(out_lane + 3 * LANES, out_lane + 4 * LANES)
    out_ref[out_row : out_row + mid, lanes] = both
    out_ref[out_row + mid : out_row + rows, lanes] = pltpu.roll(
        both.astype(jnp.float32), HALF, 1
    ).astype(out_ref.dtype)


def hidden_kernel(at_ref, *refs):
    pieces, (packed_ref, out_ref, gate_w, up_w, rows) = refs[:8], refs[8:]
    sources = packed_ref.shape[0]
    depth = gate_w.shape[0] // sources
    size = depth * 7 // 2
    group = sources // 2
    tile = pl.program_id(0)
    x, y = tile // 2, tile % 2
    me, core = at_ref[0], at_ref[1]

    @pl.when(tile == 0)
    def _():
        for at in range(sources):
            place = (core + at // group) % 2 * group + at % group
            unpack_rows(packed_ref, place, 0, depth, gate_w, at * depth, 0)
            unpack_rows(packed_ref, place, size, depth, up_w, at * depth, 0)

    mid = pieces[0].shape[1]
    for number in range(4):
        lanes = slice(number * mid, (number + 1) * mid)
        coordinate = (x, y)[number % 2]
        for value in range(2):

            @pl.when(coordinate == value)
            def _():
                rows[:, lanes] = pieces[2 * number + value][...]

    gate = jnp.dot(rows[...], gate_w[...], preferred_element_type=jnp.float32)
    up = jnp.dot(rows[...], up_w[...], preferred_element_type=jnp.float32)
    value = gate / (1.0 + jnp.exp(-gate)) * up

    wide = gate.shape[1]
    term = lax.broadcasted_iota(jnp.int32, (16, wide), 0)
    lane = lax.broadcasted_iota(jnp.int32, (16, wide), 1)
    chosen = (term % 4 == lane // LANES) & (term < 12) & (lane < wide - HALF)
    chosen = jnp.where(chosen, 1.0, 0.0).astype(jnp.bfloat16)
    block = rows.shape[0] // 4
    for at in range(4):
        source = me ^ (x + 2 * y + 4 * (at // 2) + 8 * (at % 2))
        weight = lax.dot_general(
            packed_ref[source, packed_ref.shape[1] - 16 :, :],
            chosen,
            (((0,), (0,)), ((), ())),
            preferred_element_type=jnp.float32,
        )
        span = slice(at * block, (at + 1) * block)
        out_ref[span, :] = (value[span, :] * weight).astype(out_ref.dtype)


def hidden_units(at, pieces, packed):
    total = 2 * pieces[0].shape[0]
    mid = pieces[0].shape[1]
    tile = total // 4
    wide = 4 * LANES
    model = 4 * mid
    by_x = [lambda i: (jnp.minimum(i, 1), 0), lambda i: (jnp.maximum(i - 2, 0), 0)]
    by_y = [lambda i: (i // 2, 0)] * 2
    maps = (by_x + by_y) * 2
    return pl.pallas_call(
        hidden_kernel,
        grid=(4,),
        out_shape=jax.ShapeDtypeStruct((total, wide), packed.dtype),
        in_specs=[smem()]
        + [pl.BlockSpec((tile, mid), where) for where in maps]
        + [vmem()],
        out_specs=pl.BlockSpec((tile, wide), lambda i: (i, 0)),
        scratch_shapes=[pltpu.VMEM((model, wide), packed.dtype)] * 2
        + [pltpu.VMEM((tile, model), packed.dtype)],
        compiler_params=pltpu.CompilerParams(vmem_limit_bytes=56 * MIB),
        cost_estimate=pl.CostEstimate(
            flops=4 * total * model * wide, bytes_accessed=24 * MIB, transcendentals=total * wide
        ),
        name="hidden",
    )(at, *pieces, packed)


THIRDS = ((0, 1, 2), (1, 2, 0), (2, 0, 1))


def group_spans(features, count):
    tiles = features // LANES
    cuts = [-(-tiles * at // count) * LANES for at in range(count + 1)]
    return [slice(lo, hi) for lo, hi in zip(cuts, cuts[1:])]


def stage_axis(order, stage):
    return sum(1 for bit in order[stage:] if bit < order[stage])


def half_spans(rows, axis, side):
    size = rows >> (axis + 1)
    return [slice((2 * at + side) * size, (2 * at + side + 1) * size) for at in range(1 << axis)]


def down_kernel(rows, side, orders, own_h, other_h, own_ref, other_ref, *refs):
    out_refs, (own_w, other_w) = refs[:-2], refs[-2:]
    for in_ref, w_ref in ((own_ref, own_w), (other_ref, other_w)):
        for at in range(in_ref.shape[0]):
            unpack_rows(in_ref, at, 0, rows, w_ref, at * rows, 0)
    dims = (((1,), (1,)), ((), ()))
    for number, span in enumerate(group_spans(own_w.shape[0], len(orders))):
        done = 0
        for tokens in half_spans(own_h.shape[0], stage_axis(orders[number], 0), side):
            value = lax.dot_general(
                own_h[tokens, :], own_w[span, :], dims, preferred_element_type=jnp.float32
            ) + lax.dot_general(
                other_h[tokens, :], other_w[span, :], dims, preferred_element_type=jnp.float32
            )
            size = tokens.stop - tokens.start
            out_refs[number][done : done + size, :] = value.astype(out_refs[number].dtype)
            done += size


def down_product(own_h, other_h, own, other, rows, side, orders, dtype, name):
    sources = own.shape[0]
    total, wide = own_h.shape
    tokens = total // 2
    features = sources * rows
    shapes = [
        jax.ShapeDtypeStruct((tokens, span.stop - span.start), dtype)
        for span in group_spans(features, len(orders))
    ]
    return pl.pallas_call(
        functools.partial(down_kernel, rows, side, orders),
        out_shape=shapes,
        in_specs=[vmem()] * 4,
        out_specs=[vmem()] * len(shapes),
        scratch_shapes=[pltpu.VMEM((features, wide), own.dtype)] * 2,
        compiler_params=pltpu.CompilerParams(vmem_limit_bytes=40 * MIB),
        cost_estimate=pl.CostEstimate(
            flops=4 * tokens * wide * features, bytes_accessed=8 * MIB, transcendentals=0
        ),
        name=name,
    )(own_h, other_h, own, other)


def halve_kernel(axes, *refs):
    count = len(refs) // 4 if axes else len(refs) // 2 - 1
    out_refs = refs[2 * count :]
    lane = 0
    for number in range(count):
        keep_ref, come_ref = refs[2 * number : 2 * number + 2]
        if axes:
            send_ref, left_ref = out_refs[2 * number : 2 * number + 2]
            lanes = slice(0, keep_ref.shape[1])
        else:
            send_ref, left_ref = out_refs
            lanes = slice(lane, lane + keep_ref.shape[1])
            lane = lanes.stop
        axis = axes[number] if axes else 0
        for side, out_ref in enumerate((left_ref, send_ref)):
            done = 0
            for rows in half_spans(keep_ref.shape[0], axis, side):
                size = rows.stop - rows.start
                total = keep_ref[rows, :] + come_ref[rows, :].astype(jnp.float32)
                out_ref[done : done + size, lanes] = total.astype(out_ref.dtype)
                done += size


def halve(pairs, axes):
    sizes = [(keep.shape[0] // 2, keep.shape[1]) for keep, _ in pairs]
    if not axes:
        sizes = [(sizes[0][0], sum(width for _, width in sizes))]
    shapes = []
    for size in sizes:
        shapes += [jax.ShapeDtypeStruct(size, jnp.bfloat16), jax.ShapeDtypeStruct(size, jnp.float32)]
    out = pl.pallas_call(
        functools.partial(halve_kernel, axes),
        out_shape=shapes,
        in_specs=[vmem()] * (2 * len(pairs)),
        out_specs=[vmem()] * len(shapes),
        compiler_params=pltpu.CompilerParams(vmem_limit_bytes=40 * MIB),
        cost_estimate=pl.CostEstimate(
            flops=sum(keep.size for keep, _ in pairs), bytes_accessed=4 * MIB, transcendentals=0
        ),
        name="sum_stage",
    )(*[value for pair in pairs for value in pair])
    return [(out[2 * n], out[2 * n + 1]) for n in range(len(out) // 2)]


def swap(value, bit):
    size = lax.axis_size("ep")
    return lax.ppermute(value, "ep", [(i, i ^ (1 << bit)) for i in range(size)])


def gather_bits(value, bits, order, have=()):
    have = list(have)
    for bit in order:
        axis = sum(1 for b in have if b < bit)
        value = jnp.stack([value, swap(value, bit)], axis=axis)
        have.append(bit)
    return value


def take_half(value, axis, number):
    return lax.index_in_dim(value, number, axis, keepdims=False)


def sum_stages(keep, arrived, order, left):
    left = list(left)
    for bit in order:
        axis = left.index(bit)
        total = keep + arrived.astype(jnp.float32)
        arrived = swap(take_half(total, axis, 1).astype(jnp.bfloat16), bit)
        keep = take_half(total, axis, 0)
        left.remove(bit)
    return keep, arrived


def share_of_slots(slot_ids, gate_weights, slots):
    index = jnp.arange(slots, dtype=jnp.int32)
    picked = slot_ids.T[None, :, :] == index[:, None, None]
    return jnp.sum(jnp.where(picked, gate_weights.T[None, :, :], 0.0), axis=1)


def packed_layer(
    tokens, slot_ids, gate_weights, old_expert, new_expert, gate_proj, up_proj, down_proj
):
    devices = lax.axis_size("ep")
    slots, depth, width = gate_proj.shape
    block = tokens.shape[0]
    me = lax.axis_index("ep")
    core = lax.axis_index("et")
    group = devices // 2
    tie = lax.optimization_barrier
    _, listing, slot_place = distinct_sources(old_expert, new_expert)

    def exchange(value):
        return lax.ppermute(value, "et", [(0, 1), (1, 0)])

    def move(packed):
        return lax.all_to_all(packed, "ep", 0, 0, tiled=True)

    places = []
    for dest in range(devices):
        first, half, _ = units_of(dest)
        places.append([unit // (width // LANES) for unit in (first, first + 1, first + 2, half)] * 4)
    places = jnp.asarray(places, jnp.int32)
    share = share_of_slots(slot_ids, gate_weights, slots)
    belongs = slot_place[None, None, :, None] == places[:, :, None, None]
    share = jnp.sum(jnp.where(belongs, share[None, None], 0.0), axis=2)

    near, far = swap(tokens, 2), swap(tokens, 3)
    corner = swap(far, 2)
    parts = (96, 128)
    packed = pack_first(listing, gate_proj, up_proj, down_proj, parts[0], share, devices)
    packed, near, far, corner = tie((packed, near, far, corner))

    moved = move(packed)
    mid = tokens.shape[1] // 2
    rows = jnp.concatenate([tokens, far, near, corner], axis=0)
    first, second = rows[:, :mid], rows[:, mid:]
    first = jnp.concatenate([first, swap(first, 1)], axis=0)
    second = jnp.concatenate([second, swap(second, 0)], axis=0)
    pieces = [first, swap(first, 0), second, swap(second, 1)]
    others = [exchange(piece) for piece in pieces]
    rest = pack_rest(listing, down_proj, parts[0], devices)
    moved, rest = tie((moved, rest))

    down1 = move(rest)
    at = jnp.stack([me, core]).astype(jnp.int32)
    hidden = hidden_units(at, pieces + others, moved)
    hidden_other = exchange(hidden)
    down0 = moved[:, depth * 7 : depth * 7 + parts[0] * 7 // 2]

    def products(down, rows_in, orders):
        own = lax.dynamic_slice_in_dim(down, core * group, group, 0)
        other = exchange(lax.dynamic_slice_in_dim(down, (1 - core) * group, group, 0))
        args = (hidden, hidden_other, own, other)
        sent = down_product(*args, rows_in, 1, orders, jnp.bfloat16, "down_send")
        sent, args = tie((sent, args))
        come = [swap(value, order[0]) for value, order in zip(sent, orders)]
        return down_product(*args, rows_in, 0, orders, jnp.float32, "down_keep"), come

    def stage(kept, come, number, orders):
        axes = tuple(stage_axis(order, number) for order in orders)
        out = halve(list(zip(kept, come)), axes)
        come = [swap(send, order[number]) for (send, _), order in zip(out, orders)]
        return [keep for _, keep in out], come

    def last_stage(kept, come):
        ((send, keep),) = halve(list(zip(kept, come)), None)
        come = swap(send, 3)
        return (keep + come.astype(jnp.float32)).astype(jnp.bfloat16)

    kept0, come0 = products(down0, parts[0], THIRDS)
    down1, kept0, come0[:2] = tie((down1, kept0, come0[:2]))
    kept1, come1 = products(down1, parts[1], THIRDS)
    kept0, come0 = stage(kept0, come0, 1, THIRDS)
    kept1, come1 = stage(kept1, come1, 1, THIRDS)
    kept0, come0 = stage(kept0, come0, 2, THIRDS)
    kept1, come1 = stage(kept1, come1, 2, THIRDS)
    out = []
    for rows_in, total in zip(parts, (last_stage(kept0, come0), last_stage(kept1, come1))):
        out.append(total.reshape(block, group, rows_in))
    return jnp.concatenate(out, axis=2).reshape(tokens.shape)


def plain_layer(
    tokens, slot_ids, gate_weights, old_expert, new_expert, gate_proj, up_proj, down_proj
):
    devices = lax.axis_size("ep")
    bits = devices.bit_length() - 1
    slots = gate_proj.shape[0]
    me = lax.axis_index("ep")
    source, _, _ = distinct_sources(old_expert, new_expert)

    def move(weights):
        chosen = jnp.take(weights, source, axis=0, mode="clip")
        return lax.all_to_all(chosen, "ep", 0, 0, tiled=True)

    gate_slab = move(gate_proj).reshape(-1, gate_proj.shape[-1])
    up_slab = move(up_proj).reshape(-1, up_proj.shape[-1])
    down = move(down_proj)
    order = range(bits - 1, -1, -1)
    rows = gather_bits(tokens, bits, order).reshape(-1, tokens.shape[1])
    rows = lax.all_gather(rows, "et", axis=1, tiled=True)
    share = gather_bits(share_of_slots(slot_ids, gate_weights, slots), bits, order)
    share = lax.dynamic_index_in_dim(share, me, bits, keepdims=False).reshape(-1, 1)
    gate_part = jnp.dot(rows, gate_slab, preferred_element_type=jnp.float32)
    up_part = jnp.dot(rows, up_slab, preferred_element_type=jnp.float32)
    hidden = (jax.nn.silu(gate_part) * up_part * share).astype(jnp.bfloat16)
    hidden = lax.all_gather(hidden, "et", axis=1, tiled=True)
    down = lax.all_to_all(down, "et", 0, 2, tiled=True)
    value = lax.dot_general(
        hidden,
        down.reshape(-1, down.shape[-1]),
        (((1,), (1,)), ((), ())),
        preferred_element_type=jnp.float32,
    )
    value = value.reshape((2,) * bits + (-1,) + value.shape[1:])
    arrived = swap(take_half(value, 0, 1).astype(jnp.bfloat16), 0)
    left = list(range(1, bits))
    keep, arrived = sum_stages(take_half(value, 0, 0), arrived, left, left)
    return (keep + arrived.astype(jnp.float32)).astype(jnp.bfloat16)


def per_device(tokens, slot_ids, gate_weights, old_expert, new_expert, gate_proj, up_proj, down_proj):
    slots, depth, width = gate_proj.shape
    count = slots - slots // 8
    devices = lax.axis_size("ep")
    fits = (
        lax.axis_size("et") == 2
        and depth == 224
        and width % LANES == 0
        and count * width == devices * 7 * HALF
        and devices == 16
        and tokens.shape[0] == LANES
    )
    layer = packed_layer if fits else plain_layer
    return layer(
        tokens, slot_ids, gate_weights, old_expert, new_expert, gate_proj, up_proj, down_proj
    )


def solution(mesh):
    placed = (
        P("ep", "et"),
        P("ep", None),
        P("ep", None),
        P(),
        P(),
        P(None, "ep", "et"),
        P(None, "ep", "et"),
        P(None, "ep", "et"),
    )
    return jax.shard_map(
        per_device, mesh=mesh, in_specs=placed, out_specs=P("ep", "et"), check_vma=False
    )
```

```python
import functools

import jax
import jax.numpy as jnp
from jax import lax
from jax.experimental import pallas as pl
from jax.experimental.pallas import tpu as pltpu
from jax.sharding import PartitionSpec as P

LANES = 128
HALF = 64
MIB = 1 << 20


def distinct_sources(old_expert, new_expert):
    slots = old_expert.shape[0]
    index = jnp.arange(slots, dtype=jnp.int32)
    holders = new_expert[:, None] == old_expert[None, :]
    source = jnp.min(jnp.where(holders, index[None, :], slots), axis=1)
    used = jnp.any(source[:, None] == index[None, :], axis=0)
    earlier = (index[None, :] < index[:, None]) & used[None, :]
    place = jnp.sum(earlier.astype(jnp.int32), axis=1)
    count = slots - slots // 8
    wanted = jnp.arange(count, dtype=jnp.int32)
    listing = jnp.sum(
        jnp.where(used[None, :] & (place[None, :] == wanted[:, None]), index[None, :], 0), axis=1
    )
    slot_place = jnp.sum(jnp.where(source[:, None] == index[None, :], place[None, :], 0), axis=1)
    return source, listing, slot_place


def units_of(dest):
    if dest % 2 == 0:
        start = 7 * dest // 2
        return start, start + 3, 0
    start = (7 * dest + 1) // 2
    return start, start - 1, 1


def pack_rows(slab_of, out_ref, base, dest, lo, rows, per_slab):
    first, half, side = units_of(dest)
    for number in range(3):
        unit = first + number
        ref, slab = slab_of(unit // per_slab)
        lane = (unit % per_slab) * LANES
        out_ref[dest, base + number * rows : base + (number + 1) * rows, :] = ref[
            slab, lo : lo + rows, lane : lane + LANES
        ]
    ref, slab = slab_of(half // per_slab)
    lane = (half % per_slab) * LANES
    mid = rows // 2
    top = ref[slab, lo : lo + mid, lane : lane + LANES].astype(jnp.float32)
    low = ref[slab, lo + mid : lo + rows, lane : lane + LANES].astype(jnp.float32)
    left = lax.broadcasted_iota(jnp.int32, (mid, LANES), 1) < HALF
    if side == 0:
        both = jnp.where(left, top, pltpu.roll(low, HALF, 1))
    else:
        both = jnp.where(left, pltpu.roll(top, HALF, 1), low)
    out_ref[dest, base + 3 * rows : base + 3 * rows + mid, :] = both.astype(out_ref.dtype)


def pack_first_kernel(rows, list_ref, gate_ref, up_ref, down_ref, share_ref, out_ref):
    slots, depth, width = gate_ref.shape
    size = depth * 7 // 2
    row = lax.broadcasted_iota(jnp.int32, share_ref.shape[1:], 0) // 4
    for dest in range(out_ref.shape[0]):
        for number, in_ref in enumerate((gate_ref, up_ref)):
            pack_rows(
                lambda place, in_ref=in_ref: (in_ref, list_ref[place]),
                out_ref, number * size, dest, 0, depth, width // LANES,
            )
        pack_rows(
            lambda place: (down_ref, list_ref[place]),
            out_ref, 2 * size, dest, 0, rows, width // LANES,
        )
        value = share_ref[dest]
        high = value.astype(out_ref.dtype)
        rest = value - high.astype(jnp.float32)
        middle = rest.astype(out_ref.dtype)
        low = (rest - middle.astype(jnp.float32)).astype(out_ref.dtype)
        terms = jnp.where(
            row == 0,
            high.astype(jnp.float32),
            jnp.where(
                row == 1,
                middle.astype(jnp.float32),
                jnp.where(row == 2, low.astype(jnp.float32), 0.0),
            ),
        )
        out_ref[dest, 2 * size + rows * 7 // 2 :, :] = terms.astype(out_ref.dtype)


def pack_rest_kernel(rows, list_ref, down_ref, out_ref):
    slots, depth, width = down_ref.shape
    for dest in range(out_ref.shape[0]):
        pack_rows(
            lambda place: (down_ref, list_ref[place]),
            out_ref, 0, dest, rows, depth - rows, width // LANES,
        )


def vmem():
    return pl.BlockSpec(memory_space=pltpu.VMEM)


def smem():
    return pl.BlockSpec(memory_space=pltpu.SMEM)


def pack_first(listing, gate_proj, up_proj, down_proj, rows, share, dests):
    slots, depth, width = gate_proj.shape
    shape = (dests, depth * 7 + rows * 7 // 2 + share.shape[1], LANES)
    return pl.pallas_call(
        functools.partial(pack_first_kernel, rows),
        out_shape=jax.ShapeDtypeStruct(shape, gate_proj.dtype),
        in_specs=[smem(), vmem(), vmem(), vmem(), vmem()],
        out_specs=vmem(),
        compiler_params=pltpu.CompilerParams(vmem_limit_bytes=40 * MIB),
        name="pack_first",
    )(listing, gate_proj, up_proj, down_proj, share)


def pack_rest(listing, down_proj, rows, dests):
    slots, depth, width = down_proj.shape
    shape = (dests, (depth - rows) * 7 // 2, LANES)
    return pl.pallas_call(
        functools.partial(pack_rest_kernel, rows),
        out_shape=jax.ShapeDtypeStruct(shape, down_proj.dtype),
        in_specs=[smem(), vmem()],
        out_specs=vmem(),
        compiler_params=pltpu.CompilerParams(vmem_limit_bytes=32 * MIB),
        name="pack_rest",
    )(listing, down_proj)


def unpack_rows(in_ref, at, base, rows, out_ref, out_row, out_lane):
    for number in range(3):
        out_ref[out_row : out_row + rows, out_lane + number * LANES : out_lane + (number + 1) * LANES] = (
            in_ref[at, base + number * rows : base + (number + 1) * rows, :]
        )
    mid = rows // 2
    both = in_ref[at, base + 3 * rows : base + 3 * rows + mid, :]
    lanes = slice(out_lane + 3 * LANES, out_lane + 4 * LANES)
    out_ref[out_row : out_row + mid, lanes] = both
    out_ref[out_row + mid : out_row + rows, lanes] = pltpu.roll(
        both.astype(jnp.float32), HALF, 1
    ).astype(out_ref.dtype)


def hidden_kernel(at_ref, *refs):
    pieces, (packed_ref, out_ref, gate_w, up_w, rows) = refs[:8], refs[8:]
    sources = packed_ref.shape[0]
    depth = gate_w.shape[0] // sources
    size = depth * 7 // 2
    group = sources // 2
    tile = pl.program_id(0)
    x, y, zl = tile // 4, tile // 2 % 2, tile % 2
    me, core = at_ref[0], at_ref[1]

    @pl.when(tile == 0)
    def _():
        for at in range(sources):
            place = (core + at // group) % 2 * group + at % group
            unpack_rows(packed_ref, place, 0, depth, gate_w, at * depth, 0)
            unpack_rows(packed_ref, place, size, depth, up_w, at * depth, 0)

    mid = pieces[0].shape[1]
    for number in range(4):
        lanes = slice(number * mid, (number + 1) * mid)
        coordinate = (x, y)[number % 2]
        for value in range(2):

            @pl.when(coordinate == value)
            def _():
                rows[:, lanes] = pieces[2 * number + value][...]

    gate = jnp.dot(rows[...], gate_w[...], preferred_element_type=jnp.float32)
    up = jnp.dot(rows[...], up_w[...], preferred_element_type=jnp.float32)
    value = gate / (1.0 + jnp.exp(-gate)) * up

    wide = gate.shape[1]
    term = lax.broadcasted_iota(jnp.int32, (16, wide), 0)
    lane = lax.broadcasted_iota(jnp.int32, (16, wide), 1)
    chosen = (term % 4 == lane // LANES) & (term < 12) & (lane < wide - HALF)
    chosen = jnp.where(chosen, 1.0, 0.0).astype(jnp.bfloat16)
    block = rows.shape[0] // 2
    for zh in range(2):
        source = me ^ (x + 2 * y + 4 * zl + 8 * zh)
        weight = lax.dot_general(
            packed_ref[source, packed_ref.shape[1] - 16 :, :],
            chosen,
            (((0,), (0,)), ((), ())),
            preferred_element_type=jnp.float32,
        )
        span = slice(zh * block, (zh + 1) * block)
        out_ref[span, :] = (value[span, :] * weight).astype(out_ref.dtype)


def hidden_units(at, pieces, packed):
    total = 2 * pieces[0].shape[0]
    mid = pieces[0].shape[1]
    tile = total // 8
    wide = 4 * LANES
    model = 4 * mid
    by_x = [lambda i: (jnp.minimum(i, 3), 0), lambda i: (jnp.maximum(i - 4, 0), 0)]
    by_y = [
        lambda i: (i // 4 * 2 + jnp.where(i // 2 % 2 == 0, i % 2, 1), 0),
        lambda i: (i // 4 * 2 + jnp.where(i // 2 % 2 == 1, i % 2, 0), 0),
    ]
    maps = (by_x + by_y) * 2
    return pl.pallas_call(
        hidden_kernel,
        grid=(8,),
        out_shape=jax.ShapeDtypeStruct((total, wide), packed.dtype),
        in_specs=[smem()]
        + [pl.BlockSpec((tile, mid), where) for where in maps]
        + [vmem()],
        out_specs=pl.BlockSpec((tile, wide), lambda i: (i, 0)),
        scratch_shapes=[pltpu.VMEM((model, wide), packed.dtype)] * 2
        + [pltpu.VMEM((tile, model), packed.dtype)],
        compiler_params=pltpu.CompilerParams(vmem_limit_bytes=56 * MIB),
        cost_estimate=pl.CostEstimate(
            flops=4 * total * model * wide, bytes_accessed=24 * MIB, transcendentals=total * wide
        ),
        name="hidden",
    )(at, *pieces, packed)


THIRDS = ((0, 1, 2), (1, 2, 0), (2, 0, 1))


def group_spans(features, count):
    tiles = features // LANES
    cuts = [-(-tiles * at // count) * LANES for at in range(count + 1)]
    return [slice(lo, hi) for lo, hi in zip(cuts, cuts[1:])]


def stage_axis(order, stage):
    return sum(1 for bit in order[stage:] if bit < order[stage])


def half_spans(rows, axis, side):
    size = rows >> (axis + 1)
    return [slice((2 * at + side) * size, (2 * at + side + 1) * size) for at in range(1 << axis)]


def down_kernel(rows, side, orders, own_h, other_h, own_ref, other_ref, *refs):
    out_refs, (own_w, other_w) = refs[:-2], refs[-2:]
    for in_ref, w_ref in ((own_ref, own_w), (other_ref, other_w)):
        for at in range(in_ref.shape[0]):
            unpack_rows(in_ref, at, 0, rows, w_ref, at * rows, 0)
    dims = (((1,), (1,)), ((), ()))
    for number, span in enumerate(group_spans(own_w.shape[0], len(orders))):
        done = 0
        for tokens in half_spans(own_h.shape[0], stage_axis(orders[number], 0), side):
            value = lax.dot_general(
                own_h[tokens, :], own_w[span, :], dims, preferred_element_type=jnp.float32
            ) + lax.dot_general(
                other_h[tokens, :], other_w[span, :], dims, preferred_element_type=jnp.float32
            )
            size = tokens.stop - tokens.start
            out_refs[number][done : done + size, :] = value.astype(out_refs[number].dtype)
            done += size


def down_product(own_h, other_h, own, other, rows, side, orders, dtype, name):
    sources = own.shape[0]
    total, wide = own_h.shape
    tokens = total // 2
    features = sources * rows
    shapes = [
        jax.ShapeDtypeStruct((tokens, span.stop - span.start), dtype)
        for span in group_spans(features, len(orders))
    ]
    return pl.pallas_call(
        functools.partial(down_kernel, rows, side, orders),
        out_shape=shapes,
        in_specs=[vmem()] * 4,
        out_specs=[vmem()] * len(shapes),
        scratch_shapes=[pltpu.VMEM((features, wide), own.dtype)] * 2,
        compiler_params=pltpu.CompilerParams(vmem_limit_bytes=40 * MIB),
        cost_estimate=pl.CostEstimate(
            flops=4 * tokens * wide * features, bytes_accessed=8 * MIB, transcendentals=0
        ),
        name=name,
    )(own_h, other_h, own, other)


def halve_kernel(axes, *refs):
    count = len(refs) // 4 if axes else len(refs) // 2 - 1
    out_refs = refs[2 * count :]
    lane = 0
    for number in range(count):
        keep_ref, come_ref = refs[2 * number : 2 * number + 2]
        if axes:
            send_ref, left_ref = out_refs[2 * number : 2 * number + 2]
            lanes = slice(0, keep_ref.shape[1])
        else:
            send_ref, left_ref = out_refs
            lanes = slice(lane, lane + keep_ref.shape[1])
            lane = lanes.stop
        axis = axes[number] if axes else 0
        for side, out_ref in enumerate((left_ref, send_ref)):
            done = 0
            for rows in half_spans(keep_ref.shape[0], axis, side):
                size = rows.stop - rows.start
                total = keep_ref[rows, :] + come_ref[rows, :].astype(jnp.float32)
                out_ref[done : done + size, lanes] = total.astype(out_ref.dtype)
                done += size


def halve(pairs, axes):
    sizes = [(keep.shape[0] // 2, keep.shape[1]) for keep, _ in pairs]
    if not axes:
        sizes = [(sizes[0][0], sum(width for _, width in sizes))]
    shapes = []
    for size in sizes:
        shapes += [jax.ShapeDtypeStruct(size, jnp.bfloat16), jax.ShapeDtypeStruct(size, jnp.float32)]
    out = pl.pallas_call(
        functools.partial(halve_kernel, axes),
        out_shape=shapes,
        in_specs=[vmem()] * (2 * len(pairs)),
        out_specs=[vmem()] * len(shapes),
        compiler_params=pltpu.CompilerParams(vmem_limit_bytes=40 * MIB),
        cost_estimate=pl.CostEstimate(
            flops=sum(keep.size for keep, _ in pairs), bytes_accessed=4 * MIB, transcendentals=0
        ),
        name="sum_stage",
    )(*[value for pair in pairs for value in pair])
    return [(out[2 * n], out[2 * n + 1]) for n in range(len(out) // 2)]


def swap(value, bit):
    size = lax.axis_size("ep")
    return lax.ppermute(value, "ep", [(i, i ^ (1 << bit)) for i in range(size)])


def gather_bits(value, bits, order, have=()):
    have = list(have)
    for bit in order:
        axis = sum(1 for b in have if b < bit)
        value = jnp.stack([value, swap(value, bit)], axis=axis)
        have.append(bit)
    return value


def take_half(value, axis, number):
    return lax.index_in_dim(value, number, axis, keepdims=False)


def sum_stages(keep, arrived, order, left):
    left = list(left)
    for bit in order:
        axis = left.index(bit)
        total = keep + arrived.astype(jnp.float32)
        arrived = swap(take_half(total, axis, 1).astype(jnp.bfloat16), bit)
        keep = take_half(total, axis, 0)
        left.remove(bit)
    return keep, arrived


def share_of_slots(slot_ids, gate_weights, slots):
    index = jnp.arange(slots, dtype=jnp.int32)
    picked = slot_ids.T[None, :, :] == index[:, None, None]
    return jnp.sum(jnp.where(picked, gate_weights.T[None, :, :], 0.0), axis=1)


def packed_layer(
    tokens, slot_ids, gate_weights, old_expert, new_expert, gate_proj, up_proj, down_proj
):
    devices = lax.axis_size("ep")
    slots, depth, width = gate_proj.shape
    block = tokens.shape[0]
    me = lax.axis_index("ep")
    core = lax.axis_index("et")
    group = devices // 2
    tie = lax.optimization_barrier
    _, listing, slot_place = distinct_sources(old_expert, new_expert)

    def exchange(value):
        return lax.ppermute(value, "et", [(0, 1), (1, 0)])

    def move(packed):
        return lax.all_to_all(packed, "ep", 0, 0, tiled=True)

    places = []
    for dest in range(devices):
        first, half, _ = units_of(dest)
        places.append([unit // (width // LANES) for unit in (first, first + 1, first + 2, half)] * 4)
    places = jnp.asarray(places, jnp.int32)
    share = share_of_slots(slot_ids, gate_weights, slots)
    belongs = slot_place[None, None, :, None] == places[:, :, None, None]
    share = jnp.sum(jnp.where(belongs, share[None, None], 0.0), axis=2)

    def diagonal(value):
        return lax.ppermute(value, "ep", [(i, i ^ 3) for i in range(devices)])

    mid = tokens.shape[1] // 2
    near, far = swap(tokens, 2), swap(tokens, 3)
    plane = [swap(tokens, 0), swap(tokens, 1), diagonal(tokens)]
    pair = jnp.concatenate([far, near], axis=0)
    corner = swap(far, 2)
    pair_y, pair_x = swap(pair[:, :mid], 1), swap(pair[:, mid:], 0)
    parts = (128, 96)
    packed = pack_first(listing, gate_proj, up_proj, down_proj, parts[0], share, devices)
    packed, plane, pair, corner, pair_y, pair_x = tie(
        (packed, plane, pair, corner, pair_y, pair_x)
    )

    moved = move(packed)
    corner_a, corner_b = corner[:, :mid], corner[:, mid:]
    cross = diagonal(corner)
    most_a = swap(jnp.concatenate([pair[:, :mid], corner_a, pair_y], axis=0), 0)
    most_b = swap(jnp.concatenate([pair[:, mid:], corner_b, pair_x], axis=0), 1)
    corner_y, corner_x = swap(corner_a, 1), swap(corner_b, 0)
    x_own, y_own, xy_own = plane

    def lay(*values):
        return jnp.concatenate(values, axis=0)

    at_pair, at_corner = slice(0, 2 * block), slice(2 * block, 3 * block)
    at_other = slice(3 * block, 5 * block)
    first, second = slice(0, mid), slice(mid, 2 * mid)
    pieces = [
        lay(tokens[:, first], pair[:, first], corner_a, y_own[:, first], pair_y, corner_y),
        lay(
            x_own[:, first], most_a[at_pair], most_a[at_corner],
            xy_own[:, first], most_a[at_other], cross[:, first],
        ),
        lay(tokens[:, second], pair[:, second], corner_b, x_own[:, second], pair_x, corner_x),
        lay(
            y_own[:, second], most_b[at_pair], most_b[at_corner],
            xy_own[:, second], most_b[at_other], cross[:, second],
        ),
    ]
    others = [exchange(piece) for piece in pieces]
    rest = pack_rest(listing, down_proj, parts[0], devices)
    moved, rest = tie((moved, rest))

    down1 = move(rest)
    at = jnp.stack([me, core]).astype(jnp.int32)
    hidden = hidden_units(at, pieces + others, moved)
    hidden_other = exchange(hidden)
    down0 = moved[:, depth * 7 : depth * 7 + parts[0] * 7 // 2]

    def products(down, rows_in, orders, before=None):
        own = lax.dynamic_slice_in_dim(down, core * group, group, 0)
        other = exchange(lax.dynamic_slice_in_dim(down, (1 - core) * group, group, 0))
        args = (hidden, hidden_other, own, other)
        sent = down_product(*args, rows_in, 1, orders, jnp.bfloat16, "down_send")
        sent, args = tie((sent, args))
        come = [swap(value, order[0]) for value, order in zip(sent, orders)]
        args, _ = tie((args, before))
        kept = down_product(*args, rows_in, 0, orders, jnp.float32, "down_keep")
        return kept, come

    def stage(kept, come, number, orders):
        axes = tuple(stage_axis(order, number) for order in orders)
        out = halve(list(zip(kept, come)), axes)
        come = [swap(send, order[number]) for (send, _), order in zip(out, orders)]
        return [keep for _, keep in out], come

    def last_stage(kept, come):
        ((send, keep),) = halve(list(zip(kept, come)), None)
        come = swap(send, 3)
        return (keep + come.astype(jnp.float32)).astype(jnp.bfloat16)

    kept0, come0 = products(down0, parts[0], THIRDS)
    down1, kept0 = tie((down1, kept0))
    kept1, come1 = products(down1, parts[1], THIRDS, before=come0)
    kept0, come0 = stage(kept0, come0, 1, THIRDS)
    kept1, come1 = stage(kept1, come1, 1, THIRDS)
    kept0, come0 = stage(kept0, come0, 2, THIRDS)
    kept1, come1 = stage(kept1, come1, 2, THIRDS)
    out = []
    for rows_in, total in zip(parts, (last_stage(kept0, come0), last_stage(kept1, come1))):
        out.append(total.reshape(block, group, rows_in))
    return jnp.concatenate(out, axis=2).reshape(tokens.shape)


def plain_layer(
    tokens, slot_ids, gate_weights, old_expert, new_expert, gate_proj, up_proj, down_proj
):
    devices = lax.axis_size("ep")
    bits = devices.bit_length() - 1
    slots = gate_proj.shape[0]
    me = lax.axis_index("ep")
    source, _, _ = distinct_sources(old_expert, new_expert)

    def move(weights):
        chosen = jnp.take(weights, source, axis=0, mode="clip")
        return lax.all_to_all(chosen, "ep", 0, 0, tiled=True)

    gate_slab = move(gate_proj).reshape(-1, gate_proj.shape[-1])
    up_slab = move(up_proj).reshape(-1, up_proj.shape[-1])
    down = move(down_proj)
    order = range(bits - 1, -1, -1)
    rows = gather_bits(tokens, bits, order).reshape(-1, tokens.shape[1])
    rows = lax.all_gather(rows, "et", axis=1, tiled=True)
    share = gather_bits(share_of_slots(slot_ids, gate_weights, slots), bits, order)
    share = lax.dynamic_index_in_dim(share, me, bits, keepdims=False).reshape(-1, 1)
    gate_part = jnp.dot(rows, gate_slab, preferred_element_type=jnp.float32)
    up_part = jnp.dot(rows, up_slab, preferred_element_type=jnp.float32)
    hidden = (jax.nn.silu(gate_part) * up_part * share).astype(jnp.bfloat16)
    hidden = lax.all_gather(hidden, "et", axis=1, tiled=True)
    down = lax.all_to_all(down, "et", 0, 2, tiled=True)
    value = lax.dot_general(
        hidden,
        down.reshape(-1, down.shape[-1]),
        (((1,), (1,)), ((), ())),
        preferred_element_type=jnp.float32,
    )
    value = value.reshape((2,) * bits + (-1,) + value.shape[1:])
    arrived = swap(take_half(value, 0, 1).astype(jnp.bfloat16), 0)
    left = list(range(1, bits))
    keep, arrived = sum_stages(take_half(value, 0, 0), arrived, left, left)
    return (keep + arrived.astype(jnp.float32)).astype(jnp.bfloat16)


def per_device(tokens, slot_ids, gate_weights, old_expert, new_expert, gate_proj, up_proj, down_proj):
    slots, depth, width = gate_proj.shape
    count = slots - slots // 8
    devices = lax.axis_size("ep")
    fits = (
        lax.axis_size("et") == 2
        and depth == 224
        and width % LANES == 0
        and count * width == devices * 7 * HALF
        and devices == 16
        and tokens.shape[0] == LANES
    )
    layer = packed_layer if fits else plain_layer
    return layer(
        tokens, slot_ids, gate_weights, old_expert, new_expert, gate_proj, up_proj, down_proj
    )


def solution(mesh):
    placed = (
        P("ep", "et"),
        P("ep", None),
        P("ep", None),
        P(),
        P(),
        P(None, "ep", "et"),
        P(None, "ep", "et"),
        P(None, "ep", "et"),
    )
    return jax.shard_map(
        per_device, mesh=mesh, in_specs=placed, out_specs=P("ep", "et"), check_vma=False
    )
```

```python
import functools

import jax
import jax.numpy as jnp
from jax import lax
from jax.experimental import pallas as pl
from jax.experimental.pallas import tpu as pltpu
from jax.sharding import PartitionSpec as P

LANES = 128
HALF = 64
MIB = 1 << 20


def distinct_sources(old_expert, new_expert):
    slots = old_expert.shape[0]
    index = jnp.arange(slots, dtype=jnp.int32)
    holders = new_expert[:, None] == old_expert[None, :]
    source = jnp.min(jnp.where(holders, index[None, :], slots), axis=1)
    used = jnp.any(source[:, None] == index[None, :], axis=0)
    earlier = (index[None, :] < index[:, None]) & used[None, :]
    place = jnp.sum(earlier.astype(jnp.int32), axis=1)
    count = slots - slots // 8
    wanted = jnp.arange(count, dtype=jnp.int32)
    listing = jnp.sum(
        jnp.where(used[None, :] & (place[None, :] == wanted[:, None]), index[None, :], 0), axis=1
    )
    slot_place = jnp.sum(jnp.where(source[:, None] == index[None, :], place[None, :], 0), axis=1)
    return source, listing, slot_place


def units_of(dest):
    if dest % 2 == 0:
        start = 7 * dest // 2
        return start, start + 3, 0
    start = (7 * dest + 1) // 2
    return start, start - 1, 1


def pack_rows(slab_of, out_ref, base, dest, lo, rows, per_slab):
    first, half, side = units_of(dest)
    for number in range(3):
        unit = first + number
        ref, slab = slab_of(unit // per_slab)
        lane = (unit % per_slab) * LANES
        out_ref[dest, base + number * rows : base + (number + 1) * rows, :] = ref[
            slab, lo : lo + rows, lane : lane + LANES
        ]
    ref, slab = slab_of(half // per_slab)
    lane = (half % per_slab) * LANES
    mid = rows // 2
    top = ref[slab, lo : lo + mid, lane : lane + LANES].astype(jnp.float32)
    low = ref[slab, lo + mid : lo + rows, lane : lane + LANES].astype(jnp.float32)
    left = lax.broadcasted_iota(jnp.int32, (mid, LANES), 1) < HALF
    if side == 0:
        both = jnp.where(left, top, pltpu.roll(low, HALF, 1))
    else:
        both = jnp.where(left, pltpu.roll(top, HALF, 1), low)
    out_ref[dest, base + 3 * rows : base + 3 * rows + mid, :] = both.astype(out_ref.dtype)


def pack_first_kernel(rows, list_ref, gate_ref, up_ref, down_ref, share_ref, out_ref):
    slots, depth, width = gate_ref.shape
    size = depth * 7 // 2
    row = lax.broadcasted_iota(jnp.int32, share_ref.shape[1:], 0) // 4
    for dest in range(out_ref.shape[0]):
        for number, in_ref in enumerate((gate_ref, up_ref)):
            pack_rows(
                lambda place, in_ref=in_ref: (in_ref, list_ref[place]),
                out_ref, number * size, dest, 0, depth, width // LANES,
            )
        pack_rows(
            lambda place: (down_ref, list_ref[place]),
            out_ref, 2 * size, dest, 0, rows, width // LANES,
        )
        value = share_ref[dest]
        high = value.astype(out_ref.dtype)
        rest = value - high.astype(jnp.float32)
        middle = rest.astype(out_ref.dtype)
        low = (rest - middle.astype(jnp.float32)).astype(out_ref.dtype)
        terms = jnp.where(
            row == 0,
            high.astype(jnp.float32),
            jnp.where(
                row == 1,
                middle.astype(jnp.float32),
                jnp.where(row == 2, low.astype(jnp.float32), 0.0),
            ),
        )
        out_ref[dest, 2 * size + rows * 7 // 2 :, :] = terms.astype(out_ref.dtype)


def pack_rest_kernel(rows, list_ref, down_ref, out_ref):
    slots, depth, width = down_ref.shape
    for dest in range(out_ref.shape[0]):
        pack_rows(
            lambda place: (down_ref, list_ref[place]),
            out_ref, 0, dest, rows, depth - rows, width // LANES,
        )


def vmem():
    return pl.BlockSpec(memory_space=pltpu.VMEM)


def smem():
    return pl.BlockSpec(memory_space=pltpu.SMEM)


def pack_first(listing, gate_proj, up_proj, down_proj, rows, share, dests):
    slots, depth, width = gate_proj.shape
    shape = (dests, depth * 7 + rows * 7 // 2 + share.shape[1], LANES)
    return pl.pallas_call(
        functools.partial(pack_first_kernel, rows),
        out_shape=jax.ShapeDtypeStruct(shape, gate_proj.dtype),
        in_specs=[smem(), vmem(), vmem(), vmem(), vmem()],
        out_specs=vmem(),
        compiler_params=pltpu.CompilerParams(vmem_limit_bytes=40 * MIB),
        name="pack_first",
    )(listing, gate_proj, up_proj, down_proj, share)


def pack_rest(listing, down_proj, rows, dests):
    slots, depth, width = down_proj.shape
    shape = (dests, (depth - rows) * 7 // 2, LANES)
    return pl.pallas_call(
        functools.partial(pack_rest_kernel, rows),
        out_shape=jax.ShapeDtypeStruct(shape, down_proj.dtype),
        in_specs=[smem(), vmem()],
        out_specs=vmem(),
        compiler_params=pltpu.CompilerParams(vmem_limit_bytes=32 * MIB),
        name="pack_rest",
    )(listing, down_proj)


def unpack_rows(in_ref, at, base, rows, out_ref, out_row, out_lane):
    for number in range(3):
        out_ref[out_row : out_row + rows, out_lane + number * LANES : out_lane + (number + 1) * LANES] = (
            in_ref[at, base + number * rows : base + (number + 1) * rows, :]
        )
    mid = rows // 2
    both = in_ref[at, base + 3 * rows : base + 3 * rows + mid, :]
    lanes = slice(out_lane + 3 * LANES, out_lane + 4 * LANES)
    out_ref[out_row : out_row + mid, lanes] = both
    out_ref[out_row + mid : out_row + rows, lanes] = pltpu.roll(
        both.astype(jnp.float32), HALF, 1
    ).astype(out_ref.dtype)


def hidden_kernel(at_ref, *refs):
    pieces, (packed_ref, out_ref, gate_w, up_w, rows) = refs[:8], refs[8:]
    sources = packed_ref.shape[0]
    depth = gate_w.shape[0] // sources
    size = depth * 7 // 2
    group = sources // 2
    tile = pl.program_id(0)
    x, y, zl = tile // 4, tile // 2 % 2, tile % 2
    me, core = at_ref[0], at_ref[1]

    @pl.when(tile == 0)
    def _():
        for at in range(sources):
            place = (core + at // group) % 2 * group + at % group
            unpack_rows(packed_ref, place, 0, depth, gate_w, at * depth, 0)
            unpack_rows(packed_ref, place, size, depth, up_w, at * depth, 0)

    mid = pieces[0].shape[1]
    for number in range(4):
        lanes = slice(number * mid, (number + 1) * mid)
        coordinate = (x, y)[number % 2]
        for value in range(2):

            @pl.when(coordinate == value)
            def _():
                rows[:, lanes] = pieces[2 * number + value][...]

    gate = jnp.dot(rows[...], gate_w[...], preferred_element_type=jnp.float32)
    up = jnp.dot(rows[...], up_w[...], preferred_element_type=jnp.float32)
    value = gate / (1.0 + jnp.exp(-gate)) * up

    wide = gate.shape[1]
    term = lax.broadcasted_iota(jnp.int32, (16, wide), 0)
    lane = lax.broadcasted_iota(jnp.int32, (16, wide), 1)
    chosen = (term % 4 == lane // LANES) & (term < 12) & (lane < wide - HALF)
    chosen = jnp.where(chosen, 1.0, 0.0).astype(jnp.bfloat16)
    block = rows.shape[0] // 2
    for zh in range(2):
        source = me ^ (x + 2 * y + 4 * zl + 8 * zh)
        weight = lax.dot_general(
            packed_ref[source, packed_ref.shape[1] - 16 :, :],
            chosen,
            (((0,), (0,)), ((), ())),
            preferred_element_type=jnp.float32,
        )
        span = slice(zh * block, (zh + 1) * block)
        out_ref[span, :] = (value[span, :] * weight).astype(out_ref.dtype)


def hidden_units(at, pieces, packed):
    total = 2 * pieces[0].shape[0]
    mid = pieces[0].shape[1]
    tile = total // 8
    wide = 4 * LANES
    model = 4 * mid
    by_x = [lambda i: (jnp.minimum(i, 3), 0), lambda i: (jnp.maximum(i - 4, 0), 0)]
    by_y = [
        lambda i: (i // 4 * 2 + jnp.where(i // 2 % 2 == 0, i % 2, 1), 0),
        lambda i: (i // 4 * 2 + jnp.where(i // 2 % 2 == 1, i % 2, 0), 0),
    ]
    maps = (by_x + by_y) * 2
    return pl.pallas_call(
        hidden_kernel,
        grid=(8,),
        out_shape=jax.ShapeDtypeStruct((total, wide), packed.dtype),
        in_specs=[smem()]
        + [pl.BlockSpec((tile, mid), where) for where in maps]
        + [vmem()],
        out_specs=pl.BlockSpec((tile, wide), lambda i: (i, 0)),
        scratch_shapes=[pltpu.VMEM((model, wide), packed.dtype)] * 2
        + [pltpu.VMEM((tile, model), packed.dtype)],
        compiler_params=pltpu.CompilerParams(vmem_limit_bytes=56 * MIB),
        cost_estimate=pl.CostEstimate(
            flops=4 * total * model * wide, bytes_accessed=24 * MIB, transcendentals=total * wide
        ),
        name="hidden",
    )(at, *pieces, packed)


THIRDS = ((0, 1, 2), (1, 2, 0), (2, 0, 1))


def group_spans(features, count):
    tiles = features // LANES
    cuts = [-(-tiles * at // count) * LANES for at in range(count + 1)]
    return [slice(lo, hi) for lo, hi in zip(cuts, cuts[1:])]


def stage_axis(order, stage):
    return sum(1 for bit in order[stage:] if bit < order[stage])


def half_spans(rows, axis, side):
    size = rows >> (axis + 1)
    return [slice((2 * at + side) * size, (2 * at + side + 1) * size) for at in range(1 << axis)]


def down_kernel(rows, side, orders, own_h, other_h, own_ref, other_ref, *refs):
    out_refs, (own_w, other_w) = refs[:-2], refs[-2:]
    for in_ref, w_ref in ((own_ref, own_w), (other_ref, other_w)):
        for at in range(in_ref.shape[0]):
            unpack_rows(in_ref, at, 0, rows, w_ref, at * rows, 0)
    dims = (((1,), (1,)), ((), ()))
    for number, span in enumerate(group_spans(own_w.shape[0], len(orders))):
        done = 0
        for tokens in half_spans(own_h.shape[0], stage_axis(orders[number], 0), side):
            value = lax.dot_general(
                own_h[tokens, :], own_w[span, :], dims, preferred_element_type=jnp.float32
            ) + lax.dot_general(
                other_h[tokens, :], other_w[span, :], dims, preferred_element_type=jnp.float32
            )
            size = tokens.stop - tokens.start
            out_refs[number][done : done + size, :] = value.astype(out_refs[number].dtype)
            done += size


def down_product(own_h, other_h, own, other, rows, side, orders, dtype, name):
    sources = own.shape[0]
    total, wide = own_h.shape
    tokens = total // 2
    features = sources * rows
    shapes = [
        jax.ShapeDtypeStruct((tokens, span.stop - span.start), dtype)
        for span in group_spans(features, len(orders))
    ]
    return pl.pallas_call(
        functools.partial(down_kernel, rows, side, orders),
        out_shape=shapes,
        in_specs=[vmem()] * 4,
        out_specs=[vmem()] * len(shapes),
        scratch_shapes=[pltpu.VMEM((features, wide), own.dtype)] * 2,
        compiler_params=pltpu.CompilerParams(vmem_limit_bytes=40 * MIB),
        cost_estimate=pl.CostEstimate(
            flops=4 * tokens * wide * features, bytes_accessed=8 * MIB, transcendentals=0
        ),
        name=name,
    )(own_h, other_h, own, other)


def halve_kernel(axes, *refs):
    count = len(refs) // 4 if axes else len(refs) // 2 - 1
    out_refs = refs[2 * count :]
    lane = 0
    for number in range(count):
        keep_ref, come_ref = refs[2 * number : 2 * number + 2]
        if axes:
            send_ref, left_ref = out_refs[2 * number : 2 * number + 2]
            lanes = slice(0, keep_ref.shape[1])
        else:
            send_ref, left_ref = out_refs
            lanes = slice(lane, lane + keep_ref.shape[1])
            lane = lanes.stop
        axis = axes[number] if axes else 0
        for side, out_ref in enumerate((left_ref, send_ref)):
            done = 0
            for rows in half_spans(keep_ref.shape[0], axis, side):
                size = rows.stop - rows.start
                total = keep_ref[rows, :] + come_ref[rows, :].astype(jnp.float32)
                out_ref[done : done + size, lanes] = total.astype(out_ref.dtype)
                done += size


def halve(pairs, axes):
    sizes = [(keep.shape[0] // 2, keep.shape[1]) for keep, _ in pairs]
    if not axes:
        sizes = [(sizes[0][0], sum(width for _, width in sizes))]
    shapes = []
    for size in sizes:
        shapes += [jax.ShapeDtypeStruct(size, jnp.bfloat16), jax.ShapeDtypeStruct(size, jnp.float32)]
    out = pl.pallas_call(
        functools.partial(halve_kernel, axes),
        out_shape=shapes,
        in_specs=[vmem()] * (2 * len(pairs)),
        out_specs=[vmem()] * len(shapes),
        compiler_params=pltpu.CompilerParams(vmem_limit_bytes=40 * MIB),
        cost_estimate=pl.CostEstimate(
            flops=sum(keep.size for keep, _ in pairs), bytes_accessed=4 * MIB, transcendentals=0
        ),
        name="sum_stage",
    )(*[value for pair in pairs for value in pair])
    return [(out[2 * n], out[2 * n + 1]) for n in range(len(out) // 2)]


def swap(value, bit):
    size = lax.axis_size("ep")
    return lax.ppermute(value, "ep", [(i, i ^ (1 << bit)) for i in range(size)])


def gather_bits(value, bits, order, have=()):
    have = list(have)
    for bit in order:
        axis = sum(1 for b in have if b < bit)
        value = jnp.stack([value, swap(value, bit)], axis=axis)
        have.append(bit)
    return value


def take_half(value, axis, number):
    return lax.index_in_dim(value, number, axis, keepdims=False)


def sum_stages(keep, arrived, order, left):
    left = list(left)
    for bit in order:
        axis = left.index(bit)
        total = keep + arrived.astype(jnp.float32)
        arrived = swap(take_half(total, axis, 1).astype(jnp.bfloat16), bit)
        keep = take_half(total, axis, 0)
        left.remove(bit)
    return keep, arrived


def share_of_slots(slot_ids, gate_weights, slots):
    index = jnp.arange(slots, dtype=jnp.int32)
    picked = slot_ids.T[None, :, :] == index[:, None, None]
    return jnp.sum(jnp.where(picked, gate_weights.T[None, :, :], 0.0), axis=1)


def packed_layer(
    tokens, slot_ids, gate_weights, old_expert, new_expert, gate_proj, up_proj, down_proj
):
    devices = lax.axis_size("ep")
    slots, depth, width = gate_proj.shape
    block = tokens.shape[0]
    me = lax.axis_index("ep")
    core = lax.axis_index("et")
    group = devices // 2
    tie = lax.optimization_barrier
    _, listing, slot_place = distinct_sources(old_expert, new_expert)

    def exchange(value):
        return lax.ppermute(value, "et", [(0, 1), (1, 0)])

    def move(packed):
        return lax.all_to_all(packed, "ep", 0, 0, tiled=True)

    places = []
    for dest in range(devices):
        first, half, _ = units_of(dest)
        places.append([unit // (width // LANES) for unit in (first, first + 1, first + 2, half)] * 4)
    places = jnp.asarray(places, jnp.int32)
    share = share_of_slots(slot_ids, gate_weights, slots)
    belongs = slot_place[None, None, :, None] == places[:, :, None, None]
    share = jnp.sum(jnp.where(belongs, share[None, None], 0.0), axis=2)

    mid = tokens.shape[1] // 2
    first, second = slice(0, mid), slice(mid, 2 * mid)

    def lay(*values):
        return jnp.concatenate(values, axis=0)

    near, far = swap(tokens, 2), swap(tokens, 3)
    corner = swap(far, 2)
    pair = lay(far, near)
    pair_y, pair_x = swap(pair[:, first], 1), swap(pair[:, second], 0)
    parts = (128, 96)
    packed = pack_first(listing, gate_proj, up_proj, down_proj, parts[0], share, devices)
    packed, pair, corner, pair_y, pair_x = tie((packed, pair, corner, pair_y, pair_x))

    moved = move(packed)
    column, ends = lay(tokens, pair, corner), lay(tokens, corner)
    most_a = swap(lay(column[:, first], pair_y), 0)
    most_b = swap(lay(column[:, second], pair_x), 1)
    ends_y, ends_x = swap(ends[:, first], 1), swap(ends[:, second], 0)
    cross = lax.ppermute(ends, "ep", [(i, i ^ 3) for i in range(devices)])
    pieces = [
        lay(column[:, first], ends_y[:block], pair_y, ends_y[block:]),
        lay(most_a[: 4 * block], cross[:block, first], most_a[4 * block :], cross[block:, first]),
        lay(column[:, second], ends_x[:block], pair_x, ends_x[block:]),
        lay(most_b[: 4 * block], cross[:block, second], most_b[4 * block :], cross[block:, second]),
    ]
    others = [exchange(piece) for piece in pieces]
    rest = pack_rest(listing, down_proj, parts[0], devices)
    moved, rest = tie((moved, rest))

    down1 = move(rest)
    at = jnp.stack([me, core]).astype(jnp.int32)
    hidden = hidden_units(at, pieces + others, moved)
    hidden_other = exchange(hidden)
    down0 = moved[:, depth * 7 : depth * 7 + parts[0] * 7 // 2]

    def products(down, rows_in, orders, before=None):
        own = lax.dynamic_slice_in_dim(down, core * group, group, 0)
        other = exchange(lax.dynamic_slice_in_dim(down, (1 - core) * group, group, 0))
        args = (hidden, hidden_other, own, other)
        sent = down_product(*args, rows_in, 1, orders, jnp.bfloat16, "down_send")
        sent, args = tie((sent, args))
        come = [swap(value, order[0]) for value, order in zip(sent, orders)]
        args, _ = tie((args, before))
        kept = down_product(*args, rows_in, 0, orders, jnp.float32, "down_keep")
        return kept, come, sent

    def stage(kept, come, number, orders):
        axes = tuple(stage_axis(order, number) for order in orders)
        out = halve(list(zip(kept, come)), axes)
        come = [swap(send, order[number]) for (send, _), order in zip(out, orders)]
        return [keep for _, keep in out], come

    def last_stage(kept, come):
        ((send, keep),) = halve(list(zip(kept, come)), None)
        come = swap(send, 3)
        return (keep + come.astype(jnp.float32)).astype(jnp.bfloat16)

    kept0, come0, _ = products(down0, parts[0], THIRDS)
    down1, kept0 = tie((down1, kept0))
    kept1, come1, sent1 = products(down1, parts[1], THIRDS, before=come0)
    kept0, _ = tie((kept0, sent1))
    kept0, come0 = stage(kept0, come0, 1, THIRDS)
    kept1, come1 = stage(kept1, come1, 1, THIRDS)
    kept0, come0 = stage(kept0, come0, 2, THIRDS)
    kept1, come1 = stage(kept1, come1, 2, THIRDS)
    out = []
    for rows_in, total in zip(parts, (last_stage(kept0, come0), last_stage(kept1, come1))):
        out.append(total.reshape(block, group, rows_in))
    return jnp.concatenate(out, axis=2).reshape(tokens.shape)


def plain_layer(
    tokens, slot_ids, gate_weights, old_expert, new_expert, gate_proj, up_proj, down_proj
):
    devices = lax.axis_size("ep")
    bits = devices.bit_length() - 1
    slots = gate_proj.shape[0]
    me = lax.axis_index("ep")
    source, _, _ = distinct_sources(old_expert, new_expert)

    def move(weights):
        chosen = jnp.take(weights, source, axis=0, mode="clip")
        return lax.all_to_all(chosen, "ep", 0, 0, tiled=True)

    gate_slab = move(gate_proj).reshape(-1, gate_proj.shape[-1])
    up_slab = move(up_proj).reshape(-1, up_proj.shape[-1])
    down = move(down_proj)
    order = range(bits - 1, -1, -1)
    rows = gather_bits(tokens, bits, order).reshape(-1, tokens.shape[1])
    rows = lax.all_gather(rows, "et", axis=1, tiled=True)
    share = gather_bits(share_of_slots(slot_ids, gate_weights, slots), bits, order)
    share = lax.dynamic_index_in_dim(share, me, bits, keepdims=False).reshape(-1, 1)
    gate_part = jnp.dot(rows, gate_slab, preferred_element_type=jnp.float32)
    up_part = jnp.dot(rows, up_slab, preferred_element_type=jnp.float32)
    hidden = (jax.nn.silu(gate_part) * up_part * share).astype(jnp.bfloat16)
    hidden = lax.all_gather(hidden, "et", axis=1, tiled=True)
    down = lax.all_to_all(down, "et", 0, 2, tiled=True)
    value = lax.dot_general(
        hidden,
        down.reshape(-1, down.shape[-1]),
        (((1,), (1,)), ((), ())),
        preferred_element_type=jnp.float32,
    )
    value = value.reshape((2,) * bits + (-1,) + value.shape[1:])
    arrived = swap(take_half(value, 0, 1).astype(jnp.bfloat16), 0)
    left = list(range(1, bits))
    keep, arrived = sum_stages(take_half(value, 0, 0), arrived, left, left)
    return (keep + arrived.astype(jnp.float32)).astype(jnp.bfloat16)


def per_device(tokens, slot_ids, gate_weights, old_expert, new_expert, gate_proj, up_proj, down_proj):
    slots, depth, width = gate_proj.shape
    count = slots - slots // 8
    devices = lax.axis_size("ep")
    fits = (
        lax.axis_size("et") == 2
        and depth == 224
        and width % LANES == 0
        and count * width == devices * 7 * HALF
        and devices == 16
        and tokens.shape[0] == LANES
    )
    layer = packed_layer if fits else plain_layer
    return layer(
        tokens, slot_ids, gate_weights, old_expert, new_expert, gate_proj, up_proj, down_proj
    )


def solution(mesh):
    placed = (
        P("ep", "et"),
        P("ep", None),
        P("ep", None),
        P(),
        P(),
        P(None, "ep", "et"),
        P(None, "ep", "et"),
        P(None, "ep", "et"),
    )
    return jax.shard_map(
        per_device, mesh=mesh, in_specs=placed, out_specs=P("ep", "et"), check_vma=False
    )
```

```python
import functools

import jax
import jax.numpy as jnp
from jax import lax
from jax.experimental import pallas as pl
from jax.experimental.pallas import tpu as pltpu
from jax.sharding import PartitionSpec as P

LANES = 128
HALF = 64
MIB = 1 << 20


def distinct_sources(old_expert, new_expert):
    slots = old_expert.shape[0]
    index = jnp.arange(slots, dtype=jnp.int32)
    holders = new_expert[:, None] == old_expert[None, :]
    source = jnp.min(jnp.where(holders, index[None, :], slots), axis=1)
    used = jnp.any(source[:, None] == index[None, :], axis=0)
    earlier = (index[None, :] < index[:, None]) & used[None, :]
    place = jnp.sum(earlier.astype(jnp.int32), axis=1)
    count = slots - slots // 8
    wanted = jnp.arange(count, dtype=jnp.int32)
    listing = jnp.sum(
        jnp.where(used[None, :] & (place[None, :] == wanted[:, None]), index[None, :], 0), axis=1
    )
    slot_place = jnp.sum(jnp.where(source[:, None] == index[None, :], place[None, :], 0), axis=1)
    return source, listing, slot_place


def units_of(dest):
    side = dest % 2
    first = (7 * dest + side) // 2
    return first, first + 3 - 4 * side, side


def pack_rows(dest, list_ref, in_ref, lo, rows, out_ref, at, base):
    slabs, depth, width = in_ref.shape
    per_slab = width // LANES
    first, half, side = units_of(dest)

    def unit_rows(unit, start, size):
        lane = pl.multiple_of(unit % per_slab * LANES, LANES)
        return in_ref[list_ref[unit // per_slab], start : start + size, pl.ds(lane, LANES)]

    for number in range(3):
        out_ref[at, base + number * rows : base + (number + 1) * rows, :] = unit_rows(
            first + number, lo, rows
        )
    mid = rows // 2
    top = unit_rows(half, lo, mid).astype(jnp.float32)
    low = unit_rows(half, lo + mid, mid).astype(jnp.float32)
    left = lax.broadcasted_iota(jnp.int32, (mid, LANES), 1) < HALF
    odd = jnp.full((mid, LANES), side, jnp.int32) == 1
    both = jnp.where(
        left,
        jnp.where(odd, pltpu.roll(top, HALF, 1), top),
        jnp.where(odd, low, pltpu.roll(low, HALF, 1)),
    )
    out_ref[at, base + 3 * rows : base + 3 * rows + mid, :] = both.astype(out_ref.dtype)


def pack_kernel(segments, with_terms, list_ref, *refs):
    out_refs = refs[-4:]
    me = list_ref[list_ref.shape[0] - 1]
    for j in range(16):
        dest = me ^ j
        base = 0
        for in_ref, (lo, rows) in zip(refs, segments):
            pack_rows(dest, list_ref, in_ref, lo, rows, out_refs[j // 4], j % 4, base)
            base += rows * 7 // 2
        if with_terms:
            value = refs[len(segments)][dest]
            row = lax.broadcasted_iota(jnp.int32, value.shape, 0) // 4
            high = value.astype(jnp.bfloat16).astype(jnp.float32)
            middle = (value - high).astype(jnp.bfloat16).astype(jnp.float32)
            low = value - high - middle
            terms = jnp.where(row == 0, high, jnp.where(row == 1, middle, low))
            terms = jnp.where(row == 3, 0.0, terms)
            out_refs[j // 4][j % 4, base:, :] = terms.astype(jnp.bfloat16)


def vmem():
    return pl.BlockSpec(memory_space=pltpu.VMEM)


def smem():
    return pl.BlockSpec(memory_space=pltpu.SMEM)


def pack(info, weights, segments, share, name):
    size = sum(rows * 7 // 2 for _, rows in segments)
    more = () if share is None else (share,)
    if more:
        size += share.shape[1]
    return pl.pallas_call(
        functools.partial(pack_kernel, segments, bool(more)),
        out_shape=[jax.ShapeDtypeStruct((4, size, LANES), weights[0].dtype)] * 4,
        in_specs=[smem()] + [vmem()] * (len(weights) + len(more)),
        out_specs=[vmem()] * 4,
        compiler_params=pltpu.CompilerParams(vmem_limit_bytes=32 * MIB),
        name=name,
    )(info, *weights, *more)


def unpack_rows(in_ref, at, rows, out_ref, row):
    row = pl.multiple_of(row, 16)
    for number in range(3):
        out_ref[pl.ds(row, rows), number * LANES : (number + 1) * LANES] = in_ref[
            (*at, slice(number * rows, (number + 1) * rows))
        ]
    mid = rows // 2
    both = in_ref[(*at, slice(3 * rows, 3 * rows + mid))]
    lanes = slice(3 * LANES, 4 * LANES)
    out_ref[pl.ds(row, mid), lanes] = both
    other = pltpu.roll(both.astype(jnp.float32), HALF, 1).astype(out_ref.dtype)
    out_ref[pl.ds(pl.multiple_of(row + mid, 16), mid), lanes] = other


def hidden_kernel(at_ref, *refs):
    pieces, gates, ups = refs[:8], refs[8:12], refs[12:16]
    terms_ref, out_ref, gate_w, up_w, rows = refs[16:]
    depth = gate_w.shape[0] // 16
    tile = pl.program_id(0)
    x, y, zl = tile // 4, tile // 2 % 2, tile % 2
    me, core = at_ref[0], at_ref[1]

    @pl.when(tile == 0)
    def _():
        for plane in range(4):
            for column in range(4):
                place = (me ^ (plane + 4 * column)) ^ (8 * core)
                unpack_rows(gates[plane], (column,), depth, gate_w, place * depth)
                unpack_rows(ups[plane], (column,), depth, up_w, place * depth)

    mid = pieces[0].shape[1]
    for number in range(4):
        lanes = slice(number * mid, (number + 1) * mid)
        coordinate = (x, y)[number % 2]
        for value in range(2):

            @pl.when(coordinate == value)
            def _():
                rows[:, lanes] = pieces[2 * number + value][...]

    gate = jnp.dot(rows[...], gate_w[...], preferred_element_type=jnp.float32)
    up = jnp.dot(rows[...], up_w[...], preferred_element_type=jnp.float32)
    value = gate / (1.0 + jnp.exp(-gate)) * up

    wide = gate.shape[1]
    term = lax.broadcasted_iota(jnp.int32, (16, wide), 0)
    lane = lax.broadcasted_iota(jnp.int32, (16, wide), 1)
    chosen = (term % 4 == lane // LANES) & (term < 12) & (lane < wide - HALF)
    chosen = jnp.where(chosen, 1.0, 0.0).astype(jnp.bfloat16)
    block = rows.shape[0] // 2
    for zh in range(2):
        weight = lax.dot_general(
            terms_ref[x + 2 * y, zl + 2 * zh],
            chosen,
            (((0,), (0,)), ((), ())),
            preferred_element_type=jnp.float32,
        )
        span = slice(zh * block, (zh + 1) * block)
        out_ref[span, :] = (value[span, :] * weight).astype(out_ref.dtype)


def hidden_units(at, pieces, gates, ups, terms):
    total = 2 * pieces[0].shape[0]
    mid = pieces[0].shape[1]
    tile = total // 8
    wide = 4 * LANES
    model = 4 * mid
    by_x = [lambda i: (jnp.minimum(i, 3), 0), lambda i: (jnp.maximum(i - 4, 0), 0)]
    by_y = [
        lambda i: (i // 4 * 2 + jnp.where(i // 2 % 2 == 0, i % 2, 1), 0),
        lambda i: (i // 4 * 2 + jnp.where(i // 2 % 2 == 1, i % 2, 0), 0),
    ]
    maps = (by_x + by_y) * 2
    dtype = pieces[0].dtype
    return pl.pallas_call(
        hidden_kernel,
        grid=(8,),
        out_shape=jax.ShapeDtypeStruct((total, wide), dtype),
        in_specs=[smem()]
        + [pl.BlockSpec((tile, mid), where) for where in maps]
        + [vmem()] * 9,
        out_specs=pl.BlockSpec((tile, wide), lambda i: (i, 0)),
        scratch_shapes=[pltpu.VMEM((model, wide), dtype)] * 2
        + [pltpu.VMEM((tile, model), dtype)],
        compiler_params=pltpu.CompilerParams(vmem_limit_bytes=56 * MIB),
        cost_estimate=pl.CostEstimate(
            flops=4 * total * model * wide, bytes_accessed=24 * MIB, transcendentals=total * wide
        ),
        name="hidden",
    )(at, *pieces, *gates, *ups, terms)


THIRDS = ((0, 1, 2), (1, 2, 0), (2, 0, 1))


def group_spans(features, count):
    tiles = features // LANES
    cuts = [-(-tiles * at // count) * LANES for at in range(count + 1)]
    return [slice(lo, hi) for lo, hi in zip(cuts, cuts[1:])]


def stage_axis(order, stage):
    return sum(1 for bit in order[stage:] if bit < order[stage])


def half_spans(rows, axis, side):
    size = rows >> (axis + 1)
    return [slice((2 * at + side) * size, (2 * at + side + 1) * size) for at in range(1 << axis)]


def down_kernel(rows, side, orders, at_ref, own_h, other_h, own_ref, other_ref, *refs):
    out_refs, (own_w, other_w) = refs[:-2], refs[-2:]
    for in_ref, w_ref in ((own_ref, own_w), (other_ref, other_w)):
        for plane in range(4):
            for column in range(2):
                place = (at_ref[0] ^ (plane + 4 * column)) % 8
                unpack_rows(in_ref, (plane, column), rows, w_ref, place * rows)
    dims = (((1,), (1,)), ((), ()))
    for number, span in enumerate(group_spans(own_w.shape[0], len(orders))):
        done = 0
        for tokens in half_spans(own_h.shape[0], stage_axis(orders[number], 0), side):
            value = lax.dot_general(
                own_h[tokens, :], own_w[span, :], dims, preferred_element_type=jnp.float32
            ) + lax.dot_general(
                other_h[tokens, :], other_w[span, :], dims, preferred_element_type=jnp.float32
            )
            size = tokens.stop - tokens.start
            out_refs[number][done : done + size, :] = value.astype(out_refs[number].dtype)
            done += size


def down_product(at, own_h, other_h, own, other, rows, side, orders, dtype, name):
    sources = own.shape[0] * own.shape[1]
    total, wide = own_h.shape
    tokens = total // 2
    features = sources * rows
    shapes = [
        jax.ShapeDtypeStruct((tokens, span.stop - span.start), dtype)
        for span in group_spans(features, len(orders))
    ]
    return pl.pallas_call(
        functools.partial(down_kernel, rows, side, orders),
        out_shape=shapes,
        in_specs=[smem()] + [vmem()] * 4,
        out_specs=[vmem()] * len(shapes),
        scratch_shapes=[pltpu.VMEM((features, wide), own.dtype)] * 2,
        compiler_params=pltpu.CompilerParams(vmem_limit_bytes=40 * MIB),
        cost_estimate=pl.CostEstimate(
            flops=4 * tokens * wide * features, bytes_accessed=8 * MIB, transcendentals=0
        ),
        name=name,
    )(at, own_h, other_h, own, other)


def halve_kernel(axes, *refs):
    count = len(refs) // 4 if axes else len(refs) // 2 - 1
    out_refs = refs[2 * count :]
    lane = 0
    for number in range(count):
        keep_ref, come_ref = refs[2 * number : 2 * number + 2]
        if axes:
            send_ref, left_ref = out_refs[2 * number : 2 * number + 2]
            lanes = slice(0, keep_ref.shape[1])
        else:
            send_ref, left_ref = out_refs
            lanes = slice(lane, lane + keep_ref.shape[1])
            lane = lanes.stop
        axis = axes[number] if axes else 0
        for side, out_ref in enumerate((left_ref, send_ref)):
            done = 0
            for rows in half_spans(keep_ref.shape[0], axis, side):
                size = rows.stop - rows.start
                total = keep_ref[rows, :] + come_ref[rows, :].astype(jnp.float32)
                out_ref[done : done + size, lanes] = total.astype(out_ref.dtype)
                done += size


def halve(pairs, axes):
    sizes = [(keep.shape[0] // 2, keep.shape[1]) for keep, _ in pairs]
    if not axes:
        sizes = [(sizes[0][0], sum(width for _, width in sizes))]
    shapes = []
    for size in sizes:
        shapes += [jax.ShapeDtypeStruct(size, jnp.bfloat16), jax.ShapeDtypeStruct(size, jnp.float32)]
    out = pl.pallas_call(
        functools.partial(halve_kernel, axes),
        out_shape=shapes,
        in_specs=[vmem()] * (2 * len(pairs)),
        out_specs=[vmem()] * len(shapes),
        compiler_params=pltpu.CompilerParams(vmem_limit_bytes=40 * MIB),
        cost_estimate=pl.CostEstimate(
            flops=sum(keep.size for keep, _ in pairs), bytes_accessed=4 * MIB, transcendentals=0
        ),
        name="sum_stage",
    )(*[value for pair in pairs for value in pair])
    return [(out[2 * n], out[2 * n + 1]) for n in range(len(out) // 2)]


def swap(value, bit):
    size = lax.axis_size("ep")
    return lax.ppermute(value, "ep", [(i, i ^ (1 << bit)) for i in range(size)])


def gather_bits(value, bits, order, have=()):
    have = list(have)
    for bit in order:
        axis = sum(1 for b in have if b < bit)
        value = jnp.stack([value, swap(value, bit)], axis=axis)
        have.append(bit)
    return value


def take_half(value, axis, number):
    return lax.index_in_dim(value, number, axis, keepdims=False)


def sum_stages(keep, arrived, order, left):
    left = list(left)
    for bit in order:
        axis = left.index(bit)
        total = keep + arrived.astype(jnp.float32)
        arrived = swap(take_half(total, axis, 1).astype(jnp.bfloat16), bit)
        keep = take_half(total, axis, 0)
        left.remove(bit)
    return keep, arrived


def share_of_slots(slot_ids, gate_weights, slots):
    index = jnp.arange(slots, dtype=jnp.int32)
    picked = slot_ids.T[None, :, :] == index[:, None, None]
    return jnp.sum(jnp.where(picked, gate_weights.T[None, :, :], 0.0), axis=1)


def packed_layer(
    tokens, slot_ids, gate_weights, old_expert, new_expert, gate_proj, up_proj, down_proj
):
    devices = lax.axis_size("ep")
    slots, depth, width = gate_proj.shape
    block = tokens.shape[0]
    me = lax.axis_index("ep")
    core = lax.axis_index("et")
    group = devices // 2
    tie = lax.optimization_barrier
    _, listing, slot_place = distinct_sources(old_expert, new_expert)

    def exchange(value):
        return lax.ppermute(value, "et", [(0, 1), (1, 0)])

    def across(value, number):
        return lax.ppermute(value, "ep", [(i, i ^ number) for i in range(devices)])

    def along_z(packed):
        return [packed[0]] + [across(packed[k], 4 * k) for k in (1, 2, 3)]

    def in_plane(blocks):
        parts = [jnp.stack([block[q] for block in blocks]) for q in range(4)]
        return [parts[0]] + [across(parts[q], q) for q in (1, 2, 3)]

    places = []
    for dest in range(devices):
        first, half, _ = units_of(dest)
        places.append([unit // (width // LANES) for unit in (first, first + 1, first + 2, half)] * 4)
    places = jnp.asarray(places, jnp.int32)
    share = share_of_slots(slot_ids, gate_weights, slots)
    belongs = slot_place[None, None, :, None] == places[:, :, None, None]
    share = jnp.sum(jnp.where(belongs, share[None, None], 0.0), axis=2)

    parts = (128, 96)
    size = depth * 7 // 2
    at = jnp.stack([me, core]).astype(jnp.int32)
    info = jnp.concatenate([listing, at[:1]])

    near, far = swap(tokens, 2), swap(tokens, 3)
    gate_z = along_z(pack(info, (gate_proj,), ((0, depth),), share, "pack_gate"))
    corner = swap(far, 2)
    up_packed = pack(info, (up_proj,), ((0, depth),), None, "pack_up")
    gate_z, corner, near, far, up_packed = tie((gate_z, corner, near, far, up_packed))

    up_z = along_z(up_packed)
    gates = in_plane(gate_z)
    mid = tokens.shape[1] // 2
    rows = jnp.concatenate([tokens, far, near, corner], axis=0)
    first, second = rows[:, :mid], rows[:, mid:]
    first = jnp.concatenate([first, swap(first, 1)], axis=0)
    second = jnp.concatenate([second, swap(second, 0)], axis=0)
    down_packed = [
        pack(info, (down_proj,), ((0, parts[0]),), None, "pack_down"),
        pack(info, (down_proj,), ((parts[0], parts[1]),), None, "pack_down"),
    ]
    up_z, gates, first, second, packed0 = tie((up_z, gates, first, second, down_packed[0]))

    down0_z = along_z(packed0)
    ups = in_plane(up_z)
    pieces = [first, swap(first, 0), second, swap(second, 1)]
    others = [exchange(piece) for piece in pieces]
    down0_z, ups, packed1 = tie((down0_z, ups, down_packed[1]))

    down1_z = along_z(packed1)
    downs0 = in_plane(down0_z)
    terms = jnp.stack([gate[:, size:] for gate in gates])
    hidden = hidden_units(at, pieces + others, [gate[:, :size] for gate in gates], ups, terms)
    hidden_other = exchange(hidden)
    downs0, down1_z, hidden = tie((downs0, down1_z, hidden))
    downs1 = in_plane(down1_z)

    def core_half(downs, which):
        start = 2 * (which ^ (me >> 3))
        return jnp.stack([lax.dynamic_slice_in_dim(down, start, 2, 0) for down in downs])

    def products(down, rows_in, orders):
        own, other = core_half(down, core), exchange(core_half(down, 1 - core))
        args = (at, hidden, hidden_other, own, other)
        sent = down_product(*args, rows_in, 1, orders, jnp.bfloat16, "down_send")
        sent, args = tie((sent, args))
        come = [swap(value, order[0]) for value, order in zip(sent, orders)]
        return down_product(*args, rows_in, 0, orders, jnp.float32, "down_keep"), come

    def stage(kept, come, number, orders):
        axes = tuple(stage_axis(order, number) for order in orders)
        out = halve(list(zip(kept, come)), axes)
        come = [swap(send, order[number]) for (send, _), order in zip(out, orders)]
        return [keep for _, keep in out], come

    def last_stage(kept, come):
        ((send, keep),) = halve(list(zip(kept, come)), None)
        come = swap(send, 3)
        return (keep + come.astype(jnp.float32)).astype(jnp.bfloat16)

    kept0, come0 = products(downs0, parts[0], THIRDS)
    downs1, kept0 = tie((downs1, kept0))
    kept1, come1 = products(downs1, parts[1], THIRDS)
    kept0, come0 = stage(kept0, come0, 1, THIRDS)
    kept1, come1 = stage(kept1, come1, 1, THIRDS)
    kept0, come0 = stage(kept0, come0, 2, THIRDS)
    kept1, come1 = stage(kept1, come1, 2, THIRDS)
    out = []
    for rows_in, total in zip(parts, (last_stage(kept0, come0), last_stage(kept1, come1))):
        out.append(total.reshape(block, group, rows_in))
    return jnp.concatenate(out, axis=2).reshape(tokens.shape)


def plain_layer(
    tokens, slot_ids, gate_weights, old_expert, new_expert, gate_proj, up_proj, down_proj
):
    devices = lax.axis_size("ep")
    bits = devices.bit_length() - 1
    slots = gate_proj.shape[0]
    me = lax.axis_index("ep")
    source, _, _ = distinct_sources(old_expert, new_expert)

    def move(weights):
        chosen = jnp.take(weights, source, axis=0, mode="clip")
        return lax.all_to_all(chosen, "ep", 0, 0, tiled=True)

    gate_slab = move(gate_proj).reshape(-1, gate_proj.shape[-1])
    up_slab = move(up_proj).reshape(-1, up_proj.shape[-1])
    down = move(down_proj)
    order = range(bits - 1, -1, -1)
    rows = gather_bits(tokens, bits, order).reshape(-1, tokens.shape[1])
    rows = lax.all_gather(rows, "et", axis=1, tiled=True)
    share = gather_bits(share_of_slots(slot_ids, gate_weights, slots), bits, order)
    share = lax.dynamic_index_in_dim(share, me, bits, keepdims=False).reshape(-1, 1)
    gate_part = jnp.dot(rows, gate_slab, preferred_element_type=jnp.float32)
    up_part = jnp.dot(rows, up_slab, preferred_element_type=jnp.float32)
    hidden = (jax.nn.silu(gate_part) * up_part * share).astype(jnp.bfloat16)
    hidden = lax.all_gather(hidden, "et", axis=1, tiled=True)
    down = lax.all_to_all(down, "et", 0, 2, tiled=True)
    value = lax.dot_general(
        hidden,
        down.reshape(-1, down.shape[-1]),
        (((1,), (1,)), ((), ())),
        preferred_element_type=jnp.float32,
    )
    value = value.reshape((2,) * bits + (-1,) + value.shape[1:])
    arrived = swap(take_half(value, 0, 1).astype(jnp.bfloat16), 0)
    left = list(range(1, bits))
    keep, arrived = sum_stages(take_half(value, 0, 0), arrived, left, left)
    return (keep + arrived.astype(jnp.float32)).astype(jnp.bfloat16)


def per_device(tokens, slot_ids, gate_weights, old_expert, new_expert, gate_proj, up_proj, down_proj):
    slots, depth, width = gate_proj.shape
    count = slots - slots // 8
    devices = lax.axis_size("ep")
    fits = (
        lax.axis_size("et") == 2
        and depth == 224
        and width % LANES == 0
        and count * width == devices * 7 * HALF
        and devices == 16
        and tokens.shape[0] == LANES
    )
    layer = packed_layer if fits else plain_layer
    return layer(
        tokens, slot_ids, gate_weights, old_expert, new_expert, gate_proj, up_proj, down_proj
    )


def solution(mesh):
    placed = (
        P("ep", "et"),
        P("ep", None),
        P("ep", None),
        P(),
        P(),
        P(None, "ep", "et"),
        P(None, "ep", "et"),
        P(None, "ep", "et"),
    )
    return jax.shard_map(
        per_device, mesh=mesh, in_specs=placed, out_specs=P("ep", "et"), check_vma=False
    )
```

```python
import functools

import jax
import jax.numpy as jnp
from jax import lax
from jax.experimental import pallas as pl
from jax.experimental.pallas import tpu as pltpu
from jax.sharding import PartitionSpec as P

LANES = 128
HALF = 64
MIB = 1 << 20


def distinct_sources(old_expert, new_expert):
    slots = old_expert.shape[0]
    index = jnp.arange(slots, dtype=jnp.int32)
    holders = new_expert[:, None] == old_expert[None, :]
    source = jnp.min(jnp.where(holders, index[None, :], slots), axis=1)
    used = jnp.any(source[:, None] == index[None, :], axis=0)
    earlier = (index[None, :] < index[:, None]) & used[None, :]
    place = jnp.sum(earlier.astype(jnp.int32), axis=1)
    count = slots - slots // 8
    wanted = jnp.arange(count, dtype=jnp.int32)
    listing = jnp.sum(
        jnp.where(used[None, :] & (place[None, :] == wanted[:, None]), index[None, :], 0), axis=1
    )
    slot_place = jnp.sum(jnp.where(source[:, None] == index[None, :], place[None, :], 0), axis=1)
    return source, listing, slot_place


def units_of(dest):
    side = dest % 2
    first = (7 * dest + side) // 2
    return first, first + 3 - 4 * side, side


def pack_rows(dest, list_ref, in_ref, lo, rows, out_ref, at, base):
    slabs, depth, width = in_ref.shape
    per_slab = width // LANES
    first, half, side = units_of(dest)

    def unit_rows(unit, start, size):
        lane = pl.multiple_of(unit % per_slab * LANES, LANES)
        return in_ref[list_ref[unit // per_slab], start : start + size, pl.ds(lane, LANES)]

    for number in range(3):
        out_ref[at, base + number * rows : base + (number + 1) * rows, :] = unit_rows(
            first + number, lo, rows
        )
    mid = rows // 2
    top = unit_rows(half, lo, mid).astype(jnp.float32)
    low = unit_rows(half, lo + mid, mid).astype(jnp.float32)
    left = lax.broadcasted_iota(jnp.int32, (mid, LANES), 1) < HALF
    odd = jnp.full((mid, LANES), side, jnp.int32) == 1
    both = jnp.where(
        left,
        jnp.where(odd, pltpu.roll(top, HALF, 1), top),
        jnp.where(odd, low, pltpu.roll(low, HALF, 1)),
    )
    out_ref[at, base + 3 * rows : base + 3 * rows + mid, :] = both.astype(out_ref.dtype)


def pack_kernel(segments, with_terms, list_ref, *refs):
    out_refs = refs[-4:]
    me = list_ref[list_ref.shape[0] - 1]
    for j in range(16):
        dest = (me // 4 ^ j // 4) * 4 + j % 4
        base = 0
        for in_ref, (lo, rows) in zip(refs, segments):
            pack_rows(dest, list_ref, in_ref, lo, rows, out_refs[j // 4], j % 4, base)
            base += rows * 7 // 2
        if with_terms:
            value = refs[len(segments)][dest]
            row = lax.broadcasted_iota(jnp.int32, value.shape, 0) // 4
            high = value.astype(jnp.bfloat16).astype(jnp.float32)
            middle = (value - high).astype(jnp.bfloat16).astype(jnp.float32)
            low = value - high - middle
            terms = jnp.where(row == 0, high, jnp.where(row == 1, middle, low))
            terms = jnp.where(row == 3, 0.0, terms)
            out_refs[j // 4][j % 4, base:, :] = terms.astype(jnp.bfloat16)


def vmem():
    return pl.BlockSpec(memory_space=pltpu.VMEM)


def smem():
    return pl.BlockSpec(memory_space=pltpu.SMEM)


def pack(info, weights, segments, share, name):
    size = sum(rows * 7 // 2 for _, rows in segments)
    more = () if share is None else (share,)
    if more:
        size += share.shape[1]
    return pl.pallas_call(
        functools.partial(pack_kernel, segments, bool(more)),
        out_shape=[jax.ShapeDtypeStruct((4, size, LANES), weights[0].dtype)] * 4,
        in_specs=[smem()] + [vmem()] * (len(weights) + len(more)),
        out_specs=[vmem()] * 4,
        compiler_params=pltpu.CompilerParams(vmem_limit_bytes=32 * MIB),
        name=name,
    )(info, *weights, *more)


def unpack_rows(in_ref, at, rows, out_ref, row):
    row = pl.multiple_of(row, 16)
    for number in range(3):
        out_ref[pl.ds(row, rows), number * LANES : (number + 1) * LANES] = in_ref[
            (*at, slice(number * rows, (number + 1) * rows))
        ]
    mid = rows // 2
    both = in_ref[(*at, slice(3 * rows, 3 * rows + mid))]
    lanes = slice(3 * LANES, 4 * LANES)
    out_ref[pl.ds(row, mid), lanes] = both
    other = pltpu.roll(both.astype(jnp.float32), HALF, 1).astype(out_ref.dtype)
    out_ref[pl.ds(pl.multiple_of(row + mid, 16), mid), lanes] = other


def hidden_kernel(at_ref, x_ref, gate_ref, up_ref, out_ref, gate_w, up_w):
    cores, rows, mid = x_ref.shape
    depth = gate_w.shape[0] // 16
    tile = pl.program_id(0)
    x, y, zl = tile // 4, tile // 2 % 2, tile % 2
    me = at_ref[0]

    @pl.when(tile == 0)
    def _():
        for place in range(4):
            for plane in range(4):
                row = ((me // 4 ^ plane) * 4 + place) * depth
                unpack_rows(gate_ref, (place, plane), depth, gate_w, row)
                unpack_rows(up_ref, (place, plane), depth, up_w, row)

    def product(w_ref):
        return sum(
            jnp.dot(
                x_ref[at], w_ref[at * mid : (at + 1) * mid, :], preferred_element_type=jnp.float32
            )
            for at in range(cores)
        )

    gate = product(gate_w)
    value = gate / (1.0 + jnp.exp(-gate)) * product(up_w)

    wide = gate.shape[1]
    term = lax.broadcasted_iota(jnp.int32, (16, wide), 0)
    lane = lax.broadcasted_iota(jnp.int32, (16, wide), 1)
    chosen = (term % 4 == lane // LANES) & (term < 12) & (lane < wide - HALF)
    chosen = jnp.where(chosen, 1.0, 0.0).astype(jnp.bfloat16)
    block = rows // 2
    terms_at = up_ref.shape[2]
    for zh in range(2):
        weight = lax.dot_general(
            gate_ref[me % 4 ^ (x + 2 * y), zl + 2 * zh, terms_at:, :],
            chosen,
            (((0,), (0,)), ((), ())),
            preferred_element_type=jnp.float32,
        )
        span = slice(zh * block, (zh + 1) * block)
        out_ref[span, :] = (value[span, :] * weight).astype(out_ref.dtype)


def hidden_units(at, rows, gates, ups):
    cores, total, mid = rows.shape
    tile = total // 8
    wide = 4 * LANES
    model = cores * mid
    return pl.pallas_call(
        hidden_kernel,
        grid=(8,),
        out_shape=jax.ShapeDtypeStruct((total, wide), rows.dtype),
        in_specs=[smem(), pl.BlockSpec((cores, tile, mid), lambda i: (0, i, 0)), vmem(), vmem()],
        out_specs=pl.BlockSpec((tile, wide), lambda i: (i, 0)),
        scratch_shapes=[pltpu.VMEM((model, wide), rows.dtype)] * 2,
        compiler_params=pltpu.CompilerParams(vmem_limit_bytes=56 * MIB),
        cost_estimate=pl.CostEstimate(
            flops=4 * total * model * wide, bytes_accessed=24 * MIB, transcendentals=total * wide
        ),
        name="hidden",
    )(at, rows, gates, ups)


THIRDS = ((0, 1, 2), (1, 2, 0), (2, 0, 1))


def group_spans(features, count):
    tiles = features // LANES
    cuts = [-(-tiles * at // count) * LANES for at in range(count + 1)]
    return [slice(lo, hi) for lo, hi in zip(cuts, cuts[1:])]


def stage_axis(order, stage):
    return sum(1 for bit in order[stage:] if bit < order[stage])


def half_spans(rows, axis, side):
    size = rows >> (axis + 1)
    return [slice((2 * at + side) * size, (2 * at + side + 1) * size) for at in range(1 << axis)]


def down_kernel(rows, side, orders, at_ref, own_h, other_h, own_ref, other_ref, *refs):
    out_refs, (own_w, other_w) = refs[:-2], refs[-2:]
    for in_ref, w_ref in ((own_ref, own_w), (other_ref, other_w)):
        for place in range(4):
            for plane in range(2):
                row = ((at_ref[0] // 4 % 2 ^ plane) * 4 + place) * rows
                unpack_rows(in_ref, (place, plane), rows, w_ref, row)
    dims = (((1,), (1,)), ((), ()))
    for number, span in enumerate(group_spans(own_w.shape[0], len(orders))):
        done = 0
        for tokens in half_spans(own_h.shape[0], stage_axis(orders[number], 0), side):
            value = lax.dot_general(
                own_h[tokens, :], own_w[span, :], dims, preferred_element_type=jnp.float32
            ) + lax.dot_general(
                other_h[tokens, :], other_w[span, :], dims, preferred_element_type=jnp.float32
            )
            size = tokens.stop - tokens.start
            out_refs[number][done : done + size, :] = value.astype(out_refs[number].dtype)
            done += size


def down_product(at, own_h, other_h, own, other, rows, side, orders, dtype, name):
    sources = own.shape[0] * own.shape[1]
    total, wide = own_h.shape
    tokens = total // 2
    features = sources * rows
    shapes = [
        jax.ShapeDtypeStruct((tokens, span.stop - span.start), dtype)
        for span in group_spans(features, len(orders))
    ]
    return pl.pallas_call(
        functools.partial(down_kernel, rows, side, orders),
        out_shape=shapes,
        in_specs=[smem()] + [vmem()] * 4,
        out_specs=[vmem()] * len(shapes),
        scratch_shapes=[pltpu.VMEM((features, wide), own.dtype)] * 2,
        compiler_params=pltpu.CompilerParams(vmem_limit_bytes=40 * MIB),
        cost_estimate=pl.CostEstimate(
            flops=4 * tokens * wide * features, bytes_accessed=8 * MIB, transcendentals=0
        ),
        name=name,
    )(at, own_h, other_h, own, other)


def halve_kernel(axes, *refs):
    count = len(refs) // 4 if axes else len(refs) // 2 - 1
    out_refs = refs[2 * count :]
    lane = 0
    for number in range(count):
        keep_ref, come_ref = refs[2 * number : 2 * number + 2]
        if axes:
            send_ref, left_ref = out_refs[2 * number : 2 * number + 2]
            lanes = slice(0, keep_ref.shape[1])
        else:
            send_ref, left_ref = out_refs
            lanes = slice(lane, lane + keep_ref.shape[1])
            lane = lanes.stop
        axis = axes[number] if axes else 0
        for side, out_ref in enumerate((left_ref, send_ref)):
            done = 0
            for rows in half_spans(keep_ref.shape[0], axis, side):
                size = rows.stop - rows.start
                total = keep_ref[rows, :] + come_ref[rows, :].astype(jnp.float32)
                out_ref[done : done + size, lanes] = total.astype(out_ref.dtype)
                done += size


def halve(pairs, axes):
    sizes = [(keep.shape[0] // 2, keep.shape[1]) for keep, _ in pairs]
    if not axes:
        sizes = [(sizes[0][0], sum(width for _, width in sizes))]
    shapes = []
    for size in sizes:
        shapes += [jax.ShapeDtypeStruct(size, jnp.bfloat16), jax.ShapeDtypeStruct(size, jnp.float32)]
    out = pl.pallas_call(
        functools.partial(halve_kernel, axes),
        out_shape=shapes,
        in_specs=[vmem()] * (2 * len(pairs)),
        out_specs=[vmem()] * len(shapes),
        compiler_params=pltpu.CompilerParams(vmem_limit_bytes=40 * MIB),
        cost_estimate=pl.CostEstimate(
            flops=sum(keep.size for keep, _ in pairs), bytes_accessed=4 * MIB, transcendentals=0
        ),
        name="sum_stage",
    )(*[value for pair in pairs for value in pair])
    return [(out[2 * n], out[2 * n + 1]) for n in range(len(out) // 2)]


def swap(value, bit):
    size = lax.axis_size("ep")
    return lax.ppermute(value, "ep", [(i, i ^ (1 << bit)) for i in range(size)])


def gather_bits(value, bits, order, have=()):
    have = list(have)
    for bit in order:
        axis = sum(1 for b in have if b < bit)
        value = jnp.stack([value, swap(value, bit)], axis=axis)
        have.append(bit)
    return value


def take_half(value, axis, number):
    return lax.index_in_dim(value, number, axis, keepdims=False)


def sum_stages(keep, arrived, order, left):
    left = list(left)
    for bit in order:
        axis = left.index(bit)
        total = keep + arrived.astype(jnp.float32)
        arrived = swap(take_half(total, axis, 1).astype(jnp.bfloat16), bit)
        keep = take_half(total, axis, 0)
        left.remove(bit)
    return keep, arrived


def share_of_slots(slot_ids, gate_weights, slots):
    index = jnp.arange(slots, dtype=jnp.int32)
    picked = slot_ids.T[None, :, :] == index[:, None, None]
    return jnp.sum(jnp.where(picked, gate_weights.T[None, :, :], 0.0), axis=1)


def packed_layer(
    tokens, slot_ids, gate_weights, old_expert, new_expert, gate_proj, up_proj, down_proj
):
    devices = lax.axis_size("ep")
    slots, depth, width = gate_proj.shape
    block = tokens.shape[0]
    me = lax.axis_index("ep")
    core = lax.axis_index("et")
    group = devices // 2
    tie = lax.optimization_barrier
    _, listing, slot_place = distinct_sources(old_expert, new_expert)

    def exchange(value):
        return lax.ppermute(value, "et", [(0, 1), (1, 0)])

    def across(value, number):
        return lax.ppermute(value, "ep", [(i, i ^ number) for i in range(devices)])

    def along_z(packed):
        return [packed[0]] + [across(packed[k], 4 * k) for k in (1, 2, 3)]

    planes = [[4 * z + at for at in range(4)] for z in range(devices // 4)]

    def in_plane(blocks):
        blocks = jnp.stack(blocks, axis=1)
        return lax.all_to_all(blocks, "ep", 0, 0, axis_index_groups=planes, tiled=True)

    places = []
    for dest in range(devices):
        first, half, _ = units_of(dest)
        places.append([unit // (width // LANES) for unit in (first, first + 1, first + 2, half)] * 4)
    places = jnp.asarray(places, jnp.int32)
    share = share_of_slots(slot_ids, gate_weights, slots)
    belongs = slot_place[None, None, :, None] == places[:, :, None, None]
    share = jnp.sum(jnp.where(belongs, share[None, None], 0.0), axis=2)

    parts = (128, 96)
    size = depth * 7 // 2
    at = jnp.stack([me, core]).astype(jnp.int32)
    info = jnp.concatenate([listing, at[:1]])

    near, far = swap(tokens, 2), swap(tokens, 3)
    corner = swap(far, 2)
    packed = pack(info, (gate_proj,), ((0, depth),), share, "pack_gate")
    packed, near, far, corner = tie((packed, near, far, corner))

    gate_z = along_z(packed)
    mid = tokens.shape[1] // 2
    rows = jnp.concatenate([tokens, far, near, corner], axis=0)
    rows_a = gather_bits(rows[:, :mid].reshape(2, 2, block, mid), 4, (1,), (2, 3))
    rows_b = gather_bits(rows[:, mid:].reshape(2, 2, block, mid), 4, (0,), (2, 3))
    packed = pack(info, (up_proj,), ((0, depth),), None, "pack_up")
    gate_z, rows_a, rows_b, packed = tie((gate_z, rows_a, rows_b, packed))

    up_z = along_z(packed)
    gates = in_plane(gate_z)
    rows_a = gather_bits(rows_a, 4, (0,), (1, 2, 3)).reshape(-1, mid)
    rows_b = gather_bits(rows_b, 4, (1,), (0, 2, 3)).reshape(-1, mid)
    rows = lax.all_gather(jnp.concatenate([rows_a, rows_b], axis=1), "et")
    packed = pack(info, (down_proj,), ((0, parts[0]),), None, "pack_down")
    up_z, packed = tie((up_z, packed))

    down0_z = along_z(packed)
    ups = in_plane(up_z)
    packed = pack(info, (down_proj,), ((parts[0], parts[1]),), None, "pack_down")
    down0_z, packed = tie((down0_z, packed))

    down1_z = along_z(packed)
    downs0 = in_plane(down0_z)
    hidden = hidden_units(at, rows, gates, ups)
    hidden_other = exchange(hidden)
    downs0, down1_z, hidden = tie((downs0, down1_z, hidden))
    downs1 = in_plane(down1_z)

    def core_half(downs, which):
        start = 2 * (which ^ (me >> 3))
        return lax.dynamic_slice_in_dim(downs, start, 2, 1)

    def products(down, rows_in, orders):
        own, other = core_half(down, core), exchange(core_half(down, 1 - core))
        args = (at, hidden, hidden_other, own, other)
        sent = down_product(*args, rows_in, 1, orders, jnp.bfloat16, "down_send")
        sent, args = tie((sent, args))
        come = [swap(value, order[0]) for value, order in zip(sent, orders)]
        return down_product(*args, rows_in, 0, orders, jnp.float32, "down_keep"), come

    def stage(kept, come, number, orders):
        axes = tuple(stage_axis(order, number) for order in orders)
        out = halve(list(zip(kept, come)), axes)
        come = [swap(send, order[number]) for (send, _), order in zip(out, orders)]
        return [keep for _, keep in out], come

    def last_stage(kept, come):
        ((send, keep),) = halve(list(zip(kept, come)), None)
        come = swap(send, 3)
        return (keep + come.astype(jnp.float32)).astype(jnp.bfloat16)

    kept0, come0 = products(downs0, parts[0], THIRDS)
    downs1, kept0 = tie((downs1, kept0))
    kept1, come1 = products(downs1, parts[1], THIRDS)
    kept0, come0 = stage(kept0, come0, 1, THIRDS)
    kept1, come1 = stage(kept1, come1, 1, THIRDS)
    kept0, come0 = stage(kept0, come0, 2, THIRDS)
    kept1, come1 = stage(kept1, come1, 2, THIRDS)
    out = []
    for rows_in, total in zip(parts, (last_stage(kept0, come0), last_stage(kept1, come1))):
        out.append(total.reshape(block, group, rows_in))
    return jnp.concatenate(out, axis=2).reshape(tokens.shape)


def plain_layer(
    tokens, slot_ids, gate_weights, old_expert, new_expert, gate_proj, up_proj, down_proj
):
    devices = lax.axis_size("ep")
    bits = devices.bit_length() - 1
    slots = gate_proj.shape[0]
    me = lax.axis_index("ep")
    source, _, _ = distinct_sources(old_expert, new_expert)

    def move(weights):
        chosen = jnp.take(weights, source, axis=0, mode="clip")
        return lax.all_to_all(chosen, "ep", 0, 0, tiled=True)

    gate_slab = move(gate_proj).reshape(-1, gate_proj.shape[-1])
    up_slab = move(up_proj).reshape(-1, up_proj.shape[-1])
    down = move(down_proj)
    order = range(bits - 1, -1, -1)
    rows = gather_bits(tokens, bits, order).reshape(-1, tokens.shape[1])
    rows = lax.all_gather(rows, "et", axis=1, tiled=True)
    share = gather_bits(share_of_slots(slot_ids, gate_weights, slots), bits, order)
    share = lax.dynamic_index_in_dim(share, me, bits, keepdims=False).reshape(-1, 1)
    gate_part = jnp.dot(rows, gate_slab, preferred_element_type=jnp.float32)
    up_part = jnp.dot(rows, up_slab, preferred_element_type=jnp.float32)
    hidden = (jax.nn.silu(gate_part) * up_part * share).astype(jnp.bfloat16)
    hidden = lax.all_gather(hidden, "et", axis=1, tiled=True)
    down = lax.all_to_all(down, "et", 0, 2, tiled=True)
    value = lax.dot_general(
        hidden,
        down.reshape(-1, down.shape[-1]),
        (((1,), (1,)), ((), ())),
        preferred_element_type=jnp.float32,
    )
    value = value.reshape((2,) * bits + (-1,) + value.shape[1:])
    arrived = swap(take_half(value, 0, 1).astype(jnp.bfloat16), 0)
    left = list(range(1, bits))
    keep, arrived = sum_stages(take_half(value, 0, 0), arrived, left, left)
    return (keep + arrived.astype(jnp.float32)).astype(jnp.bfloat16)


def per_device(tokens, slot_ids, gate_weights, old_expert, new_expert, gate_proj, up_proj, down_proj):
    slots, depth, width = gate_proj.shape
    count = slots - slots // 8
    devices = lax.axis_size("ep")
    fits = (
        lax.axis_size("et") == 2
        and depth == 224
        and width % LANES == 0
        and count * width == devices * 7 * HALF
        and devices == 16
        and tokens.shape[0] == LANES
    )
    layer = packed_layer if fits else plain_layer
    return layer(
        tokens, slot_ids, gate_weights, old_expert, new_expert, gate_proj, up_proj, down_proj
    )


def solution(mesh):
    placed = (
        P("ep", "et"),
        P("ep", None),
        P("ep", None),
        P(),
        P(),
        P(None, "ep", "et"),
        P(None, "ep", "et"),
        P(None, "ep", "et"),
    )
    return jax.shard_map(
        per_device, mesh=mesh, in_specs=placed, out_specs=P("ep", "et"), check_vma=False
    )
```

```python
import functools

import jax
import jax.numpy as jnp
from jax import lax
from jax.experimental import pallas as pl
from jax.experimental.pallas import tpu as pltpu
from jax.sharding import PartitionSpec as P

LANES = 128
HALF = 64
MIB = 1 << 20


def distinct_sources(old_expert, new_expert):
    slots = old_expert.shape[0]
    index = jnp.arange(slots, dtype=jnp.int32)
    holders = new_expert[:, None] == old_expert[None, :]
    source = jnp.min(jnp.where(holders, index[None, :], slots), axis=1)
    used = jnp.any(source[:, None] == index[None, :], axis=0)
    earlier = (index[None, :] < index[:, None]) & used[None, :]
    place = jnp.sum(earlier.astype(jnp.int32), axis=1)
    count = slots - slots // 8
    wanted = jnp.arange(count, dtype=jnp.int32)
    listing = jnp.sum(
        jnp.where(used[None, :] & (place[None, :] == wanted[:, None]), index[None, :], 0), axis=1
    )
    slot_place = jnp.sum(jnp.where(source[:, None] == index[None, :], place[None, :], 0), axis=1)
    return source, listing, slot_place


def units_of(dest):
    if dest % 2 == 0:
        start = 7 * dest // 2
        return start, start + 3, 0
    start = (7 * dest + 1) // 2
    return start, start - 1, 1


def pack_rows(slab_of, out_ref, base, dest, lo, rows, per_slab):
    first, half, side = units_of(dest)
    for number in range(3):
        unit = first + number
        ref, slab = slab_of(unit // per_slab)
        lane = (unit % per_slab) * LANES
        out_ref[dest, base + number * rows : base + (number + 1) * rows, :] = ref[
            slab, lo : lo + rows, lane : lane + LANES
        ]
    ref, slab = slab_of(half // per_slab)
    lane = (half % per_slab) * LANES
    mid = rows // 2
    top = ref[slab, lo : lo + mid, lane : lane + LANES].astype(jnp.float32)
    low = ref[slab, lo + mid : lo + rows, lane : lane + LANES].astype(jnp.float32)
    left = lax.broadcasted_iota(jnp.int32, (mid, LANES), 1) < HALF
    if side == 0:
        both = jnp.where(left, top, pltpu.roll(low, HALF, 1))
    else:
        both = jnp.where(left, pltpu.roll(top, HALF, 1), low)
    out_ref[dest, base + 3 * rows : base + 3 * rows + mid, :] = both.astype(out_ref.dtype)


def pack_first_kernel(rows, list_ref, gate_ref, up_ref, down_ref, share_ref, out_ref):
    slots, depth, width = gate_ref.shape
    size = depth * 7 // 2
    row = lax.broadcasted_iota(jnp.int32, share_ref.shape[1:], 0) // 4
    for dest in range(out_ref.shape[0]):
        for number, in_ref in enumerate((gate_ref, up_ref)):
            pack_rows(
                lambda place, in_ref=in_ref: (in_ref, list_ref[place]),
                out_ref, number * size, dest, 0, depth, width // LANES,
            )
        pack_rows(
            lambda place: (down_ref, list_ref[place]),
            out_ref, 2 * size, dest, 0, rows, width // LANES,
        )
        value = share_ref[dest]
        high = value.astype(out_ref.dtype)
        rest = value - high.astype(jnp.float32)
        middle = rest.astype(out_ref.dtype)
        low = (rest - middle.astype(jnp.float32)).astype(out_ref.dtype)
        terms = jnp.where(
            row == 0,
            high.astype(jnp.float32),
            jnp.where(
                row == 1,
                middle.astype(jnp.float32),
                jnp.where(row == 2, low.astype(jnp.float32), 0.0),
            ),
        )
        out_ref[dest, 2 * size + rows * 7 // 2 :, :] = terms.astype(out_ref.dtype)


def pack_rest_kernel(rows, list_ref, down_ref, out_ref):
    slots, depth, width = down_ref.shape
    for dest in range(out_ref.shape[0]):
        pack_rows(
            lambda place: (down_ref, list_ref[place]),
            out_ref, 0, dest, rows, depth - rows, width // LANES,
        )


def vmem():
    return pl.BlockSpec(memory_space=pltpu.VMEM)


def smem():
    return pl.BlockSpec(memory_space=pltpu.SMEM)


def pack_first(listing, gate_proj, up_proj, down_proj, rows, share, dests):
    slots, depth, width = gate_proj.shape
    shape = (dests, depth * 7 + rows * 7 // 2 + share.shape[1], LANES)
    return pl.pallas_call(
        functools.partial(pack_first_kernel, rows),
        out_shape=jax.ShapeDtypeStruct(shape, gate_proj.dtype),
        in_specs=[smem(), vmem(), vmem(), vmem(), vmem()],
        out_specs=vmem(),
        compiler_params=pltpu.CompilerParams(vmem_limit_bytes=40 * MIB),
        name="pack_first",
    )(listing, gate_proj, up_proj, down_proj, share)


def pack_rest(listing, down_proj, rows, dests):
    slots, depth, width = down_proj.shape
    shape = (dests, (depth - rows) * 7 // 2, LANES)
    return pl.pallas_call(
        functools.partial(pack_rest_kernel, rows),
        out_shape=jax.ShapeDtypeStruct(shape, down_proj.dtype),
        in_specs=[smem(), vmem()],
        out_specs=vmem(),
        compiler_params=pltpu.CompilerParams(vmem_limit_bytes=32 * MIB),
        name="pack_rest",
    )(listing, down_proj)


def unpack_rows(in_ref, at, base, rows, out_ref, out_row, out_lane):
    for number in range(3):
        out_ref[out_row : out_row + rows, out_lane + number * LANES : out_lane + (number + 1) * LANES] = (
            in_ref[at, base + number * rows : base + (number + 1) * rows, :]
        )
    mid = rows // 2
    both = in_ref[at, base + 3 * rows : base + 3 * rows + mid, :]
    lanes = slice(out_lane + 3 * LANES, out_lane + 4 * LANES)
    out_ref[out_row : out_row + mid, lanes] = both
    out_ref[out_row + mid : out_row + rows, lanes] = pltpu.roll(
        both.astype(jnp.float32), HALF, 1
    ).astype(out_ref.dtype)


def hidden_kernel(at_ref, x_ref, packed_ref, out_ref, gate_w, up_w):
    cores, rows, mid = x_ref.shape
    sources = packed_ref.shape[0]
    depth = gate_w.shape[0] // sources
    size = depth * 7 // 2
    tile = pl.program_id(0)
    x, y, zl = tile // 4, tile // 2 % 2, tile % 2

    @pl.when(tile == 0)
    def _():
        for at in range(sources):
            unpack_rows(packed_ref, at, 0, depth, gate_w, at * depth, 0)
            unpack_rows(packed_ref, at, size, depth, up_w, at * depth, 0)

    def product(w_ref):
        return sum(
            jnp.dot(
                x_ref[at], w_ref[at * mid : (at + 1) * mid, :], preferred_element_type=jnp.float32
            )
            for at in range(cores)
        )

    gate = product(gate_w)
    value = gate / (1.0 + jnp.exp(-gate)) * product(up_w)

    wide = gate.shape[1]
    term = lax.broadcasted_iota(jnp.int32, (16, wide), 0)
    lane = lax.broadcasted_iota(jnp.int32, (16, wide), 1)
    chosen = (term % 4 == lane // LANES) & (term < 12) & (lane < wide - HALF)
    chosen = jnp.where(chosen, 1.0, 0.0).astype(jnp.bfloat16)
    block = rows // 2
    for zh in range(2):
        source = at_ref[0] ^ (x + 2 * y + 4 * zl + 8 * zh)
        weight = lax.dot_general(
            packed_ref[source, packed_ref.shape[1] - 16 :, :],
            chosen,
            (((0,), (0,)), ((), ())),
            preferred_element_type=jnp.float32,
        )
        span = slice(zh * block, (zh + 1) * block)
        out_ref[span, :] = (value[span, :] * weight).astype(out_ref.dtype)


def hidden_units(at, rows, packed):
    cores, total, mid = rows.shape
    tile = total // 8
    wide = 4 * LANES
    model = cores * mid
    return pl.pallas_call(
        hidden_kernel,
        grid=(8,),
        out_shape=jax.ShapeDtypeStruct((total, wide), rows.dtype),
        in_specs=[smem(), pl.BlockSpec((cores, tile, mid), lambda i: (0, i, 0)), vmem()],
        out_specs=pl.BlockSpec((tile, wide), lambda i: (i, 0)),
        scratch_shapes=[pltpu.VMEM((model, wide), rows.dtype)] * 2,
        compiler_params=pltpu.CompilerParams(vmem_limit_bytes=56 * MIB),
        cost_estimate=pl.CostEstimate(
            flops=4 * total * model * wide, bytes_accessed=24 * MIB, transcendentals=total * wide
        ),
        name="hidden",
    )(at, rows, packed)


HALVES = ((0, 1, 2), (1, 0, 2))
THIRDS = ((0, 1, 2), (1, 2, 0), (2, 0, 1))


def group_spans(features, count):
    tiles = features // LANES
    cuts = [-(-tiles * at // count) * LANES for at in range(count + 1)]
    return [slice(lo, hi) for lo, hi in zip(cuts, cuts[1:])]


def stage_axis(order, stage):
    return sum(1 for bit in order[stage:] if bit < order[stage])


def half_spans(rows, axis, side):
    size = rows >> (axis + 1)
    return [slice((2 * at + side) * size, (2 * at + side + 1) * size) for at in range(1 << axis)]


def down_kernel(rows, side, orders, own_h, other_h, own_ref, other_ref, *refs):
    out_refs, (own_w, other_w) = refs[:-2], refs[-2:]
    for in_ref, w_ref in ((own_ref, own_w), (other_ref, other_w)):
        for at in range(in_ref.shape[0]):
            unpack_rows(in_ref, at, 0, rows, w_ref, at * rows, 0)
    dims = (((1,), (1,)), ((), ()))
    for number, span in enumerate(group_spans(own_w.shape[0], len(orders))):
        done = 0
        for tokens in half_spans(own_h.shape[0], stage_axis(orders[number], 0), side):
            value = lax.dot_general(
                own_h[tokens, :], own_w[span, :], dims, preferred_element_type=jnp.float32
            ) + lax.dot_general(
                other_h[tokens, :], other_w[span, :], dims, preferred_element_type=jnp.float32
            )
            size = tokens.stop - tokens.start
            out_refs[number][done : done + size, :] = value.astype(out_refs[number].dtype)
            done += size


def down_product(own_h, other_h, own, other, rows, side, orders, dtype, name):
    sources = own.shape[0]
    total, wide = own_h.shape
    tokens = total // 2
    features = sources * rows
    shapes = [
        jax.ShapeDtypeStruct((tokens, span.stop - span.start), dtype)
        for span in group_spans(features, len(orders))
    ]
    return pl.pallas_call(
        functools.partial(down_kernel, rows, side, orders),
        out_shape=shapes,
        in_specs=[vmem()] * 4,
        out_specs=[vmem()] * len(shapes),
        scratch_shapes=[pltpu.VMEM((features, wide), own.dtype)] * 2,
        compiler_params=pltpu.CompilerParams(vmem_limit_bytes=40 * MIB),
        cost_estimate=pl.CostEstimate(
            flops=4 * tokens * wide * features, bytes_accessed=8 * MIB, transcendentals=0
        ),
        name=name,
    )(own_h, other_h, own, other)


def halve_kernel(axes, *refs):
    count = len(refs) // 4 if axes else len(refs) // 2 - 1
    out_refs = refs[2 * count :]
    lane = 0
    for number in range(count):
        keep_ref, come_ref = refs[2 * number : 2 * number + 2]
        if axes:
            send_ref, left_ref = out_refs[2 * number : 2 * number + 2]
            lanes = slice(0, keep_ref.shape[1])
        else:
            send_ref, left_ref = out_refs
            lanes = slice(lane, lane + keep_ref.shape[1])
            lane = lanes.stop
        axis = axes[number] if axes else 0
        for side, out_ref in enumerate((left_ref, send_ref)):
            done = 0
            for rows in half_spans(keep_ref.shape[0], axis, side):
                size = rows.stop - rows.start
                total = keep_ref[rows, :] + come_ref[rows, :].astype(jnp.float32)
                out_ref[done : done + size, lanes] = total.astype(out_ref.dtype)
                done += size


def halve(pairs, axes):
    sizes = [(keep.shape[0] // 2, keep.shape[1]) for keep, _ in pairs]
    if not axes:
        sizes = [(sizes[0][0], sum(width for _, width in sizes))]
    shapes = []
    for size in sizes:
        shapes += [jax.ShapeDtypeStruct(size, jnp.bfloat16), jax.ShapeDtypeStruct(size, jnp.float32)]
    out = pl.pallas_call(
        functools.partial(halve_kernel, axes),
        out_shape=shapes,
        in_specs=[vmem()] * (2 * len(pairs)),
        out_specs=[vmem()] * len(shapes),
        compiler_params=pltpu.CompilerParams(vmem_limit_bytes=40 * MIB),
        cost_estimate=pl.CostEstimate(
            flops=sum(keep.size for keep, _ in pairs), bytes_accessed=4 * MIB, transcendentals=0
        ),
        name="sum_stage",
    )(*[value for pair in pairs for value in pair])
    return [(out[2 * n], out[2 * n + 1]) for n in range(len(out) // 2)]


def swap(value, bit):
    size = lax.axis_size("ep")
    return lax.ppermute(value, "ep", [(i, i ^ (1 << bit)) for i in range(size)])


def gather_bits(value, bits, order, have=()):
    have = list(have)
    for bit in order:
        axis = sum(1 for b in have if b < bit)
        value = jnp.stack([value, swap(value, bit)], axis=axis)
        have.append(bit)
    return value


def take_half(value, axis, number):
    return lax.index_in_dim(value, number, axis, keepdims=False)


def sum_stages(keep, arrived, order, left):
    left = list(left)
    for bit in order:
        axis = left.index(bit)
        total = keep + arrived.astype(jnp.float32)
        arrived = swap(take_half(total, axis, 1).astype(jnp.bfloat16), bit)
        keep = take_half(total, axis, 0)
        left.remove(bit)
    return keep, arrived


def share_of_slots(slot_ids, gate_weights, slots):
    index = jnp.arange(slots, dtype=jnp.int32)
    picked = slot_ids.T[None, :, :] == index[:, None, None]
    return jnp.sum(jnp.where(picked, gate_weights.T[None, :, :], 0.0), axis=1)


def packed_layer(
    tokens, slot_ids, gate_weights, old_expert, new_expert, gate_proj, up_proj, down_proj
):
    devices = lax.axis_size("ep")
    slots, depth, width = gate_proj.shape
    block = tokens.shape[0]
    me = lax.axis_index("ep")
    core = lax.axis_index("et")
    group = devices // 2
    tie = lax.optimization_barrier
    _, listing, slot_place = distinct_sources(old_expert, new_expert)

    def exchange(value):
        return lax.ppermute(value, "et", [(0, 1), (1, 0)])

    def move(packed):
        return lax.all_to_all(packed, "ep", 0, 0, tiled=True)

    places = []
    for dest in range(devices):
        first, half, _ = units_of(dest)
        places.append([unit // (width // LANES) for unit in (first, first + 1, first + 2, half)] * 4)
    places = jnp.asarray(places, jnp.int32)
    share = share_of_slots(slot_ids, gate_weights, slots)
    belongs = slot_place[None, None, :, None] == places[:, :, None, None]
    share = jnp.sum(jnp.where(belongs, share[None, None], 0.0), axis=2)

    mid = tokens.shape[1] // 2
    first, second = slice(0, mid), slice(mid, 2 * mid)

    def lay(*values):
        return jnp.concatenate(values, axis=0)

    parts = (128, 96)
    packed = pack_first(listing, gate_proj, up_proj, down_proj, parts[0], share, devices)
    far_a, far_b = swap(tokens[:, first], 3), swap(tokens[:, second], 3)
    near = swap(tokens, 2)
    far_a, packed = tie((far_a, packed))
    corner_a, corner_b = swap(far_a, 2), swap(far_b, 2)
    pair_a, pair_b = lay(far_a, near[:, first]), lay(far_b, near[:, second])
    pair_y, pair_x = swap(pair_a, 1), swap(pair_b, 0)
    packed, pair_a, pair_b, corner_a, corner_b, pair_y, pair_x = tie(
        (packed, pair_a, pair_b, corner_a, corner_b, pair_y, pair_x)
    )

    moved = move(packed)
    column_a = lay(tokens[:, first], pair_a, corner_a)
    column_b = lay(tokens[:, second], pair_b, corner_b)
    ends_a, ends_b = lay(tokens[:, first], corner_a), lay(tokens[:, second], corner_b)
    most_a, most_b = swap(lay(column_a, pair_y), 0), swap(lay(column_b, pair_x), 1)
    ends_y, ends_x = swap(ends_a, 1), swap(ends_b, 0)
    cross = jnp.concatenate([ends_a, ends_b], axis=1)
    cross = lax.ppermute(cross, "ep", [(i, i ^ 3) for i in range(devices)])
    top, low = slice(0, block), slice(block, 2 * block)
    four, rest_two = slice(0, 4 * block), slice(4 * block, 6 * block)
    y_side = lay(ends_y[top], pair_y, ends_y[low])
    x_side = lay(ends_x[top], pair_x, ends_x[low])
    cross_a = lay(cross[top, first], most_a[rest_two], cross[low, first])
    cross_b = lay(cross[top, second], most_b[rest_two], cross[low, second])
    rows = jnp.concatenate(
        [
            lay(column_a, y_side, most_a[four], cross_a),
            lay(column_b, most_b[four], x_side, cross_b),
        ],
        axis=1,
    )
    rows = lax.all_gather(rows, "et")
    rest = pack_rest(listing, down_proj, parts[0], devices)
    moved, rest, rows = tie((moved, rest, rows))

    down1 = move(rest)
    at = jnp.stack([me, core]).astype(jnp.int32)
    hidden = hidden_units(at, rows, moved)
    hidden_other = exchange(hidden)
    down0 = moved[:, depth * 7 : depth * 7 + parts[0] * 7 // 2]

    def slivers(down):
        own = lax.dynamic_slice_in_dim(down, core * group, group, 0)
        return own, exchange(lax.dynamic_slice_in_dim(down, (1 - core) * group, group, 0))

    def product(weights, rows_in, side, orders, after=None):
        args, _ = tie(((hidden, hidden_other, *weights), after))
        kind = ((jnp.float32, "down_keep"), (jnp.bfloat16, "down_send"))[side]
        return down_product(*args, rows_in, side, orders, *kind)

    def send(values, orders):
        return [swap(value, order[0]) for value, order in zip(values, orders)]

    def stage(kept, come, number, orders):
        axes = tuple(stage_axis(order, number) for order in orders)
        out = halve(list(zip(kept, come)), axes)
        come = [swap(send, order[number]) for (send, _), order in zip(out, orders)]
        return [keep for _, keep in out], come

    def last_stage(kept, come):
        ((send, keep),) = halve(list(zip(kept, come)), None)
        come = swap(send, 3)
        return (keep + come.astype(jnp.float32)).astype(jnp.bfloat16)

    weights0 = slivers(down0)
    sent0 = product(weights0, parts[0], 1, HALVES)
    come0 = send(sent0, HALVES)
    weights1 = slivers(tie((down1, sent0))[0])
    sent1 = product(weights1, parts[1], 1, THIRDS)
    come1 = send(sent1, THIRDS)
    kept0 = product(weights0, parts[0], 0, HALVES, after=sent1)
    kept1 = product(weights1, parts[1], 0, THIRDS, after=sent1)
    kept0, come0 = stage(kept0, come0, 1, HALVES)
    kept1, come1 = stage(kept1, come1, 1, THIRDS)
    kept0, come0 = stage(kept0, come0, 2, HALVES)
    kept1, come1 = stage(kept1, come1, 2, THIRDS)
    out = []
    for rows_in, total in zip(parts, (last_stage(kept0, come0), last_stage(kept1, come1))):
        out.append(total.reshape(block, group, rows_in))
    return jnp.concatenate(out, axis=2).reshape(tokens.shape)


def plain_layer(
    tokens, slot_ids, gate_weights, old_expert, new_expert, gate_proj, up_proj, down_proj
):
    devices = lax.axis_size("ep")
    bits = devices.bit_length() - 1
    slots = gate_proj.shape[0]
    me = lax.axis_index("ep")
    source, _, _ = distinct_sources(old_expert, new_expert)

    def move(weights):
        chosen = jnp.take(weights, source, axis=0, mode="clip")
        return lax.all_to_all(chosen, "ep", 0, 0, tiled=True)

    gate_slab = move(gate_proj).reshape(-1, gate_proj.shape[-1])
    up_slab = move(up_proj).reshape(-1, up_proj.shape[-1])
    down = move(down_proj)
    order = range(bits - 1, -1, -1)
    rows = gather_bits(tokens, bits, order).reshape(-1, tokens.shape[1])
    rows = lax.all_gather(rows, "et", axis=1, tiled=True)
    share = gather_bits(share_of_slots(slot_ids, gate_weights, slots), bits, order)
    share = lax.dynamic_index_in_dim(share, me, bits, keepdims=False).reshape(-1, 1)
    gate_part = jnp.dot(rows, gate_slab, preferred_element_type=jnp.float32)
    up_part = jnp.dot(rows, up_slab, preferred_element_type=jnp.float32)
    hidden = (jax.nn.silu(gate_part) * up_part * share).astype(jnp.bfloat16)
    hidden = lax.all_gather(hidden, "et", axis=1, tiled=True)
    down = lax.all_to_all(down, "et", 0, 2, tiled=True)
    value = lax.dot_general(
        hidden,
        down.reshape(-1, down.shape[-1]),
        (((1,), (1,)), ((), ())),
        preferred_element_type=jnp.float32,
    )
    value = value.reshape((2,) * bits + (-1,) + value.shape[1:])
    arrived = swap(take_half(value, 0, 1).astype(jnp.bfloat16), 0)
    left = list(range(1, bits))
    keep, arrived = sum_stages(take_half(value, 0, 0), arrived, left, left)
    return (keep + arrived.astype(jnp.float32)).astype(jnp.bfloat16)


def per_device(tokens, slot_ids, gate_weights, old_expert, new_expert, gate_proj, up_proj, down_proj):
    slots, depth, width = gate_proj.shape
    count = slots - slots // 8
    devices = lax.axis_size("ep")
    fits = (
        lax.axis_size("et") == 2
        and depth == 224
        and width % LANES == 0
        and count * width == devices * 7 * HALF
        and devices == 16
        and tokens.shape[0] == LANES
    )
    layer = packed_layer if fits else plain_layer
    return layer(
        tokens, slot_ids, gate_weights, old_expert, new_expert, gate_proj, up_proj, down_proj
    )


def solution(mesh):
    placed = (
        P("ep", "et"),
        P("ep", None),
        P("ep", None),
        P(),
        P(),
        P(None, "ep", "et"),
        P(None, "ep", "et"),
        P(None, "ep", "et"),
    )
    return jax.shard_map(
        per_device, mesh=mesh, in_specs=placed, out_specs=P("ep", "et"), check_vma=False
    )
```

```python
import functools

import jax
import jax.numpy as jnp
from jax import lax
from jax.experimental import pallas as pl
from jax.experimental.pallas import tpu as pltpu
from jax.sharding import PartitionSpec as P

LANES = 128
HALF = 64
MIB = 1 << 20


def distinct_sources(old_expert, new_expert):
    slots = old_expert.shape[0]
    index = jnp.arange(slots, dtype=jnp.int32)
    holders = new_expert[:, None] == old_expert[None, :]
    source = jnp.min(jnp.where(holders, index[None, :], slots), axis=1)
    used = jnp.any(source[:, None] == index[None, :], axis=0)
    earlier = (index[None, :] < index[:, None]) & used[None, :]
    place = jnp.sum(earlier.astype(jnp.int32), axis=1)
    count = slots - slots // 8
    wanted = jnp.arange(count, dtype=jnp.int32)
    listing = jnp.sum(
        jnp.where(used[None, :] & (place[None, :] == wanted[:, None]), index[None, :], 0), axis=1
    )
    slot_place = jnp.sum(jnp.where(source[:, None] == index[None, :], place[None, :], 0), axis=1)
    return source, listing, slot_place


def units_of(dest):
    if dest % 2 == 0:
        start = 7 * dest // 2
        return start, start + 3, 0
    start = (7 * dest + 1) // 2
    return start, start - 1, 1


def pack_rows(slab_of, out_ref, base, dest, lo, rows, per_slab):
    first, half, side = units_of(dest)
    for number in range(3):
        unit = first + number
        ref, slab = slab_of(unit // per_slab)
        lane = (unit % per_slab) * LANES
        out_ref[dest, base + number * rows : base + (number + 1) * rows, :] = ref[
            slab, lo : lo + rows, lane : lane + LANES
        ]
    ref, slab = slab_of(half // per_slab)
    lane = (half % per_slab) * LANES
    mid = rows // 2
    top = ref[slab, lo : lo + mid, lane : lane + LANES].astype(jnp.float32)
    low = ref[slab, lo + mid : lo + rows, lane : lane + LANES].astype(jnp.float32)
    left = lax.broadcasted_iota(jnp.int32, (mid, LANES), 1) < HALF
    if side == 0:
        both = jnp.where(left, top, pltpu.roll(low, HALF, 1))
    else:
        both = jnp.where(left, pltpu.roll(top, HALF, 1), low)
    out_ref[dest, base + 3 * rows : base + 3 * rows + mid, :] = both.astype(out_ref.dtype)


def pack_first_kernel(rows, list_ref, gate_ref, up_ref, down_ref, share_ref, out_ref):
    slots, depth, width = gate_ref.shape
    size = depth * 7 // 2
    row = lax.broadcasted_iota(jnp.int32, share_ref.shape[1:], 0) // 4
    for dest in range(out_ref.shape[0]):
        for number, in_ref in enumerate((gate_ref, up_ref)):
            pack_rows(
                lambda place, in_ref=in_ref: (in_ref, list_ref[place]),
                out_ref, number * size, dest, 0, depth, width // LANES,
            )
        pack_rows(
            lambda place: (down_ref, list_ref[place]),
            out_ref, 2 * size, dest, 0, rows, width // LANES,
        )
        value = share_ref[dest]
        high = value.astype(out_ref.dtype)
        rest = value - high.astype(jnp.float32)
        middle = rest.astype(out_ref.dtype)
        low = (rest - middle.astype(jnp.float32)).astype(out_ref.dtype)
        terms = jnp.where(
            row == 0,
            high.astype(jnp.float32),
            jnp.where(
                row == 1,
                middle.astype(jnp.float32),
                jnp.where(row == 2, low.astype(jnp.float32), 0.0),
            ),
        )
        out_ref[dest, 2 * size + rows * 7 // 2 :, :] = terms.astype(out_ref.dtype)


def pack_rest_kernel(rows, list_ref, down_ref, out_ref):
    slots, depth, width = down_ref.shape
    for dest in range(out_ref.shape[0]):
        pack_rows(
            lambda place: (down_ref, list_ref[place]),
            out_ref, 0, dest, rows, depth - rows, width // LANES,
        )


def vmem():
    return pl.BlockSpec(memory_space=pltpu.VMEM)


def smem():
    return pl.BlockSpec(memory_space=pltpu.SMEM)


def pack_first(listing, gate_proj, up_proj, down_proj, rows, share, dests):
    slots, depth, width = gate_proj.shape
    shape = (dests, depth * 7 + rows * 7 // 2 + share.shape[1], LANES)
    return pl.pallas_call(
        functools.partial(pack_first_kernel, rows),
        out_shape=jax.ShapeDtypeStruct(shape, gate_proj.dtype),
        in_specs=[smem(), vmem(), vmem(), vmem(), vmem()],
        out_specs=vmem(),
        compiler_params=pltpu.CompilerParams(vmem_limit_bytes=40 * MIB),
        name="pack_first",
    )(listing, gate_proj, up_proj, down_proj, share)


def pack_rest(listing, down_proj, rows, dests):
    slots, depth, width = down_proj.shape
    shape = (dests, (depth - rows) * 7 // 2, LANES)
    return pl.pallas_call(
        functools.partial(pack_rest_kernel, rows),
        out_shape=jax.ShapeDtypeStruct(shape, down_proj.dtype),
        in_specs=[smem(), vmem()],
        out_specs=vmem(),
        compiler_params=pltpu.CompilerParams(vmem_limit_bytes=32 * MIB),
        name="pack_rest",
    )(listing, down_proj)


def unpack_rows(in_ref, at, base, rows, out_ref, out_row, out_lane):
    for number in range(3):
        out_ref[out_row : out_row + rows, out_lane + number * LANES : out_lane + (number + 1) * LANES] = (
            in_ref[at, base + number * rows : base + (number + 1) * rows, :]
        )
    mid = rows // 2
    both = in_ref[at, base + 3 * rows : base + 3 * rows + mid, :]
    lanes = slice(out_lane + 3 * LANES, out_lane + 4 * LANES)
    out_ref[out_row : out_row + mid, lanes] = both
    out_ref[out_row + mid : out_row + rows, lanes] = pltpu.roll(
        both.astype(jnp.float32), HALF, 1
    ).astype(out_ref.dtype)


def hidden_kernel(at_ref, own_ref, other_ref, packed_ref, out_ref, gate_w, up_w):
    rows, mid = own_ref.shape
    sources = packed_ref.shape[0]
    depth = gate_w.shape[0] // sources
    size = depth * 7 // 2
    tile = pl.program_id(0)
    x, y, zl = tile // 4, tile // 2 % 2, tile % 2

    @pl.when(tile == 0)
    def _():
        for at in range(sources):
            place = at_ref[1] * (sources // 2) ^ at
            unpack_rows(packed_ref, place, 0, depth, gate_w, at * depth, 0)
            unpack_rows(packed_ref, place, size, depth, up_w, at * depth, 0)

    def product(w_ref):
        return jnp.dot(
            own_ref[...], w_ref[:mid, :], preferred_element_type=jnp.float32
        ) + jnp.dot(other_ref[...], w_ref[mid:, :], preferred_element_type=jnp.float32)

    gate = product(gate_w)
    value = gate / (1.0 + jnp.exp(-gate)) * product(up_w)

    wide = gate.shape[1]
    term = lax.broadcasted_iota(jnp.int32, (16, wide), 0)
    lane = lax.broadcasted_iota(jnp.int32, (16, wide), 1)
    chosen = (term % 4 == lane // LANES) & (term < 12) & (lane < wide - HALF)
    chosen = jnp.where(chosen, 1.0, 0.0).astype(jnp.bfloat16)
    block = rows // 2
    for zh in range(2):
        source = at_ref[0] ^ (x + 2 * y + 4 * zl + 8 * zh)
        weight = lax.dot_general(
            packed_ref[source, packed_ref.shape[1] - 16 :, :],
            chosen,
            (((0,), (0,)), ((), ())),
            preferred_element_type=jnp.float32,
        )
        span = slice(zh * block, (zh + 1) * block)
        out_ref[span, :] = (value[span, :] * weight).astype(out_ref.dtype)


def hidden_units(at, own, other, packed):
    total, mid = own.shape
    tile = total // 8
    wide = 4 * LANES
    model = 2 * mid
    return pl.pallas_call(
        hidden_kernel,
        grid=(8,),
        out_shape=jax.ShapeDtypeStruct((total, wide), own.dtype),
        in_specs=[smem()] + [pl.BlockSpec((tile, mid), lambda i: (i, 0))] * 2 + [vmem()],
        out_specs=pl.BlockSpec((tile, wide), lambda i: (i, 0)),
        scratch_shapes=[pltpu.VMEM((model, wide), own.dtype)] * 2,
        compiler_params=pltpu.CompilerParams(vmem_limit_bytes=56 * MIB),
        cost_estimate=pl.CostEstimate(
            flops=4 * total * model * wide, bytes_accessed=24 * MIB, transcendentals=total * wide
        ),
        name="hidden",
    )(at, own, other, packed)


HALVES = ((0, 1, 2), (1, 0, 2))
THIRDS = ((0, 1, 2), (1, 2, 0), (2, 0, 1))


def group_spans(features, count):
    tiles = features // LANES
    cuts = [-(-tiles * at // count) * LANES for at in range(count + 1)]
    return [slice(lo, hi) for lo, hi in zip(cuts, cuts[1:])]


def stage_axis(order, stage):
    return sum(1 for bit in order[stage:] if bit < order[stage])


def half_spans(rows, axis, side):
    size = rows >> (axis + 1)
    return [slice((2 * at + side) * size, (2 * at + side + 1) * size) for at in range(1 << axis)]


def down_kernel(rows, side, orders, own_h, other_h, own_ref, other_ref, *refs):
    out_refs, (own_w, other_w) = refs[:-2], refs[-2:]
    for in_ref, w_ref in ((own_ref, own_w), (other_ref, other_w)):
        for at in range(in_ref.shape[0]):
            unpack_rows(in_ref, at, 0, rows, w_ref, at * rows, 0)
    dims = (((1,), (1,)), ((), ()))
    for number, span in enumerate(group_spans(own_w.shape[0], len(orders))):
        done = 0
        for tokens in half_spans(own_h.shape[0], stage_axis(orders[number], 0), side):
            value = lax.dot_general(
                own_h[tokens, :], own_w[span, :], dims, preferred_element_type=jnp.float32
            ) + lax.dot_general(
                other_h[tokens, :], other_w[span, :], dims, preferred_element_type=jnp.float32
            )
            size = tokens.stop - tokens.start
            out_refs[number][done : done + size, :] = value.astype(out_refs[number].dtype)
            done += size


def down_product(own_h, other_h, own, other, rows, side, orders, dtype, name):
    sources = own.shape[0]
    total, wide = own_h.shape
    tokens = total // 2
    features = sources * rows
    shapes = [
        jax.ShapeDtypeStruct((tokens, span.stop - span.start), dtype)
        for span in group_spans(features, len(orders))
    ]
    return pl.pallas_call(
        functools.partial(down_kernel, rows, side, orders),
        out_shape=shapes,
        in_specs=[vmem()] * 4,
        out_specs=[vmem()] * len(shapes),
        scratch_shapes=[pltpu.VMEM((features, wide), own.dtype)] * 2,
        compiler_params=pltpu.CompilerParams(vmem_limit_bytes=40 * MIB),
        cost_estimate=pl.CostEstimate(
            flops=4 * tokens * wide * features, bytes_accessed=8 * MIB, transcendentals=0
        ),
        name=name,
    )(own_h, other_h, own, other)


def halve_kernel(axes, *refs):
    count = len(refs) // 4 if axes else len(refs) // 2 - 1
    out_refs = refs[2 * count :]
    lane = 0
    for number in range(count):
        keep_ref, come_ref = refs[2 * number : 2 * number + 2]
        if axes:
            send_ref, left_ref = out_refs[2 * number : 2 * number + 2]
            lanes = slice(0, keep_ref.shape[1])
        else:
            send_ref, left_ref = out_refs
            lanes = slice(lane, lane + keep_ref.shape[1])
            lane = lanes.stop
        axis = axes[number] if axes else 0
        for side, out_ref in enumerate((left_ref, send_ref)):
            done = 0
            for rows in half_spans(keep_ref.shape[0], axis, side):
                size = rows.stop - rows.start
                total = keep_ref[rows, :] + come_ref[rows, :].astype(jnp.float32)
                out_ref[done : done + size, lanes] = total.astype(out_ref.dtype)
                done += size


def halve(pairs, axes):
    sizes = [(keep.shape[0] // 2, keep.shape[1]) for keep, _ in pairs]
    if not axes:
        sizes = [(sizes[0][0], sum(width for _, width in sizes))]
    shapes = []
    for size in sizes:
        shapes += [jax.ShapeDtypeStruct(size, jnp.bfloat16), jax.ShapeDtypeStruct(size, jnp.float32)]
    out = pl.pallas_call(
        functools.partial(halve_kernel, axes),
        out_shape=shapes,
        in_specs=[vmem()] * (2 * len(pairs)),
        out_specs=[vmem()] * len(shapes),
        compiler_params=pltpu.CompilerParams(vmem_limit_bytes=40 * MIB),
        cost_estimate=pl.CostEstimate(
            flops=sum(keep.size for keep, _ in pairs), bytes_accessed=4 * MIB, transcendentals=0
        ),
        name="sum_stage",
    )(*[value for pair in pairs for value in pair])
    return [(out[2 * n], out[2 * n + 1]) for n in range(len(out) // 2)]


def swap(value, bit):
    size = lax.axis_size("ep")
    return lax.ppermute(value, "ep", [(i, i ^ (1 << bit)) for i in range(size)])


def gather_bits(value, bits, order, have=()):
    have = list(have)
    for bit in order:
        axis = sum(1 for b in have if b < bit)
        value = jnp.stack([value, swap(value, bit)], axis=axis)
        have.append(bit)
    return value


def take_half(value, axis, number):
    return lax.index_in_dim(value, number, axis, keepdims=False)


def sum_stages(keep, arrived, order, left):
    left = list(left)
    for bit in order:
        axis = left.index(bit)
        total = keep + arrived.astype(jnp.float32)
        arrived = swap(take_half(total, axis, 1).astype(jnp.bfloat16), bit)
        keep = take_half(total, axis, 0)
        left.remove(bit)
    return keep, arrived


def share_of_slots(slot_ids, gate_weights, slots):
    index = jnp.arange(slots, dtype=jnp.int32)
    picked = slot_ids.T[None, :, :] == index[:, None, None]
    return jnp.sum(jnp.where(picked, gate_weights.T[None, :, :], 0.0), axis=1)


def packed_layer(
    tokens, slot_ids, gate_weights, old_expert, new_expert, gate_proj, up_proj, down_proj
):
    devices = lax.axis_size("ep")
    slots, depth, width = gate_proj.shape
    block = tokens.shape[0]
    me = lax.axis_index("ep")
    core = lax.axis_index("et")
    group = devices // 2
    tie = lax.optimization_barrier
    _, listing, slot_place = distinct_sources(old_expert, new_expert)

    def exchange(value):
        return lax.ppermute(value, "et", [(0, 1), (1, 0)])

    def move(packed):
        return lax.all_to_all(packed, "ep", 0, 0, tiled=True)

    places = []
    for dest in range(devices):
        first, half, _ = units_of(dest)
        places.append([unit // (width // LANES) for unit in (first, first + 1, first + 2, half)] * 4)
    places = jnp.asarray(places, jnp.int32)
    share = share_of_slots(slot_ids, gate_weights, slots)
    belongs = slot_place[None, None, :, None] == places[:, :, None, None]
    share = jnp.sum(jnp.where(belongs, share[None, None], 0.0), axis=2)

    def diagonal(value):
        return lax.ppermute(value, "ep", [(i, i ^ 3) for i in range(devices)])

    mid = tokens.shape[1] // 2
    near, far = swap(tokens, 2), swap(tokens, 3)
    x_own, y_own = swap(tokens, 0), swap(tokens, 1)
    parts = (128, 96)
    packed = pack_first(listing, gate_proj, up_proj, down_proj, parts[0], share, devices)
    far, packed = tie((far, packed))
    corner = swap(far, 2)
    pair = jnp.concatenate([far, near], axis=0)
    pair_y, pair_x = swap(pair[:, :mid], 1), swap(pair[:, mid:], 0)
    packed, x_own, y_own, pair, corner, pair_y, pair_x = tie(
        (packed, x_own, y_own, pair, corner, pair_y, pair_x)
    )

    moved = move(packed)
    corner_a, corner_b = corner[:, :mid], corner[:, mid:]
    cross = diagonal(jnp.concatenate([tokens, corner], axis=0))
    most_a = swap(jnp.concatenate([pair[:, :mid], corner_a, pair_y], axis=0), 0)
    most_b = swap(jnp.concatenate([pair[:, mid:], corner_b, pair_x], axis=0), 1)
    corner_y, corner_x = swap(corner_a, 1), swap(corner_b, 0)

    def lay(*values):
        return jnp.concatenate(values, axis=0)

    three, two = slice(0, 3 * block), slice(3 * block, 5 * block)
    top, low = slice(0, block), slice(block, 2 * block)
    first, second = slice(0, mid), slice(mid, 2 * mid)
    rows = jnp.concatenate(
        [
            lay(
                tokens[:, first], pair[:, first], corner_a,
                y_own[:, first], pair_y, corner_y,
                x_own[:, first], most_a[three],
                cross[top, first], most_a[two], cross[low, first],
            ),
            lay(
                tokens[:, second], pair[:, second], corner_b,
                y_own[:, second], most_b[three],
                x_own[:, second], pair_x, corner_x,
                cross[top, second], most_b[two], cross[low, second],
            ),
        ],
        axis=1,
    )
    rows_other = exchange(rows)
    rest = pack_rest(listing, down_proj, parts[0], devices)
    moved, rest, rows, rows_other = tie((moved, rest, rows, rows_other))

    down1 = move(rest)
    at = jnp.stack([me, core]).astype(jnp.int32)
    hidden = hidden_units(at, rows, rows_other, moved)
    hidden_other = exchange(hidden)
    down0 = moved[:, depth * 7 : depth * 7 + parts[0] * 7 // 2]

    def products(down, rows_in, orders):
        own = lax.dynamic_slice_in_dim(down, core * group, group, 0)
        other = exchange(lax.dynamic_slice_in_dim(down, (1 - core) * group, group, 0))
        args = (hidden, hidden_other, own, other)
        sent = down_product(*args, rows_in, 1, orders, jnp.bfloat16, "down_send")
        sent, args = tie((sent, args))
        come = [swap(value, order[0]) for value, order in zip(sent, orders)]
        kept = down_product(*args, rows_in, 0, orders, jnp.float32, "down_keep")
        return kept, come

    def stage(kept, come, number, orders):
        axes = tuple(stage_axis(order, number) for order in orders)
        out = halve(list(zip(kept, come)), axes)
        come = [swap(send, order[number]) for (send, _), order in zip(out, orders)]
        return [keep for _, keep in out], come

    def last_stage(kept, come):
        ((send, keep),) = halve(list(zip(kept, come)), None)
        come = swap(send, 3)
        return (keep + come.astype(jnp.float32)).astype(jnp.bfloat16)

    kept0, come0 = products(down0, parts[0], HALVES)
    down1, kept0 = tie((down1, kept0))
    kept1, come1 = products(down1, parts[1], THIRDS)
    kept0, come0 = stage(kept0, come0, 1, HALVES)
    kept1, come1 = stage(kept1, come1, 1, THIRDS)
    kept0, come0 = stage(kept0, come0, 2, HALVES)
    kept1, come1 = stage(kept1, come1, 2, THIRDS)
    out = []
    for rows_in, total in zip(parts, (last_stage(kept0, come0), last_stage(kept1, come1))):
        out.append(total.reshape(block, group, rows_in))
    return jnp.concatenate(out, axis=2).reshape(tokens.shape)


def plain_layer(
    tokens, slot_ids, gate_weights, old_expert, new_expert, gate_proj, up_proj, down_proj
):
    devices = lax.axis_size("ep")
    bits = devices.bit_length() - 1
    slots = gate_proj.shape[0]
    me = lax.axis_index("ep")
    source, _, _ = distinct_sources(old_expert, new_expert)

    def move(weights):
        chosen = jnp.take(weights, source, axis=0, mode="clip")
        return lax.all_to_all(chosen, "ep", 0, 0, tiled=True)

    gate_slab = move(gate_proj).reshape(-1, gate_proj.shape[-1])
    up_slab = move(up_proj).reshape(-1, up_proj.shape[-1])
    down = move(down_proj)
    order = range(bits - 1, -1, -1)
    rows = gather_bits(tokens, bits, order).reshape(-1, tokens.shape[1])
    rows = lax.all_gather(rows, "et", axis=1, tiled=True)
    share = gather_bits(share_of_slots(slot_ids, gate_weights, slots), bits, order)
    share = lax.dynamic_index_in_dim(share, me, bits, keepdims=False).reshape(-1, 1)
    gate_part = jnp.dot(rows, gate_slab, preferred_element_type=jnp.float32)
    up_part = jnp.dot(rows, up_slab, preferred_element_type=jnp.float32)
    hidden = (jax.nn.silu(gate_part) * up_part * share).astype(jnp.bfloat16)
    hidden = lax.all_gather(hidden, "et", axis=1, tiled=True)
    down = lax.all_to_all(down, "et", 0, 2, tiled=True)
    value = lax.dot_general(
        hidden,
        down.reshape(-1, down.shape[-1]),
        (((1,), (1,)), ((), ())),
        preferred_element_type=jnp.float32,
    )
    value = value.reshape((2,) * bits + (-1,) + value.shape[1:])
    arrived = swap(take_half(value, 0, 1).astype(jnp.bfloat16), 0)
    left = list(range(1, bits))
    keep, arrived = sum_stages(take_half(value, 0, 0), arrived, left, left)
    return (keep + arrived.astype(jnp.float32)).astype(jnp.bfloat16)


def per_device(tokens, slot_ids, gate_weights, old_expert, new_expert, gate_proj, up_proj, down_proj):
    slots, depth, width = gate_proj.shape
    count = slots - slots // 8
    devices = lax.axis_size("ep")
    fits = (
        lax.axis_size("et") == 2
        and depth == 224
        and width % LANES == 0
        and count * width == devices * 7 * HALF
        and devices == 16
        and tokens.shape[0] == LANES
    )
    layer = packed_layer if fits else plain_layer
    return layer(
        tokens, slot_ids, gate_weights, old_expert, new_expert, gate_proj, up_proj, down_proj
    )


def solution(mesh):
    placed = (
        P("ep", "et"),
        P("ep", None),
        P("ep", None),
        P(),
        P(),
        P(None, "ep", "et"),
        P(None, "ep", "et"),
        P(None, "ep", "et"),
    )
    return jax.shard_map(
        per_device, mesh=mesh, in_specs=placed, out_specs=P("ep", "et"), check_vma=False
    )
```

```python
import functools

import jax
import jax.numpy as jnp
from jax import lax
from jax.experimental import pallas as pl
from jax.experimental.pallas import tpu as pltpu
from jax.sharding import PartitionSpec as P

LANES = 128
HALF = 64
MIB = 1 << 20


def distinct_sources(old_expert, new_expert):
    slots = old_expert.shape[0]
    index = jnp.arange(slots, dtype=jnp.int32)
    holders = new_expert[:, None] == old_expert[None, :]
    source = jnp.min(jnp.where(holders, index[None, :], slots), axis=1)
    used = jnp.any(source[:, None] == index[None, :], axis=0)
    earlier = (index[None, :] < index[:, None]) & used[None, :]
    place = jnp.sum(earlier.astype(jnp.int32), axis=1)
    count = slots - slots // 8
    wanted = jnp.arange(count, dtype=jnp.int32)
    listing = jnp.sum(
        jnp.where(used[None, :] & (place[None, :] == wanted[:, None]), index[None, :], 0), axis=1
    )
    slot_place = jnp.sum(jnp.where(source[:, None] == index[None, :], place[None, :], 0), axis=1)
    return source, listing, slot_place


def units_of(dest):
    if dest % 2 == 0:
        start = 7 * dest // 2
        return start, start + 3, 0
    start = (7 * dest + 1) // 2
    return start, start - 1, 1


def pack_rows(slab_of, out_ref, base, dest, lo, rows, per_slab):
    first, half, side = units_of(dest)
    for number in range(3):
        unit = first + number
        ref, slab = slab_of(unit // per_slab)
        lane = (unit % per_slab) * LANES
        out_ref[dest, base + number * rows : base + (number + 1) * rows, :] = ref[
            slab, lo : lo + rows, lane : lane + LANES
        ]
    ref, slab = slab_of(half // per_slab)
    lane = (half % per_slab) * LANES
    mid = rows // 2
    top = ref[slab, lo : lo + mid, lane : lane + LANES].astype(jnp.float32)
    low = ref[slab, lo + mid : lo + rows, lane : lane + LANES].astype(jnp.float32)
    left = lax.broadcasted_iota(jnp.int32, (mid, LANES), 1) < HALF
    if side == 0:
        both = jnp.where(left, top, pltpu.roll(low, HALF, 1))
    else:
        both = jnp.where(left, pltpu.roll(top, HALF, 1), low)
    out_ref[dest, base + 3 * rows : base + 3 * rows + mid, :] = both.astype(out_ref.dtype)


def pack_first_kernel(rows, list_ref, gate_ref, up_ref, down_ref, share_ref, out_ref):
    slots, depth, width = gate_ref.shape
    size = depth * 7 // 2
    row = lax.broadcasted_iota(jnp.int32, share_ref.shape[1:], 0) // 4
    for dest in range(out_ref.shape[0]):
        for number, in_ref in enumerate((gate_ref, up_ref)):
            pack_rows(
                lambda place, in_ref=in_ref: (in_ref, list_ref[place]),
                out_ref, number * size, dest, 0, depth, width // LANES,
            )
        pack_rows(
            lambda place: (down_ref, list_ref[place]),
            out_ref, 2 * size, dest, 0, rows, width // LANES,
        )
        value = share_ref[dest]
        high = value.astype(out_ref.dtype)
        rest = value - high.astype(jnp.float32)
        middle = rest.astype(out_ref.dtype)
        low = (rest - middle.astype(jnp.float32)).astype(out_ref.dtype)
        terms = jnp.where(
            row == 0,
            high.astype(jnp.float32),
            jnp.where(
                row == 1,
                middle.astype(jnp.float32),
                jnp.where(row == 2, low.astype(jnp.float32), 0.0),
            ),
        )
        out_ref[dest, 2 * size + rows * 7 // 2 :, :] = terms.astype(out_ref.dtype)


def pack_rest_kernel(rows, list_ref, down_ref, out_ref):
    slots, depth, width = down_ref.shape
    for dest in range(out_ref.shape[0]):
        pack_rows(
            lambda place: (down_ref, list_ref[place]),
            out_ref, 0, dest, rows, depth - rows, width // LANES,
        )


def vmem():
    return pl.BlockSpec(memory_space=pltpu.VMEM)


def smem():
    return pl.BlockSpec(memory_space=pltpu.SMEM)


def pack_first(listing, gate_proj, up_proj, down_proj, rows, share, dests):
    slots, depth, width = gate_proj.shape
    shape = (dests, depth * 7 + rows * 7 // 2 + share.shape[1], LANES)
    return pl.pallas_call(
        functools.partial(pack_first_kernel, rows),
        out_shape=jax.ShapeDtypeStruct(shape, gate_proj.dtype),
        in_specs=[smem(), vmem(), vmem(), vmem(), vmem()],
        out_specs=vmem(),
        compiler_params=pltpu.CompilerParams(vmem_limit_bytes=40 * MIB),
        name="pack_first",
    )(listing, gate_proj, up_proj, down_proj, share)


def pack_rest(listing, down_proj, rows, dests):
    slots, depth, width = down_proj.shape
    shape = (dests, (depth - rows) * 7 // 2, LANES)
    return pl.pallas_call(
        functools.partial(pack_rest_kernel, rows),
        out_shape=jax.ShapeDtypeStruct(shape, down_proj.dtype),
        in_specs=[smem(), vmem()],
        out_specs=vmem(),
        compiler_params=pltpu.CompilerParams(vmem_limit_bytes=32 * MIB),
        name="pack_rest",
    )(listing, down_proj)


def unpack_rows(in_ref, at, base, rows, out_ref, out_row, out_lane):
    for number in range(3):
        out_ref[out_row : out_row + rows, out_lane + number * LANES : out_lane + (number + 1) * LANES] = (
            in_ref[at, base + number * rows : base + (number + 1) * rows, :]
        )
    mid = rows // 2
    both = in_ref[at, base + 3 * rows : base + 3 * rows + mid, :]
    lanes = slice(out_lane + 3 * LANES, out_lane + 4 * LANES)
    out_ref[out_row : out_row + mid, lanes] = both
    out_ref[out_row + mid : out_row + rows, lanes] = pltpu.roll(
        both.astype(jnp.float32), HALF, 1
    ).astype(out_ref.dtype)


def hidden_kernel(at_ref, own_ref, other_ref, packed_ref, out_ref, gate_w, up_w):
    rows, mid = own_ref.shape
    sources = packed_ref.shape[0]
    depth = gate_w.shape[0] // sources
    size = depth * 7 // 2
    tile = pl.program_id(0)
    x, y, zl = tile // 4, tile // 2 % 2, tile % 2

    @pl.when(tile == 0)
    def _():
        for at in range(sources):
            place = at_ref[1] * (sources // 2) ^ at
            unpack_rows(packed_ref, place, 0, depth, gate_w, at * depth, 0)
            unpack_rows(packed_ref, place, size, depth, up_w, at * depth, 0)

    def product(w_ref):
        return jnp.dot(
            own_ref[...], w_ref[:mid, :], preferred_element_type=jnp.float32
        ) + jnp.dot(other_ref[...], w_ref[mid:, :], preferred_element_type=jnp.float32)

    gate = product(gate_w)
    value = gate / (1.0 + jnp.exp(-gate)) * product(up_w)

    wide = gate.shape[1]
    term = lax.broadcasted_iota(jnp.int32, (16, wide), 0)
    lane = lax.broadcasted_iota(jnp.int32, (16, wide), 1)
    chosen = (term % 4 == lane // LANES) & (term < 12) & (lane < wide - HALF)
    chosen = jnp.where(chosen, 1.0, 0.0).astype(jnp.bfloat16)
    block = rows // 2
    for zh in range(2):
        source = at_ref[0] ^ (x + 2 * y + 4 * zl + 8 * zh)
        weight = lax.dot_general(
            packed_ref[source, packed_ref.shape[1] - 16 :, :],
            chosen,
            (((0,), (0,)), ((), ())),
            preferred_element_type=jnp.float32,
        )
        span = slice(zh * block, (zh + 1) * block)
        out_ref[span, :] = (value[span, :] * weight).astype(out_ref.dtype)


def hidden_units(at, own, other, packed):
    total, mid = own.shape
    tile = total // 8
    wide = 4 * LANES
    model = 2 * mid
    return pl.pallas_call(
        hidden_kernel,
        grid=(8,),
        out_shape=jax.ShapeDtypeStruct((total, wide), own.dtype),
        in_specs=[smem()] + [pl.BlockSpec((tile, mid), lambda i: (i, 0))] * 2 + [vmem()],
        out_specs=pl.BlockSpec((tile, wide), lambda i: (i, 0)),
        scratch_shapes=[pltpu.VMEM((model, wide), own.dtype)] * 2,
        compiler_params=pltpu.CompilerParams(vmem_limit_bytes=56 * MIB),
        cost_estimate=pl.CostEstimate(
            flops=4 * total * model * wide, bytes_accessed=24 * MIB, transcendentals=total * wide
        ),
        name="hidden",
    )(at, own, other, packed)


THIRDS = ((0, 1, 2), (1, 2, 0), (2, 0, 1))


def group_spans(features, count):
    tiles = features // LANES
    cuts = [-(-tiles * at // count) * LANES for at in range(count + 1)]
    return [slice(lo, hi) for lo, hi in zip(cuts, cuts[1:])]


def stage_axis(order, stage):
    return sum(1 for bit in order[stage:] if bit < order[stage])


def half_spans(rows, axis, side):
    size = rows >> (axis + 1)
    return [slice((2 * at + side) * size, (2 * at + side + 1) * size) for at in range(1 << axis)]


def down_kernel(rows, side, orders, own_h, other_h, own_ref, other_ref, *refs):
    out_refs, (own_w, other_w) = refs[:-2], refs[-2:]
    for in_ref, w_ref in ((own_ref, own_w), (other_ref, other_w)):
        for at in range(in_ref.shape[0]):
            unpack_rows(in_ref, at, 0, rows, w_ref, at * rows, 0)
    dims = (((1,), (1,)), ((), ()))
    for number, span in enumerate(group_spans(own_w.shape[0], len(orders))):
        done = 0
        for tokens in half_spans(own_h.shape[0], stage_axis(orders[number], 0), side):
            value = lax.dot_general(
                own_h[tokens, :], own_w[span, :], dims, preferred_element_type=jnp.float32
            ) + lax.dot_general(
                other_h[tokens, :], other_w[span, :], dims, preferred_element_type=jnp.float32
            )
            size = tokens.stop - tokens.start
            out_refs[number][done : done + size, :] = value.astype(out_refs[number].dtype)
            done += size


def down_product(own_h, other_h, own, other, rows, side, orders, dtype, name):
    sources = own.shape[0]
    total, wide = own_h.shape
    tokens = total // 2
    features = sources * rows
    shapes = [
        jax.ShapeDtypeStruct((tokens, span.stop - span.start), dtype)
        for span in group_spans(features, len(orders))
    ]
    return pl.pallas_call(
        functools.partial(down_kernel, rows, side, orders),
        out_shape=shapes,
        in_specs=[vmem()] * 4,
        out_specs=[vmem()] * len(shapes),
        scratch_shapes=[pltpu.VMEM((features, wide), own.dtype)] * 2,
        compiler_params=pltpu.CompilerParams(vmem_limit_bytes=40 * MIB),
        cost_estimate=pl.CostEstimate(
            flops=4 * tokens * wide * features, bytes_accessed=8 * MIB, transcendentals=0
        ),
        name=name,
    )(own_h, other_h, own, other)


def halve_kernel(axes, *refs):
    count = len(refs) // 4 if axes else len(refs) // 2 - 1
    out_refs = refs[2 * count :]
    lane = 0
    for number in range(count):
        keep_ref, come_ref = refs[2 * number : 2 * number + 2]
        if axes:
            send_ref, left_ref = out_refs[2 * number : 2 * number + 2]
            lanes = slice(0, keep_ref.shape[1])
        else:
            send_ref, left_ref = out_refs
            lanes = slice(lane, lane + keep_ref.shape[1])
            lane = lanes.stop
        axis = axes[number] if axes else 0
        for side, out_ref in enumerate((left_ref, send_ref)):
            done = 0
            for rows in half_spans(keep_ref.shape[0], axis, side):
                size = rows.stop - rows.start
                total = keep_ref[rows, :] + come_ref[rows, :].astype(jnp.float32)
                out_ref[done : done + size, lanes] = total.astype(out_ref.dtype)
                done += size


def halve(pairs, axes):
    sizes = [(keep.shape[0] // 2, keep.shape[1]) for keep, _ in pairs]
    if not axes:
        sizes = [(sizes[0][0], sum(width for _, width in sizes))]
    shapes = []
    for size in sizes:
        shapes += [jax.ShapeDtypeStruct(size, jnp.bfloat16), jax.ShapeDtypeStruct(size, jnp.float32)]
    out = pl.pallas_call(
        functools.partial(halve_kernel, axes),
        out_shape=shapes,
        in_specs=[vmem()] * (2 * len(pairs)),
        out_specs=[vmem()] * len(shapes),
        compiler_params=pltpu.CompilerParams(vmem_limit_bytes=40 * MIB),
        cost_estimate=pl.CostEstimate(
            flops=sum(keep.size for keep, _ in pairs), bytes_accessed=4 * MIB, transcendentals=0
        ),
        name="sum_stage",
    )(*[value for pair in pairs for value in pair])
    return [(out[2 * n], out[2 * n + 1]) for n in range(len(out) // 2)]


def swap(value, bit):
    size = lax.axis_size("ep")
    return lax.ppermute(value, "ep", [(i, i ^ (1 << bit)) for i in range(size)])


def gather_bits(value, bits, order, have=()):
    have = list(have)
    for bit in order:
        axis = sum(1 for b in have if b < bit)
        value = jnp.stack([value, swap(value, bit)], axis=axis)
        have.append(bit)
    return value


def take_half(value, axis, number):
    return lax.index_in_dim(value, number, axis, keepdims=False)


def sum_stages(keep, arrived, order, left):
    left = list(left)
    for bit in order:
        axis = left.index(bit)
        total = keep + arrived.astype(jnp.float32)
        arrived = swap(take_half(total, axis, 1).astype(jnp.bfloat16), bit)
        keep = take_half(total, axis, 0)
        left.remove(bit)
    return keep, arrived


def share_of_slots(slot_ids, gate_weights, slots):
    index = jnp.arange(slots, dtype=jnp.int32)
    picked = slot_ids.T[None, :, :] == index[:, None, None]
    return jnp.sum(jnp.where(picked, gate_weights.T[None, :, :], 0.0), axis=1)


def packed_layer(
    tokens, slot_ids, gate_weights, old_expert, new_expert, gate_proj, up_proj, down_proj
):
    devices = lax.axis_size("ep")
    slots, depth, width = gate_proj.shape
    block = tokens.shape[0]
    me = lax.axis_index("ep")
    core = lax.axis_index("et")
    group = devices // 2
    tie = lax.optimization_barrier
    _, listing, slot_place = distinct_sources(old_expert, new_expert)

    def exchange(value):
        return lax.ppermute(value, "et", [(0, 1), (1, 0)])

    def move(packed):
        return lax.all_to_all(packed, "ep", 0, 0, tiled=True)

    places = []
    for dest in range(devices):
        first, half, _ = units_of(dest)
        places.append([unit // (width // LANES) for unit in (first, first + 1, first + 2, half)] * 4)
    places = jnp.asarray(places, jnp.int32)
    share = share_of_slots(slot_ids, gate_weights, slots)
    belongs = slot_place[None, None, :, None] == places[:, :, None, None]
    share = jnp.sum(jnp.where(belongs, share[None, None], 0.0), axis=2)

    def diagonal(value):
        return lax.ppermute(value, "ep", [(i, i ^ 3) for i in range(devices)])

    mid = tokens.shape[1] // 2
    near, far = swap(tokens, 2), swap(tokens, 3)
    x_own, y_own, xy_own = swap(tokens, 0), swap(tokens, 1), diagonal(tokens)
    parts = (128, 96)
    packed = pack_first(listing, gate_proj, up_proj, down_proj, parts[0], share, devices)
    far, packed = tie((far, packed))
    corner = swap(far, 2)
    pair = jnp.concatenate([far, near], axis=0)
    pair_y, pair_x = swap(pair[:, :mid], 1), swap(pair[:, mid:], 0)
    packed, x_own, y_own, xy_own, pair, corner, pair_y, pair_x = tie(
        (packed, x_own, y_own, xy_own, pair, corner, pair_y, pair_x)
    )

    moved = move(packed)
    corner_a, corner_b = corner[:, :mid], corner[:, mid:]
    cross = diagonal(corner)
    most_a = swap(jnp.concatenate([pair[:, :mid], corner_a, pair_y], axis=0), 0)
    most_b = swap(jnp.concatenate([pair[:, mid:], corner_b, pair_x], axis=0), 1)
    corner_y, corner_x = swap(corner_a, 1), swap(corner_b, 0)

    def lay(*values):
        return jnp.concatenate(values, axis=0)

    three, two = slice(0, 3 * block), slice(3 * block, 5 * block)
    first, second = slice(0, mid), slice(mid, 2 * mid)
    rows = jnp.concatenate(
        [
            lay(
                tokens[:, first], pair[:, first], corner_a,
                y_own[:, first], pair_y, corner_y,
                x_own[:, first], most_a[three],
                xy_own[:, first], most_a[two], cross[:, first],
            ),
            lay(
                tokens[:, second], pair[:, second], corner_b,
                y_own[:, second], most_b[three],
                x_own[:, second], pair_x, corner_x,
                xy_own[:, second], most_b[two], cross[:, second],
            ),
        ],
        axis=1,
    )
    rows_other = exchange(rows)
    rest = pack_rest(listing, down_proj, parts[0], devices)
    moved, rest, rows, rows_other = tie((moved, rest, rows, rows_other))

    down1 = move(rest)
    at = jnp.stack([me, core]).astype(jnp.int32)
    hidden = hidden_units(at, rows, rows_other, moved)
    hidden_other = exchange(hidden)
    down0 = moved[:, depth * 7 : depth * 7 + parts[0] * 7 // 2]

    def products(down, rows_in, orders, before=None):
        own = lax.dynamic_slice_in_dim(down, core * group, group, 0)
        other = exchange(lax.dynamic_slice_in_dim(down, (1 - core) * group, group, 0))
        args = (hidden, hidden_other, own, other)
        sent = down_product(*args, rows_in, 1, orders, jnp.bfloat16, "down_send")
        sent, args = tie((sent, args))
        come = [swap(value, order[0]) for value, order in zip(sent, orders)]
        args, _ = tie((args, before))
        kept = down_product(*args, rows_in, 0, orders, jnp.float32, "down_keep")
        return kept, come

    def stage(kept, come, number, orders):
        axes = tuple(stage_axis(order, number) for order in orders)
        out = halve(list(zip(kept, come)), axes)
        come = [swap(send, order[number]) for (send, _), order in zip(out, orders)]
        return [keep for _, keep in out], come

    def last_stage(kept, come):
        ((send, keep),) = halve(list(zip(kept, come)), None)
        come = swap(send, 3)
        return (keep + come.astype(jnp.float32)).astype(jnp.bfloat16)

    kept0, come0 = products(down0, parts[0], THIRDS)
    down1, kept0 = tie((down1, kept0))
    kept1, come1 = products(down1, parts[1], THIRDS, before=come0)
    kept0, come0 = stage(kept0, come0, 1, THIRDS)
    kept1, come1 = stage(kept1, come1, 1, THIRDS)
    kept0, come0 = stage(kept0, come0, 2, THIRDS)
    kept1, come1 = stage(kept1, come1, 2, THIRDS)
    out = []
    for rows_in, total in zip(parts, (last_stage(kept0, come0), last_stage(kept1, come1))):
        out.append(total.reshape(block, group, rows_in))
    return jnp.concatenate(out, axis=2).reshape(tokens.shape)


def plain_layer(
    tokens, slot_ids, gate_weights, old_expert, new_expert, gate_proj, up_proj, down_proj
):
    devices = lax.axis_size("ep")
    bits = devices.bit_length() - 1
    slots = gate_proj.shape[0]
    me = lax.axis_index("ep")
    source, _, _ = distinct_sources(old_expert, new_expert)

    def move(weights):
        chosen = jnp.take(weights, source, axis=0, mode="clip")
        return lax.all_to_all(chosen, "ep", 0, 0, tiled=True)

    gate_slab = move(gate_proj).reshape(-1, gate_proj.shape[-1])
    up_slab = move(up_proj).reshape(-1, up_proj.shape[-1])
    down = move(down_proj)
    order = range(bits - 1, -1, -1)
    rows = gather_bits(tokens, bits, order).reshape(-1, tokens.shape[1])
    rows = lax.all_gather(rows, "et", axis=1, tiled=True)
    share = gather_bits(share_of_slots(slot_ids, gate_weights, slots), bits, order)
    share = lax.dynamic_index_in_dim(share, me, bits, keepdims=False).reshape(-1, 1)
    gate_part = jnp.dot(rows, gate_slab, preferred_element_type=jnp.float32)
    up_part = jnp.dot(rows, up_slab, preferred_element_type=jnp.float32)
    hidden = (jax.nn.silu(gate_part) * up_part * share).astype(jnp.bfloat16)
    hidden = lax.all_gather(hidden, "et", axis=1, tiled=True)
    down = lax.all_to_all(down, "et", 0, 2, tiled=True)
    value = lax.dot_general(
        hidden,
        down.reshape(-1, down.shape[-1]),
        (((1,), (1,)), ((), ())),
        preferred_element_type=jnp.float32,
    )
    value = value.reshape((2,) * bits + (-1,) + value.shape[1:])
    arrived = swap(take_half(value, 0, 1).astype(jnp.bfloat16), 0)
    left = list(range(1, bits))
    keep, arrived = sum_stages(take_half(value, 0, 0), arrived, left, left)
    return (keep + arrived.astype(jnp.float32)).astype(jnp.bfloat16)


def per_device(tokens, slot_ids, gate_weights, old_expert, new_expert, gate_proj, up_proj, down_proj):
    slots, depth, width = gate_proj.shape
    count = slots - slots // 8
    devices = lax.axis_size("ep")
    fits = (
        lax.axis_size("et") == 2
        and depth == 224
        and width % LANES == 0
        and count * width == devices * 7 * HALF
        and devices == 16
        and tokens.shape[0] == LANES
    )
    layer = packed_layer if fits else plain_layer
    return layer(
        tokens, slot_ids, gate_weights, old_expert, new_expert, gate_proj, up_proj, down_proj
    )


def solution(mesh):
    placed = (
        P("ep", "et"),
        P("ep", None),
        P("ep", None),
        P(),
        P(),
        P(None, "ep", "et"),
        P(None, "ep", "et"),
        P(None, "ep", "et"),
    )
    return jax.shard_map(
        per_device, mesh=mesh, in_specs=placed, out_specs=P("ep", "et"), check_vma=False
    )
```

```python
import functools

import jax
import jax.numpy as jnp
from jax import lax
from jax.experimental import pallas as pl
from jax.experimental.pallas import tpu as pltpu
from jax.sharding import PartitionSpec as P

LANES = 128
HALF = 64
MIB = 1 << 20


def distinct_sources(old_expert, new_expert):
    slots = old_expert.shape[0]
    index = jnp.arange(slots, dtype=jnp.int32)
    holders = new_expert[:, None] == old_expert[None, :]
    source = jnp.min(jnp.where(holders, index[None, :], slots), axis=1)
    used = jnp.any(source[:, None] == index[None, :], axis=0)
    earlier = (index[None, :] < index[:, None]) & used[None, :]
    place = jnp.sum(earlier.astype(jnp.int32), axis=1)
    count = slots - slots // 8
    wanted = jnp.arange(count, dtype=jnp.int32)
    listing = jnp.sum(
        jnp.where(used[None, :] & (place[None, :] == wanted[:, None]), index[None, :], 0), axis=1
    )
    slot_place = jnp.sum(jnp.where(source[:, None] == index[None, :], place[None, :], 0), axis=1)
    return source, listing, slot_place


def units_of(dest):
    if dest % 2 == 0:
        start = 7 * dest // 2
        return start, start + 3, 0
    start = (7 * dest + 1) // 2
    return start, start - 1, 1


def pack_rows(slab_of, out_ref, base, dest, lo, rows, per_slab):
    first, half, side = units_of(dest)
    for number in range(3):
        unit = first + number
        ref, slab = slab_of(unit // per_slab)
        lane = (unit % per_slab) * LANES
        out_ref[dest, base + number * rows : base + (number + 1) * rows, :] = ref[
            slab, lo : lo + rows, lane : lane + LANES
        ]
    ref, slab = slab_of(half // per_slab)
    lane = (half % per_slab) * LANES
    mid = rows // 2
    top = ref[slab, lo : lo + mid, lane : lane + LANES].astype(jnp.float32)
    low = ref[slab, lo + mid : lo + rows, lane : lane + LANES].astype(jnp.float32)
    left = lax.broadcasted_iota(jnp.int32, (mid, LANES), 1) < HALF
    if side == 0:
        both = jnp.where(left, top, pltpu.roll(low, HALF, 1))
    else:
        both = jnp.where(left, pltpu.roll(top, HALF, 1), low)
    out_ref[dest, base + 3 * rows : base + 3 * rows + mid, :] = both.astype(out_ref.dtype)


def pack_first_kernel(rows, list_ref, gate_ref, up_ref, down_ref, share_ref, out_ref):
    slots, depth, width = gate_ref.shape
    size = depth * 7 // 2
    row = lax.broadcasted_iota(jnp.int32, share_ref.shape[1:], 0) // 4
    for dest in range(out_ref.shape[0]):
        for number, in_ref in enumerate((gate_ref, up_ref)):
            pack_rows(
                lambda place, in_ref=in_ref: (in_ref, list_ref[place]),
                out_ref, number * size, dest, 0, depth, width // LANES,
            )
        pack_rows(
            lambda place: (down_ref, list_ref[place]),
            out_ref, 2 * size, dest, 0, rows, width // LANES,
        )
        value = share_ref[dest]
        high = value.astype(out_ref.dtype)
        rest = value - high.astype(jnp.float32)
        middle = rest.astype(out_ref.dtype)
        low = (rest - middle.astype(jnp.float32)).astype(out_ref.dtype)
        terms = jnp.where(
            row == 0,
            high.astype(jnp.float32),
            jnp.where(
                row == 1,
                middle.astype(jnp.float32),
                jnp.where(row == 2, low.astype(jnp.float32), 0.0),
            ),
        )
        out_ref[dest, 2 * size + rows * 7 // 2 :, :] = terms.astype(out_ref.dtype)


def pack_rest_kernel(rows, list_ref, down_ref, out_ref):
    slots, depth, width = down_ref.shape
    for dest in range(out_ref.shape[0]):
        pack_rows(
            lambda place: (down_ref, list_ref[place]),
            out_ref, 0, dest, rows, depth - rows, width // LANES,
        )


def vmem():
    return pl.BlockSpec(memory_space=pltpu.VMEM)


def smem():
    return pl.BlockSpec(memory_space=pltpu.SMEM)


def pack_first(listing, gate_proj, up_proj, down_proj, rows, share, dests):
    slots, depth, width = gate_proj.shape
    shape = (dests, depth * 7 + rows * 7 // 2 + share.shape[1], LANES)
    return pl.pallas_call(
        functools.partial(pack_first_kernel, rows),
        out_shape=jax.ShapeDtypeStruct(shape, gate_proj.dtype),
        in_specs=[smem(), vmem(), vmem(), vmem(), vmem()],
        out_specs=vmem(),
        compiler_params=pltpu.CompilerParams(vmem_limit_bytes=40 * MIB),
        name="pack_first",
    )(listing, gate_proj, up_proj, down_proj, share)


def pack_rest(listing, down_proj, rows, dests):
    slots, depth, width = down_proj.shape
    shape = (dests, (depth - rows) * 7 // 2, LANES)
    return pl.pallas_call(
        functools.partial(pack_rest_kernel, rows),
        out_shape=jax.ShapeDtypeStruct(shape, down_proj.dtype),
        in_specs=[smem(), vmem()],
        out_specs=vmem(),
        compiler_params=pltpu.CompilerParams(vmem_limit_bytes=32 * MIB),
        name="pack_rest",
    )(listing, down_proj)


def unpack_rows(in_ref, at, base, rows, out_ref, out_row, out_lane):
    for number in range(3):
        out_ref[out_row : out_row + rows, out_lane + number * LANES : out_lane + (number + 1) * LANES] = (
            in_ref[at, base + number * rows : base + (number + 1) * rows, :]
        )
    mid = rows // 2
    both = in_ref[at, base + 3 * rows : base + 3 * rows + mid, :]
    lanes = slice(out_lane + 3 * LANES, out_lane + 4 * LANES)
    out_ref[out_row : out_row + mid, lanes] = both
    out_ref[out_row + mid : out_row + rows, lanes] = pltpu.roll(
        both.astype(jnp.float32), HALF, 1
    ).astype(out_ref.dtype)


def hidden_kernel(at_ref, own_ref, other_ref, packed_ref, out_ref, gate_w, up_w):
    rows, mid = own_ref.shape
    sources = packed_ref.shape[0]
    depth = gate_w.shape[0] // sources
    size = depth * 7 // 2
    tile = pl.program_id(0)
    x, y, zl = tile // 4, tile // 2 % 2, tile % 2

    @pl.when(tile == 0)
    def _():
        for at in range(sources):
            place = at_ref[1] * (sources // 2) ^ at
            unpack_rows(packed_ref, place, 0, depth, gate_w, at * depth, 0)
            unpack_rows(packed_ref, place, size, depth, up_w, at * depth, 0)

    def product(w_ref):
        return jnp.dot(
            own_ref[...], w_ref[:mid, :], preferred_element_type=jnp.float32
        ) + jnp.dot(other_ref[...], w_ref[mid:, :], preferred_element_type=jnp.float32)

    gate = product(gate_w)
    value = gate / (1.0 + jnp.exp(-gate)) * product(up_w)

    wide = gate.shape[1]
    term = lax.broadcasted_iota(jnp.int32, (16, wide), 0)
    lane = lax.broadcasted_iota(jnp.int32, (16, wide), 1)
    chosen = (term % 4 == lane // LANES) & (term < 12) & (lane < wide - HALF)
    chosen = jnp.where(chosen, 1.0, 0.0).astype(jnp.bfloat16)
    block = rows // 2
    for zh in range(2):
        source = at_ref[0] ^ (x + 2 * y + 4 * zl + 8 * zh)
        weight = lax.dot_general(
            packed_ref[source, packed_ref.shape[1] - 16 :, :],
            chosen,
            (((0,), (0,)), ((), ())),
            preferred_element_type=jnp.float32,
        )
        span = slice(zh * block, (zh + 1) * block)
        out_ref[span, :] = (value[span, :] * weight).astype(out_ref.dtype)


def hidden_units(at, own, other, packed):
    total, mid = own.shape
    tile = total // 8
    wide = 4 * LANES
    model = 2 * mid
    return pl.pallas_call(
        hidden_kernel,
        grid=(8,),
        out_shape=jax.ShapeDtypeStruct((total, wide), own.dtype),
        in_specs=[smem()] + [pl.BlockSpec((tile, mid), lambda i: (i, 0))] * 2 + [vmem()],
        out_specs=pl.BlockSpec((tile, wide), lambda i: (i, 0)),
        scratch_shapes=[pltpu.VMEM((model, wide), own.dtype)] * 2,
        compiler_params=pltpu.CompilerParams(vmem_limit_bytes=56 * MIB),
        cost_estimate=pl.CostEstimate(
            flops=4 * total * model * wide, bytes_accessed=24 * MIB, transcendentals=total * wide
        ),
        name="hidden",
    )(at, own, other, packed)


THIRDS = ((0, 1, 2), (1, 2, 0), (2, 0, 1))


def group_spans(features, count):
    tiles = features // LANES
    cuts = [-(-tiles * at // count) * LANES for at in range(count + 1)]
    return [slice(lo, hi) for lo, hi in zip(cuts, cuts[1:])]


def stage_axis(order, stage):
    return sum(1 for bit in order[stage:] if bit < order[stage])


def half_spans(rows, axis, side):
    size = rows >> (axis + 1)
    return [slice((2 * at + side) * size, (2 * at + side + 1) * size) for at in range(1 << axis)]


def down_kernel(rows, side, orders, own_h, other_h, own_ref, other_ref, *refs):
    out_refs, (own_w, other_w) = refs[:-2], refs[-2:]
    for in_ref, w_ref in ((own_ref, own_w), (other_ref, other_w)):
        for at in range(in_ref.shape[0]):
            unpack_rows(in_ref, at, 0, rows, w_ref, at * rows, 0)
    dims = (((1,), (1,)), ((), ()))
    for number, span in enumerate(group_spans(own_w.shape[0], len(orders))):
        done = 0
        for tokens in half_spans(own_h.shape[0], stage_axis(orders[number], 0), side):
            value = lax.dot_general(
                own_h[tokens, :], own_w[span, :], dims, preferred_element_type=jnp.float32
            ) + lax.dot_general(
                other_h[tokens, :], other_w[span, :], dims, preferred_element_type=jnp.float32
            )
            size = tokens.stop - tokens.start
            out_refs[number][done : done + size, :] = value.astype(out_refs[number].dtype)
            done += size


def down_product(own_h, other_h, own, other, rows, side, orders, dtype, name):
    sources = own.shape[0]
    total, wide = own_h.shape
    tokens = total // 2
    features = sources * rows
    shapes = [
        jax.ShapeDtypeStruct((tokens, span.stop - span.start), dtype)
        for span in group_spans(features, len(orders))
    ]
    return pl.pallas_call(
        functools.partial(down_kernel, rows, side, orders),
        out_shape=shapes,
        in_specs=[vmem()] * 4,
        out_specs=[vmem()] * len(shapes),
        scratch_shapes=[pltpu.VMEM((features, wide), own.dtype)] * 2,
        compiler_params=pltpu.CompilerParams(vmem_limit_bytes=40 * MIB),
        cost_estimate=pl.CostEstimate(
            flops=4 * tokens * wide * features, bytes_accessed=8 * MIB, transcendentals=0
        ),
        name=name,
    )(own_h, other_h, own, other)


def halve_kernel(axes, *refs):
    count = len(refs) // 4 if axes else len(refs) // 2 - 1
    out_refs = refs[2 * count :]
    lane = 0
    for number in range(count):
        keep_ref, come_ref = refs[2 * number : 2 * number + 2]
        if axes:
            send_ref, left_ref = out_refs[2 * number : 2 * number + 2]
            lanes = slice(0, keep_ref.shape[1])
        else:
            send_ref, left_ref = out_refs
            lanes = slice(lane, lane + keep_ref.shape[1])
            lane = lanes.stop
        axis = axes[number] if axes else 0
        for side, out_ref in enumerate((left_ref, send_ref)):
            done = 0
            for rows in half_spans(keep_ref.shape[0], axis, side):
                size = rows.stop - rows.start
                total = keep_ref[rows, :] + come_ref[rows, :].astype(jnp.float32)
                out_ref[done : done + size, lanes] = total.astype(out_ref.dtype)
                done += size


def halve(pairs, axes):
    sizes = [(keep.shape[0] // 2, keep.shape[1]) for keep, _ in pairs]
    if not axes:
        sizes = [(sizes[0][0], sum(width for _, width in sizes))]
    shapes = []
    for size in sizes:
        shapes += [jax.ShapeDtypeStruct(size, jnp.bfloat16), jax.ShapeDtypeStruct(size, jnp.float32)]
    out = pl.pallas_call(
        functools.partial(halve_kernel, axes),
        out_shape=shapes,
        in_specs=[vmem()] * (2 * len(pairs)),
        out_specs=[vmem()] * len(shapes),
        compiler_params=pltpu.CompilerParams(vmem_limit_bytes=40 * MIB),
        cost_estimate=pl.CostEstimate(
            flops=sum(keep.size for keep, _ in pairs), bytes_accessed=4 * MIB, transcendentals=0
        ),
        name="sum_stage",
    )(*[value for pair in pairs for value in pair])
    return [(out[2 * n], out[2 * n + 1]) for n in range(len(out) // 2)]


def swap(value, bit):
    size = lax.axis_size("ep")
    return lax.ppermute(value, "ep", [(i, i ^ (1 << bit)) for i in range(size)])


def gather_bits(value, bits, order, have=()):
    have = list(have)
    for bit in order:
        axis = sum(1 for b in have if b < bit)
        value = jnp.stack([value, swap(value, bit)], axis=axis)
        have.append(bit)
    return value


def take_half(value, axis, number):
    return lax.index_in_dim(value, number, axis, keepdims=False)


def sum_stages(keep, arrived, order, left):
    left = list(left)
    for bit in order:
        axis = left.index(bit)
        total = keep + arrived.astype(jnp.float32)
        arrived = swap(take_half(total, axis, 1).astype(jnp.bfloat16), bit)
        keep = take_half(total, axis, 0)
        left.remove(bit)
    return keep, arrived


def share_of_slots(slot_ids, gate_weights, slots):
    index = jnp.arange(slots, dtype=jnp.int32)
    picked = slot_ids.T[None, :, :] == index[:, None, None]
    return jnp.sum(jnp.where(picked, gate_weights.T[None, :, :], 0.0), axis=1)


def packed_layer(
    tokens, slot_ids, gate_weights, old_expert, new_expert, gate_proj, up_proj, down_proj
):
    devices = lax.axis_size("ep")
    slots, depth, width = gate_proj.shape
    block = tokens.shape[0]
    me = lax.axis_index("ep")
    core = lax.axis_index("et")
    group = devices // 2
    tie = lax.optimization_barrier
    _, listing, slot_place = distinct_sources(old_expert, new_expert)

    def exchange(value):
        return lax.ppermute(value, "et", [(0, 1), (1, 0)])

    def move(packed):
        return lax.all_to_all(packed, "ep", 0, 0, tiled=True)

    places = []
    for dest in range(devices):
        first, half, _ = units_of(dest)
        places.append([unit // (width // LANES) for unit in (first, first + 1, first + 2, half)] * 4)
    places = jnp.asarray(places, jnp.int32)
    share = share_of_slots(slot_ids, gate_weights, slots)
    belongs = slot_place[None, None, :, None] == places[:, :, None, None]
    share = jnp.sum(jnp.where(belongs, share[None, None], 0.0), axis=2)

    def diagonal(value):
        return lax.ppermute(value, "ep", [(i, i ^ 3) for i in range(devices)])

    mid = tokens.shape[1] // 2
    near, far = swap(tokens, 2), swap(tokens, 3)
    x_own, y_own, xy_own = swap(tokens, 0), swap(tokens, 1), diagonal(tokens)
    parts = (96, 128)
    packed = pack_first(listing, gate_proj, up_proj, down_proj, parts[0], share, devices)
    far, packed = tie((far, packed))
    corner = swap(far, 2)
    pair = jnp.concatenate([far, near], axis=0)
    pair_y, pair_x = swap(pair[:, :mid], 1), swap(pair[:, mid:], 0)
    packed, x_own, y_own, xy_own, pair, corner, pair_y, pair_x = tie(
        (packed, x_own, y_own, xy_own, pair, corner, pair_y, pair_x)
    )

    moved = move(packed)
    corner_a, corner_b = corner[:, :mid], corner[:, mid:]
    cross = diagonal(corner)
    most_a = swap(jnp.concatenate([pair[:, :mid], corner_a, pair_y], axis=0), 0)
    most_b = swap(jnp.concatenate([pair[:, mid:], corner_b, pair_x], axis=0), 1)
    corner_y, corner_x = swap(corner_a, 1), swap(corner_b, 0)

    def lay(*values):
        return jnp.concatenate(values, axis=0)

    three, two = slice(0, 3 * block), slice(3 * block, 5 * block)
    first, second = slice(0, mid), slice(mid, 2 * mid)
    rows = jnp.concatenate(
        [
            lay(
                tokens[:, first], pair[:, first], corner_a,
                y_own[:, first], pair_y, corner_y,
                x_own[:, first], most_a[three],
                xy_own[:, first], most_a[two], cross[:, first],
            ),
            lay(
                tokens[:, second], pair[:, second], corner_b,
                y_own[:, second], most_b[three],
                x_own[:, second], pair_x, corner_x,
                xy_own[:, second], most_b[two], cross[:, second],
            ),
        ],
        axis=1,
    )
    rows_other = exchange(rows)
    rest = pack_rest(listing, down_proj, parts[0], devices)
    moved, rest, rows, rows_other = tie((moved, rest, rows, rows_other))

    down1 = move(rest)
    at = jnp.stack([me, core]).astype(jnp.int32)
    hidden = hidden_units(at, rows, rows_other, moved)
    hidden_other = exchange(hidden)
    down0 = moved[:, depth * 7 : depth * 7 + parts[0] * 7 // 2]

    def products(down, rows_in, orders, before=None):
        own = lax.dynamic_slice_in_dim(down, core * group, group, 0)
        other = exchange(lax.dynamic_slice_in_dim(down, (1 - core) * group, group, 0))
        args = (hidden, hidden_other, own, other)
        sent = down_product(*args, rows_in, 1, orders, jnp.bfloat16, "down_send")
        sent, args = tie((sent, args))
        come = [swap(value, order[0]) for value, order in zip(sent, orders)]
        args, _ = tie((args, before))
        kept = down_product(*args, rows_in, 0, orders, jnp.float32, "down_keep")
        return kept, come

    def stage(kept, come, number, orders):
        axes = tuple(stage_axis(order, number) for order in orders)
        out = halve(list(zip(kept, come)), axes)
        come = [swap(send, order[number]) for (send, _), order in zip(out, orders)]
        return [keep for _, keep in out], come

    def last_stage(kept, come):
        ((send, keep),) = halve(list(zip(kept, come)), None)
        come = swap(send, 3)
        return (keep + come.astype(jnp.float32)).astype(jnp.bfloat16)

    kept0, come0 = products(down0, parts[0], THIRDS)
    down1, kept0 = tie((down1, kept0))
    kept1, come1 = products(down1, parts[1], THIRDS, before=come0)
    kept0, come0 = stage(kept0, come0, 1, THIRDS)
    kept1, come1 = stage(kept1, come1, 1, THIRDS)
    kept0, come0 = stage(kept0, come0, 2, THIRDS)
    kept1, come1 = stage(kept1, come1, 2, THIRDS)
    out = []
    for rows_in, total in zip(parts, (last_stage(kept0, come0), last_stage(kept1, come1))):
        out.append(total.reshape(block, group, rows_in))
    return jnp.concatenate(out, axis=2).reshape(tokens.shape)


def plain_layer(
    tokens, slot_ids, gate_weights, old_expert, new_expert, gate_proj, up_proj, down_proj
):
    devices = lax.axis_size("ep")
    bits = devices.bit_length() - 1
    slots = gate_proj.shape[0]
    me = lax.axis_index("ep")
    source, _, _ = distinct_sources(old_expert, new_expert)

    def move(weights):
        chosen = jnp.take(weights, source, axis=0, mode="clip")
        return lax.all_to_all(chosen, "ep", 0, 0, tiled=True)

    gate_slab = move(gate_proj).reshape(-1, gate_proj.shape[-1])
    up_slab = move(up_proj).reshape(-1, up_proj.shape[-1])
    down = move(down_proj)
    order = range(bits - 1, -1, -1)
    rows = gather_bits(tokens, bits, order).reshape(-1, tokens.shape[1])
    rows = lax.all_gather(rows, "et", axis=1, tiled=True)
    share = gather_bits(share_of_slots(slot_ids, gate_weights, slots), bits, order)
    share = lax.dynamic_index_in_dim(share, me, bits, keepdims=False).reshape(-1, 1)
    gate_part = jnp.dot(rows, gate_slab, preferred_element_type=jnp.float32)
    up_part = jnp.dot(rows, up_slab, preferred_element_type=jnp.float32)
    hidden = (jax.nn.silu(gate_part) * up_part * share).astype(jnp.bfloat16)
    hidden = lax.all_gather(hidden, "et", axis=1, tiled=True)
    down = lax.all_to_all(down, "et", 0, 2, tiled=True)
    value = lax.dot_general(
        hidden,
        down.reshape(-1, down.shape[-1]),
        (((1,), (1,)), ((), ())),
        preferred_element_type=jnp.float32,
    )
    value = value.reshape((2,) * bits + (-1,) + value.shape[1:])
    arrived = swap(take_half(value, 0, 1).astype(jnp.bfloat16), 0)
    left = list(range(1, bits))
    keep, arrived = sum_stages(take_half(value, 0, 0), arrived, left, left)
    return (keep + arrived.astype(jnp.float32)).astype(jnp.bfloat16)


def per_device(tokens, slot_ids, gate_weights, old_expert, new_expert, gate_proj, up_proj, down_proj):
    slots, depth, width = gate_proj.shape
    count = slots - slots // 8
    devices = lax.axis_size("ep")
    fits = (
        lax.axis_size("et") == 2
        and depth == 224
        and width % LANES == 0
        and count * width == devices * 7 * HALF
        and devices == 16
        and tokens.shape[0] == LANES
    )
    layer = packed_layer if fits else plain_layer
    return layer(
        tokens, slot_ids, gate_weights, old_expert, new_expert, gate_proj, up_proj, down_proj
    )


def solution(mesh):
    placed = (
        P("ep", "et"),
        P("ep", None),
        P("ep", None),
        P(),
        P(),
        P(None, "ep", "et"),
        P(None, "ep", "et"),
        P(None, "ep", "et"),
    )
    return jax.shard_map(
        per_device, mesh=mesh, in_specs=placed, out_specs=P("ep", "et"), check_vma=False
    )
```

```python
import functools

import jax
import jax.numpy as jnp
from jax import lax
from jax.experimental import pallas as pl
from jax.experimental.pallas import tpu as pltpu
from jax.sharding import PartitionSpec as P

LANES = 128
HALF = 64
MIB = 1 << 20


def distinct_sources(old_expert, new_expert):
    slots = old_expert.shape[0]
    index = jnp.arange(slots, dtype=jnp.int32)
    holders = new_expert[:, None] == old_expert[None, :]
    source = jnp.min(jnp.where(holders, index[None, :], slots), axis=1)
    used = jnp.any(source[:, None] == index[None, :], axis=0)
    earlier = (index[None, :] < index[:, None]) & used[None, :]
    place = jnp.sum(earlier.astype(jnp.int32), axis=1)
    count = slots - slots // 8
    wanted = jnp.arange(count, dtype=jnp.int32)
    listing = jnp.sum(
        jnp.where(used[None, :] & (place[None, :] == wanted[:, None]), index[None, :], 0), axis=1
    )
    slot_place = jnp.sum(jnp.where(source[:, None] == index[None, :], place[None, :], 0), axis=1)
    return source, listing, slot_place


def units_of(dest):
    if dest % 2 == 0:
        start = 7 * dest // 2
        return start, start + 3, 0
    start = (7 * dest + 1) // 2
    return start, start - 1, 1


def pack_rows(slab_of, out_ref, base, dest, lo, rows, per_slab):
    first, half, side = units_of(dest)
    for number in range(3):
        unit = first + number
        ref, slab = slab_of(unit // per_slab)
        lane = (unit % per_slab) * LANES
        out_ref[dest, base + number * rows : base + (number + 1) * rows, :] = ref[
            slab, lo : lo + rows, lane : lane + LANES
        ]
    ref, slab = slab_of(half // per_slab)
    lane = (half % per_slab) * LANES
    mid = rows // 2
    top = ref[slab, lo : lo + mid, lane : lane + LANES].astype(jnp.float32)
    low = ref[slab, lo + mid : lo + rows, lane : lane + LANES].astype(jnp.float32)
    left = lax.broadcasted_iota(jnp.int32, (mid, LANES), 1) < HALF
    if side == 0:
        both = jnp.where(left, top, pltpu.roll(low, HALF, 1))
    else:
        both = jnp.where(left, pltpu.roll(top, HALF, 1), low)
    out_ref[dest, base + 3 * rows : base + 3 * rows + mid, :] = both.astype(out_ref.dtype)


def pack_first_kernel(rows, list_ref, gate_ref, up_ref, down_ref, share_ref, out_ref):
    slots, depth, width = gate_ref.shape
    size = depth * 7 // 2
    row = lax.broadcasted_iota(jnp.int32, share_ref.shape[1:], 0) // 4
    for dest in range(out_ref.shape[0]):
        for number, in_ref in enumerate((gate_ref, up_ref)):
            pack_rows(
                lambda place, in_ref=in_ref: (in_ref, list_ref[place]),
                out_ref, number * size, dest, 0, depth, width // LANES,
            )
        pack_rows(
            lambda place: (down_ref, list_ref[place]),
            out_ref, 2 * size, dest, 0, rows, width // LANES,
        )
        value = share_ref[dest]
        high = value.astype(out_ref.dtype)
        rest = value - high.astype(jnp.float32)
        middle = rest.astype(out_ref.dtype)
        low = (rest - middle.astype(jnp.float32)).astype(out_ref.dtype)
        terms = jnp.where(
            row == 0,
            high.astype(jnp.float32),
            jnp.where(
                row == 1,
                middle.astype(jnp.float32),
                jnp.where(row == 2, low.astype(jnp.float32), 0.0),
            ),
        )
        out_ref[dest, 2 * size + rows * 7 // 2 :, :] = terms.astype(out_ref.dtype)


def pack_rest_kernel(rows, list_ref, down_ref, out_ref):
    slots, depth, width = down_ref.shape
    for dest in range(out_ref.shape[0]):
        pack_rows(
            lambda place: (down_ref, list_ref[place]),
            out_ref, 0, dest, rows, depth - rows, width // LANES,
        )


def vmem():
    return pl.BlockSpec(memory_space=pltpu.VMEM)


def smem():
    return pl.BlockSpec(memory_space=pltpu.SMEM)


def pack_first(listing, gate_proj, up_proj, down_proj, rows, share, dests):
    slots, depth, width = gate_proj.shape
    shape = (dests, depth * 7 + rows * 7 // 2 + share.shape[1], LANES)
    return pl.pallas_call(
        functools.partial(pack_first_kernel, rows),
        out_shape=jax.ShapeDtypeStruct(shape, gate_proj.dtype),
        in_specs=[smem(), vmem(), vmem(), vmem(), vmem()],
        out_specs=vmem(),
        compiler_params=pltpu.CompilerParams(vmem_limit_bytes=40 * MIB),
        name="pack_first",
    )(listing, gate_proj, up_proj, down_proj, share)


def pack_rest(listing, down_proj, rows, dests):
    slots, depth, width = down_proj.shape
    shape = (dests, (depth - rows) * 7 // 2, LANES)
    return pl.pallas_call(
        functools.partial(pack_rest_kernel, rows),
        out_shape=jax.ShapeDtypeStruct(shape, down_proj.dtype),
        in_specs=[smem(), vmem()],
        out_specs=vmem(),
        compiler_params=pltpu.CompilerParams(vmem_limit_bytes=32 * MIB),
        name="pack_rest",
    )(listing, down_proj)


def unpack_rows(in_ref, at, base, rows, out_ref, out_row, out_lane):
    for number in range(3):
        out_ref[out_row : out_row + rows, out_lane + number * LANES : out_lane + (number + 1) * LANES] = (
            in_ref[at, base + number * rows : base + (number + 1) * rows, :]
        )
    mid = rows // 2
    both = in_ref[at, base + 3 * rows : base + 3 * rows + mid, :]
    lanes = slice(out_lane + 3 * LANES, out_lane + 4 * LANES)
    out_ref[out_row : out_row + mid, lanes] = both
    out_ref[out_row + mid : out_row + rows, lanes] = pltpu.roll(
        both.astype(jnp.float32), HALF, 1
    ).astype(out_ref.dtype)


def hidden_kernel(at_ref, own_ref, other_ref, packed_ref, out_ref, gate_w, up_w):
    rows, mid = own_ref.shape
    sources = packed_ref.shape[0]
    depth = gate_w.shape[0] // sources
    size = depth * 7 // 2
    tile = pl.program_id(0)
    x, y, zl = tile // 4, tile // 2 % 2, tile % 2

    @pl.when(tile == 0)
    def _():
        for at in range(sources):
            place = at_ref[1] * (sources // 2) ^ at
            unpack_rows(packed_ref, place, 0, depth, gate_w, at * depth, 0)
            unpack_rows(packed_ref, place, size, depth, up_w, at * depth, 0)

    def product(w_ref):
        return jnp.dot(
            own_ref[...], w_ref[:mid, :], preferred_element_type=jnp.float32
        ) + jnp.dot(other_ref[...], w_ref[mid:, :], preferred_element_type=jnp.float32)

    gate = product(gate_w)
    value = gate / (1.0 + jnp.exp(-gate)) * product(up_w)

    wide = gate.shape[1]
    term = lax.broadcasted_iota(jnp.int32, (16, wide), 0)
    lane = lax.broadcasted_iota(jnp.int32, (16, wide), 1)
    chosen = (term % 4 == lane // LANES) & (term < 12) & (lane < wide - HALF)
    chosen = jnp.where(chosen, 1.0, 0.0).astype(jnp.bfloat16)
    block = rows // 2
    for zh in range(2):
        source = at_ref[0] ^ (x + 2 * y + 4 * zl + 8 * zh)
        weight = lax.dot_general(
            packed_ref[source, packed_ref.shape[1] - 16 :, :],
            chosen,
            (((0,), (0,)), ((), ())),
            preferred_element_type=jnp.float32,
        )
        span = slice(zh * block, (zh + 1) * block)
        out_ref[span, :] = (value[span, :] * weight).astype(out_ref.dtype)


def hidden_units(at, own, other, packed):
    total, mid = own.shape
    tile = total // 8
    wide = 4 * LANES
    model = 2 * mid
    return pl.pallas_call(
        hidden_kernel,
        grid=(8,),
        out_shape=jax.ShapeDtypeStruct((total, wide), own.dtype),
        in_specs=[smem()] + [pl.BlockSpec((tile, mid), lambda i: (i, 0))] * 2 + [vmem()],
        out_specs=pl.BlockSpec((tile, wide), lambda i: (i, 0)),
        scratch_shapes=[pltpu.VMEM((model, wide), own.dtype)] * 2,
        compiler_params=pltpu.CompilerParams(vmem_limit_bytes=56 * MIB),
        cost_estimate=pl.CostEstimate(
            flops=4 * total * model * wide, bytes_accessed=24 * MIB, transcendentals=total * wide
        ),
        name="hidden",
    )(at, own, other, packed)


THIRDS = ((0, 1, 2), (1, 2, 0), (2, 0, 1))


def group_spans(features, count):
    tiles = features // LANES
    cuts = [-(-tiles * at // count) * LANES for at in range(count + 1)]
    return [slice(lo, hi) for lo, hi in zip(cuts, cuts[1:])]


def stage_axis(order, stage):
    return sum(1 for bit in order[stage:] if bit < order[stage])


def half_spans(rows, axis, side):
    size = rows >> (axis + 1)
    return [slice((2 * at + side) * size, (2 * at + side + 1) * size) for at in range(1 << axis)]


def down_kernel(rows, side, orders, own_h, other_h, own_ref, other_ref, *refs):
    out_refs, (own_w, other_w) = refs[:-2], refs[-2:]
    for in_ref, w_ref in ((own_ref, own_w), (other_ref, other_w)):
        for at in range(in_ref.shape[0]):
            unpack_rows(in_ref, at, 0, rows, w_ref, at * rows, 0)
    dims = (((1,), (1,)), ((), ()))
    for number, span in enumerate(group_spans(own_w.shape[0], len(orders))):
        done = 0
        for tokens in half_spans(own_h.shape[0], stage_axis(orders[number], 0), side):
            value = lax.dot_general(
                own_h[tokens, :], own_w[span, :], dims, preferred_element_type=jnp.float32
            ) + lax.dot_general(
                other_h[tokens, :], other_w[span, :], dims, preferred_element_type=jnp.float32
            )
            size = tokens.stop - tokens.start
            out_refs[number][done : done + size, :] = value.astype(out_refs[number].dtype)
            done += size


def down_product(own_h, other_h, own, other, rows, side, orders, dtype, name):
    sources = own.shape[0]
    total, wide = own_h.shape
    tokens = total // 2
    features = sources * rows
    shapes = [
        jax.ShapeDtypeStruct((tokens, span.stop - span.start), dtype)
        for span in group_spans(features, len(orders))
    ]
    return pl.pallas_call(
        functools.partial(down_kernel, rows, side, orders),
        out_shape=shapes,
        in_specs=[vmem()] * 4,
        out_specs=[vmem()] * len(shapes),
        scratch_shapes=[pltpu.VMEM((features, wide), own.dtype)] * 2,
        compiler_params=pltpu.CompilerParams(vmem_limit_bytes=40 * MIB),
        cost_estimate=pl.CostEstimate(
            flops=4 * tokens * wide * features, bytes_accessed=8 * MIB, transcendentals=0
        ),
        name=name,
    )(own_h, other_h, own, other)


def halve_kernel(axes, *refs):
    count = len(refs) // 4 if axes else len(refs) // 2 - 1
    out_refs = refs[2 * count :]
    lane = 0
    for number in range(count):
        keep_ref, come_ref = refs[2 * number : 2 * number + 2]
        if axes:
            send_ref, left_ref = out_refs[2 * number : 2 * number + 2]
            lanes = slice(0, keep_ref.shape[1])
        else:
            send_ref, left_ref = out_refs
            lanes = slice(lane, lane + keep_ref.shape[1])
            lane = lanes.stop
        axis = axes[number] if axes else 0
        for side, out_ref in enumerate((left_ref, send_ref)):
            done = 0
            for rows in half_spans(keep_ref.shape[0], axis, side):
                size = rows.stop - rows.start
                total = keep_ref[rows, :] + come_ref[rows, :].astype(jnp.float32)
                out_ref[done : done + size, lanes] = total.astype(out_ref.dtype)
                done += size


def halve(pairs, axes):
    sizes = [(keep.shape[0] // 2, keep.shape[1]) for keep, _ in pairs]
    if not axes:
        sizes = [(sizes[0][0], sum(width for _, width in sizes))]
    shapes = []
    for size in sizes:
        shapes += [jax.ShapeDtypeStruct(size, jnp.bfloat16), jax.ShapeDtypeStruct(size, jnp.float32)]
    out = pl.pallas_call(
        functools.partial(halve_kernel, axes),
        out_shape=shapes,
        in_specs=[vmem()] * (2 * len(pairs)),
        out_specs=[vmem()] * len(shapes),
        compiler_params=pltpu.CompilerParams(vmem_limit_bytes=40 * MIB),
        cost_estimate=pl.CostEstimate(
            flops=sum(keep.size for keep, _ in pairs), bytes_accessed=4 * MIB, transcendentals=0
        ),
        name="sum_stage",
    )(*[value for pair in pairs for value in pair])
    return [(out[2 * n], out[2 * n + 1]) for n in range(len(out) // 2)]


def swap(value, bit):
    size = lax.axis_size("ep")
    return lax.ppermute(value, "ep", [(i, i ^ (1 << bit)) for i in range(size)])


def gather_bits(value, bits, order, have=()):
    have = list(have)
    for bit in order:
        axis = sum(1 for b in have if b < bit)
        value = jnp.stack([value, swap(value, bit)], axis=axis)
        have.append(bit)
    return value


def take_half(value, axis, number):
    return lax.index_in_dim(value, number, axis, keepdims=False)


def sum_stages(keep, arrived, order, left):
    left = list(left)
    for bit in order:
        axis = left.index(bit)
        total = keep + arrived.astype(jnp.float32)
        arrived = swap(take_half(total, axis, 1).astype(jnp.bfloat16), bit)
        keep = take_half(total, axis, 0)
        left.remove(bit)
    return keep, arrived


def share_of_slots(slot_ids, gate_weights, slots):
    index = jnp.arange(slots, dtype=jnp.int32)
    picked = slot_ids.T[None, :, :] == index[:, None, None]
    return jnp.sum(jnp.where(picked, gate_weights.T[None, :, :], 0.0), axis=1)


def packed_layer(
    tokens, slot_ids, gate_weights, old_expert, new_expert, gate_proj, up_proj, down_proj
):
    devices = lax.axis_size("ep")
    slots, depth, width = gate_proj.shape
    block = tokens.shape[0]
    me = lax.axis_index("ep")
    core = lax.axis_index("et")
    group = devices // 2
    tie = lax.optimization_barrier
    _, listing, slot_place = distinct_sources(old_expert, new_expert)

    def exchange(value):
        return lax.ppermute(value, "et", [(0, 1), (1, 0)])

    def move(packed):
        return lax.all_to_all(packed, "ep", 0, 0, tiled=True)

    places = []
    for dest in range(devices):
        first, half, _ = units_of(dest)
        places.append([unit // (width // LANES) for unit in (first, first + 1, first + 2, half)] * 4)
    places = jnp.asarray(places, jnp.int32)
    share = share_of_slots(slot_ids, gate_weights, slots)
    belongs = slot_place[None, None, :, None] == places[:, :, None, None]
    share = jnp.sum(jnp.where(belongs, share[None, None], 0.0), axis=2)

    def diagonal(value):
        return lax.ppermute(value, "ep", [(i, i ^ 3) for i in range(devices)])

    mid = tokens.shape[1] // 2
    near, far = swap(tokens, 2), swap(tokens, 3)
    x_own, y_own, xy_own = swap(tokens, 0), swap(tokens, 1), diagonal(tokens)
    parts = (96, 128)
    packed = pack_first(listing, gate_proj, up_proj, down_proj, parts[0], share, devices)
    far, packed = tie((far, packed))
    corner = swap(far, 2)
    pair = jnp.concatenate([far, near], axis=0)
    pair_y, pair_x = swap(pair[:, :mid], 1), swap(pair[:, mid:], 0)
    packed, x_own, y_own, xy_own, pair, corner, pair_y, pair_x = tie(
        (packed, x_own, y_own, xy_own, pair, corner, pair_y, pair_x)
    )

    moved = move(packed)
    corner_a, corner_b = corner[:, :mid], corner[:, mid:]
    cross = diagonal(corner)
    most_a = swap(jnp.concatenate([pair[:, :mid], corner_a, pair_y], axis=0), 0)
    most_b = swap(jnp.concatenate([pair[:, mid:], corner_b, pair_x], axis=0), 1)
    corner_y, corner_x = swap(corner_a, 1), swap(corner_b, 0)

    def lay(*values):
        return jnp.concatenate(values, axis=0)

    three, two = slice(0, 3 * block), slice(3 * block, 5 * block)
    first, second = slice(0, mid), slice(mid, 2 * mid)
    rows = jnp.concatenate(
        [
            lay(
                tokens[:, first], pair[:, first], corner_a,
                y_own[:, first], pair_y, corner_y,
                x_own[:, first], most_a[three],
                xy_own[:, first], most_a[two], cross[:, first],
            ),
            lay(
                tokens[:, second], pair[:, second], corner_b,
                y_own[:, second], most_b[three],
                x_own[:, second], pair_x, corner_x,
                xy_own[:, second], most_b[two], cross[:, second],
            ),
        ],
        axis=1,
    )
    rows_other = exchange(rows)
    rest = pack_rest(listing, down_proj, parts[0], devices)
    moved, rest, rows, rows_other = tie((moved, rest, rows, rows_other))

    down1 = move(rest)
    at = jnp.stack([me, core]).astype(jnp.int32)
    hidden = hidden_units(at, rows, rows_other, moved)
    hidden_other = exchange(hidden)
    down0 = moved[:, depth * 7 : depth * 7 + parts[0] * 7 // 2]

    def products(down, rows_in, orders, before=None):
        own = lax.dynamic_slice_in_dim(down, core * group, group, 0)
        other = exchange(lax.dynamic_slice_in_dim(down, (1 - core) * group, group, 0))
        args, _ = tie(((hidden, hidden_other, own, other), before))
        sent = down_product(*args, rows_in, 1, orders, jnp.bfloat16, "down_send")
        sent, args = tie((sent, args))
        come = [swap(value, order[0]) for value, order in zip(sent, orders)]
        kept = down_product(*args, rows_in, 0, orders, jnp.float32, "down_keep")
        return kept, come

    def stage(kept, come, number, orders):
        axes = tuple(stage_axis(order, number) for order in orders)
        out = halve(list(zip(kept, come)), axes)
        come = [swap(send, order[number]) for (send, _), order in zip(out, orders)]
        return [keep for _, keep in out], come

    def last_stage(kept, come):
        ((send, keep),) = halve(list(zip(kept, come)), None)
        come = swap(send, 3)
        return (keep + come.astype(jnp.float32)).astype(jnp.bfloat16)

    kept0, come0 = products(down0, parts[0], THIRDS)
    kept1, come1 = products(down1, parts[1], THIRDS, before=come0)
    kept0, come0 = stage(kept0, come0, 1, THIRDS)
    kept1, come1 = stage(kept1, come1, 1, THIRDS)
    kept0, come0 = stage(kept0, come0, 2, THIRDS)
    kept1, come1 = stage(kept1, come1, 2, THIRDS)
    out = []
    for rows_in, total in zip(parts, (last_stage(kept0, come0), last_stage(kept1, come1))):
        out.append(total.reshape(block, group, rows_in))
    return jnp.concatenate(out, axis=2).reshape(tokens.shape)


def plain_layer(
    tokens, slot_ids, gate_weights, old_expert, new_expert, gate_proj, up_proj, down_proj
):
    devices = lax.axis_size("ep")
    bits = devices.bit_length() - 1
    slots = gate_proj.shape[0]
    me = lax.axis_index("ep")
    source, _, _ = distinct_sources(old_expert, new_expert)

    def move(weights):
        chosen = jnp.take(weights, source, axis=0, mode="clip")
        return lax.all_to_all(chosen, "ep", 0, 0, tiled=True)

    gate_slab = move(gate_proj).reshape(-1, gate_proj.shape[-1])
    up_slab = move(up_proj).reshape(-1, up_proj.shape[-1])
    down = move(down_proj)
    order = range(bits - 1, -1, -1)
    rows = gather_bits(tokens, bits, order).reshape(-1, tokens.shape[1])
    rows = lax.all_gather(rows, "et", axis=1, tiled=True)
    share = gather_bits(share_of_slots(slot_ids, gate_weights, slots), bits, order)
    share = lax.dynamic_index_in_dim(share, me, bits, keepdims=False).reshape(-1, 1)
    gate_part = jnp.dot(rows, gate_slab, preferred_element_type=jnp.float32)
    up_part = jnp.dot(rows, up_slab, preferred_element_type=jnp.float32)
    hidden = (jax.nn.silu(gate_part) * up_part * share).astype(jnp.bfloat16)
    hidden = lax.all_gather(hidden, "et", axis=1, tiled=True)
    down = lax.all_to_all(down, "et", 0, 2, tiled=True)
    value = lax.dot_general(
        hidden,
        down.reshape(-1, down.shape[-1]),
        (((1,), (1,)), ((), ())),
        preferred_element_type=jnp.float32,
    )
    value = value.reshape((2,) * bits + (-1,) + value.shape[1:])
    arrived = swap(take_half(value, 0, 1).astype(jnp.bfloat16), 0)
    left = list(range(1, bits))
    keep, arrived = sum_stages(take_half(value, 0, 0), arrived, left, left)
    return (keep + arrived.astype(jnp.float32)).astype(jnp.bfloat16)


def per_device(tokens, slot_ids, gate_weights, old_expert, new_expert, gate_proj, up_proj, down_proj):
    slots, depth, width = gate_proj.shape
    count = slots - slots // 8
    devices = lax.axis_size("ep")
    fits = (
        lax.axis_size("et") == 2
        and depth == 224
        and width % LANES == 0
        and count * width == devices * 7 * HALF
        and devices == 16
        and tokens.shape[0] == LANES
    )
    layer = packed_layer if fits else plain_layer
    return layer(
        tokens, slot_ids, gate_weights, old_expert, new_expert, gate_proj, up_proj, down_proj
    )


def solution(mesh):
    placed = (
        P("ep", "et"),
        P("ep", None),
        P("ep", None),
        P(),
        P(),
        P(None, "ep", "et"),
        P(None, "ep", "et"),
        P(None, "ep", "et"),
    )
    return jax.shard_map(
        per_device, mesh=mesh, in_specs=placed, out_specs=P("ep", "et"), check_vma=False
    )
```

```python
import functools

import jax
import jax.numpy as jnp
from jax import lax
from jax.experimental import pallas as pl
from jax.experimental.pallas import tpu as pltpu
from jax.sharding import PartitionSpec as P

LANES = 128
HALF = 64
MIB = 1 << 20


def distinct_sources(old_expert, new_expert):
    slots = old_expert.shape[0]
    index = jnp.arange(slots, dtype=jnp.int32)
    holders = new_expert[:, None] == old_expert[None, :]
    source = jnp.min(jnp.where(holders, index[None, :], slots), axis=1)
    used = jnp.any(source[:, None] == index[None, :], axis=0)
    earlier = (index[None, :] < index[:, None]) & used[None, :]
    place = jnp.sum(earlier.astype(jnp.int32), axis=1)
    count = slots - slots // 8
    wanted = jnp.arange(count, dtype=jnp.int32)
    listing = jnp.sum(
        jnp.where(used[None, :] & (place[None, :] == wanted[:, None]), index[None, :], 0), axis=1
    )
    slot_place = jnp.sum(jnp.where(source[:, None] == index[None, :], place[None, :], 0), axis=1)
    return source, listing, slot_place


def units_of(dest):
    if dest % 2 == 0:
        start = 7 * dest // 2
        return start, start + 3, 0
    start = (7 * dest + 1) // 2
    return start, start - 1, 1


def pack_rows(slab_of, out_ref, base, dest, lo, rows, per_slab):
    first, half, side = units_of(dest)
    for number in range(3):
        unit = first + number
        ref, slab = slab_of(unit // per_slab)
        lane = (unit % per_slab) * LANES
        out_ref[dest, base + number * rows : base + (number + 1) * rows, :] = ref[
            slab, lo : lo + rows, lane : lane + LANES
        ]
    ref, slab = slab_of(half // per_slab)
    lane = (half % per_slab) * LANES
    mid = rows // 2
    top = ref[slab, lo : lo + mid, lane : lane + LANES].astype(jnp.float32)
    low = ref[slab, lo + mid : lo + rows, lane : lane + LANES].astype(jnp.float32)
    left = lax.broadcasted_iota(jnp.int32, (mid, LANES), 1) < HALF
    if side == 0:
        both = jnp.where(left, top, pltpu.roll(low, HALF, 1))
    else:
        both = jnp.where(left, pltpu.roll(top, HALF, 1), low)
    out_ref[dest, base + 3 * rows : base + 3 * rows + mid, :] = both.astype(out_ref.dtype)


def pack_first_kernel(rows, list_ref, gate_ref, up_ref, down_ref, share_ref, out_ref):
    slots, depth, width = gate_ref.shape
    size = depth * 7 // 2
    row = lax.broadcasted_iota(jnp.int32, share_ref.shape[1:], 0) // 4
    for dest in range(out_ref.shape[0]):
        for number, in_ref in enumerate((gate_ref, up_ref)):
            pack_rows(
                lambda place, in_ref=in_ref: (in_ref, list_ref[place]),
                out_ref, number * size, dest, 0, depth, width // LANES,
            )
        pack_rows(
            lambda place: (down_ref, list_ref[place]),
            out_ref, 2 * size, dest, 0, rows, width // LANES,
        )
        value = share_ref[dest]
        high = value.astype(out_ref.dtype)
        rest = value - high.astype(jnp.float32)
        middle = rest.astype(out_ref.dtype)
        low = (rest - middle.astype(jnp.float32)).astype(out_ref.dtype)
        terms = jnp.where(
            row == 0,
            high.astype(jnp.float32),
            jnp.where(
                row == 1,
                middle.astype(jnp.float32),
                jnp.where(row == 2, low.astype(jnp.float32), 0.0),
            ),
        )
        out_ref[dest, 2 * size + rows * 7 // 2 :, :] = terms.astype(out_ref.dtype)


def pack_rest_kernel(rows, list_ref, down_ref, out_ref):
    slots, depth, width = down_ref.shape
    for dest in range(out_ref.shape[0]):
        pack_rows(
            lambda place: (down_ref, list_ref[place]),
            out_ref, 0, dest, rows, depth - rows, width // LANES,
        )


def vmem():
    return pl.BlockSpec(memory_space=pltpu.VMEM)


def smem():
    return pl.BlockSpec(memory_space=pltpu.SMEM)


def pack_first(listing, gate_proj, up_proj, down_proj, rows, share, dests):
    slots, depth, width = gate_proj.shape
    shape = (dests, depth * 7 + rows * 7 // 2 + share.shape[1], LANES)
    return pl.pallas_call(
        functools.partial(pack_first_kernel, rows),
        out_shape=jax.ShapeDtypeStruct(shape, gate_proj.dtype),
        in_specs=[smem(), vmem(), vmem(), vmem(), vmem()],
        out_specs=vmem(),
        compiler_params=pltpu.CompilerParams(vmem_limit_bytes=40 * MIB),
        name="pack_first",
    )(listing, gate_proj, up_proj, down_proj, share)


def pack_rest(listing, down_proj, rows, dests):
    slots, depth, width = down_proj.shape
    shape = (dests, (depth - rows) * 7 // 2, LANES)
    return pl.pallas_call(
        functools.partial(pack_rest_kernel, rows),
        out_shape=jax.ShapeDtypeStruct(shape, down_proj.dtype),
        in_specs=[smem(), vmem()],
        out_specs=vmem(),
        compiler_params=pltpu.CompilerParams(vmem_limit_bytes=32 * MIB),
        name="pack_rest",
    )(listing, down_proj)


def unpack_rows(in_ref, at, base, rows, out_ref, out_row, out_lane):
    for number in range(3):
        out_ref[out_row : out_row + rows, out_lane + number * LANES : out_lane + (number + 1) * LANES] = (
            in_ref[at, base + number * rows : base + (number + 1) * rows, :]
        )
    mid = rows // 2
    both = in_ref[at, base + 3 * rows : base + 3 * rows + mid, :]
    lanes = slice(out_lane + 3 * LANES, out_lane + 4 * LANES)
    out_ref[out_row : out_row + mid, lanes] = both
    out_ref[out_row + mid : out_row + rows, lanes] = pltpu.roll(
        both.astype(jnp.float32), HALF, 1
    ).astype(out_ref.dtype)


def hidden_kernel(at_ref, own_ref, other_ref, packed_ref, out_ref, gate_w, up_w):
    rows, mid = own_ref.shape
    sources = packed_ref.shape[0]
    depth = gate_w.shape[0] // sources
    size = depth * 7 // 2
    tile = pl.program_id(0)
    x, y, zl = tile // 4, tile // 2 % 2, tile % 2

    @pl.when(tile == 0)
    def _():
        for at in range(sources):
            place = at_ref[1] * (sources // 2) ^ at
            unpack_rows(packed_ref, place, 0, depth, gate_w, at * depth, 0)
            unpack_rows(packed_ref, place, size, depth, up_w, at * depth, 0)

    def product(w_ref):
        return jnp.dot(
            own_ref[...], w_ref[:mid, :], preferred_element_type=jnp.float32
        ) + jnp.dot(other_ref[...], w_ref[mid:, :], preferred_element_type=jnp.float32)

    gate = product(gate_w)
    value = gate / (1.0 + jnp.exp(-gate)) * product(up_w)

    wide = gate.shape[1]
    term = lax.broadcasted_iota(jnp.int32, (16, wide), 0)
    lane = lax.broadcasted_iota(jnp.int32, (16, wide), 1)
    chosen = (term % 4 == lane // LANES) & (term < 12) & (lane < wide - HALF)
    chosen = jnp.where(chosen, 1.0, 0.0).astype(jnp.bfloat16)
    block = rows // 2
    for zh in range(2):
        source = at_ref[0] ^ (x + 2 * y + 4 * zl + 8 * zh)
        weight = lax.dot_general(
            packed_ref[source, packed_ref.shape[1] - 16 :, :],
            chosen,
            (((0,), (0,)), ((), ())),
            preferred_element_type=jnp.float32,
        )
        span = slice(zh * block, (zh + 1) * block)
        out_ref[span, :] = (value[span, :] * weight).astype(out_ref.dtype)


def hidden_units(at, own, other, packed):
    total, mid = own.shape
    tile = total // 8
    wide = 4 * LANES
    model = 2 * mid
    return pl.pallas_call(
        hidden_kernel,
        grid=(8,),
        out_shape=jax.ShapeDtypeStruct((total, wide), own.dtype),
        in_specs=[smem()] + [pl.BlockSpec((tile, mid), lambda i: (i, 0))] * 2 + [vmem()],
        out_specs=pl.BlockSpec((tile, wide), lambda i: (i, 0)),
        scratch_shapes=[pltpu.VMEM((model, wide), own.dtype)] * 2,
        compiler_params=pltpu.CompilerParams(vmem_limit_bytes=56 * MIB),
        cost_estimate=pl.CostEstimate(
            flops=4 * total * model * wide, bytes_accessed=24 * MIB, transcendentals=total * wide
        ),
        name="hidden",
    )(at, own, other, packed)


THIRDS = ((0, 1, 2), (1, 2, 0), (2, 0, 1))


def group_spans(features, count):
    tiles = features // LANES
    cuts = [-(-tiles * at // count) * LANES for at in range(count + 1)]
    return [slice(lo, hi) for lo, hi in zip(cuts, cuts[1:])]


def stage_axis(order, stage):
    return sum(1 for bit in order[stage:] if bit < order[stage])


def half_spans(rows, axis, side):
    size = rows >> (axis + 1)
    return [slice((2 * at + side) * size, (2 * at + side + 1) * size) for at in range(1 << axis)]


def down_kernel(rows, side, orders, own_h, other_h, own_ref, other_ref, *refs):
    out_refs, (own_w, other_w) = refs[:-2], refs[-2:]
    for in_ref, w_ref in ((own_ref, own_w), (other_ref, other_w)):
        for at in range(in_ref.shape[0]):
            unpack_rows(in_ref, at, 0, rows, w_ref, at * rows, 0)
    dims = (((1,), (1,)), ((), ()))
    for number, span in enumerate(group_spans(own_w.shape[0], len(orders))):
        done = 0
        for tokens in half_spans(own_h.shape[0], stage_axis(orders[number], 0), side):
            value = lax.dot_general(
                own_h[tokens, :], own_w[span, :], dims, preferred_element_type=jnp.float32
            ) + lax.dot_general(
                other_h[tokens, :], other_w[span, :], dims, preferred_element_type=jnp.float32
            )
            size = tokens.stop - tokens.start
            out_refs[number][done : done + size, :] = value.astype(out_refs[number].dtype)
            done += size


def down_product(own_h, other_h, own, other, rows, side, orders, dtype, name):
    sources = own.shape[0]
    total, wide = own_h.shape
    tokens = total // 2
    features = sources * rows
    shapes = [
        jax.ShapeDtypeStruct((tokens, span.stop - span.start), dtype)
        for span in group_spans(features, len(orders))
    ]
    return pl.pallas_call(
        functools.partial(down_kernel, rows, side, orders),
        out_shape=shapes,
        in_specs=[vmem()] * 4,
        out_specs=[vmem()] * len(shapes),
        scratch_shapes=[pltpu.VMEM((features, wide), own.dtype)] * 2,
        compiler_params=pltpu.CompilerParams(vmem_limit_bytes=40 * MIB),
        cost_estimate=pl.CostEstimate(
            flops=4 * tokens * wide * features, bytes_accessed=8 * MIB, transcendentals=0
        ),
        name=name,
    )(own_h, other_h, own, other)


def halve_kernel(axes, *refs):
    count = len(refs) // 4 if axes else len(refs) // 2 - 1
    out_refs = refs[2 * count :]
    lane = 0
    for number in range(count):
        keep_ref, come_ref = refs[2 * number : 2 * number + 2]
        if axes:
            send_ref, left_ref = out_refs[2 * number : 2 * number + 2]
            lanes = slice(0, keep_ref.shape[1])
        else:
            send_ref, left_ref = out_refs
            lanes = slice(lane, lane + keep_ref.shape[1])
            lane = lanes.stop
        axis = axes[number] if axes else 0
        for side, out_ref in enumerate((left_ref, send_ref)):
            done = 0
            for rows in half_spans(keep_ref.shape[0], axis, side):
                size = rows.stop - rows.start
                total = keep_ref[rows, :] + come_ref[rows, :].astype(jnp.float32)
                out_ref[done : done + size, lanes] = total.astype(out_ref.dtype)
                done += size


def halve(pairs, axes):
    sizes = [(keep.shape[0] // 2, keep.shape[1]) for keep, _ in pairs]
    if not axes:
        sizes = [(sizes[0][0], sum(width for _, width in sizes))]
    shapes = []
    for size in sizes:
        shapes += [jax.ShapeDtypeStruct(size, jnp.bfloat16), jax.ShapeDtypeStruct(size, jnp.float32)]
    out = pl.pallas_call(
        functools.partial(halve_kernel, axes),
        out_shape=shapes,
        in_specs=[vmem()] * (2 * len(pairs)),
        out_specs=[vmem()] * len(shapes),
        compiler_params=pltpu.CompilerParams(vmem_limit_bytes=40 * MIB),
        cost_estimate=pl.CostEstimate(
            flops=sum(keep.size for keep, _ in pairs), bytes_accessed=4 * MIB, transcendentals=0
        ),
        name="sum_stage",
    )(*[value for pair in pairs for value in pair])
    return [(out[2 * n], out[2 * n + 1]) for n in range(len(out) // 2)]


def swap(value, bit):
    size = lax.axis_size("ep")
    return lax.ppermute(value, "ep", [(i, i ^ (1 << bit)) for i in range(size)])


def gather_bits(value, bits, order, have=()):
    have = list(have)
    for bit in order:
        axis = sum(1 for b in have if b < bit)
        value = jnp.stack([value, swap(value, bit)], axis=axis)
        have.append(bit)
    return value


def take_half(value, axis, number):
    return lax.index_in_dim(value, number, axis, keepdims=False)


def sum_stages(keep, arrived, order, left):
    left = list(left)
    for bit in order:
        axis = left.index(bit)
        total = keep + arrived.astype(jnp.float32)
        arrived = swap(take_half(total, axis, 1).astype(jnp.bfloat16), bit)
        keep = take_half(total, axis, 0)
        left.remove(bit)
    return keep, arrived


def share_of_slots(slot_ids, gate_weights, slots):
    index = jnp.arange(slots, dtype=jnp.int32)
    picked = slot_ids.T[None, :, :] == index[:, None, None]
    return jnp.sum(jnp.where(picked, gate_weights.T[None, :, :], 0.0), axis=1)


def packed_layer(
    tokens, slot_ids, gate_weights, old_expert, new_expert, gate_proj, up_proj, down_proj
):
    devices = lax.axis_size("ep")
    slots, depth, width = gate_proj.shape
    block = tokens.shape[0]
    me = lax.axis_index("ep")
    core = lax.axis_index("et")
    group = devices // 2
    tie = lax.optimization_barrier
    _, listing, slot_place = distinct_sources(old_expert, new_expert)

    def exchange(value):
        return lax.ppermute(value, "et", [(0, 1), (1, 0)])

    def move(packed):
        return lax.all_to_all(packed, "ep", 0, 0, tiled=True)

    places = []
    for dest in range(devices):
        first, half, _ = units_of(dest)
        places.append([unit // (width // LANES) for unit in (first, first + 1, first + 2, half)] * 4)
    places = jnp.asarray(places, jnp.int32)
    share = share_of_slots(slot_ids, gate_weights, slots)
    belongs = slot_place[None, None, :, None] == places[:, :, None, None]
    share = jnp.sum(jnp.where(belongs, share[None, None], 0.0), axis=2)

    def diagonal(value):
        return lax.ppermute(value, "ep", [(i, i ^ 3) for i in range(devices)])

    mid = tokens.shape[1] // 2
    near, far = swap(tokens, 2), swap(tokens, 3)
    x_own, y_own, xy_own = swap(tokens, 0), swap(tokens, 1), diagonal(tokens)
    parts = (96, 128)
    packed = pack_first(listing, gate_proj, up_proj, down_proj, parts[0], share, devices)
    far, packed = tie((far, packed))
    corner = swap(far, 2)
    pair = jnp.concatenate([far, near], axis=0)
    pair_y, pair_x = swap(pair[:, :mid], 1), swap(pair[:, mid:], 0)
    packed, x_own, y_own, xy_own, pair, corner, pair_y, pair_x = tie(
        (packed, x_own, y_own, xy_own, pair, corner, pair_y, pair_x)
    )

    moved = move(packed)
    corner_a, corner_b = corner[:, :mid], corner[:, mid:]
    cross = diagonal(corner)
    most_a = swap(jnp.concatenate([pair[:, :mid], corner_a, pair_y], axis=0), 0)
    most_b = swap(jnp.concatenate([pair[:, mid:], corner_b, pair_x], axis=0), 1)
    corner_y, corner_x = swap(corner_a, 1), swap(corner_b, 0)

    def lay(*values):
        return jnp.concatenate(values, axis=0)

    three, two = slice(0, 3 * block), slice(3 * block, 5 * block)
    first, second = slice(0, mid), slice(mid, 2 * mid)
    rows = jnp.concatenate(
        [
            lay(
                tokens[:, first], pair[:, first], corner_a,
                y_own[:, first], pair_y, corner_y,
                x_own[:, first], most_a[three],
                xy_own[:, first], most_a[two], cross[:, first],
            ),
            lay(
                tokens[:, second], pair[:, second], corner_b,
                y_own[:, second], most_b[three],
                x_own[:, second], pair_x, corner_x,
                xy_own[:, second], most_b[two], cross[:, second],
            ),
        ],
        axis=1,
    )
    rows_other = exchange(rows)
    rest = pack_rest(listing, down_proj, parts[0], devices)
    moved, rest, rows, rows_other = tie((moved, rest, rows, rows_other))

    down1 = move(rest)
    at = jnp.stack([me, core]).astype(jnp.int32)
    hidden = hidden_units(at, rows, rows_other, moved)
    hidden_other = exchange(hidden)
    down0 = moved[:, depth * 7 : depth * 7 + parts[0] * 7 // 2]

    def products(down, rows_in, orders, before=None):
        own = lax.dynamic_slice_in_dim(down, core * group, group, 0)
        other = exchange(lax.dynamic_slice_in_dim(down, (1 - core) * group, group, 0))
        args, _ = tie(((hidden, hidden_other, own, other), before))
        sent = down_product(*args, rows_in, 1, orders, jnp.bfloat16, "down_send")
        sent, args = tie((sent, args))
        come = [swap(value, order[0]) for value, order in zip(sent, orders)]
        kept = down_product(*args, rows_in, 0, orders, jnp.float32, "down_keep")
        return kept, come, sent

    def stage(kept, come, number, orders):
        axes = tuple(stage_axis(order, number) for order in orders)
        out = halve(list(zip(kept, come)), axes)
        come = [swap(send, order[number]) for (send, _), order in zip(out, orders)]
        return [keep for _, keep in out], come

    def last_stage(kept, come):
        ((send, keep),) = halve(list(zip(kept, come)), None)
        come = swap(send, 3)
        return (keep + come.astype(jnp.float32)).astype(jnp.bfloat16)

    kept0, come0, sent0 = products(down0, parts[0], THIRDS)
    down1, _ = tie((down1, sent0))
    kept1, come1, _ = products(down1, parts[1], THIRDS, before=come0)
    kept0, come0 = stage(kept0, come0, 1, THIRDS)
    kept1, come1 = stage(kept1, come1, 1, THIRDS)
    kept0, come0 = stage(kept0, come0, 2, THIRDS)
    kept1, come1 = stage(kept1, come1, 2, THIRDS)
    out = []
    for rows_in, total in zip(parts, (last_stage(kept0, come0), last_stage(kept1, come1))):
        out.append(total.reshape(block, group, rows_in))
    return jnp.concatenate(out, axis=2).reshape(tokens.shape)


def plain_layer(
    tokens, slot_ids, gate_weights, old_expert, new_expert, gate_proj, up_proj, down_proj
):
    devices = lax.axis_size("ep")
    bits = devices.bit_length() - 1
    slots = gate_proj.shape[0]
    me = lax.axis_index("ep")
    source, _, _ = distinct_sources(old_expert, new_expert)

    def move(weights):
        chosen = jnp.take(weights, source, axis=0, mode="clip")
        return lax.all_to_all(chosen, "ep", 0, 0, tiled=True)

    gate_slab = move(gate_proj).reshape(-1, gate_proj.shape[-1])
    up_slab = move(up_proj).reshape(-1, up_proj.shape[-1])
    down = move(down_proj)
    order = range(bits - 1, -1, -1)
    rows = gather_bits(tokens, bits, order).reshape(-1, tokens.shape[1])
    rows = lax.all_gather(rows, "et", axis=1, tiled=True)
    share = gather_bits(share_of_slots(slot_ids, gate_weights, slots), bits, order)
    share = lax.dynamic_index_in_dim(share, me, bits, keepdims=False).reshape(-1, 1)
    gate_part = jnp.dot(rows, gate_slab, preferred_element_type=jnp.float32)
    up_part = jnp.dot(rows, up_slab, preferred_element_type=jnp.float32)
    hidden = (jax.nn.silu(gate_part) * up_part * share).astype(jnp.bfloat16)
    hidden = lax.all_gather(hidden, "et", axis=1, tiled=True)
    down = lax.all_to_all(down, "et", 0, 2, tiled=True)
    value = lax.dot_general(
        hidden,
        down.reshape(-1, down.shape[-1]),
        (((1,), (1,)), ((), ())),
        preferred_element_type=jnp.float32,
    )
    value = value.reshape((2,) * bits + (-1,) + value.shape[1:])
    arrived = swap(take_half(value, 0, 1).astype(jnp.bfloat16), 0)
    left = list(range(1, bits))
    keep, arrived = sum_stages(take_half(value, 0, 0), arrived, left, left)
    return (keep + arrived.astype(jnp.float32)).astype(jnp.bfloat16)


def per_device(tokens, slot_ids, gate_weights, old_expert, new_expert, gate_proj, up_proj, down_proj):
    slots, depth, width = gate_proj.shape
    count = slots - slots // 8
    devices = lax.axis_size("ep")
    fits = (
        lax.axis_size("et") == 2
        and depth == 224
        and width % LANES == 0
        and count * width == devices * 7 * HALF
        and devices == 16
        and tokens.shape[0] == LANES
    )
    layer = packed_layer if fits else plain_layer
    return layer(
        tokens, slot_ids, gate_weights, old_expert, new_expert, gate_proj, up_proj, down_proj
    )


def solution(mesh):
    placed = (
        P("ep", "et"),
        P("ep", None),
        P("ep", None),
        P(),
        P(),
        P(None, "ep", "et"),
        P(None, "ep", "et"),
        P(None, "ep", "et"),
    )
    return jax.shard_map(
        per_device, mesh=mesh, in_specs=placed, out_specs=P("ep", "et"), check_vma=False
    )
```

```python
import functools

import jax
import jax.numpy as jnp
from jax import lax
from jax.experimental import pallas as pl
from jax.experimental.pallas import tpu as pltpu
from jax.sharding import PartitionSpec as P

LANES = 128
HALF = 64
MIB = 1 << 20


def distinct_sources(old_expert, new_expert):
    slots = old_expert.shape[0]
    index = jnp.arange(slots, dtype=jnp.int32)
    holders = new_expert[:, None] == old_expert[None, :]
    source = jnp.min(jnp.where(holders, index[None, :], slots), axis=1)
    used = jnp.any(source[:, None] == index[None, :], axis=0)
    earlier = (index[None, :] < index[:, None]) & used[None, :]
    place = jnp.sum(earlier.astype(jnp.int32), axis=1)
    count = slots - slots // 8
    wanted = jnp.arange(count, dtype=jnp.int32)
    listing = jnp.sum(
        jnp.where(used[None, :] & (place[None, :] == wanted[:, None]), index[None, :], 0), axis=1
    )
    slot_place = jnp.sum(jnp.where(source[:, None] == index[None, :], place[None, :], 0), axis=1)
    return source, listing, slot_place


def units_of(dest):
    if dest % 2 == 0:
        start = 7 * dest // 2
        return start, start + 3, 0
    start = (7 * dest + 1) // 2
    return start, start - 1, 1


def pack_rows(slab_of, out_ref, base, dest, lo, rows, per_slab):
    first, half, side = units_of(dest)
    for number in range(3):
        unit = first + number
        ref, slab = slab_of(unit // per_slab)
        lane = (unit % per_slab) * LANES
        out_ref[dest, base + number * rows : base + (number + 1) * rows, :] = ref[
            slab, lo : lo + rows, lane : lane + LANES
        ]
    ref, slab = slab_of(half // per_slab)
    lane = (half % per_slab) * LANES
    mid = rows // 2
    top = ref[slab, lo : lo + mid, lane : lane + LANES].astype(jnp.float32)
    low = ref[slab, lo + mid : lo + rows, lane : lane + LANES].astype(jnp.float32)
    left = lax.broadcasted_iota(jnp.int32, (mid, LANES), 1) < HALF
    if side == 0:
        both = jnp.where(left, top, pltpu.roll(low, HALF, 1))
    else:
        both = jnp.where(left, pltpu.roll(top, HALF, 1), low)
    out_ref[dest, base + 3 * rows : base + 3 * rows + mid, :] = both.astype(out_ref.dtype)


def pack_first_kernel(rows, list_ref, gate_ref, up_ref, down_ref, share_ref, out_ref):
    slots, depth, width = gate_ref.shape
    size = depth * 7 // 2
    row = lax.broadcasted_iota(jnp.int32, share_ref.shape[1:], 0) // 4
    for dest in range(out_ref.shape[0]):
        for number, in_ref in enumerate((gate_ref, up_ref)):
            pack_rows(
                lambda place, in_ref=in_ref: (in_ref, list_ref[place]),
                out_ref, number * size, dest, 0, depth, width // LANES,
            )
        pack_rows(
            lambda place: (down_ref, list_ref[place]),
            out_ref, 2 * size, dest, 0, rows, width // LANES,
        )
        value = share_ref[dest]
        high = value.astype(out_ref.dtype)
        rest = value - high.astype(jnp.float32)
        middle = rest.astype(out_ref.dtype)
        low = (rest - middle.astype(jnp.float32)).astype(out_ref.dtype)
        terms = jnp.where(
            row == 0,
            high.astype(jnp.float32),
            jnp.where(
                row == 1,
                middle.astype(jnp.float32),
                jnp.where(row == 2, low.astype(jnp.float32), 0.0),
            ),
        )
        out_ref[dest, 2 * size + rows * 7 // 2 :, :] = terms.astype(out_ref.dtype)


def pack_rest_kernel(rows, list_ref, down_ref, out_ref):
    slots, depth, width = down_ref.shape
    for dest in range(out_ref.shape[0]):
        pack_rows(
            lambda place: (down_ref, list_ref[place]),
            out_ref, 0, dest, rows, depth - rows, width // LANES,
        )


def vmem():
    return pl.BlockSpec(memory_space=pltpu.VMEM)


def smem():
    return pl.BlockSpec(memory_space=pltpu.SMEM)


def pack_first(listing, gate_proj, up_proj, down_proj, rows, share, dests):
    slots, depth, width = gate_proj.shape
    shape = (dests, depth * 7 + rows * 7 // 2 + share.shape[1], LANES)
    return pl.pallas_call(
        functools.partial(pack_first_kernel, rows),
        out_shape=jax.ShapeDtypeStruct(shape, gate_proj.dtype),
        in_specs=[smem(), vmem(), vmem(), vmem(), vmem()],
        out_specs=vmem(),
        compiler_params=pltpu.CompilerParams(vmem_limit_bytes=40 * MIB),
        name="pack_first",
    )(listing, gate_proj, up_proj, down_proj, share)


def pack_rest(listing, down_proj, rows, dests):
    slots, depth, width = down_proj.shape
    shape = (dests, (depth - rows) * 7 // 2, LANES)
    return pl.pallas_call(
        functools.partial(pack_rest_kernel, rows),
        out_shape=jax.ShapeDtypeStruct(shape, down_proj.dtype),
        in_specs=[smem(), vmem()],
        out_specs=vmem(),
        compiler_params=pltpu.CompilerParams(vmem_limit_bytes=32 * MIB),
        name="pack_rest",
    )(listing, down_proj)


def unpack_rows(in_ref, at, base, rows, out_ref, out_row, out_lane):
    for number in range(3):
        out_ref[out_row : out_row + rows, out_lane + number * LANES : out_lane + (number + 1) * LANES] = (
            in_ref[at, base + number * rows : base + (number + 1) * rows, :]
        )
    mid = rows // 2
    both = in_ref[at, base + 3 * rows : base + 3 * rows + mid, :]
    lanes = slice(out_lane + 3 * LANES, out_lane + 4 * LANES)
    out_ref[out_row : out_row + mid, lanes] = both
    out_ref[out_row + mid : out_row + rows, lanes] = pltpu.roll(
        both.astype(jnp.float32), HALF, 1
    ).astype(out_ref.dtype)


def hidden_kernel(at_ref, own_ref, other_ref, packed_ref, out_ref, gate_w, up_w):
    rows, mid = own_ref.shape
    sources = packed_ref.shape[0]
    depth = gate_w.shape[0] // sources
    size = depth * 7 // 2
    tile = pl.program_id(0)
    x, y, zl = tile // 4, tile // 2 % 2, tile % 2

    @pl.when(tile == 0)
    def _():
        for at in range(sources):
            place = at_ref[1] * (sources // 2) ^ at
            unpack_rows(packed_ref, place, 0, depth, gate_w, at * depth, 0)
            unpack_rows(packed_ref, place, size, depth, up_w, at * depth, 0)

    def product(w_ref):
        return jnp.dot(
            own_ref[...], w_ref[:mid, :], preferred_element_type=jnp.float32
        ) + jnp.dot(other_ref[...], w_ref[mid:, :], preferred_element_type=jnp.float32)

    gate = product(gate_w)
    value = gate / (1.0 + jnp.exp(-gate)) * product(up_w)

    wide = gate.shape[1]
    term = lax.broadcasted_iota(jnp.int32, (16, wide), 0)
    lane = lax.broadcasted_iota(jnp.int32, (16, wide), 1)
    chosen = (term % 4 == lane // LANES) & (term < 12) & (lane < wide - HALF)
    chosen = jnp.where(chosen, 1.0, 0.0).astype(jnp.bfloat16)
    block = rows // 2
    for zh in range(2):
        source = at_ref[0] ^ (x + 2 * y + 4 * zl + 8 * zh)
        weight = lax.dot_general(
            packed_ref[source, packed_ref.shape[1] - 16 :, :],
            chosen,
            (((0,), (0,)), ((), ())),
            preferred_element_type=jnp.float32,
        )
        span = slice(zh * block, (zh + 1) * block)
        out_ref[span, :] = (value[span, :] * weight).astype(out_ref.dtype)


def hidden_units(at, own, other, packed):
    total, mid = own.shape
    tile = total // 8
    wide = 4 * LANES
    model = 2 * mid
    return pl.pallas_call(
        hidden_kernel,
        grid=(8,),
        out_shape=jax.ShapeDtypeStruct((total, wide), own.dtype),
        in_specs=[smem()] + [pl.BlockSpec((tile, mid), lambda i: (i, 0))] * 2 + [vmem()],
        out_specs=pl.BlockSpec((tile, wide), lambda i: (i, 0)),
        scratch_shapes=[pltpu.VMEM((model, wide), own.dtype)] * 2,
        compiler_params=pltpu.CompilerParams(vmem_limit_bytes=56 * MIB),
        cost_estimate=pl.CostEstimate(
            flops=4 * total * model * wide, bytes_accessed=24 * MIB, transcendentals=total * wide
        ),
        name="hidden",
    )(at, own, other, packed)


THIRDS = ((0, 1, 2), (1, 2, 0), (2, 0, 1))


def group_spans(features, count):
    tiles = features // LANES
    cuts = [-(-tiles * at // count) * LANES for at in range(count + 1)]
    return [slice(lo, hi) for lo, hi in zip(cuts, cuts[1:])]


def stage_axis(order, stage):
    return sum(1 for bit in order[stage:] if bit < order[stage])


def half_spans(rows, axis, side):
    size = rows >> (axis + 1)
    return [slice((2 * at + side) * size, (2 * at + side + 1) * size) for at in range(1 << axis)]


def down_kernel(rows, side, orders, own_h, other_h, own_ref, other_ref, *refs):
    out_refs, (own_w, other_w) = refs[:-2], refs[-2:]
    for in_ref, w_ref in ((own_ref, own_w), (other_ref, other_w)):
        for at in range(in_ref.shape[0]):
            unpack_rows(in_ref, at, 0, rows, w_ref, at * rows, 0)
    dims = (((1,), (1,)), ((), ()))
    for number, span in enumerate(group_spans(own_w.shape[0], len(orders))):
        done = 0
        for tokens in half_spans(own_h.shape[0], stage_axis(orders[number], 0), side):
            value = lax.dot_general(
                own_h[tokens, :], own_w[span, :], dims, preferred_element_type=jnp.float32
            ) + lax.dot_general(
                other_h[tokens, :], other_w[span, :], dims, preferred_element_type=jnp.float32
            )
            size = tokens.stop - tokens.start
            out_refs[number][done : done + size, :] = value.astype(out_refs[number].dtype)
            done += size


def down_product(own_h, other_h, own, other, rows, side, orders, dtype, name):
    sources = own.shape[0]
    total, wide = own_h.shape
    tokens = total // 2
    features = sources * rows
    shapes = [
        jax.ShapeDtypeStruct((tokens, span.stop - span.start), dtype)
        for span in group_spans(features, len(orders))
    ]
    return pl.pallas_call(
        functools.partial(down_kernel, rows, side, orders),
        out_shape=shapes,
        in_specs=[vmem()] * 4,
        out_specs=[vmem()] * len(shapes),
        scratch_shapes=[pltpu.VMEM((features, wide), own.dtype)] * 2,
        compiler_params=pltpu.CompilerParams(vmem_limit_bytes=40 * MIB),
        cost_estimate=pl.CostEstimate(
            flops=4 * tokens * wide * features, bytes_accessed=8 * MIB, transcendentals=0
        ),
        name=name,
    )(own_h, other_h, own, other)


def halve_kernel(axes, *refs):
    count = len(refs) // 4 if axes else len(refs) // 2 - 1
    out_refs = refs[2 * count :]
    lane = 0
    for number in range(count):
        keep_ref, come_ref = refs[2 * number : 2 * number + 2]
        if axes:
            send_ref, left_ref = out_refs[2 * number : 2 * number + 2]
            lanes = slice(0, keep_ref.shape[1])
        else:
            send_ref, left_ref = out_refs
            lanes = slice(lane, lane + keep_ref.shape[1])
            lane = lanes.stop
        axis = axes[number] if axes else 0
        for side, out_ref in enumerate((left_ref, send_ref)):
            done = 0
            for rows in half_spans(keep_ref.shape[0], axis, side):
                size = rows.stop - rows.start
                total = keep_ref[rows, :] + come_ref[rows, :].astype(jnp.float32)
                out_ref[done : done + size, lanes] = total.astype(out_ref.dtype)
                done += size


def halve(pairs, axes):
    sizes = [(keep.shape[0] // 2, keep.shape[1]) for keep, _ in pairs]
    if not axes:
        sizes = [(sizes[0][0], sum(width for _, width in sizes))]
    shapes = []
    for size in sizes:
        shapes += [jax.ShapeDtypeStruct(size, jnp.bfloat16), jax.ShapeDtypeStruct(size, jnp.float32)]
    out = pl.pallas_call(
        functools.partial(halve_kernel, axes),
        out_shape=shapes,
        in_specs=[vmem()] * (2 * len(pairs)),
        out_specs=[vmem()] * len(shapes),
        compiler_params=pltpu.CompilerParams(vmem_limit_bytes=40 * MIB),
        cost_estimate=pl.CostEstimate(
            flops=sum(keep.size for keep, _ in pairs), bytes_accessed=4 * MIB, transcendentals=0
        ),
        name="sum_stage",
    )(*[value for pair in pairs for value in pair])
    return [(out[2 * n], out[2 * n + 1]) for n in range(len(out) // 2)]


def swap(value, bit):
    size = lax.axis_size("ep")
    return lax.ppermute(value, "ep", [(i, i ^ (1 << bit)) for i in range(size)])


def gather_bits(value, bits, order, have=()):
    have = list(have)
    for bit in order:
        axis = sum(1 for b in have if b < bit)
        value = jnp.stack([value, swap(value, bit)], axis=axis)
        have.append(bit)
    return value


def take_half(value, axis, number):
    return lax.index_in_dim(value, number, axis, keepdims=False)


def sum_stages(keep, arrived, order, left):
    left = list(left)
    for bit in order:
        axis = left.index(bit)
        total = keep + arrived.astype(jnp.float32)
        arrived = swap(take_half(total, axis, 1).astype(jnp.bfloat16), bit)
        keep = take_half(total, axis, 0)
        left.remove(bit)
    return keep, arrived


def share_of_slots(slot_ids, gate_weights, slots):
    index = jnp.arange(slots, dtype=jnp.int32)
    picked = slot_ids.T[None, :, :] == index[:, None, None]
    return jnp.sum(jnp.where(picked, gate_weights.T[None, :, :], 0.0), axis=1)


def packed_layer(
    tokens, slot_ids, gate_weights, old_expert, new_expert, gate_proj, up_proj, down_proj
):
    devices = lax.axis_size("ep")
    slots, depth, width = gate_proj.shape
    block = tokens.shape[0]
    me = lax.axis_index("ep")
    core = lax.axis_index("et")
    group = devices // 2
    tie = lax.optimization_barrier
    _, listing, slot_place = distinct_sources(old_expert, new_expert)

    def exchange(value):
        return lax.ppermute(value, "et", [(0, 1), (1, 0)])

    def move(packed):
        return lax.all_to_all(packed, "ep", 0, 0, tiled=True)

    places = []
    for dest in range(devices):
        first, half, _ = units_of(dest)
        places.append([unit // (width // LANES) for unit in (first, first + 1, first + 2, half)] * 4)
    places = jnp.asarray(places, jnp.int32)
    share = share_of_slots(slot_ids, gate_weights, slots)
    belongs = slot_place[None, None, :, None] == places[:, :, None, None]
    share = jnp.sum(jnp.where(belongs, share[None, None], 0.0), axis=2)

    def diagonal(value):
        return lax.ppermute(value, "ep", [(i, i ^ 3) for i in range(devices)])

    mid = tokens.shape[1] // 2
    near, far = swap(tokens, 2), swap(tokens, 3)
    x_own, y_own, xy_own = swap(tokens, 0), swap(tokens, 1), diagonal(tokens)
    parts = (128, 96)
    packed = pack_first(listing, gate_proj, up_proj, down_proj, parts[0], share, devices)
    far, packed = tie((far, packed))
    corner = swap(far, 2)
    pair = jnp.concatenate([far, near], axis=0)
    pair_y, pair_x = swap(pair[:, :mid], 1), swap(pair[:, mid:], 0)
    packed, x_own, y_own, xy_own, pair, corner, pair_y, pair_x = tie(
        (packed, x_own, y_own, xy_own, pair, corner, pair_y, pair_x)
    )

    moved = move(packed)
    corner_a, corner_b = corner[:, :mid], corner[:, mid:]
    cross = diagonal(corner)
    most_a = swap(jnp.concatenate([pair[:, :mid], corner_a, pair_y], axis=0), 0)
    most_b = swap(jnp.concatenate([pair[:, mid:], corner_b, pair_x], axis=0), 1)
    corner_y, corner_x = swap(corner_a, 1), swap(corner_b, 0)

    def lay(*values):
        return jnp.concatenate(values, axis=0)

    three, two = slice(0, 3 * block), slice(3 * block, 5 * block)
    first, second = slice(0, mid), slice(mid, 2 * mid)
    rows = jnp.concatenate(
        [
            lay(
                tokens[:, first], pair[:, first], corner_a,
                y_own[:, first], pair_y, corner_y,
                x_own[:, first], most_a[three],
                xy_own[:, first], most_a[two], cross[:, first],
            ),
            lay(
                tokens[:, second], pair[:, second], corner_b,
                y_own[:, second], most_b[three],
                x_own[:, second], pair_x, corner_x,
                xy_own[:, second], most_b[two], cross[:, second],
            ),
        ],
        axis=1,
    )
    rows_other = exchange(rows)
    rest = pack_rest(listing, down_proj, parts[0], devices)
    moved, rest, rows, rows_other = tie((moved, rest, rows, rows_other))

    down1 = move(rest)
    at = jnp.stack([me, core]).astype(jnp.int32)
    hidden = hidden_units(at, rows, rows_other, moved)
    hidden_other = exchange(hidden)
    down0 = moved[:, depth * 7 : depth * 7 + parts[0] * 7 // 2]

    def products(down, rows_in, orders, before=None):
        own = lax.dynamic_slice_in_dim(down, core * group, group, 0)
        other = exchange(lax.dynamic_slice_in_dim(down, (1 - core) * group, group, 0))
        args, _ = tie(((hidden, hidden_other, own, other), before))
        sent = down_product(*args, rows_in, 1, orders, jnp.bfloat16, "down_send")
        sent, args = tie((sent, args))
        come = [swap(value, order[0]) for value, order in zip(sent, orders)]
        kept = down_product(*args, rows_in, 0, orders, jnp.float32, "down_keep")
        return kept, come, sent

    def stage(kept, come, number, orders):
        axes = tuple(stage_axis(order, number) for order in orders)
        out = halve(list(zip(kept, come)), axes)
        come = [swap(send, order[number]) for (send, _), order in zip(out, orders)]
        return [keep for _, keep in out], come

    def last_stage(kept, come):
        ((send, keep),) = halve(list(zip(kept, come)), None)
        come = swap(send, 3)
        return (keep + come.astype(jnp.float32)).astype(jnp.bfloat16)

    kept0, come0, sent0 = products(down0, parts[0], THIRDS)
    down1, _ = tie((down1, sent0))
    kept1, come1, _ = products(down1, parts[1], THIRDS, before=come0)
    kept0, come0 = stage(kept0, come0, 1, THIRDS)
    kept1, come1 = stage(kept1, come1, 1, THIRDS)
    kept0, come0 = stage(kept0, come0, 2, THIRDS)
    kept1, come1 = stage(kept1, come1, 2, THIRDS)
    out = []
    for rows_in, total in zip(parts, (last_stage(kept0, come0), last_stage(kept1, come1))):
        out.append(total.reshape(block, group, rows_in))
    return jnp.concatenate(out, axis=2).reshape(tokens.shape)


def plain_layer(
    tokens, slot_ids, gate_weights, old_expert, new_expert, gate_proj, up_proj, down_proj
):
    devices = lax.axis_size("ep")
    bits = devices.bit_length() - 1
    slots = gate_proj.shape[0]
    me = lax.axis_index("ep")
    source, _, _ = distinct_sources(old_expert, new_expert)

    def move(weights):
        chosen = jnp.take(weights, source, axis=0, mode="clip")
        return lax.all_to_all(chosen, "ep", 0, 0, tiled=True)

    gate_slab = move(gate_proj).reshape(-1, gate_proj.shape[-1])
    up_slab = move(up_proj).reshape(-1, up_proj.shape[-1])
    down = move(down_proj)
    order = range(bits - 1, -1, -1)
    rows = gather_bits(tokens, bits, order).reshape(-1, tokens.shape[1])
    rows = lax.all_gather(rows, "et", axis=1, tiled=True)
    share = gather_bits(share_of_slots(slot_ids, gate_weights, slots), bits, order)
    share = lax.dynamic_index_in_dim(share, me, bits, keepdims=False).reshape(-1, 1)
    gate_part = jnp.dot(rows, gate_slab, preferred_element_type=jnp.float32)
    up_part = jnp.dot(rows, up_slab, preferred_element_type=jnp.float32)
    hidden = (jax.nn.silu(gate_part) * up_part * share).astype(jnp.bfloat16)
    hidden = lax.all_gather(hidden, "et", axis=1, tiled=True)
    down = lax.all_to_all(down, "et", 0, 2, tiled=True)
    value = lax.dot_general(
        hidden,
        down.reshape(-1, down.shape[-1]),
        (((1,), (1,)), ((), ())),
        preferred_element_type=jnp.float32,
    )
    value = value.reshape((2,) * bits + (-1,) + value.shape[1:])
    arrived = swap(take_half(value, 0, 1).astype(jnp.bfloat16), 0)
    left = list(range(1, bits))
    keep, arrived = sum_stages(take_half(value, 0, 0), arrived, left, left)
    return (keep + arrived.astype(jnp.float32)).astype(jnp.bfloat16)


def per_device(tokens, slot_ids, gate_weights, old_expert, new_expert, gate_proj, up_proj, down_proj):
    slots, depth, width = gate_proj.shape
    count = slots - slots // 8
    devices = lax.axis_size("ep")
    fits = (
        lax.axis_size("et") == 2
        and depth == 224
        and width % LANES == 0
        and count * width == devices * 7 * HALF
        and devices == 16
        and tokens.shape[0] == LANES
    )
    layer = packed_layer if fits else plain_layer
    return layer(
        tokens, slot_ids, gate_weights, old_expert, new_expert, gate_proj, up_proj, down_proj
    )


def solution(mesh):
    placed = (
        P("ep", "et"),
        P("ep", None),
        P("ep", None),
        P(),
        P(),
        P(None, "ep", "et"),
        P(None, "ep", "et"),
        P(None, "ep", "et"),
    )
    return jax.shard_map(
        per_device, mesh=mesh, in_specs=placed, out_specs=P("ep", "et"), check_vma=False
    )
```
